512 devices in a mesh: box: 512 (over x, z, y, core).
Axes of the slice: x: 4, y: 8, z: 8, core: 2. Of those that a mesh axis runs over, the one named last changes fastest.
Arguments:
- coords: float32 [3, 1048576], P(None, 'box'), may hold values from 0 to 1
- loads: bfloat16 [8, 1048576], P(None, 'box'), may hold values from -6 to 6
- occupancy: int32 [4096], P('box'), may hold values from 64 to 256, as said below
- basis: bfloat16 [4096, 64, 256], P('box'), may hold values from -0.375 to 0.375
- transfer: float32 [6, 2, 64, 64], replicated, may hold values from -0.5 to 0.5
Outputs:
- potential: float32 [8, 1048576], P(None, 'box')
The draws below stay inside these ranges and needn't reach their ends.
Inputs may be any that keep to these rules, and one draw needn't show every extreme that they name: occupancy[l] is the number of live centres of leaf l; they fill its first slots, and every leaf keeps at least its 64 skeleton centres.
All inputs are finite; a program needn't handle non-finite values.
Results may differ from the reference program's by a relative error of at most 0.0029.
Values sent between devices are 32-bit elements; how exact they have to be, the bound alone decides.
A program may use at most 64 MiB of HBM per device.

```python
import math
import jax
import jax.numpy as jnp
from jax import lax

LEAF_PTS = 256
SKEL = 64
COLS = 8
LEVELS = 6
LEAVES = 4096
NPTS = 1048576


def draw_coords(key, part):
    key = jax.random.fold_in(key, 11)
    centre_key, scale_key, offset_key = jax.random.split(key, 3)
    centre = jax.random.uniform(centre_key, (3, 1), jnp.float32, 0.35, 0.65)
    spread = jnp.exp(jax.random.uniform(scale_key, (1, NPTS), jnp.float32, math.log(0.003), math.log(0.35)))
    offset = jax.random.uniform(offset_key, (3, NPTS), jnp.float32, -1.0, 1.0)
    return centre + spread * offset


def draw_occupancy(key, part):
    key = jax.random.fold_in(key, 7)
    first_key, second_key = jax.random.split(key)
    partial_fill = jax.random.randint(first_key, (LEAVES,), SKEL, LEAF_PTS + 1)
    full_leaf = jax.random.randint(second_key, (LEAVES,), 0, 4) == 0
    counts = jnp.where(full_leaf, LEAF_PTS, partial_fill)
    return counts.at[0].set(LEAF_PTS).astype(jnp.int32)


def block_levels(key, dims, shards, low, largest):
    factor_of = 1.0
    for axis_at, shards_of in shards:
        draws = jax.random.uniform(jax.random.fold_in(jax.random.fold_in(key, 6), axis_at), (shards_of,), jnp.float32, low / len(shards), largest / len(shards))
        factor_of = factor_of * jnp.repeat(jnp.exp(draws), dims[axis_at] // shards_of).reshape((-1,) + (1,) * (len(dims) - 1 - axis_at))
    return factor_of


def normal_values(own_key, dims, scale, bound, pieces=(), kind=jnp.bfloat16):
    entries = jax.random.normal(own_key, dims, jnp.float32) * scale
    if len(pieces) > 0:
        entries = block_levels(own_key, dims, pieces, -0.22, 0.18) * entries
    return jnp.clip(entries, min=-bound, max=bound).astype(kind)


def setup_inputs(seed: int = 0) -> dict:
    splits = jax.random.split(jax.random.key(seed), 6)
    coords = draw_coords(jax.random.fold_in(splits[5], 71), 0)
    loads = normal_values(splits[1], (COLS, NPTS), 1.0, 6.0, ((1, 512),))
    occupancy = draw_occupancy(jax.random.fold_in(splits[5], 71), 0)
    basis = normal_values(splits[3], (LEAVES, SKEL, LEAF_PTS), LEAF_PTS ** -0.5, 0.375, ((0, 512),))
    transfer = normal_values(splits[4], (LEVELS, 2, SKEL, SKEL), (2 * SKEL) ** -0.5, 0.5, (), jnp.float32)
    return {"coords": coords, "loads": loads, "occupancy": occupancy, "basis": basis, "transfer": transfer}


soften = 1e-4
near_scale = 0.0625
far_scale = 0.125
highest = lax.Precision.HIGHEST
cousin_offsets = ((-3, 0.0, 1.0), (-2, 1.0, 1.0), (2, 1.0, 1.0), (3, 1.0, 0.0))


def spline(receivers, emitters):
    delta_x = receivers[..., 0, :, None] - emitters[..., 0, None, :]
    delta_y = receivers[..., 1, :, None] - emitters[..., 1, None, :]
    delta_z = receivers[..., 2, :, None] - emitters[..., 2, None, :]
    squared = delta_x * delta_x + delta_y * delta_y + delta_z * delta_z
    return 0.5 * squared * jnp.log(squared + soften)


def coupling(source_coef, source_skel, target_skel):
    kernel_tile = spline(source_skel, target_skel) * far_scale
    return jnp.einsum("bcs,bst->bct", source_coef, kernel_tile, precision=highest)


def raise_level(coefficients, skeleton, level_maps):
    raised = jnp.einsum("bcs,st->bct", coefficients[0::2], level_maps[0], precision=highest)
    raised = raised + jnp.einsum("bcs,st->bct", coefficients[1::2], level_maps[1], precision=highest)
    skel_up = jnp.concatenate([skeleton[0::2][:, :, 0::2], skeleton[1::2][:, :, 0::2]], axis=2)
    return raised, skel_up


def cousin_level(coefficients, skeleton):
    box_count = coefficients.shape[0]
    pad_coef = jnp.pad(coefficients, ((3, 3), (0, 0), (0, 0)))
    pad_skel = jnp.pad(skeleton, ((3, 3), (0, 0), (0, 0)))
    parity = jnp.arange(box_count, dtype=jnp.int32) % 2
    summed = jnp.zeros_like(coefficients)
    for offset, even_weight, odd_weight in cousin_offsets:
        weight = jnp.where(parity == 0, even_weight, odd_weight).astype(jnp.float32)
        contribution = coupling(pad_coef[3 + offset:3 + offset + box_count], pad_skel[3 + offset:3 + offset + box_count], skeleton)
        summed = summed + weight[:, None, None] * contribution
    return summed


def top_level(coefficients, skeleton):
    box_count = coefficients.shape[0]
    box_index = jnp.arange(box_count, dtype=jnp.int32)

    def one_target(target):
        weight = (jnp.abs(box_index - target) >= 2).astype(jnp.float32)
        own_skel = lax.dynamic_index_in_dim(skeleton, target, 0, keepdims=True)
        kernel_tile = spline(skeleton, own_skel) * far_scale
        return jnp.einsum("bcs,bst->ct", coefficients * weight[:, None, None], kernel_tile, precision=highest)

    return lax.map(one_target, box_index)


def reference(coords, loads, occupancy, basis, transfer):
    slots = jnp.arange(LEAF_PTS, dtype=jnp.int32)[None, :]
    live_mask = slots < occupancy[:, None]
    leaf_loads = loads.reshape(COLS, LEAVES, LEAF_PTS).transpose(1, 0, 2)
    live = jnp.where(live_mask[:, None, :], leaf_loads, jnp.zeros((), jnp.bfloat16))
    targets = coords.reshape(3, LEAVES, LEAF_PTS).transpose(1, 0, 2)
    pad_targets = jnp.pad(targets, ((1, 1), (0, 0), (0, 0)))
    sources = jnp.concatenate([pad_targets[:-2], pad_targets[1:-1], pad_targets[2:]], axis=2)
    pad_live = jnp.pad(live, ((1, 1), (0, 0), (0, 0)))
    source_loads = jnp.concatenate([pad_live[:-2], pad_live[1:-1], pad_live[2:]], axis=2)
    leaf_block = min(64, LEAVES)
    block_count = LEAVES // leaf_block

    def near_block(block_items):
        target_block, source_block, load_block = block_items
        kernel_tile = (spline(target_block, source_block) * near_scale).astype(jnp.bfloat16)
        kernel_tile = lax.optimization_barrier(kernel_tile).astype(jnp.float32)
        return jnp.einsum("lts,lcs->lct", kernel_tile, load_block.astype(jnp.float32))

    near_field = lax.map(near_block, (
        targets.reshape(block_count, leaf_block, 3, LEAF_PTS),
        sources.reshape(block_count, leaf_block, 3, 3 * LEAF_PTS),
        source_loads.reshape(block_count, leaf_block, COLS, 3 * LEAF_PTS))).reshape(LEAVES, COLS, LEAF_PTS)

    coefficients = jnp.einsum("lcp,lsp->lcs", live.astype(jnp.float32), basis.astype(jnp.float32))
    skeleton = targets[:, :, :SKEL]
    coef_levels = [coefficients]
    skel_levels = [skeleton]
    for tree_level in range(1, LEVELS + 1):
        coefficients, skeleton = raise_level(coefficients, skeleton, transfer[tree_level - 1])
        coef_levels.append(coefficients)
        skel_levels.append(skeleton)
    local_terms = [cousin_level(coef_levels[index], skel_levels[index]) for index in range(LEVELS)]
    local_terms.append(top_level(coef_levels[LEVELS], skel_levels[LEVELS]))
    downward = local_terms[LEVELS]
    for tree_level in range(LEVELS, 0, -1):
        level_maps = transfer[tree_level - 1]
        left_part = jnp.einsum("bct,st->bcs", downward, level_maps[0], precision=highest)
        right_part = jnp.einsum("bct,st->bcs", downward, level_maps[1], precision=highest)
        downward = local_terms[tree_level - 1] + jnp.stack([left_part, right_part], axis=1).reshape(-1, COLS, SKEL)
    rounded = lax.optimization_barrier(downward.astype(jnp.bfloat16)).astype(jnp.float32)
    far_field = jnp.einsum("lcs,lsp->lcp", rounded, basis.astype(jnp.float32))
    potential = jnp.where(live_mask[:, None, :], near_field + far_field, 0.0)
    return potential.transpose(1, 0, 2).reshape(COLS, NPTS)
```

```python
import functools

import jax
import jax.numpy as jnp
from jax import lax
from jax.experimental import pallas as pl
from jax.experimental.pallas import tpu as pltpu
from jax.sharding import PartitionSpec as P

LEAF = 256
COLS = 8
LEAVES = 8
MEMBERS = 8
OWN = LEAF * LEAVES

f32 = jnp.float32
bf16 = jnp.bfloat16
soften = 0.0001
near_scale = 0.0625
far_scale = 0.125
NN = (((1,), (0,)), ((), ()))
NT = (((1,), (1,)), ((), ()))
MESH = pl.DeviceIdType.MESH


def phi(tx, ty, tz, sx, sy, sz, scale):
    dx = tx - sx
    dy = ty - sy
    dz = tz - sz
    r2 = dx * dx + dy * dy + dz * dz
    return (r2 * (0.5 * scale)) * jnp.log(r2 + soften)


def split(x):
    high = x.astype(bf16)
    return high, (x - high.astype(f32)).astype(bf16)


def mm(a, b, dims):
    rows = a.shape[0]
    high = a.astype(bf16).astype(f32)
    stacked = jnp.concatenate([high, a - high], axis=0).astype(bf16)
    both = lax.dot_general(stacked, b[0], dims, preferred_element_type=f32)
    low = lax.dot_general(stacked[:rows], b[1], dims, preferred_element_type=f32)
    return both[:rows] + (both[rows:] + low)


def low_half(shape):
    return lax.broadcasted_iota(jnp.int32, shape, len(shape) - 1) < 64


def merge(rows):
    count = rows.shape[0] // 16
    low = low_half((8, 128))
    return [
        jnp.where(low, rows[16 * i : 16 * i + 8], rows[16 * i + 8 : 16 * i + 16])
        for i in range(count)
    ]


def raise_coef(pairs, level_map):
    rows = mm(jnp.concatenate(pairs, axis=0), level_map, NN)
    return merge(rows) if len(pairs) > 1 else [rows]


def raise_skel(pairs, every_second):
    x = jnp.concatenate(pairs, axis=0)
    rows = x.shape[0]
    a = x.astype(bf16).astype(f32)
    b = (x - a).astype(bf16).astype(f32)
    c = (x - a) - b
    stacked = jnp.concatenate([a, b, c], axis=0).astype(bf16)
    picked = lax.dot_general(stacked, every_second, NN, preferred_element_type=f32)
    rows_up = picked[:rows] + picked[rows : 2 * rows] + picked[2 * rows :]
    return merge(rows_up) if len(pairs) > 1 else [rows_up]


def cousins(target, left, right):
    low = low_half((8, 128))
    column = target.T
    tx, ty, tz = column[:, 0:1], column[:, 1:2], column[:, 2:3]
    tiles = []
    for _, skel in (left, right):
        tiles.append(phi(tx, ty, tz, skel[0:1], skel[1:2], skel[2:3], far_scale))
    tile = jnp.concatenate(tiles, axis=1)
    before, after = left[0], right[0]
    even = jnp.concatenate([jnp.where(low, before, 0.0), after], axis=1)
    odd = jnp.concatenate([before, jnp.where(low, 0.0, after)], axis=1)
    rows = mm(jnp.concatenate([even, odd], axis=0), split(tile), NT)
    return jnp.where(low, rows[:8], rows[8:])


def lower(pairs, level_map):
    low = low_half((8, 128))
    stacked = []
    for pair in pairs:
        stacked += [jnp.where(low, pair, 0.0), jnp.where(low, 0.0, pair)]
    rows = mm(jnp.concatenate(stacked, axis=0), level_map, NT)
    return [rows[8 * i : 8 * i + 8] for i in range(2 * len(pairs))]


def kernel(
    boxes,
    coords_ref,
    loads_ref,
    occ_ref,
    basis_hbm,
    transfer_hbm,
    out_ref,
    basis,
    transfer,
    field,
    column,
    near,
    tile,
    edge_send,
    edge_recv,
    g_buf,
    g3,
    g4,
    bound_send,
    bound_recv,
    far_send,
    far_buf,
    part_buf,
    load_sem,
    near_send_sem,
    near_recv_sem,
    edge_send_sem,
    edge_recv_sem,
    g_send_sem,
    g_recv_sem,
    bound_send_sem,
    bound_recv_sem,
    far_send_sem,
    far_recv_sem,
    part_send_sem,
    part_recv_sem,
):
    device = lax.axis_index("box")
    total = boxes * MEMBERS
    box = device // MEMBERS
    member = device % MEMBERS
    low = low_half((8, 128))
    half = lax.broadcasted_iota(jnp.int32, (8, 128), 1) // 64

    basis_copy = pltpu.make_async_copy(basis_hbm, basis, load_sem.at[0])
    transfer_copy = pltpu.make_async_copy(transfer_hbm, transfer, load_sem.at[1])
    basis_copy.start()
    transfer_copy.start()

    left_device = (device + total - 1) % total
    right_device = (device + 1) % total
    left_box = ((box + boxes - 1) % boxes) * MEMBERS + member
    right_box = ((box + 1) % boxes) * MEMBERS + member
    mates = [box * MEMBERS + (member + r) % MEMBERS for r in range(1, MEMBERS)]
    strides = boxes // MEMBERS
    far_to = [
        (((box // MEMBERS + k) % strides) * MEMBERS + member) * MEMBERS + box % MEMBERS
        for k in range(strides)
    ]
    far_from = [
        ((box // MEMBERS + strides - k) % strides) * MEMBERS + member for k in range(strides)
    ]
    alone = box % MEMBERS == member

    barrier = pltpu.get_barrier_semaphore()

    def greet(target):
        pl.semaphore_signal(barrier, inc=1, device_id=(target,), device_id_type=MESH)

    for target in [left_device, right_device, left_box, right_box] + mates:
        greet(target)
    for k in range(1, strides):
        greet(far_from[k] * MEMBERS + box % MEMBERS)

    @pl.when(jnp.logical_not(alone))
    def _():
        greet(far_from[0] * MEMBERS + box % MEMBERS)

    points = jnp.concatenate([coords_ref[...], jnp.zeros((5, OWN), f32)], axis=0)
    field[0, :, LEAF : LEAF + OWN] = points
    slots = lax.broadcasted_iota(jnp.int32, (COLS, LEAF), 1)
    live = []
    for leaf in range(LEAVES):
        part = loads_ref[:, leaf * LEAF : (leaf + 1) * LEAF].astype(f32)
        part = jnp.where(slots < occ_ref[leaf], part, 0.0)
        field[1, :, (leaf + 1) * LEAF : (leaf + 2) * LEAF] = part
        live.append(part)
    for at in range(0, OWN, 128):
        column[at : at + 128, :] = points[:, at : at + 128].T
    near[...] = jnp.zeros_like(near)

    picks = lax.broadcasted_iota(jnp.int32, (128, 128), 1) % 64 * 2
    every_second = (
        (lax.broadcasted_iota(jnp.int32, (128, 128), 0) == picks).astype(f32).astype(bf16)
    )
    s0 = [
        jnp.concatenate(
            [points[:, 512 * p : 512 * p + 64], points[:, 512 * p + 256 : 512 * p + 320]], axis=1
        )
        for p in range(4)
    ]
    s1 = raise_skel(s0, every_second)
    s2 = raise_skel(s1, every_second)
    s3 = raise_skel(s2, every_second)[0]

    transfer_copy.wait()
    maps = []
    for level in range(6):
        once = transfer[level]
        maps.append(split(jnp.concatenate([once, once], axis=1)))
    basis_copy.wait()
    c0 = []
    for p in range(4):
        two = jnp.concatenate([live[2 * p], live[2 * p + 1]], axis=0).astype(bf16)
        rows = lax.dot_general(
            two, basis[128 * p : 128 * p + 128, :], NT, preferred_element_type=f32
        )
        c0.append(jnp.where(low, rows[:8], rows[8:]))
    c1 = raise_coef(c0, maps[0])
    c2 = raise_coef(c1, maps[1])
    c3 = raise_coef(c2, maps[2])[0]

    g_buf[member] = jnp.where(half == member % 2, c3, s3)
    for at, pair in enumerate([c0[3], c1[1], c2[0], s0[3], s1[1], s2[0]]):
        edge_send[0, at] = pair
    for at, pair in enumerate([c0[0], c1[0], c2[0], s0[0], s1[0], s2[0]]):
        edge_send[1, at] = pair

    pl.semaphore_wait(barrier, 4 + MEMBERS - 1 + strides - alone.astype(jnp.int32))

    started = []

    def send(src, dst, send_sem, recv_sem, target):
        copy = pltpu.make_async_remote_copy(
            src_ref=src,
            dst_ref=dst,
            send_sem=send_sem,
            recv_sem=recv_sem,
            device_id=(target,),
            device_id_type=MESH,
        )
        copy.start()
        started.append(copy)
        return copy

    g_copies = []
    for r, mate in enumerate(mates):
        g_copies.append(
            send(g_buf.at[member], g_buf.at[member], g_send_sem.at[r], g_recv_sem.at[r], mate)
        )
    last = LEAF * LEAVES
    near_copies = [
        send(
            field.at[:, :, last : last + LEAF],
            field.at[:, :, 0:LEAF],
            near_send_sem.at[0],
            near_recv_sem.at[0],
            right_device,
        ),
        send(
            field.at[:, :, LEAF : 2 * LEAF],
            field.at[:, :, last + LEAF : last + 2 * LEAF],
            near_send_sem.at[1],
            near_recv_sem.at[1],
            left_device,
        ),
    ]
    edge_copies = [
        send(
            edge_send.at[0],
            edge_recv.at[0],
            edge_send_sem.at[0],
            edge_recv_sem.at[0],
            right_device,
        ),
        send(
            edge_send.at[1], edge_recv.at[1], edge_send_sem.at[1], edge_recv_sem.at[1], left_device
        ),
    ]

    def fill_tile(row, col, width):
        sx = field[0, 0:1, pl.ds(col, width)]
        sy = field[0, 1:2, pl.ds(col, width)]
        sz = field[0, 2:3, pl.ds(col, width)]
        for at in range(0, LEAF, 16):
            rows = column[pl.ds(row + at, 16), :]
            tile[at : at + 16, 0:width] = phi(
                rows[:, 0:1], rows[:, 1:2], rows[:, 2:3], sx, sy, sz, near_scale
            ).astype(bf16)

    def near_step(leaf, carry):
        row = pl.multiple_of(leaf * LEAF, LEAF)
        col = pl.multiple_of(row + LEAF, LEAF)
        fill_tile(row, col, 2 * LEAF)
        loads_two = field[1, :, pl.ds(col, 2 * LEAF)].astype(bf16)
        near[:, pl.ds(row, LEAF)] += lax.dot_general(
            loads_two, tile[...], NT, preferred_element_type=f32
        )
        near[:, pl.ds(col, LEAF)] += lax.dot_general(
            loads_two[:, :LEAF], tile[:, LEAF:], NN, preferred_element_type=f32
        )
        return carry

    lax.fori_loop(0, 4, near_step, 0)

    for copy in g_copies:
        copy.wait_recv()
    c3s, s3s = [], []
    for p in range(4):
        even, odd = g_buf[2 * p], g_buf[2 * p + 1]
        c3s.append(jnp.where(low, even, odd))
        s3s.append(pltpu.roll(jnp.where(low, odd, even), 64, 1))
    c4s, s4s = raise_coef(c3s, maps[3]), raise_skel(s3s, every_second)
    c5, s5 = raise_coef(c4s, maps[4])[0], raise_skel(s4s, every_second)[0]
    c6, s6 = raise_coef([c5], maps[5])[0], raise_skel([s5], every_second)[0]
    far_send[...] = jnp.where(low, c6, s6)

    @pl.when(alone)
    def _():
        far_buf[0] = far_send[...]

    far_copies = []
    for k in range(1, strides):
        far_copies.append(
            send(far_send, far_buf.at[k], far_send_sem.at[k], far_recv_sem.at[k], far_to[k])
        )
    first_far = pltpu.make_async_remote_copy(
        src_ref=far_send,
        dst_ref=far_buf.at[0],
        send_sem=far_send_sem.at[0],
        recv_sem=far_recv_sem.at[0],
        device_id=(far_to[0],),
        device_id_type=MESH,
    )

    @pl.when(jnp.logical_not(alone))
    def _():
        first_far.start()

    for at, pair in enumerate([c3s[3], c4s[1], c5, s3s[3], s4s[1], s5]):
        bound_send[0, at] = pair
    for at, pair in enumerate([c3s[0], c4s[0], c5, s3s[0], s4s[0], s5]):
        bound_send[1, at] = pair
    bound_copies = [
        send(
            bound_send.at[0],
            bound_recv.at[0],
            bound_send_sem.at[0],
            bound_recv_sem.at[0],
            right_box,
        ),
        send(
            bound_send.at[1], bound_recv.at[1], bound_send_sem.at[1], bound_recv_sem.at[1], left_box
        ),
    ]
    for p in range(4):
        g3[p + 1, 0] = c3s[p]
        g3[p + 1, 1] = s3s[p]
    for p in range(2):
        g4[p + 1, 0] = c4s[p]
        g4[p + 1, 1] = s4s[p]

    lax.fori_loop(4, 7, near_step, 0)

    for copy in near_copies:
        copy.wait_recv()

    @pl.when(device == 0)
    def _():
        field[1, :, 0:LEAF] = jnp.zeros((COLS, LEAF), f32)

    @pl.when(device == total - 1)
    def _():
        field[1, :, last + LEAF : last + 2 * LEAF] = jnp.zeros((COLS, LEAF), f32)

    lax.fori_loop(7, 8, near_step, 0)
    fill_tile(0, 0, LEAF)
    near[:, 0:LEAF] += lax.dot_general(
        field[1, :, 0:LEAF].astype(bf16), tile[:, :LEAF], NT, preferred_element_type=f32
    )

    for copy in edge_copies:
        copy.wait_recv()
    before = [(jnp.where(device == 0, 0.0, edge_recv[0, i]), edge_recv[0, i + 3]) for i in range(3)]
    after = [
        (jnp.where(device == total - 1, 0.0, edge_recv[1, i]), edge_recv[1, i + 3])
        for i in range(3)
    ]
    local = []
    for level, (coefs, skels) in enumerate([(c0, s0), (c1, s1), (c2, s2)]):
        chain = [before[level]] + list(zip(coefs, skels)) + [after[level]]
        local.append(
            [cousins(skels[p], chain[p], chain[p + 2]) for p in range(len(skels))]
        )

    for copy in far_copies:
        copy.wait_recv()

    @pl.when(jnp.logical_not(alone))
    def _():
        first_far.wait_recv()

    top_coef, top_skel = [], []
    for k in range(0, strides, 2):
        halves = []
        for at in (k, k + 1):
            apart = far_from[at] - box
            counts = jnp.logical_or(apart >= 2, apart <= -2)
            halves.append((far_buf[at], counts))
        (one, one_counts), (two, two_counts) = halves
        top_coef.append(
            jnp.where(
                low,
                jnp.where(one_counts, one, 0.0),
                jnp.where(two_counts, pltpu.roll(two, 64, 1), 0.0),
            )
        )
        top_skel.append(jnp.where(low, pltpu.roll(one, 64, 1), two))
    top_column = s6.T[:64]
    tx, ty, tz = top_column[:, 0:1], top_column[:, 1:2], top_column[:, 2:3]
    top_tile = jnp.concatenate(
        [phi(tx, ty, tz, s[0:1], s[1:2], s[2:3], far_scale) for s in top_skel], axis=1
    )
    top = mm(jnp.concatenate(top_coef, axis=1), split(top_tile), NT)
    part_buf[member] = jnp.concatenate([top, jnp.zeros((8, 64), f32)], axis=1)
    part_copies = []
    for r, mate in enumerate(mates):
        part_copies.append(
            send(
                part_buf.at[member],
                part_buf.at[member],
                part_send_sem.at[r],
                part_recv_sem.at[r],
                mate,
            )
        )

    for copy in bound_copies:
        copy.wait_recv()
    start = [(jnp.where(box == 0, 0.0, bound_recv[0, i]), bound_recv[0, i + 3]) for i in range(3)]
    end = [
        (jnp.where(box == boxes - 1, 0.0, bound_recv[1, i]), bound_recv[1, i + 3])
        for i in range(3)
    ]
    for part in range(2):
        g3[0, part] = start[0][part]
        g3[5, part] = end[0][part]
        g4[0, part] = start[1][part]
        g4[3, part] = end[1][part]
    at3 = member // 2
    at4 = member // 4
    local3 = cousins(
        g3[at3 + 1, 1], (g3[at3, 0], g3[at3, 1]), (g3[at3 + 2, 0], g3[at3 + 2, 1])
    )
    local4 = cousins(
        g4[at4 + 1, 1], (g4[at4, 0], g4[at4, 1]), (g4[at4 + 2, 0], g4[at4 + 2, 1])
    )
    local5 = cousins(s5, start[2], end[2])

    for copy in part_copies:
        copy.wait_recv()
    d6 = part_buf[0]
    for at in range(1, MEMBERS):
        d6 = d6 + part_buf[at]
    d5 = local5 + mm(d6, maps[5], NT)
    d4 = local4 + mm(jnp.where(half == member // 4, d5, 0.0), maps[4], NT)
    d3 = local3 + mm(jnp.where(half == member // 2 % 2, d4, 0.0), maps[3], NT)
    d2 = local[2][0] + mm(jnp.where(half == member % 2, d3, 0.0), maps[2], NT)
    d1 = [a + b for a, b in zip(local[1], lower([d2], maps[1]))]
    d0 = [a + b for a, b in zip(local[0], lower(d1, maps[0]))]
    for p in range(4):
        two = jnp.concatenate([jnp.where(low, d0[p], 0.0), jnp.where(low, 0.0, d0[p])], axis=0)
        rows = lax.dot_general(
            two.astype(bf16),
            basis[128 * p : 128 * p + 128, :],
            NN,
            preferred_element_type=f32,
        )
        for t in range(2):
            at = (2 * p + t) * LEAF
            out_ref[:, at : at + LEAF] = near[:, at : at + LEAF] + rows[8 * t : 8 * t + 8]

    for copy in started:
        copy.wait_send()

    @pl.when(jnp.logical_not(alone))
    def _():
        first_far.wait_send()


def body(boxes, coords, loads, occupancy, basis, transfer):
    strides = boxes // MEMBERS
    vmem = pl.BlockSpec(memory_space=pltpu.VMEM)
    hbm = pl.BlockSpec(memory_space=pl.ANY)
    dma = pltpu.SemaphoreType.DMA
    combined = pl.pallas_call(
        functools.partial(kernel, boxes),
        out_shape=jax.ShapeDtypeStruct((COLS, OWN), f32),
        in_specs=[vmem, vmem, pl.BlockSpec(memory_space=pltpu.SMEM), hbm, hbm],
        out_specs=vmem,
        scratch_shapes=[
            pltpu.VMEM((LEAVES * 64, LEAF), bf16),
            pltpu.VMEM((6, 128, 64), f32),
            pltpu.VMEM((2, 8, OWN + 2 * LEAF), f32),
            pltpu.VMEM((OWN, 8), f32),
            pltpu.VMEM((COLS, OWN + LEAF), f32),
            pltpu.VMEM((LEAF, 2 * LEAF), bf16),
            pltpu.VMEM((2, 6, 8, 128), f32),
            pltpu.VMEM((2, 6, 8, 128), f32),
            pltpu.VMEM((MEMBERS, 8, 128), f32),
            pltpu.VMEM((6, 2, 8, 128), f32),
            pltpu.VMEM((4, 2, 8, 128), f32),
            pltpu.VMEM((2, 6, 8, 128), f32),
            pltpu.VMEM((2, 6, 8, 128), f32),
            pltpu.VMEM((8, 128), f32),
            pltpu.VMEM((strides, 8, 128), f32),
            pltpu.VMEM((MEMBERS, 8, 128), f32),
            dma((2,)),
            dma((2,)),
            dma((2,)),
            dma((2,)),
            dma((2,)),
            dma((MEMBERS - 1,)),
            dma((MEMBERS - 1,)),
            dma((2,)),
            dma((2,)),
            dma((strides,)),
            dma((strides,)),
            dma((MEMBERS - 1,)),
            dma((MEMBERS - 1,)),
        ],
        compiler_params=pltpu.CompilerParams(
            collective_id=0, has_side_effects=True, vmem_limit_bytes=32 * 1024 * 1024
        ),
    )(
        coords,
        loads,
        occupancy,
        basis.reshape(LEAVES * 64, LEAF),
        transfer.reshape(6, 128, 64),
    )
    slots = lax.broadcasted_iota(jnp.int32, (LEAVES, LEAF), 1)
    mask = (slots < occupancy[:, None]).reshape(1, OWN)
    return jnp.where(mask, combined, 0.0)


def solution(mesh):
    boxes = mesh.shape["box"] // MEMBERS
    return jax.shard_map(
        functools.partial(body, boxes),
        mesh=mesh,
        in_specs=(P(None, "box"), P(None, "box"), P("box"), P("box", None, None), P()),
        out_specs=P(None, "box"),
        check_vma=False,
    )
```

```python
import functools

import jax
import jax.numpy as jnp
from jax import lax
from jax.experimental import pallas as pl
from jax.experimental.pallas import tpu as pltpu
from jax.sharding import PartitionSpec as P

LEAF = 256
COLS = 8
LEAVES = 8
MEMBERS = 8
OWN = LEAF * LEAVES

f32 = jnp.float32
bf16 = jnp.bfloat16
soften = 0.0001
near_scale = 0.0625
far_scale = 0.125
NN = (((1,), (0,)), ((), ()))
NT = (((1,), (1,)), ((), ()))
MESH = pl.DeviceIdType.MESH


def phi(tx, ty, tz, sx, sy, sz, scale):
    dx = tx - sx
    dy = ty - sy
    dz = tz - sz
    r2 = dx * dx + dy * dy + dz * dz
    return (r2 * (0.5 * scale)) * jnp.log(r2 + soften)


def split(x):
    high = x.astype(bf16)
    return high, (x - high.astype(f32)).astype(bf16)


def mm(a, b, dims):
    rows = a.shape[0]
    high = a.astype(bf16).astype(f32)
    stacked = jnp.concatenate([high, a - high], axis=0).astype(bf16)
    both = lax.dot_general(stacked, b[0][...], dims, preferred_element_type=f32)
    low = lax.dot_general(stacked[:rows], b[1][...], dims, preferred_element_type=f32)
    return both[:rows] + (both[rows:] + low)


def low_half(shape):
    return lax.broadcasted_iota(jnp.int32, shape, len(shape) - 1) < 64


def merge(rows):
    count = rows.shape[0] // 16
    low = low_half((8, 128))
    return [
        jnp.where(low, rows[16 * i : 16 * i + 8], rows[16 * i + 8 : 16 * i + 16])
        for i in range(count)
    ]


def raise_coef(pairs, level_map):
    rows = mm(jnp.concatenate(pairs, axis=0), level_map, NN)
    return merge(rows) if len(pairs) > 1 else [rows]


def raise_skel(pairs, every_second):
    x = jnp.concatenate(pairs, axis=0)
    rows = x.shape[0]
    a = x.astype(bf16).astype(f32)
    b = (x - a).astype(bf16).astype(f32)
    c = (x - a) - b
    stacked = jnp.concatenate([a, b, c], axis=0).astype(bf16)
    picked = lax.dot_general(stacked, every_second, NN, preferred_element_type=f32)
    rows_up = picked[:rows] + picked[rows : 2 * rows] + picked[2 * rows :]
    return merge(rows_up) if len(pairs) > 1 else [rows_up]


def cousins(chain, slot):
    low = low_half((8, 128))
    column = chain[slot, 1].T
    tx, ty, tz = column[:, 0:1], column[:, 1:2], column[:, 2:3]
    before, after = chain[slot - 1, 0], chain[slot + 1, 0]
    tiles = []
    for skel in (chain[slot - 1, 1], chain[slot + 1, 1]):
        tiles.append(phi(tx, ty, tz, skel[0:1], skel[1:2], skel[2:3], far_scale))
    tile = jnp.concatenate(tiles, axis=1)
    even = jnp.concatenate([jnp.where(low, before, 0.0), after], axis=1)
    odd = jnp.concatenate([before, jnp.where(low, 0.0, after)], axis=1)
    rows = mm(jnp.concatenate([even, odd], axis=0), split(tile), NT)
    return jnp.where(low, rows[:8], rows[8:])


def lower(pairs, level_map):
    height = pairs[0].shape[0]
    low = low_half((height, 128))
    stacked = []
    for pair in pairs:
        stacked += [jnp.where(low, pair, 0.0), jnp.where(low, 0.0, pair)]
    rows = mm(jnp.concatenate(stacked, axis=0), level_map, NT)
    return [rows[height * i : height * (i + 1)] for i in range(2 * len(pairs))]


def kernel(
    boxes,
    coords_hbm,
    loads_hbm,
    occ_hbm,
    basis_hbm,
    transfer_hbm,
    out_ref,
    coords,
    loads,
    occ,
    basis,
    transfer,
    map_high,
    map_low,
    field,
    column,
    near,
    tile,
    chain,
    g_chain,
    local,
    edge_send,
    edge_recv,
    g_buf,
    bound_send,
    bound_recv,
    far_send,
    far_buf,
    part_buf,
    load_sem,
    near_send_sem,
    near_recv_sem,
    edge_send_sem,
    edge_recv_sem,
    g_send_sem,
    g_recv_sem,
    bound_send_sem,
    bound_recv_sem,
    far_send_sem,
    far_recv_sem,
    part_send_sem,
    part_recv_sem,
):
    loading = [
        pltpu.make_async_copy(src, dst, load_sem.at[at])
        for at, (src, dst) in enumerate(
            [
                (coords_hbm, coords),
                (transfer_hbm, transfer),
                (loads_hbm, loads),
                (occ_hbm, occ),
                (basis_hbm, basis),
            ]
        )
    ]
    for copy in loading:
        copy.start()

    device = lax.axis_index("box")
    total = boxes * MEMBERS
    box = device // MEMBERS
    member = device % MEMBERS
    low = low_half((8, 128))
    half = lax.broadcasted_iota(jnp.int32, (8, 128), 1) // 64

    left_device = (device + total - 1) % total
    right_device = (device + 1) % total
    left_box = ((box + boxes - 1) % boxes) * MEMBERS + member
    right_box = ((box + 1) % boxes) * MEMBERS + member
    mates = [box * MEMBERS + (member + r) % MEMBERS for r in range(1, MEMBERS)]
    strides = boxes // MEMBERS
    far_to = [
        (((box // MEMBERS + k) % strides) * MEMBERS + member) * MEMBERS + box % MEMBERS
        for k in range(strides)
    ]
    far_from = [
        ((box // MEMBERS + strides - k) % strides) * MEMBERS + member for k in range(strides)
    ]
    alone = box % MEMBERS == member

    barrier = pltpu.get_barrier_semaphore()

    def greet(target):
        pl.semaphore_signal(barrier, inc=1, device_id=(target,), device_id_type=MESH)

    for target in mates + [left_device, right_device, left_box, right_box]:
        greet(target)
    for k in range(1, strides):
        greet(far_from[k] * MEMBERS + box % MEMBERS)

    @pl.when(jnp.logical_not(alone))
    def _():
        greet(far_from[0] * MEMBERS + box % MEMBERS)

    picks = lax.broadcasted_iota(jnp.int32, (128, 128), 1) % 64 * 2
    every_second = (
        (lax.broadcasted_iota(jnp.int32, (128, 128), 0) == picks).astype(f32).astype(bf16)
    )
    loading[0].wait()
    points = jnp.concatenate([coords[...], jnp.zeros((5, OWN), f32)], axis=0)
    s0 = [
        jnp.concatenate(
            [points[:, 512 * p : 512 * p + 64], points[:, 512 * p + 256 : 512 * p + 320]], axis=1
        )
        for p in range(4)
    ]
    s1 = raise_skel(s0, every_second)
    s2 = raise_skel(s1, every_second)
    s3 = raise_skel(s2, every_second)[0]

    loading[1].wait()
    maps = []
    for level in range(6):
        once = transfer[level]
        high, rest = split(jnp.concatenate([once, once], axis=1))
        map_high[level] = high
        map_low[level] = rest
        maps.append((map_high.at[level], map_low.at[level]))
    loading[2].wait()
    loading[3].wait()
    slots = lax.broadcasted_iota(jnp.int32, (COLS, LEAF), 1)
    live = []
    for leaf in range(LEAVES):
        part = loads[:, leaf * LEAF : (leaf + 1) * LEAF].astype(f32)
        live.append(jnp.where(slots < occ[leaf], part, 0.0))
    loading[4].wait()
    c0 = []
    for p in range(4):
        two = jnp.concatenate([live[2 * p], live[2 * p + 1]], axis=0).astype(bf16)
        rows = lax.dot_general(
            two, basis[128 * p : 128 * p + 128, :], NT, preferred_element_type=f32
        )
        c0.append(jnp.where(low, rows[:8], rows[8:]))
    c1 = raise_coef(c0, maps[0])
    c2 = raise_coef(c1, maps[1])
    c3 = raise_coef(c2, maps[2])[0]

    g_buf[member] = jnp.where(half == member % 2, c3, s3)

    pl.semaphore_wait(barrier, 4 + MEMBERS - 1 + strides - alone.astype(jnp.int32))

    started = []

    def send(src, dst, send_sem, recv_sem, target):
        copy = pltpu.make_async_remote_copy(
            src_ref=src,
            dst_ref=dst,
            send_sem=send_sem,
            recv_sem=recv_sem,
            device_id=(target,),
            device_id_type=MESH,
        )
        copy.start()
        started.append(copy)
        return copy

    g_copies = []
    for r, mate in enumerate(mates):
        g_copies.append(
            send(g_buf.at[member], g_buf.at[member], g_send_sem.at[r], g_recv_sem.at[r], mate)
        )

    field[0, :, LEAF : LEAF + OWN] = points
    for leaf in range(LEAVES):
        field[1, :, (leaf + 1) * LEAF : (leaf + 2) * LEAF] = live[leaf]
    for at, (pairs, skels) in enumerate([(c0, s0), (c1, s1), (c2, s2)]):
        first = (1, 7, 11)[at]
        for p in range(len(pairs)):
            chain[first + p, 0] = pairs[p]
            chain[first + p, 1] = skels[p]
        edge_send[0, at, 0] = pairs[-1]
        edge_send[0, at, 1] = skels[-1]
        edge_send[1, at, 0] = pairs[0]
        edge_send[1, at, 1] = skels[0]
    last = LEAF * LEAVES
    near_copies = [
        send(
            field.at[:, :, last : last + LEAF],
            field.at[:, :, 0:LEAF],
            near_send_sem.at[0],
            near_recv_sem.at[0],
            right_device,
        ),
        send(
            field.at[:, :, LEAF : 2 * LEAF],
            field.at[:, :, last + LEAF : last + 2 * LEAF],
            near_send_sem.at[1],
            near_recv_sem.at[1],
            left_device,
        ),
    ]
    edge_copies = [
        send(
            edge_send.at[side],
            edge_recv.at[side],
            edge_send_sem.at[side],
            edge_recv_sem.at[side],
            (right_device, left_device)[side],
        )
        for side in range(2)
    ]

    def set_column(at, carry):
        at = pl.multiple_of(at * 128, 128)
        column[pl.ds(at, 128), :] = field[0, :, pl.ds(at + LEAF, 128)].T
        return carry

    lax.fori_loop(0, OWN // 128, set_column, 0)
    near[...] = jnp.zeros_like(near)

    def fill_tile(row, col, width):
        def fill_rows(step, carry):
            at = pl.multiple_of(step * 64, 64)
            rows = column[pl.ds(row + at, 64), :]
            sx = field[0, 0:1, pl.ds(col, width)]
            sy = field[0, 1:2, pl.ds(col, width)]
            sz = field[0, 2:3, pl.ds(col, width)]
            tile[pl.ds(at, 64), 0:width] = phi(
                rows[:, 0:1], rows[:, 1:2], rows[:, 2:3], sx, sy, sz, near_scale
            ).astype(bf16)
            return carry

        lax.fori_loop(0, LEAF // 64, fill_rows, 0)

    def near_step(leaf, carry):
        row = pl.multiple_of(leaf * LEAF, LEAF)
        col = pl.multiple_of(row + LEAF, LEAF)
        fill_tile(row, col, 2 * LEAF)
        loads_two = field[1, :, pl.ds(col, 2 * LEAF)].astype(bf16)
        near[:, pl.ds(row, LEAF)] += lax.dot_general(
            loads_two, tile[...], NT, preferred_element_type=f32
        )
        near[:, pl.ds(col, LEAF)] += lax.dot_general(
            loads_two[:, :LEAF], tile[:, LEAF:], NN, preferred_element_type=f32
        )
        return carry

    lax.fori_loop(0, 3, near_step, 0)

    for copy in g_copies:
        copy.wait_recv()
    c3s, s3s = [], []
    for p in range(4):
        even, odd = g_buf[2 * p], g_buf[2 * p + 1]
        c3s.append(jnp.where(low, even, odd))
        s3s.append(pltpu.roll(jnp.where(low, odd, even), 64, 1))
    c4s, s4s = raise_coef(c3s, maps[3]), raise_skel(s3s, every_second)
    c5s, s5s = raise_coef(c4s, maps[4]), raise_skel(s4s, every_second)
    c6, s6 = raise_coef(c5s, maps[5])[0], raise_skel(s5s, every_second)[0]
    far_send[...] = jnp.where(low, c6, s6)

    @pl.when(alone)
    def _():
        far_buf[0] = far_send[...]

    far_copies = []
    for k in range(1, strides):
        far_copies.append(
            send(far_send, far_buf.at[k], far_send_sem.at[k], far_recv_sem.at[k], far_to[k])
        )
    first_far = pltpu.make_async_remote_copy(
        src_ref=far_send,
        dst_ref=far_buf.at[0],
        send_sem=far_send_sem.at[0],
        recv_sem=far_recv_sem.at[0],
        device_id=(far_to[0],),
        device_id_type=MESH,
    )

    @pl.when(jnp.logical_not(alone))
    def _():
        first_far.start()

    for at, (pairs, skels) in enumerate([(c3s, s3s), (c4s, s4s), (c5s, s5s)]):
        first = (1, 7, 11)[at]
        for p in range(len(pairs)):
            g_chain[first + p, 0] = pairs[p]
            g_chain[first + p, 1] = skels[p]
        bound_send[0, at, 0] = pairs[-1]
        bound_send[0, at, 1] = skels[-1]
        bound_send[1, at, 0] = pairs[0]
        bound_send[1, at, 1] = skels[0]
    bound_copies = [
        send(
            bound_send.at[side],
            bound_recv.at[side],
            bound_send_sem.at[side],
            bound_recv_sem.at[side],
            (right_box, left_box)[side],
        )
        for side in range(2)
    ]

    for copy in near_copies:
        copy.wait_recv()

    @pl.when(device == 0)
    def _():
        field[1, :, 0:LEAF] = jnp.zeros((COLS, LEAF), f32)

    @pl.when(device == total - 1)
    def _():
        field[1, :, last + LEAF : last + 2 * LEAF] = jnp.zeros((COLS, LEAF), f32)

    lax.fori_loop(3, 8, near_step, 0)
    fill_tile(0, 0, LEAF)
    near[:, 0:LEAF] += lax.dot_general(
        field[1, :, 0:LEAF].astype(bf16), tile[:, :LEAF], NT, preferred_element_type=f32
    )

    def set_ends(ends, into, at_start, at_end):
        for level in range(3):
            before, after = (0, 6, 10)[level], (5, 9, 12)[level]
            into[before, 0] = jnp.where(at_start, 0.0, ends[0, level, 0])
            into[before, 1] = ends[0, level, 1]
            into[after, 0] = jnp.where(at_end, 0.0, ends[1, level, 0])
            into[after, 1] = ends[1, level, 1]

    for copy in edge_copies:
        copy.wait_recv()
    set_ends(edge_recv, chain, device == 0, device == total - 1)

    def cousin_step(pair, carry):
        local[pair] = cousins(chain, pair + 1 + 2 * (pair // 4) + 2 * (pair // 6))
        return carry

    lax.fori_loop(0, 7, cousin_step, 0)

    for copy in far_copies:
        copy.wait_recv()

    @pl.when(jnp.logical_not(alone))
    def _():
        first_far.wait_recv()

    top_coef, top_skel = [], []
    for k in range(0, strides, 2):
        halves = []
        for at in (k, k + 1):
            apart = far_from[at] - box
            counts = jnp.logical_or(apart >= 2, apart <= -2)
            halves.append((far_buf[at], counts))
        (one, one_counts), (two, two_counts) = halves
        top_coef.append(
            jnp.where(
                low,
                jnp.where(one_counts, one, 0.0),
                jnp.where(two_counts, pltpu.roll(two, 64, 1), 0.0),
            )
        )
        top_skel.append(jnp.where(low, pltpu.roll(one, 64, 1), two))
    top_column = s6.T[:64]
    tx, ty, tz = top_column[:, 0:1], top_column[:, 1:2], top_column[:, 2:3]
    top_tile = jnp.concatenate(
        [phi(tx, ty, tz, s[0:1], s[1:2], s[2:3], far_scale) for s in top_skel], axis=1
    )
    top = mm(jnp.concatenate(top_coef, axis=1), split(top_tile), NT)
    part_buf[member] = jnp.concatenate([top, jnp.zeros((8, 64), f32)], axis=1)
    part_copies = []
    for r, mate in enumerate(mates):
        part_copies.append(
            send(
                part_buf.at[member],
                part_buf.at[member],
                part_send_sem.at[r],
                part_recv_sem.at[r],
                mate,
            )
        )

    for copy in bound_copies:
        copy.wait_recv()
    set_ends(bound_recv, g_chain, box == 0, box == boxes - 1)

    def box_cousin_step(level, carry):
        first = 6 * level - 2 * (level // 2)
        local[7 + level] = cousins(g_chain, first + 1 + member // (2 + 2 * level + 2 * (level // 2)))
        return carry

    lax.fori_loop(0, 3, box_cousin_step, 0)

    def side(block, at):
        lanes = lax.broadcasted_iota(jnp.int32, block.shape, 1) // 64
        return jnp.where(lanes == at, block, 0.0)

    zeros = jnp.zeros((64, 128), f32)

    def plus(block, at):
        return block + jnp.concatenate([local[at], zeros], axis=0)

    x5 = jnp.concatenate([local[9], transfer[5].T], axis=0)
    x4 = plus(mm(side(x5, member // 4), maps[4], NT), 8)
    x3 = plus(mm(side(x4, member // 2 % 2), maps[3], NT), 7)
    x2 = plus(mm(side(x3, member % 2), maps[2], NT), 6)
    x1 = [plus(x, 4 + at) for at, x in enumerate(lower([x2], maps[1]))]
    x0 = lower(x1, maps[0])
    lower_part = jnp.concatenate([x[:8] + local[at] for at, x in enumerate(x0)], axis=1)
    path = split(jnp.concatenate([x[8:] for x in x0], axis=1))

    for copy in part_copies:
        copy.wait_recv()
    d6 = part_buf[0]
    for at in range(1, MEMBERS):
        d6 = d6 + part_buf[at]
    d0 = lower_part + mm(d6[:, :64], path, NN)
    for p in range(4):
        pair = d0[:, 128 * p : 128 * p + 128]
        two = jnp.concatenate([jnp.where(low, pair, 0.0), jnp.where(low, 0.0, pair)], axis=0)
        rows = lax.dot_general(
            two.astype(bf16),
            basis[128 * p : 128 * p + 128, :],
            NN,
            preferred_element_type=f32,
        )
        for t in range(2):
            leaf = 2 * p + t
            at = leaf * LEAF
            out_ref[:, at : at + LEAF] = jnp.where(
                slots < occ[leaf], near[:, at : at + LEAF] + rows[8 * t : 8 * t + 8], 0.0
            )

    for copy in started:
        copy.wait_send()

    @pl.when(jnp.logical_not(alone))
    def _():
        first_far.wait_send()


def body(boxes, coords, loads, occupancy, basis, transfer):
    strides = boxes // MEMBERS
    hbm = pl.BlockSpec(memory_space=pl.ANY)
    dma = pltpu.SemaphoreType.DMA
    return pl.pallas_call(
        functools.partial(kernel, boxes),
        out_shape=jax.ShapeDtypeStruct((COLS, OWN), f32),
        in_specs=[hbm] * 5,
        out_specs=pl.BlockSpec(memory_space=pltpu.VMEM),
        scratch_shapes=[
            pltpu.VMEM((3, OWN), f32),
            pltpu.VMEM((COLS, OWN), bf16),
            pltpu.SMEM((LEAVES,), jnp.int32),
            pltpu.VMEM((LEAVES * 64, LEAF), bf16),
            pltpu.VMEM((6, 128, 64), f32),
            pltpu.VMEM((6, 128, 128), bf16),
            pltpu.VMEM((6, 128, 128), bf16),
            pltpu.VMEM((2, 8, OWN + 2 * LEAF), f32),
            pltpu.VMEM((OWN, 8), f32),
            pltpu.VMEM((COLS, OWN + LEAF), f32),
            pltpu.VMEM((LEAF, 2 * LEAF), bf16),
            pltpu.VMEM((13, 2, 8, 128), f32),
            pltpu.VMEM((13, 2, 8, 128), f32),
            pltpu.VMEM((10, 8, 128), f32),
            pltpu.VMEM((2, 3, 2, 8, 128), f32),
            pltpu.VMEM((2, 3, 2, 8, 128), f32),
            pltpu.VMEM((MEMBERS, 8, 128), f32),
            pltpu.VMEM((2, 3, 2, 8, 128), f32),
            pltpu.VMEM((2, 3, 2, 8, 128), f32),
            pltpu.VMEM((8, 128), f32),
            pltpu.VMEM((strides, 8, 128), f32),
            pltpu.VMEM((MEMBERS, 8, 128), f32),
            dma((5,)),
            dma((2,)),
            dma((2,)),
            dma((2,)),
            dma((2,)),
            dma((MEMBERS - 1,)),
            dma((MEMBERS - 1,)),
            dma((2,)),
            dma((2,)),
            dma((strides,)),
            dma((strides,)),
            dma((MEMBERS - 1,)),
            dma((MEMBERS - 1,)),
        ],
        compiler_params=pltpu.CompilerParams(
            collective_id=0, has_side_effects=True, vmem_limit_bytes=60 * 1024 * 1024
        ),
    )(
        coords,
        loads,
        occupancy,
        basis.reshape(LEAVES * 64, LEAF),
        transfer.reshape(6, 128, 64),
    )


def solution(mesh):
    boxes = mesh.shape["box"] // MEMBERS
    return jax.shard_map(
        functools.partial(body, boxes),
        mesh=mesh,
        in_specs=(P(None, "box"), P(None, "box"), P("box"), P("box", None, None), P()),
        out_specs=P(None, "box"),
        check_vma=False,
    )
```

```python
import functools

import jax
import jax.numpy as jnp
from jax import lax
from jax.experimental import pallas as pl
from jax.experimental.pallas import tpu as pltpu
from jax.sharding import PartitionSpec as P

LEAF = 256
COLS = 8
LEAVES = 8
MEMBERS = 8
OWN = LEAF * LEAVES

f32 = jnp.float32
bf16 = jnp.bfloat16
soften = 0.0001
near_scale = 0.0625
far_scale = 0.125
NN = (((1,), (0,)), ((), ()))
NT = (((1,), (1,)), ((), ()))
MESH = pl.DeviceIdType.MESH


def phi(tx, ty, tz, sx, sy, sz, scale):
    dx = tx - sx
    dy = ty - sy
    dz = tz - sz
    r2 = dx * dx + dy * dy + dz * dz
    return (r2 * (0.5 * scale)) * jnp.log(r2 + soften)


def split(x):
    high = x.astype(bf16)
    return high, (x - high.astype(f32)).astype(bf16)


def mm(a, b, dims):
    rows = a.shape[0]
    high = a.astype(bf16).astype(f32)
    stacked = jnp.concatenate([high, a - high], axis=0).astype(bf16)
    both = lax.dot_general(stacked, b[0][...], dims, preferred_element_type=f32)
    low = lax.dot_general(stacked[:rows], b[1][...], dims, preferred_element_type=f32)
    return both[:rows] + (both[rows:] + low)


def low_half(shape):
    return lax.broadcasted_iota(jnp.int32, shape, len(shape) - 1) < 64


def merge(rows):
    count = rows.shape[0] // 16
    low = low_half((8, 128))
    return [
        jnp.where(low, rows[16 * i : 16 * i + 8], rows[16 * i + 8 : 16 * i + 16])
        for i in range(count)
    ]


def raise_coef(pairs, level_map):
    rows = mm(jnp.concatenate(pairs, axis=0), level_map, NN)
    return merge(rows) if len(pairs) > 1 else [rows]


def pick(x, entries):
    rows = x.shape[0]
    a = x.astype(bf16).astype(f32)
    b = (x - a).astype(bf16).astype(f32)
    c = (x - a) - b
    stacked = jnp.concatenate([a, b, c], axis=0).astype(bf16)
    picked = lax.dot_general(stacked, entries, NN, preferred_element_type=f32)
    return picked[:rows] + picked[rows : 2 * rows] + picked[2 * rows :]


def raise_skel(pairs, every_second):
    rows_up = pick(jnp.concatenate(pairs, axis=0), every_second)
    return merge(rows_up) if len(pairs) > 1 else [rows_up]


def cousins(chain, slot):
    low = low_half((8, 128))
    column = chain[slot, 1].T
    tx, ty, tz = column[:, 0:1], column[:, 1:2], column[:, 2:3]
    before, after = chain[slot - 1, 0], chain[slot + 1, 0]
    tiles = []
    for skel in (chain[slot - 1, 1], chain[slot + 1, 1]):
        tiles.append(phi(tx, ty, tz, skel[0:1], skel[1:2], skel[2:3], far_scale))
    tile = jnp.concatenate(tiles, axis=1)
    even = jnp.concatenate([jnp.where(low, before, 0.0), after], axis=1)
    odd = jnp.concatenate([before, jnp.where(low, 0.0, after)], axis=1)
    rows = mm(jnp.concatenate([even, odd], axis=0), split(tile), NT)
    return jnp.where(low, rows[:8], rows[8:])


def lower(pairs, level_map):
    height = pairs[0].shape[0]
    low = low_half((height, 128))
    stacked = []
    for pair in pairs:
        stacked += [jnp.where(low, pair, 0.0), jnp.where(low, 0.0, pair)]
    rows = mm(jnp.concatenate(stacked, axis=0), level_map, NT)
    return [rows[height * i : height * (i + 1)] for i in range(2 * len(pairs))]


def kernel(
    boxes,
    coords_hbm,
    loads_hbm,
    occ_hbm,
    basis_hbm,
    transfer_hbm,
    out_ref,
    coords,
    loads,
    occ,
    basis,
    transfer,
    map_high,
    map_low,
    path_map,
    path_high,
    path_low,
    field,
    column,
    near,
    tile,
    chain,
    g_chain,
    local,
    edge_send,
    edge_recv,
    g_buf,
    bound_send,
    bound_recv,
    far_send,
    far_buf,
    part_buf,
    load_sem,
    near_send_sem,
    near_recv_sem,
    edge_send_sem,
    edge_recv_sem,
    g_send_sem,
    g_recv_sem,
    bound_send_sem,
    bound_recv_sem,
    far_send_sem,
    far_recv_sem,
    part_send_sem,
    part_recv_sem,
):
    loading = [
        pltpu.make_async_copy(src, dst, load_sem.at[at])
        for at, (src, dst) in enumerate(
            [
                (coords_hbm, coords),
                (transfer_hbm, transfer),
                (loads_hbm, loads),
                (occ_hbm, occ),
                (basis_hbm, basis),
            ]
        )
    ]
    for copy in loading:
        copy.start()

    device = lax.axis_index("box")
    total = boxes * MEMBERS
    box = device // MEMBERS
    member = device % MEMBERS
    low = low_half((8, 128))
    half = lax.broadcasted_iota(jnp.int32, (8, 128), 1) // 64

    left_device = (device + total - 1) % total
    right_device = (device + 1) % total
    left_box = ((box + boxes - 1) % boxes) * MEMBERS + member
    right_box = ((box + 1) % boxes) * MEMBERS + member
    mates = [box * MEMBERS + (member + r) % MEMBERS for r in range(1, MEMBERS)]
    strides = boxes // MEMBERS
    far_to = [
        (((box // MEMBERS + k) % strides) * MEMBERS + member) * MEMBERS + box % MEMBERS
        for k in range(strides)
    ]
    far_from = [
        ((box // MEMBERS + strides - k) % strides) * MEMBERS + member for k in range(strides)
    ]
    alone = box % MEMBERS == member

    barrier = pltpu.get_barrier_semaphore()

    def greet(target):
        pl.semaphore_signal(barrier, inc=1, device_id=(target,), device_id_type=MESH)

    for target in mates + [left_device, right_device, left_box, right_box]:
        greet(target)
    for k in range(1, strides):
        greet(far_from[k] * MEMBERS + box % MEMBERS)

    @pl.when(jnp.logical_not(alone))
    def _():
        greet(far_from[0] * MEMBERS + box % MEMBERS)

    picks = lax.broadcasted_iota(jnp.int32, (128, 128), 1) % 64 * 2
    every_second = (
        (lax.broadcasted_iota(jnp.int32, (128, 128), 0) == picks).astype(f32).astype(bf16)
    )
    loading[0].wait()
    points = jnp.concatenate([coords[...], jnp.zeros((5, OWN), f32)], axis=0)
    s0 = [
        jnp.concatenate(
            [points[:, 512 * p : 512 * p + 64], points[:, 512 * p + 256 : 512 * p + 320]], axis=1
        )
        for p in range(4)
    ]
    s1 = raise_skel(s0, every_second)
    s2 = raise_skel(s1, every_second)
    s3 = raise_skel(s2, every_second)[0]

    loading[1].wait()
    maps = []
    for level in range(6):
        once = transfer[level]
        high, rest = split(jnp.concatenate([once, once], axis=1))
        map_high[level] = high
        map_low[level] = rest
        maps.append((map_high.at[level], map_low.at[level]))
    paths = lower(lower([transfer[5].T], maps[4]), maps[3])
    for p in range(4):
        path_map[p] = paths[p]
    padded = jnp.concatenate(
        [jnp.concatenate(paths, axis=1), jnp.zeros((64, 512), f32)], axis=0
    )
    path_high[...], path_low[...] = split(padded)
    every_eighth = lax.broadcasted_iota(jnp.int32, (512, 128), 1) * 8 - 512
    every_eighth = (
        (lax.broadcasted_iota(jnp.int32, (512, 128), 0) == every_eighth).astype(f32).astype(bf16)
    )

    loading[2].wait()
    loading[3].wait()
    slots = lax.broadcasted_iota(jnp.int32, (COLS, LEAF), 1)
    live = []
    for leaf in range(LEAVES):
        part = loads[:, leaf * LEAF : (leaf + 1) * LEAF].astype(f32)
        live.append(jnp.where(slots < occ[leaf], part, 0.0))
    loading[4].wait()
    c0 = []
    for p in range(4):
        two = jnp.concatenate([live[2 * p], live[2 * p + 1]], axis=0).astype(bf16)
        rows = lax.dot_general(
            two, basis[128 * p : 128 * p + 128, :], NT, preferred_element_type=f32
        )
        c0.append(jnp.where(low, rows[:8], rows[8:]))
    c1 = raise_coef(c0, maps[0])
    c2 = raise_coef(c1, maps[1])
    c3 = raise_coef(c2, maps[2])[0]

    g_buf[member] = jnp.where(half == member % 2, c3, s3)

    pl.semaphore_wait(barrier, 4 + MEMBERS - 1 + strides - alone.astype(jnp.int32))

    started = []

    def send(src, dst, send_sem, recv_sem, target):
        copy = pltpu.make_async_remote_copy(
            src_ref=src,
            dst_ref=dst,
            send_sem=send_sem,
            recv_sem=recv_sem,
            device_id=(target,),
            device_id_type=MESH,
        )
        copy.start()
        started.append(copy)
        return copy

    g_copies = []
    for r, mate in enumerate(mates):
        g_copies.append(
            send(g_buf.at[member], g_buf.at[member], g_send_sem.at[r], g_recv_sem.at[r], mate)
        )

    for copy in g_copies:
        copy.wait_recv()
    c3s, s3s = [], []
    for p in range(4):
        even, odd = g_buf[2 * p], g_buf[2 * p + 1]
        c3s.append(jnp.where(low, even, odd))
        s3s.append(pltpu.roll(jnp.where(low, odd, even), 64, 1))
    c6 = mm(jnp.concatenate(c3s, axis=1), (path_high, path_low), NT)
    far_send[...] = c6 + pick(jnp.concatenate(s3s, axis=1), every_eighth)

    @pl.when(alone)
    def _():
        far_buf[0] = far_send[...]

    far_copies = []
    for k in range(1, strides):
        far_copies.append(
            send(far_send, far_buf.at[k], far_send_sem.at[k], far_recv_sem.at[k], far_to[k])
        )
    first_far = pltpu.make_async_remote_copy(
        src_ref=far_send,
        dst_ref=far_buf.at[0],
        send_sem=far_send_sem.at[0],
        recv_sem=far_recv_sem.at[0],
        device_id=(far_to[0],),
        device_id_type=MESH,
    )

    @pl.when(jnp.logical_not(alone))
    def _():
        first_far.start()

    c4s, s4s = raise_coef(c3s, maps[3]), raise_skel(s3s, every_second)
    c5s, s5s = raise_coef(c4s, maps[4]), raise_skel(s4s, every_second)
    s6 = raise_skel(s5s, every_second)[0]
    for at, (pairs, skels) in enumerate([(c3s, s3s), (c4s, s4s), (c5s, s5s)]):
        first = (1, 7, 11)[at]
        for p in range(len(pairs)):
            g_chain[first + p, 0] = pairs[p]
            g_chain[first + p, 1] = skels[p]
        bound_send[0, at, 0] = pairs[-1]
        bound_send[0, at, 1] = skels[-1]
        bound_send[1, at, 0] = pairs[0]
        bound_send[1, at, 1] = skels[0]
    bound_copies = [
        send(
            bound_send.at[side],
            bound_recv.at[side],
            bound_send_sem.at[side],
            bound_recv_sem.at[side],
            (right_box, left_box)[side],
        )
        for side in range(2)
    ]

    field[0, :, LEAF : LEAF + OWN] = points
    for leaf in range(LEAVES):
        field[1, :, (leaf + 1) * LEAF : (leaf + 2) * LEAF] = live[leaf]
    for at, (pairs, skels) in enumerate([(c0, s0), (c1, s1), (c2, s2)]):
        first = (1, 7, 11)[at]
        for p in range(len(pairs)):
            chain[first + p, 0] = pairs[p]
            chain[first + p, 1] = skels[p]
        edge_send[0, at, 0] = pairs[-1]
        edge_send[0, at, 1] = skels[-1]
        edge_send[1, at, 0] = pairs[0]
        edge_send[1, at, 1] = skels[0]
    last = LEAF * LEAVES
    near_copies = [
        send(
            field.at[:, :, last : last + LEAF],
            field.at[:, :, 0:LEAF],
            near_send_sem.at[0],
            near_recv_sem.at[0],
            right_device,
        ),
        send(
            field.at[:, :, LEAF : 2 * LEAF],
            field.at[:, :, last + LEAF : last + 2 * LEAF],
            near_send_sem.at[1],
            near_recv_sem.at[1],
            left_device,
        ),
    ]
    edge_copies = [
        send(
            edge_send.at[side],
            edge_recv.at[side],
            edge_send_sem.at[side],
            edge_recv_sem.at[side],
            (right_device, left_device)[side],
        )
        for side in range(2)
    ]

    def set_column(at, carry):
        at = pl.multiple_of(at * 128, 128)
        column[pl.ds(at, 128), :] = field[0, :, pl.ds(at + LEAF, 128)].T
        return carry

    lax.fori_loop(0, OWN // 128, set_column, 0)
    near[...] = jnp.zeros_like(near)

    def fill_tile(row, col, width):
        def fill_rows(step, carry):
            at = pl.multiple_of(step * 64, 64)
            rows = column[pl.ds(row + at, 64), :]
            sx = field[0, 0:1, pl.ds(col, width)]
            sy = field[0, 1:2, pl.ds(col, width)]
            sz = field[0, 2:3, pl.ds(col, width)]
            tile[pl.ds(at, 64), 0:width] = phi(
                rows[:, 0:1], rows[:, 1:2], rows[:, 2:3], sx, sy, sz, near_scale
            ).astype(bf16)
            return carry

        lax.fori_loop(0, LEAF // 64, fill_rows, 0)

    def near_step(leaf, carry):
        row = pl.multiple_of(leaf * LEAF, LEAF)
        col = pl.multiple_of(row + LEAF, LEAF)
        fill_tile(row, col, 2 * LEAF)
        loads_two = field[1, :, pl.ds(col, 2 * LEAF)].astype(bf16)
        near[:, pl.ds(row, LEAF)] += lax.dot_general(
            loads_two, tile[...], NT, preferred_element_type=f32
        )
        near[:, pl.ds(col, LEAF)] += lax.dot_general(
            loads_two[:, :LEAF], tile[:, LEAF:], NN, preferred_element_type=f32
        )
        return carry

    for copy in near_copies:
        copy.wait_recv()

    @pl.when(device == 0)
    def _():
        field[1, :, 0:LEAF] = jnp.zeros((COLS, LEAF), f32)

    @pl.when(device == total - 1)
    def _():
        field[1, :, last + LEAF : last + 2 * LEAF] = jnp.zeros((COLS, LEAF), f32)

    lax.fori_loop(0, 8, near_step, 0)
    fill_tile(0, 0, LEAF)
    near[:, 0:LEAF] += lax.dot_general(
        field[1, :, 0:LEAF].astype(bf16), tile[:, :LEAF], NT, preferred_element_type=f32
    )

    def set_ends(ends, into, at_start, at_end):
        for level in range(3):
            before, after = (0, 6, 10)[level], (5, 9, 12)[level]
            into[before, 0] = jnp.where(at_start, 0.0, ends[0, level, 0])
            into[before, 1] = ends[0, level, 1]
            into[after, 0] = jnp.where(at_end, 0.0, ends[1, level, 0])
            into[after, 1] = ends[1, level, 1]

    for copy in edge_copies:
        copy.wait_recv()
    set_ends(edge_recv, chain, device == 0, device == total - 1)

    def cousin_step(pair, carry):
        local[pair] = cousins(chain, pair + 1 + 2 * (pair // 4) + 2 * (pair // 6))
        return carry

    lax.fori_loop(0, 7, cousin_step, 0)

    for copy in bound_copies:
        copy.wait_recv()
    set_ends(bound_recv, g_chain, box == 0, box == boxes - 1)

    def box_cousin_step(level, carry):
        first = 6 * level - 2 * (level // 2)
        local[7 + level] = cousins(g_chain, first + 1 + member // (2 + 2 * level + 2 * (level // 2)))
        return carry

    lax.fori_loop(0, 3, box_cousin_step, 0)

    def side(block, at):
        lanes = lax.broadcasted_iota(jnp.int32, block.shape, 1) // 64
        return jnp.where(lanes == at, block, 0.0)

    zeros = jnp.zeros((64, 128), f32)

    def plus(block, at):
        return block + jnp.concatenate([local[at], zeros], axis=0)

    x4 = local[8] + mm(side(local[9], member // 4), maps[4], NT)
    x3 = local[7] + mm(side(x4, member // 2 % 2), maps[3], NT)
    x3 = jnp.concatenate([x3, path_map[member // 2]], axis=0)
    x2 = plus(mm(side(x3, member % 2), maps[2], NT), 6)
    x1 = [plus(x, 4 + at) for at, x in enumerate(lower([x2], maps[1]))]
    x0 = lower(x1, maps[0])
    lower_part = jnp.concatenate([x[:8] + local[at] for at, x in enumerate(x0)], axis=1)
    path = split(jnp.concatenate([x[8:] for x in x0], axis=1))

    for copy in far_copies:
        copy.wait_recv()

    @pl.when(jnp.logical_not(alone))
    def _():
        first_far.wait_recv()

    top_coef, top_skel = [], []
    for k in range(0, strides, 2):
        halves = []
        for at in (k, k + 1):
            apart = far_from[at] - box
            counts = jnp.logical_or(apart >= 2, apart <= -2)
            halves.append((far_buf[at], counts))
        (one, one_counts), (two, two_counts) = halves
        top_coef.append(
            jnp.where(
                low,
                jnp.where(one_counts, one, 0.0),
                jnp.where(two_counts, pltpu.roll(two, 64, 1), 0.0),
            )
        )
        top_skel.append(jnp.where(low, pltpu.roll(one, 64, 1), two))
    top_column = s6.T[:64]
    tx, ty, tz = top_column[:, 0:1], top_column[:, 1:2], top_column[:, 2:3]
    top_tile = jnp.concatenate(
        [phi(tx, ty, tz, s[0:1], s[1:2], s[2:3], far_scale) for s in top_skel], axis=1
    )
    top = mm(jnp.concatenate(top_coef, axis=1), split(top_tile), NT)
    part_buf[member] = jnp.concatenate([top, jnp.zeros((8, 64), f32)], axis=1)
    part_copies = []
    for r, mate in enumerate(mates):
        part_copies.append(
            send(
                part_buf.at[member],
                part_buf.at[member],
                part_send_sem.at[r],
                part_recv_sem.at[r],
                mate,
            )
        )

    for copy in part_copies:
        copy.wait_recv()
    d6 = part_buf[0]
    for at in range(1, MEMBERS):
        d6 = d6 + part_buf[at]
    d0 = lower_part + mm(d6[:, :64], path, NN)
    for p in range(4):
        pair = d0[:, 128 * p : 128 * p + 128]
        two = jnp.concatenate([jnp.where(low, pair, 0.0), jnp.where(low, 0.0, pair)], axis=0)
        rows = lax.dot_general(
            two.astype(bf16),
            basis[128 * p : 128 * p + 128, :],
            NN,
            preferred_element_type=f32,
        )
        for t in range(2):
            leaf = 2 * p + t
            at = leaf * LEAF
            out_ref[:, at : at + LEAF] = jnp.where(
                slots < occ[leaf], near[:, at : at + LEAF] + rows[8 * t : 8 * t + 8], 0.0
            )

    for copy in started:
        copy.wait_send()

    @pl.when(jnp.logical_not(alone))
    def _():
        first_far.wait_send()


def body(boxes, coords, loads, occupancy, basis, transfer):
    strides = boxes // MEMBERS
    hbm = pl.BlockSpec(memory_space=pl.ANY)
    dma = pltpu.SemaphoreType.DMA
    return pl.pallas_call(
        functools.partial(kernel, boxes),
        out_shape=jax.ShapeDtypeStruct((COLS, OWN), f32),
        in_specs=[hbm] * 5,
        out_specs=pl.BlockSpec(memory_space=pltpu.VMEM),
        scratch_shapes=[
            pltpu.VMEM((3, OWN), f32),
            pltpu.VMEM((COLS, OWN), bf16),
            pltpu.SMEM((LEAVES,), jnp.int32),
            pltpu.VMEM((LEAVES * 64, LEAF), bf16),
            pltpu.VMEM((6, 128, 64), f32),
            pltpu.VMEM((6, 128, 128), bf16),
            pltpu.VMEM((6, 128, 128), bf16),
            pltpu.VMEM((4, 64, 128), f32),
            pltpu.VMEM((128, 512), bf16),
            pltpu.VMEM((128, 512), bf16),
            pltpu.VMEM((2, 8, OWN + 2 * LEAF), f32),
            pltpu.VMEM((OWN, 8), f32),
            pltpu.VMEM((COLS, OWN + LEAF), f32),
            pltpu.VMEM((LEAF, 2 * LEAF), bf16),
            pltpu.VMEM((13, 2, 8, 128), f32),
            pltpu.VMEM((13, 2, 8, 128), f32),
            pltpu.VMEM((10, 8, 128), f32),
            pltpu.VMEM((2, 3, 2, 8, 128), f32),
            pltpu.VMEM((2, 3, 2, 8, 128), f32),
            pltpu.VMEM((MEMBERS, 8, 128), f32),
            pltpu.VMEM((2, 3, 2, 8, 128), f32),
            pltpu.VMEM((2, 3, 2, 8, 128), f32),
            pltpu.VMEM((8, 128), f32),
            pltpu.VMEM((strides, 8, 128), f32),
            pltpu.VMEM((MEMBERS, 8, 128), f32),
            dma((5,)),
            dma((2,)),
            dma((2,)),
            dma((2,)),
            dma((2,)),
            dma((MEMBERS - 1,)),
            dma((MEMBERS - 1,)),
            dma((2,)),
            dma((2,)),
            dma((strides,)),
            dma((strides,)),
            dma((MEMBERS - 1,)),
            dma((MEMBERS - 1,)),
        ],
        compiler_params=pltpu.CompilerParams(
            collective_id=0, has_side_effects=True, vmem_limit_bytes=32 * 1024 * 1024
        ),
    )(
        *[
            pltpu.with_memory_space_constraint(x, pltpu.HBM)
            for x in (
                coords,
                loads,
                occupancy,
                basis.reshape(LEAVES * 64, LEAF),
                transfer.reshape(6, 128, 64),
            )
        ]
    )


def solution(mesh):
    boxes = mesh.shape["box"] // MEMBERS
    return jax.shard_map(
        functools.partial(body, boxes),
        mesh=mesh,
        in_specs=(P(None, "box"), P(None, "box"), P("box"), P("box", None, None), P()),
        out_specs=P(None, "box"),
        check_vma=False,
    )
```

```python
import functools

import jax
import jax.numpy as jnp
from jax import lax
from jax.experimental import pallas as pl
from jax.experimental.pallas import tpu as pltpu
from jax.sharding import PartitionSpec as P

LEAF = 256
COLS = 8
LEAVES = 8
MEMBERS = 8
OWN = LEAF * LEAVES

f32 = jnp.float32
bf16 = jnp.bfloat16
soften = 0.0001
near_scale = 0.0625
far_scale = 0.125
NN = (((1,), (0,)), ((), ()))
NT = (((1,), (1,)), ((), ()))
MESH = pl.DeviceIdType.MESH


def phi(tx, ty, tz, sx, sy, sz, scale):
    dx = tx - sx
    dy = ty - sy
    dz = tz - sz
    r2 = dx * dx + dy * dy + dz * dz
    return (r2 * (0.5 * scale)) * jnp.log(r2 + soften)


def split(x):
    high = x.astype(bf16)
    return high, (x - high.astype(f32)).astype(bf16)


def mm(a, b, dims):
    rows = a.shape[0]
    high = a.astype(bf16).astype(f32)
    stacked = jnp.concatenate([high, a - high], axis=0).astype(bf16)
    both = lax.dot_general(stacked, b[0][...], dims, preferred_element_type=f32)
    low = lax.dot_general(stacked[:rows], b[1][...], dims, preferred_element_type=f32)
    return both[:rows] + (both[rows:] + low)


def low_half(shape):
    return lax.broadcasted_iota(jnp.int32, shape, len(shape) - 1) < 64


def merge(rows):
    count = rows.shape[0] // 16
    low = low_half((8, 128))
    return [
        jnp.where(low, rows[16 * i : 16 * i + 8], rows[16 * i + 8 : 16 * i + 16])
        for i in range(count)
    ]


def raise_coef(pairs, level_map):
    rows = mm(jnp.concatenate(pairs, axis=0), level_map, NN)
    return merge(rows) if len(pairs) > 1 else [rows]


def pick(x, entries):
    rows = x.shape[0]
    a = x.astype(bf16).astype(f32)
    b = (x - a).astype(bf16).astype(f32)
    c = (x - a) - b
    stacked = jnp.concatenate([a, b, c], axis=0).astype(bf16)
    picked = lax.dot_general(stacked, entries, NN, preferred_element_type=f32)
    return picked[:rows] + picked[rows : 2 * rows] + picked[2 * rows :]


def raise_skel(pairs, every_second):
    rows_up = pick(jnp.concatenate(pairs, axis=0), every_second)
    return merge(rows_up) if len(pairs) > 1 else [rows_up]


def cousins(chain, slot):
    low = low_half((8, 128))
    column = chain[slot, 1].T
    tx, ty, tz = column[:, 0:1], column[:, 1:2], column[:, 2:3]
    before, after = chain[slot - 1, 0], chain[slot + 1, 0]
    tiles = []
    for skel in (chain[slot - 1, 1], chain[slot + 1, 1]):
        tiles.append(phi(tx, ty, tz, skel[0:1], skel[1:2], skel[2:3], far_scale))
    tile = jnp.concatenate(tiles, axis=1)
    even = jnp.concatenate([jnp.where(low, before, 0.0), after], axis=1)
    odd = jnp.concatenate([before, jnp.where(low, 0.0, after)], axis=1)
    rows = mm(jnp.concatenate([even, odd], axis=0), split(tile), NT)
    return jnp.where(low, rows[:8], rows[8:])


def lower(pairs, level_map):
    height = pairs[0].shape[0]
    low = low_half((height, 128))
    stacked = []
    for pair in pairs:
        stacked += [jnp.where(low, pair, 0.0), jnp.where(low, 0.0, pair)]
    rows = mm(jnp.concatenate(stacked, axis=0), level_map, NT)
    return [rows[height * i : height * (i + 1)] for i in range(2 * len(pairs))]


def kernel(
    boxes,
    coords_hbm,
    loads_hbm,
    occ_hbm,
    basis_hbm,
    transfer_hbm,
    out_ref,
    coords,
    loads,
    occ,
    basis,
    transfer,
    map_high,
    map_low,
    path_map,
    path_high,
    path_low,
    field,
    column,
    leaf_high,
    leaf_low,
    near,
    tile_a,
    tile_b,
    tile_c,
    chain,
    g_chain,
    local,
    edge_send,
    edge_recv,
    g_buf,
    bound_send,
    bound_recv,
    far_send,
    far_buf,
    part_buf,
    load_sem,
    near_send_sem,
    near_recv_sem,
    edge_send_sem,
    edge_recv_sem,
    g_send_sem,
    g_recv_sem,
    bound_send_sem,
    bound_recv_sem,
    far_send_sem,
    far_recv_sem,
    part_send_sem,
    part_recv_sem,
):
    loading = [
        pltpu.make_async_copy(src, dst, load_sem.at[at])
        for at, (src, dst) in enumerate(
            [
                (coords_hbm, coords),
                (transfer_hbm, transfer),
                (loads_hbm, loads),
                (occ_hbm, occ),
                (basis_hbm, basis),
            ]
        )
    ]
    for copy in loading:
        copy.start()

    device = lax.axis_index("box")
    total = boxes * MEMBERS
    box = device // MEMBERS
    member = device % MEMBERS
    low = low_half((8, 128))
    half = lax.broadcasted_iota(jnp.int32, (8, 128), 1) // 64

    left_device = (device + total - 1) % total
    right_device = (device + 1) % total
    left_box = ((box + boxes - 1) % boxes) * MEMBERS + member
    right_box = ((box + 1) % boxes) * MEMBERS + member
    mates = [box * MEMBERS + (member + r) % MEMBERS for r in range(1, MEMBERS)]
    strides = boxes // MEMBERS
    far_to = [
        (((box // MEMBERS + k) % strides) * MEMBERS + member) * MEMBERS + box % MEMBERS
        for k in range(strides)
    ]
    far_from = [
        ((box // MEMBERS + strides - k) % strides) * MEMBERS + member for k in range(strides)
    ]
    alone = box % MEMBERS == member

    barrier = pltpu.get_barrier_semaphore()

    def greet(target):
        pl.semaphore_signal(barrier, inc=1, device_id=(target,), device_id_type=MESH)

    for target in mates + [left_device, right_device, left_box, right_box]:
        greet(target)
    for k in range(1, strides):
        greet(far_from[k] * MEMBERS + box % MEMBERS)

    @pl.when(jnp.logical_not(alone))
    def _():
        greet(far_from[0] * MEMBERS + box % MEMBERS)

    eighths = lax.broadcasted_iota(jnp.int32, (512, 128), 1) % 64 * 8
    every_eighth = (
        (lax.broadcasted_iota(jnp.int32, (512, 128), 0) == eighths).astype(f32).astype(bf16)
    )
    loading[0].wait()
    points = jnp.concatenate([coords[...], jnp.zeros((5, OWN), f32)], axis=0)
    s0 = [
        jnp.concatenate(
            [points[:, 512 * p : 512 * p + 64], points[:, 512 * p + 256 : 512 * p + 320]], axis=1
        )
        for p in range(4)
    ]
    s3 = pick(jnp.concatenate(s0, axis=1), every_eighth)

    loading[1].wait()
    maps = [(map_high.at[level], map_low.at[level]) for level in range(6)]

    def set_map(level):
        once = transfer[level]
        map_high[level], map_low[level] = split(jnp.concatenate([once, once], axis=1))

    for level in range(3):
        set_map(level)
    loading[2].wait()
    loading[3].wait()
    slots = lax.broadcasted_iota(jnp.int32, (COLS, LEAF), 1)
    live = []
    for leaf in range(LEAVES):
        part = loads[:, leaf * LEAF : (leaf + 1) * LEAF].astype(f32)
        live.append(jnp.where(slots < occ[leaf], part, 0.0))
    loading[4].wait()
    c0 = []
    for p in range(4):
        two = jnp.concatenate([live[2 * p], live[2 * p + 1]], axis=0).astype(bf16)
        rows = lax.dot_general(
            two, basis[128 * p : 128 * p + 128, :], NT, preferred_element_type=f32
        )
        c0.append(jnp.where(low, rows[:8], rows[8:]))
    c1 = raise_coef(c0, maps[0])
    c2 = raise_coef(c1, maps[1])
    c3 = raise_coef(c2, maps[2])[0]

    g_buf[member] = jnp.where(half == member % 2, c3, s3)

    pl.semaphore_wait(barrier, 4 + MEMBERS - 1 + strides - alone.astype(jnp.int32))

    started = []

    def send(src, dst, send_sem, recv_sem, target):
        copy = pltpu.make_async_remote_copy(
            src_ref=src,
            dst_ref=dst,
            send_sem=send_sem,
            recv_sem=recv_sem,
            device_id=(target,),
            device_id_type=MESH,
        )
        copy.start()
        started.append(copy)
        return copy

    g_copies = []
    for r, mate in enumerate(mates):
        g_copies.append(
            send(g_buf.at[member], g_buf.at[member], g_send_sem.at[r], g_recv_sem.at[r], mate)
        )

    field[0, :, LEAF : LEAF + OWN] = points
    for leaf in range(LEAVES):
        field[1, :, (leaf + 1) * LEAF : (leaf + 2) * LEAF] = live[leaf]
    last = LEAF * LEAVES
    near_copies = [
        send(
            field.at[:, :, last : last + LEAF],
            field.at[:, :, 0:LEAF],
            near_send_sem.at[0],
            near_recv_sem.at[0],
            right_device,
        ),
        send(
            field.at[:, :, LEAF : 2 * LEAF],
            field.at[:, :, last + LEAF : last + 2 * LEAF],
            near_send_sem.at[1],
            near_recv_sem.at[1],
            left_device,
        ),
    ]

    picks = lax.broadcasted_iota(jnp.int32, (128, 128), 1) % 64 * 2
    every_second = (
        (lax.broadcasted_iota(jnp.int32, (128, 128), 0) == picks).astype(f32).astype(bf16)
    )
    s1 = raise_skel(s0, every_second)
    s2 = raise_skel(s1, every_second)

    def set_chain(levels, into, ends):
        for at, (pairs, skels) in enumerate(levels):
            first = (1, 7, 11)[at]
            for p in range(len(pairs)):
                into[first + p, 0] = pairs[p]
                into[first + p, 1] = skels[p]
            ends[0, at, 0] = pairs[-1]
            ends[0, at, 1] = skels[-1]
            ends[1, at, 0] = pairs[0]
            ends[1, at, 1] = skels[0]

    set_chain([(c0, s0), (c1, s1), (c2, s2)], chain, edge_send)
    edge_copies = [
        send(
            edge_send.at[side],
            edge_recv.at[side],
            edge_send_sem.at[side],
            edge_recv_sem.at[side],
            (right_device, left_device)[side],
        )
        for side in range(2)
    ]

    for level in range(3, 6):
        set_map(level)
    paths = lower(lower([transfer[5].T], maps[4]), maps[3])
    for p in range(4):
        path_map[p] = paths[p]
    padded = jnp.concatenate(
        [jnp.concatenate(paths, axis=1), jnp.zeros((64, 512), f32)], axis=0
    )
    path_high[...], path_low[...] = split(padded)

    for at in range(0, OWN, 128):
        column[at : at + 128, :] = points[:, at : at + 128].T
    near[...] = jnp.zeros_like(near)

    def fill_tile(tile, row, col, width):
        sx = field[0, 0:1, pl.ds(col, width)]
        sy = field[0, 1:2, pl.ds(col, width)]
        sz = field[0, 2:3, pl.ds(col, width)]
        for at in range(0, LEAF, 16):
            rows = column[pl.ds(row + at, 16), :]
            tile[at : at + 16, 0:width] = phi(
                rows[:, 0:1], rows[:, 1:2], rows[:, 2:3], sx, sy, sz, near_scale
            ).astype(bf16)

    def near_leaf(tile, row):
        col = row + LEAF
        fill_tile(tile, row, col, 2 * LEAF)
        loads_two = field[1, :, pl.ds(col, 2 * LEAF)].astype(bf16)
        this = lax.dot_general(loads_two, tile[...], NT, preferred_element_type=f32)
        after = lax.dot_general(
            loads_two[:, :LEAF], tile[:, LEAF:], NN, preferred_element_type=f32
        )
        return this, after

    def near_two(row):
        first, second_part = near_leaf(tile_a, row)
        second, third = near_leaf(tile_b, row + LEAF)
        near[:, pl.ds(row, LEAF)] += first
        near[:, pl.ds(row + LEAF, LEAF)] += second_part + second
        near[:, pl.ds(row + 2 * LEAF, LEAF)] += third

    def near_step(pair, carry):
        near_two(pl.multiple_of(pair * (2 * LEAF), 2 * LEAF))
        return carry

    lax.fori_loop(0, 3, near_step, 0)

    for copy in g_copies:
        copy.wait_recv()
    c3s, s3s = [], []
    for p in range(4):
        even, odd = g_buf[2 * p], g_buf[2 * p + 1]
        c3s.append(jnp.where(low, even, odd))
        s3s.append(pltpu.roll(jnp.where(low, odd, even), 64, 1))
    c6 = mm(jnp.concatenate(c3s, axis=1), (path_high, path_low), NT)
    s6 = pick(jnp.concatenate(s3s, axis=1), every_eighth)
    far_send[...] = jnp.where(low, c6, s6)

    @pl.when(alone)
    def _():
        far_buf[0] = far_send[...]

    far_copies = []
    for k in range(1, strides):
        far_copies.append(
            send(far_send, far_buf.at[k], far_send_sem.at[k], far_recv_sem.at[k], far_to[k])
        )
    first_far = pltpu.make_async_remote_copy(
        src_ref=far_send,
        dst_ref=far_buf.at[0],
        send_sem=far_send_sem.at[0],
        recv_sem=far_recv_sem.at[0],
        device_id=(far_to[0],),
        device_id_type=MESH,
    )

    @pl.when(jnp.logical_not(alone))
    def _():
        first_far.start()

    c4s, s4s = raise_coef(c3s, maps[3]), raise_skel(s3s, every_second)
    c5s, s5s = raise_coef(c4s, maps[4]), raise_skel(s4s, every_second)
    set_chain([(c3s, s3s), (c4s, s4s), (c5s, s5s)], g_chain, bound_send)
    bound_copies = [
        send(
            bound_send.at[side],
            bound_recv.at[side],
            bound_send_sem.at[side],
            bound_recv_sem.at[side],
            (right_box, left_box)[side],
        )
        for side in range(2)
    ]

    for copy in near_copies:
        copy.wait_recv()

    @pl.when(device == 0)
    def _():
        field[1, :, 0:LEAF] = jnp.zeros((COLS, LEAF), f32)

    @pl.when(device == total - 1)
    def _():
        field[1, :, last + LEAF : last + 2 * LEAF] = jnp.zeros((COLS, LEAF), f32)

    near_two((LEAVES - 2) * LEAF)
    fill_tile(tile_c, 0, 0, LEAF)
    near[:, 0:LEAF] += lax.dot_general(
        field[1, :, 0:LEAF].astype(bf16), tile_c[...], NT, preferred_element_type=f32
    )

    def set_ends(ends, into, at_start, at_end):
        for level in range(3):
            before, after = (0, 6, 10)[level], (5, 9, 12)[level]
            into[before, 0] = jnp.where(at_start, 0.0, ends[0, level, 0])
            into[before, 1] = ends[0, level, 1]
            into[after, 0] = jnp.where(at_end, 0.0, ends[1, level, 0])
            into[after, 1] = ends[1, level, 1]

    for copy in edge_copies:
        copy.wait_recv()
    set_ends(edge_recv, chain, device == 0, device == total - 1)
    for pair, slot in enumerate([1, 2, 3, 4, 7, 8, 11]):
        local[pair] = cousins(chain, slot)

    def side(block, at):
        lanes = lax.broadcasted_iota(jnp.int32, block.shape, 1) // 64
        return jnp.where(lanes == at, block, 0.0)

    x2 = mm(side(path_map[member // 2], member % 2), maps[2], NT)
    x0 = lower(lower([x2], maps[1]), maps[0])
    leaf_high[...], leaf_low[...] = split(jnp.concatenate(x0, axis=1))

    for copy in far_copies:
        copy.wait_recv()

    @pl.when(jnp.logical_not(alone))
    def _():
        first_far.wait_recv()

    top_coef, top_skel = [], []
    for k in range(0, strides, 2):
        halves = []
        for at in (k, k + 1):
            apart = far_from[at] - box
            counts = jnp.logical_or(apart >= 2, apart <= -2)
            halves.append((far_buf[at], counts))
        (one, one_counts), (two, two_counts) = halves
        top_coef.append(
            jnp.where(
                low,
                jnp.where(one_counts, one, 0.0),
                jnp.where(two_counts, pltpu.roll(two, 64, 1), 0.0),
            )
        )
        top_skel.append(jnp.where(low, pltpu.roll(one, 64, 1), two))
    top_column = s6.T[:64]
    tx, ty, tz = top_column[:, 0:1], top_column[:, 1:2], top_column[:, 2:3]
    top_tile = jnp.concatenate(
        [phi(tx, ty, tz, s[0:1], s[1:2], s[2:3], far_scale) for s in top_skel], axis=1
    )
    top = mm(jnp.concatenate(top_coef, axis=1), split(top_tile), NT)
    part_buf[member] = jnp.concatenate([top, jnp.zeros((8, 64), f32)], axis=1)
    part_copies = []
    for r, mate in enumerate(mates):
        part_copies.append(
            send(
                part_buf.at[member],
                part_buf.at[member],
                part_send_sem.at[r],
                part_recv_sem.at[r],
                mate,
            )
        )

    for copy in bound_copies:
        copy.wait_recv()
    set_ends(bound_recv, g_chain, box == 0, box == boxes - 1)
    local3 = cousins(g_chain, 1 + member // 2)
    local4 = cousins(g_chain, 7 + member // 4)
    local5 = cousins(g_chain, 11)
    y4 = local4 + mm(side(local5, member // 4), maps[4], NT)
    y3 = local3 + mm(side(y4, member // 2 % 2), maps[3], NT)
    y2 = local[6] + mm(side(y3, member % 2), maps[2], NT)
    y1 = [y + local[4 + at] for at, y in enumerate(lower([y2], maps[1]))]
    y0 = [y + local[at] for at, y in enumerate(lower(y1, maps[0]))]

    for copy in part_copies:
        copy.wait_recv()
    d6 = part_buf[0]
    for at in range(1, MEMBERS):
        d6 = d6 + part_buf[at]
    d0 = jnp.concatenate(y0, axis=1) + mm(d6[:, :64], (leaf_high, leaf_low), NN)
    for p in range(4):
        pair = d0[:, 128 * p : 128 * p + 128]
        two = jnp.concatenate([jnp.where(low, pair, 0.0), jnp.where(low, 0.0, pair)], axis=0)
        rows = lax.dot_general(
            two.astype(bf16),
            basis[128 * p : 128 * p + 128, :],
            NN,
            preferred_element_type=f32,
        )
        for t in range(2):
            leaf = 2 * p + t
            at = leaf * LEAF
            out_ref[:, at : at + LEAF] = jnp.where(
                slots < occ[leaf], near[:, at : at + LEAF] + rows[8 * t : 8 * t + 8], 0.0
            )

    for copy in started:
        copy.wait_send()

    @pl.when(jnp.logical_not(alone))
    def _():
        first_far.wait_send()


def body(boxes, coords, loads, occupancy, basis, transfer):
    strides = boxes // MEMBERS
    hbm = pl.BlockSpec(memory_space=pl.ANY)
    dma = pltpu.SemaphoreType.DMA
    return pl.pallas_call(
        functools.partial(kernel, boxes),
        out_shape=jax.ShapeDtypeStruct((COLS, OWN), f32),
        in_specs=[hbm] * 5,
        out_specs=pl.BlockSpec(memory_space=pltpu.VMEM),
        scratch_shapes=[
            pltpu.VMEM((3, OWN), f32),
            pltpu.VMEM((COLS, OWN), bf16),
            pltpu.SMEM((LEAVES,), jnp.int32),
            pltpu.VMEM((LEAVES * 64, LEAF), bf16),
            pltpu.VMEM((6, 128, 64), f32),
            pltpu.VMEM((6, 128, 128), bf16),
            pltpu.VMEM((6, 128, 128), bf16),
            pltpu.VMEM((4, 64, 128), f32),
            pltpu.VMEM((128, 512), bf16),
            pltpu.VMEM((128, 512), bf16),
            pltpu.VMEM((2, 8, OWN + 2 * LEAF), f32),
            pltpu.VMEM((OWN, 8), f32),
            pltpu.VMEM((64, 512), bf16),
            pltpu.VMEM((64, 512), bf16),
            pltpu.VMEM((COLS, OWN + LEAF), f32),
            pltpu.VMEM((LEAF, 2 * LEAF), bf16),
            pltpu.VMEM((LEAF, 2 * LEAF), bf16),
            pltpu.VMEM((LEAF, LEAF), bf16),
            pltpu.VMEM((13, 2, 8, 128), f32),
            pltpu.VMEM((13, 2, 8, 128), f32),
            pltpu.VMEM((7, 8, 128), f32),
            pltpu.VMEM((2, 3, 2, 8, 128), f32),
            pltpu.VMEM((2, 3, 2, 8, 128), f32),
            pltpu.VMEM((MEMBERS, 8, 128), f32),
            pltpu.VMEM((2, 3, 2, 8, 128), f32),
            pltpu.VMEM((2, 3, 2, 8, 128), f32),
            pltpu.VMEM((8, 128), f32),
            pltpu.VMEM((strides, 8, 128), f32),
            pltpu.VMEM((MEMBERS, 8, 128), f32),
            dma((5,)),
            dma((2,)),
            dma((2,)),
            dma((2,)),
            dma((2,)),
            dma((MEMBERS - 1,)),
            dma((MEMBERS - 1,)),
            dma((2,)),
            dma((2,)),
            dma((strides,)),
            dma((strides,)),
            dma((MEMBERS - 1,)),
            dma((MEMBERS - 1,)),
        ],
        compiler_params=pltpu.CompilerParams(
            collective_id=0, has_side_effects=True, vmem_limit_bytes=32 * 1024 * 1024
        ),
    )(
        *[
            pltpu.with_memory_space_constraint(x, pltpu.HBM)
            for x in (
                coords,
                loads,
                occupancy,
                basis.reshape(LEAVES * 64, LEAF),
                transfer.reshape(6, 128, 64),
            )
        ]
    )


def solution(mesh):
    boxes = mesh.shape["box"] // MEMBERS
    return jax.shard_map(
        functools.partial(body, boxes),
        mesh=mesh,
        in_specs=(P(None, "box"), P(None, "box"), P("box"), P("box", None, None), P()),
        out_specs=P(None, "box"),
        check_vma=False,
    )
```

```python
import functools

import jax
import jax.numpy as jnp
from jax import lax
from jax.experimental import pallas as pl
from jax.experimental.pallas import tpu as pltpu
from jax.sharding import PartitionSpec as P

LEAF = 256
COLS = 8
LEAVES = 8
MEMBERS = 8
OWN = LEAF * LEAVES

f32 = jnp.float32
bf16 = jnp.bfloat16
soften = 0.0001
near_scale = 0.0625
far_scale = 0.125
NN = (((1,), (0,)), ((), ()))
NT = (((1,), (1,)), ((), ()))
MESH = pl.DeviceIdType.MESH


def phi(tx, ty, tz, sx, sy, sz, scale):
    dx = tx - sx
    dy = ty - sy
    dz = tz - sz
    r2 = dx * dx + dy * dy + dz * dz
    return (r2 * (0.5 * scale)) * jnp.log(r2 + soften)


def split(x):
    high = x.astype(bf16)
    return high, (x - high.astype(f32)).astype(bf16)


def mm(a, b, dims):
    rows = a.shape[0]
    high = a.astype(bf16).astype(f32)
    stacked = jnp.concatenate([high, a - high], axis=0).astype(bf16)
    both = lax.dot_general(stacked, b[0][...], dims, preferred_element_type=f32)
    low = lax.dot_general(stacked[:rows], b[1][...], dims, preferred_element_type=f32)
    return both[:rows] + (both[rows:] + low)


def low_half(shape):
    return lax.broadcasted_iota(jnp.int32, shape, len(shape) - 1) < 64


def merge(rows):
    count = rows.shape[0] // 16
    low = low_half((8, 128))
    return [
        jnp.where(low, rows[16 * i : 16 * i + 8], rows[16 * i + 8 : 16 * i + 16])
        for i in range(count)
    ]


def raise_coef(pairs, level_map):
    rows = mm(jnp.concatenate(pairs, axis=0), level_map, NN)
    return merge(rows) if len(pairs) > 1 else [rows]


def pick(x, entries):
    rows = x.shape[0]
    a = x.astype(bf16).astype(f32)
    b = (x - a).astype(bf16).astype(f32)
    c = (x - a) - b
    stacked = jnp.concatenate([a, b, c], axis=0).astype(bf16)
    picked = lax.dot_general(stacked, entries, NN, preferred_element_type=f32)
    return picked[:rows] + picked[rows : 2 * rows] + picked[2 * rows :]


def raise_skel(pairs, every_second):
    rows_up = pick(jnp.concatenate(pairs, axis=0), every_second)
    return merge(rows_up) if len(pairs) > 1 else [rows_up]


def cousins(chain, slot):
    low = low_half((8, 128))
    column = chain[slot, 1].T
    tx, ty, tz = column[:, 0:1], column[:, 1:2], column[:, 2:3]
    before, after = chain[slot - 1, 0], chain[slot + 1, 0]
    tiles = []
    for skel in (chain[slot - 1, 1], chain[slot + 1, 1]):
        tiles.append(phi(tx, ty, tz, skel[0:1], skel[1:2], skel[2:3], far_scale))
    tile = jnp.concatenate(tiles, axis=1)
    even = jnp.concatenate([jnp.where(low, before, 0.0), after], axis=1)
    odd = jnp.concatenate([before, jnp.where(low, 0.0, after)], axis=1)
    rows = mm(jnp.concatenate([even, odd], axis=0), split(tile), NT)
    return jnp.where(low, rows[:8], rows[8:])


def lower(pairs, level_map):
    height = pairs[0].shape[0]
    low = low_half((height, 128))
    stacked = []
    for pair in pairs:
        stacked += [jnp.where(low, pair, 0.0), jnp.where(low, 0.0, pair)]
    rows = mm(jnp.concatenate(stacked, axis=0), level_map, NT)
    return [rows[height * i : height * (i + 1)] for i in range(2 * len(pairs))]


def kernel(
    boxes,
    coords_hbm,
    loads_hbm,
    occ_hbm,
    basis_hbm,
    transfer_hbm,
    out_ref,
    coords,
    loads,
    occ,
    basis,
    transfer,
    map_high,
    map_low,
    path_map,
    path_high,
    path_low,
    field,
    column,
    leaf_high,
    leaf_low,
    near,
    tile_a,
    tile_b,
    tile_c,
    chain,
    g_chain,
    local,
    edge_send,
    edge_recv,
    g_buf,
    bound_send,
    bound_recv,
    quad_recv,
    rim_recv,
    far_send,
    far_buf,
    part_buf,
    load_sem,
    near_send_sem,
    near_recv_sem,
    edge_send_sem,
    edge_recv_sem,
    g_send_sem,
    g_recv_sem,
    bound_send_sem,
    bound_recv_sem,
    rim_send_sem,
    rim_recv_sem,
    far_send_sem,
    far_recv_sem,
    part_send_sem,
    part_recv_sem,
):
    loading = [
        pltpu.make_async_copy(src, dst, load_sem.at[at])
        for at, (src, dst) in enumerate(
            [
                (coords_hbm, coords),
                (transfer_hbm, transfer),
                (loads_hbm, loads),
                (occ_hbm, occ),
                (basis_hbm, basis),
            ]
        )
    ]
    for copy in loading:
        copy.start()

    device = lax.axis_index("box")
    total = boxes * MEMBERS
    box = device // MEMBERS
    member = device % MEMBERS
    low = low_half((8, 128))
    half = lax.broadcasted_iota(jnp.int32, (8, 128), 1) // 64

    left_device = (device + total - 1) % total
    right_device = (device + 1) % total
    left_box = ((box + boxes - 1) % boxes) * MEMBERS + member
    right_box = ((box + 1) % boxes) * MEMBERS + member
    mates = [box * MEMBERS + (member + r) % MEMBERS for r in range(1, MEMBERS)]
    strides = boxes // MEMBERS
    far_to = [
        (((box // MEMBERS + k) % strides) * MEMBERS + member) * MEMBERS + box % MEMBERS
        for k in range(strides)
    ]
    far_from = [
        ((box // MEMBERS + strides - k) % strides) * MEMBERS + member for k in range(strides)
    ]
    alone = box % MEMBERS == member
    pair = member // 2
    upper = pair // 3
    at_rim = pair % 3 == 0
    rim_box = (box + boxes + 2 * upper - 1) % boxes
    rim_devices = [rim_box * MEMBERS + 6 - 6 * upper + t for t in range(2)]
    quad = member // 4
    quad_device = ((box + boxes + 1 - 2 * quad) % boxes) * MEMBERS + member

    barrier = pltpu.get_barrier_semaphore()

    def greet(target):
        pl.semaphore_signal(barrier, inc=1, device_id=(target,), device_id_type=MESH)

    for target in mates + [left_device, right_device, left_box, right_box]:
        greet(target)
    for k in range(1, strides):
        greet(far_from[k] * MEMBERS + box % MEMBERS)

    @pl.when(jnp.logical_not(alone))
    def _():
        greet(far_from[0] * MEMBERS + box % MEMBERS)

    @pl.when(at_rim)
    def _():
        for target in rim_devices:
            greet(target)

    eighths = lax.broadcasted_iota(jnp.int32, (512, 128), 1) % 64 * 8
    every_eighth = (
        (lax.broadcasted_iota(jnp.int32, (512, 128), 0) == eighths).astype(f32).astype(bf16)
    )
    loading[0].wait()
    points = jnp.concatenate([coords[...], jnp.zeros((5, OWN), f32)], axis=0)
    s0 = [
        jnp.concatenate(
            [points[:, 512 * p : 512 * p + 64], points[:, 512 * p + 256 : 512 * p + 320]], axis=1
        )
        for p in range(4)
    ]
    s3 = pick(jnp.concatenate(s0, axis=1), every_eighth)

    loading[1].wait()
    maps = [(map_high.at[level], map_low.at[level]) for level in range(6)]

    def set_map(level):
        once = transfer[level]
        map_high[level], map_low[level] = split(jnp.concatenate([once, once], axis=1))

    for level in range(3):
        set_map(level)
    loading[2].wait()
    loading[3].wait()
    slots = lax.broadcasted_iota(jnp.int32, (COLS, LEAF), 1)
    live = []
    for leaf in range(LEAVES):
        part = loads[:, leaf * LEAF : (leaf + 1) * LEAF].astype(f32)
        live.append(jnp.where(slots < occ[leaf], part, 0.0))
    loading[4].wait()
    c0 = []
    for p in range(4):
        two = jnp.concatenate([live[2 * p], live[2 * p + 1]], axis=0).astype(bf16)
        rows = lax.dot_general(
            two, basis[128 * p : 128 * p + 128, :], NT, preferred_element_type=f32
        )
        c0.append(jnp.where(low, rows[:8], rows[8:]))
    c1 = raise_coef(c0, maps[0])
    c2 = raise_coef(c1, maps[1])
    c3 = raise_coef(c2, maps[2])[0]

    g_buf[member] = jnp.where(half == member % 2, c3, s3)

    pl.semaphore_wait(
        barrier,
        4 + MEMBERS - 1 + strides - alone.astype(jnp.int32) + 2 * at_rim.astype(jnp.int32),
    )

    started = []

    def send(src, dst, send_sem, recv_sem, target):
        copy = pltpu.make_async_remote_copy(
            src_ref=src,
            dst_ref=dst,
            send_sem=send_sem,
            recv_sem=recv_sem,
            device_id=(target,),
            device_id_type=MESH,
        )
        copy.start()
        started.append(copy)
        return copy

    g_copies = []
    for r, mate in enumerate(mates):
        g_copies.append(
            send(g_buf.at[member], g_buf.at[member], g_send_sem.at[r], g_recv_sem.at[r], mate)
        )

    rim_copies = [
        pltpu.make_async_remote_copy(
            src_ref=g_buf.at[member],
            dst_ref=rim_recv.at[member % 2],
            send_sem=rim_send_sem.at[t],
            recv_sem=rim_recv_sem.at[member % 2],
            device_id=(rim_devices[t],),
            device_id_type=MESH,
        )
        for t in range(2)
    ]

    @pl.when(at_rim)
    def _():
        for copy in rim_copies:
            copy.start()

    field[0, :, LEAF : LEAF + OWN] = points
    for leaf in range(LEAVES):
        field[1, :, (leaf + 1) * LEAF : (leaf + 2) * LEAF] = live[leaf]
    last = LEAF * LEAVES
    near_copies = [
        send(
            field.at[:, :, last : last + LEAF],
            field.at[:, :, 0:LEAF],
            near_send_sem.at[0],
            near_recv_sem.at[0],
            right_device,
        ),
        send(
            field.at[:, :, LEAF : 2 * LEAF],
            field.at[:, :, last + LEAF : last + 2 * LEAF],
            near_send_sem.at[1],
            near_recv_sem.at[1],
            left_device,
        ),
    ]

    picks = lax.broadcasted_iota(jnp.int32, (128, 128), 1) % 64 * 2
    every_second = (
        (lax.broadcasted_iota(jnp.int32, (128, 128), 0) == picks).astype(f32).astype(bf16)
    )
    s1 = raise_skel(s0, every_second)
    s2 = raise_skel(s1, every_second)

    def set_chain(levels, into):
        for at, (pairs, skels) in enumerate(levels):
            first = (1, 7, 11)[at]
            for p in range(len(pairs)):
                into[first + p, 0] = pairs[p]
                into[first + p, 1] = skels[p]

    set_chain([(c0, s0), (c1, s1), (c2, s2)], chain)
    for at, (pairs, skels) in enumerate([(c0, s0), (c1, s1), (c2, s2)]):
        edge_send[0, at, 0] = pairs[-1]
        edge_send[0, at, 1] = skels[-1]
        edge_send[1, at, 0] = pairs[0]
        edge_send[1, at, 1] = skels[0]
    edge_copies = [
        send(
            edge_send.at[side],
            edge_recv.at[side],
            edge_send_sem.at[side],
            edge_recv_sem.at[side],
            (right_device, left_device)[side],
        )
        for side in range(2)
    ]

    for level in range(3, 6):
        set_map(level)
    paths = lower(lower([transfer[5].T], maps[4]), maps[3])
    for p in range(4):
        path_map[p] = paths[p]
    padded = jnp.concatenate(
        [jnp.concatenate(paths, axis=1), jnp.zeros((64, 512), f32)], axis=0
    )
    path_high[...], path_low[...] = split(padded)

    for at in range(0, OWN, 128):
        column[at : at + 128, :] = points[:, at : at + 128].T
    near[...] = jnp.zeros_like(near)

    def fill_tile(tile, row, col, width):
        sx = field[0, 0:1, pl.ds(col, width)]
        sy = field[0, 1:2, pl.ds(col, width)]
        sz = field[0, 2:3, pl.ds(col, width)]
        for at in range(0, LEAF, 16):
            rows = column[pl.ds(row + at, 16), :]
            tile[at : at + 16, 0:width] = phi(
                rows[:, 0:1], rows[:, 1:2], rows[:, 2:3], sx, sy, sz, near_scale
            ).astype(bf16)

    def near_leaf(tile, row):
        col = row + LEAF
        fill_tile(tile, row, col, 2 * LEAF)
        loads_two = field[1, :, pl.ds(col, 2 * LEAF)].astype(bf16)
        this = lax.dot_general(loads_two, tile[...], NT, preferred_element_type=f32)
        after = lax.dot_general(
            loads_two[:, :LEAF], tile[:, LEAF:], NN, preferred_element_type=f32
        )
        return this, after

    def near_two(row):
        first, second_part = near_leaf(tile_a, row)
        second, third = near_leaf(tile_b, row + LEAF)
        near[:, pl.ds(row, LEAF)] += first
        near[:, pl.ds(row + LEAF, LEAF)] += second_part + second
        near[:, pl.ds(row + 2 * LEAF, LEAF)] += third

    def near_step(pair, carry):
        near_two(pl.multiple_of(pair * (2 * LEAF), 2 * LEAF))
        return carry

    lax.fori_loop(0, 3, near_step, 0)

    for copy in g_copies:
        copy.wait_recv()
    c3s, s3s = [], []
    for p in range(4):
        even, odd = g_buf[2 * p], g_buf[2 * p + 1]
        c3s.append(jnp.where(low, even, odd))
        s3s.append(pltpu.roll(jnp.where(low, odd, even), 64, 1))
    c6 = mm(jnp.concatenate(c3s, axis=1), (path_high, path_low), NT)
    s6 = pick(jnp.concatenate(s3s, axis=1), every_eighth)
    far_send[...] = jnp.where(low, c6, s6)

    @pl.when(alone)
    def _():
        far_buf[0] = far_send[...]

    far_copies = []
    for k in range(1, strides):
        far_copies.append(
            send(far_send, far_buf.at[k], far_send_sem.at[k], far_recv_sem.at[k], far_to[k])
        )
    first_far = pltpu.make_async_remote_copy(
        src_ref=far_send,
        dst_ref=far_buf.at[0],
        send_sem=far_send_sem.at[0],
        recv_sem=far_recv_sem.at[0],
        device_id=(far_to[0],),
        device_id_type=MESH,
    )

    @pl.when(jnp.logical_not(alone))
    def _():
        first_far.start()

    c4s, s4s = raise_coef(c3s, maps[3]), raise_skel(s3s, every_second)
    c5s, s5s = raise_coef(c4s, maps[4]), raise_skel(s4s, every_second)
    set_chain([(c3s, s3s), (c4s, s4s), (c5s, s5s)], g_chain)
    for at in range(2):
        bound_send[at, 0] = c5s[0]
        bound_send[at, 1] = s5s[0] + pltpu.roll(s4s[1 - at], 3, 0)
    bound_copies = [
        send(
            bound_send.at[side],
            bound_recv.at[side],
            bound_send_sem.at[side],
            bound_recv_sem.at[side],
            (right_box, left_box)[side],
        )
        for side in range(2)
    ]
    bound_copies.append(
        send(
            g_chain.at[8 - quad, 0],
            quad_recv,
            bound_send_sem.at[2],
            bound_recv_sem.at[2],
            quad_device,
        )
    )

    for copy in near_copies:
        copy.wait_recv()

    @pl.when(device == 0)
    def _():
        field[1, :, 0:LEAF] = jnp.zeros((COLS, LEAF), f32)

    @pl.when(device == total - 1)
    def _():
        field[1, :, last + LEAF : last + 2 * LEAF] = jnp.zeros((COLS, LEAF), f32)

    near_two((LEAVES - 2) * LEAF)
    fill_tile(tile_c, 0, 0, LEAF)
    near[:, 0:LEAF] += lax.dot_general(
        field[1, :, 0:LEAF].astype(bf16), tile_c[...], NT, preferred_element_type=f32
    )

    def set_ends(ends, into, at_start, at_end):
        for level in range(3):
            before, after = (0, 6, 10)[level], (5, 9, 12)[level]
            into[before, 0] = jnp.where(at_start, 0.0, ends[0, level, 0])
            into[before, 1] = ends[0, level, 1]
            into[after, 0] = jnp.where(at_end, 0.0, ends[1, level, 0])
            into[after, 1] = ends[1, level, 1]

    for copy in edge_copies:
        copy.wait_recv()
    set_ends(edge_recv, chain, device == 0, device == total - 1)
    for pair, slot in enumerate([1, 2, 3, 4, 7, 8, 11]):
        local[pair] = cousins(chain, slot)

    def side(block, at):
        lanes = lax.broadcasted_iota(jnp.int32, block.shape, 1) // 64
        return jnp.where(lanes == at, block, 0.0)

    x2 = mm(side(path_map[member // 2], member % 2), maps[2], NT)
    x0 = lower(lower([x2], maps[1]), maps[0])
    leaf_high[...], leaf_low[...] = split(jnp.concatenate(x0, axis=1))

    for copy in far_copies:
        copy.wait_recv()

    @pl.when(jnp.logical_not(alone))
    def _():
        first_far.wait_recv()

    top_coef, top_skel = [], []
    for k in range(0, strides, 2):
        halves = []
        for at in (k, k + 1):
            apart = far_from[at] - box
            counts = jnp.logical_or(apart >= 2, apart <= -2)
            halves.append((far_buf[at], counts))
        (one, one_counts), (two, two_counts) = halves
        top_coef.append(
            jnp.where(
                low,
                jnp.where(one_counts, one, 0.0),
                jnp.where(two_counts, pltpu.roll(two, 64, 1), 0.0),
            )
        )
        top_skel.append(jnp.where(low, pltpu.roll(one, 64, 1), two))
    top_column = s6.T[:64]
    tx, ty, tz = top_column[:, 0:1], top_column[:, 1:2], top_column[:, 2:3]
    top_tile = jnp.concatenate(
        [phi(tx, ty, tz, s[0:1], s[1:2], s[2:3], far_scale) for s in top_skel], axis=1
    )
    top = mm(jnp.concatenate(top_coef, axis=1), split(top_tile), NT)
    part_buf[member] = jnp.concatenate([top, jnp.zeros((8, 64), f32)], axis=1)
    part_copies = []
    for r, mate in enumerate(mates):
        part_copies.append(
            send(
                part_buf.at[member],
                part_buf.at[member],
                part_send_sem.at[r],
                part_recv_sem.at[r],
                mate,
            )
        )

    for copy in bound_copies:
        copy.wait_recv()
    at_start, at_end = box == 0, box == boxes - 1
    outside = jnp.logical_or(
        jnp.logical_and(quad == 0, at_start), jnp.logical_and(quad == 1, at_end)
    )
    start_skel, end_skel = bound_recv[0, 1], bound_recv[1, 1]
    g_chain[10, 0] = jnp.where(at_start, 0.0, bound_recv[0, 0])
    g_chain[10, 1] = start_skel
    g_chain[12, 0] = jnp.where(at_end, 0.0, bound_recv[1, 0])
    g_chain[12, 1] = end_skel
    quad_coef = jnp.where(outside, 0.0, quad_recv[...])
    g_chain[6, 0] = quad_coef
    g_chain[6, 1] = pltpu.roll(start_skel, 5, 0)
    g_chain[9, 0] = quad_coef
    g_chain[9, 1] = pltpu.roll(end_skel, 5, 0)

    @pl.when(at_rim)
    def _():
        for copy in rim_copies:
            copy.wait_send()
        for t in range(2):
            pltpu.make_async_remote_copy(
                src_ref=g_buf.at[member],
                dst_ref=rim_recv.at[t],
                send_sem=rim_send_sem.at[t],
                recv_sem=rim_recv_sem.at[t],
                device_id=(rim_devices[t],),
                device_id_type=MESH,
            ).wait_recv()
        even, odd = rim_recv[0], rim_recv[1]
        rim_coef = jnp.where(outside, 0.0, jnp.where(low, even, odd))
        rim_skel = pltpu.roll(jnp.where(low, odd, even), 64, 1)
        for slot in (0, 5):
            g_chain[slot, 0] = rim_coef
            g_chain[slot, 1] = rim_skel

    local3 = cousins(g_chain, 1 + member // 2)
    local4 = cousins(g_chain, 7 + member // 4)
    local5 = cousins(g_chain, 11)
    y4 = local4 + mm(side(local5, member // 4), maps[4], NT)
    y3 = local3 + mm(side(y4, member // 2 % 2), maps[3], NT)
    y2 = local[6] + mm(side(y3, member % 2), maps[2], NT)
    y1 = [y + local[4 + at] for at, y in enumerate(lower([y2], maps[1]))]
    y0 = [y + local[at] for at, y in enumerate(lower(y1, maps[0]))]

    for copy in part_copies:
        copy.wait_recv()
    d6 = part_buf[0]
    for at in range(1, MEMBERS):
        d6 = d6 + part_buf[at]
    d0 = jnp.concatenate(y0, axis=1) + mm(d6[:, :64], (leaf_high, leaf_low), NN)
    for p in range(4):
        pair = d0[:, 128 * p : 128 * p + 128]
        two = jnp.concatenate([jnp.where(low, pair, 0.0), jnp.where(low, 0.0, pair)], axis=0)
        rows = lax.dot_general(
            two.astype(bf16),
            basis[128 * p : 128 * p + 128, :],
            NN,
            preferred_element_type=f32,
        )
        for t in range(2):
            leaf = 2 * p + t
            at = leaf * LEAF
            out_ref[:, at : at + LEAF] = jnp.where(
                slots < occ[leaf], near[:, at : at + LEAF] + rows[8 * t : 8 * t + 8], 0.0
            )

    for copy in started:
        copy.wait_send()

    @pl.when(jnp.logical_not(alone))
    def _():
        first_far.wait_send()


def body(boxes, coords, loads, occupancy, basis, transfer):
    strides = boxes // MEMBERS
    hbm = pl.BlockSpec(memory_space=pl.ANY)
    dma = pltpu.SemaphoreType.DMA
    return pl.pallas_call(
        functools.partial(kernel, boxes),
        out_shape=jax.ShapeDtypeStruct((COLS, OWN), f32),
        in_specs=[hbm] * 5,
        out_specs=pl.BlockSpec(memory_space=pltpu.VMEM),
        scratch_shapes=[
            pltpu.VMEM((3, OWN), f32),
            pltpu.VMEM((COLS, OWN), bf16),
            pltpu.SMEM((LEAVES,), jnp.int32),
            pltpu.VMEM((LEAVES * 64, LEAF), bf16),
            pltpu.VMEM((6, 128, 64), f32),
            pltpu.VMEM((6, 128, 128), bf16),
            pltpu.VMEM((6, 128, 128), bf16),
            pltpu.VMEM((4, 64, 128), f32),
            pltpu.VMEM((128, 512), bf16),
            pltpu.VMEM((128, 512), bf16),
            pltpu.VMEM((2, 8, OWN + 2 * LEAF), f32),
            pltpu.VMEM((OWN, 8), f32),
            pltpu.VMEM((64, 512), bf16),
            pltpu.VMEM((64, 512), bf16),
            pltpu.VMEM((COLS, OWN + LEAF), f32),
            pltpu.VMEM((LEAF, 2 * LEAF), bf16),
            pltpu.VMEM((LEAF, 2 * LEAF), bf16),
            pltpu.VMEM((LEAF, LEAF), bf16),
            pltpu.VMEM((13, 2, 8, 128), f32),
            pltpu.VMEM((13, 2, 8, 128), f32),
            pltpu.VMEM((7, 8, 128), f32),
            pltpu.VMEM((2, 3, 2, 8, 128), f32),
            pltpu.VMEM((2, 3, 2, 8, 128), f32),
            pltpu.VMEM((MEMBERS, 8, 128), f32),
            pltpu.VMEM((2, 2, 8, 128), f32),
            pltpu.VMEM((2, 2, 8, 128), f32),
            pltpu.VMEM((8, 128), f32),
            pltpu.VMEM((2, 8, 128), f32),
            pltpu.VMEM((8, 128), f32),
            pltpu.VMEM((strides, 8, 128), f32),
            pltpu.VMEM((MEMBERS, 8, 128), f32),
            dma((5,)),
            dma((2,)),
            dma((2,)),
            dma((2,)),
            dma((2,)),
            dma((MEMBERS - 1,)),
            dma((MEMBERS - 1,)),
            dma((3,)),
            dma((3,)),
            dma((2,)),
            dma((2,)),
            dma((strides,)),
            dma((strides,)),
            dma((MEMBERS - 1,)),
            dma((MEMBERS - 1,)),
        ],
        compiler_params=pltpu.CompilerParams(
            collective_id=0, has_side_effects=True, vmem_limit_bytes=32 * 1024 * 1024
        ),
    )(
        *[
            pltpu.with_memory_space_constraint(x, pltpu.HBM)
            for x in (
                coords,
                loads,
                occupancy,
                basis.reshape(LEAVES * 64, LEAF),
                transfer.reshape(6, 128, 64),
            )
        ]
    )


def solution(mesh):
    boxes = mesh.shape["box"] // MEMBERS
    return jax.shard_map(
        functools.partial(body, boxes),
        mesh=mesh,
        in_specs=(P(None, "box"), P(None, "box"), P("box"), P("box", None, None), P()),
        out_specs=P(None, "box"),
        check_vma=False,
    )
```

```python
import functools

import jax
import jax.numpy as jnp
from jax import lax
from jax.experimental import pallas as pl
from jax.experimental.pallas import tpu as pltpu
from jax.sharding import PartitionSpec as P

LEAF = 256
COLS = 8
LEAVES = 8
MEMBERS = 8
OWN = LEAF * LEAVES

f32 = jnp.float32
bf16 = jnp.bfloat16
soften = 0.0001
near_scale = 0.0625
far_scale = 0.125
NN = (((1,), (0,)), ((), ()))
NT = (((1,), (1,)), ((), ()))
MESH = pl.DeviceIdType.MESH


def phi(tx, ty, tz, sx, sy, sz, scale):
    dx = tx - sx
    dy = ty - sy
    dz = tz - sz
    r2 = dx * dx + dy * dy + dz * dz
    return (r2 * (0.5 * scale)) * jnp.log(r2 + soften)


def split(x):
    high = x.astype(bf16)
    return high, (x - high.astype(f32)).astype(bf16)


def mm(a, b, dims):
    rows = a.shape[0]
    high = a.astype(bf16).astype(f32)
    stacked = jnp.concatenate([high, a - high], axis=0).astype(bf16)
    both = lax.dot_general(stacked, b[0][...], dims, preferred_element_type=f32)
    low = lax.dot_general(stacked[:rows], b[1][...], dims, preferred_element_type=f32)
    return both[:rows] + (both[rows:] + low)


def low_half(shape):
    return lax.broadcasted_iota(jnp.int32, shape, len(shape) - 1) < 64


def merge(rows):
    count = rows.shape[0] // 16
    low = low_half((8, 128))
    return [
        jnp.where(low, rows[16 * i : 16 * i + 8], rows[16 * i + 8 : 16 * i + 16])
        for i in range(count)
    ]


def raise_coef(pairs, level_map):
    rows = mm(jnp.concatenate(pairs, axis=0), level_map, NN)
    return merge(rows) if len(pairs) > 1 else [rows]


def pick(x, entries):
    rows = x.shape[0]
    a = x.astype(bf16).astype(f32)
    b = (x - a).astype(bf16).astype(f32)
    c = (x - a) - b
    stacked = jnp.concatenate([a, b, c], axis=0).astype(bf16)
    picked = lax.dot_general(stacked, entries, NN, preferred_element_type=f32)
    return picked[:rows] + picked[rows : 2 * rows] + picked[2 * rows :]


def raise_skel(pairs, every_second):
    rows_up = pick(jnp.concatenate(pairs, axis=0), every_second)
    return merge(rows_up) if len(pairs) > 1 else [rows_up]


def cousins(chain, slot):
    low = low_half((8, 128))
    column = chain[slot, 1].T
    tx, ty, tz = column[:, 0:1], column[:, 1:2], column[:, 2:3]
    before, after = chain[slot - 1, 0], chain[slot + 1, 0]
    tiles = []
    for skel in (chain[slot - 1, 1], chain[slot + 1, 1]):
        tiles.append(phi(tx, ty, tz, skel[0:1], skel[1:2], skel[2:3], far_scale))
    tile = jnp.concatenate(tiles, axis=1)
    even = jnp.concatenate([jnp.where(low, before, 0.0), after], axis=1)
    odd = jnp.concatenate([before, jnp.where(low, 0.0, after)], axis=1)
    rows = mm(jnp.concatenate([even, odd], axis=0), split(tile), NT)
    return jnp.where(low, rows[:8], rows[8:])


def lower(pairs, level_map):
    height = pairs[0].shape[0]
    low = low_half((height, 128))
    stacked = []
    for pair in pairs:
        stacked += [jnp.where(low, pair, 0.0), jnp.where(low, 0.0, pair)]
    rows = mm(jnp.concatenate(stacked, axis=0), level_map, NT)
    return [rows[height * i : height * (i + 1)] for i in range(2 * len(pairs))]


def kernel(
    boxes,
    ahead,
    coords_hbm,
    loads_hbm,
    occ_hbm,
    basis_hbm,
    transfer_hbm,
    out_ref,
    coords,
    loads,
    occ,
    basis,
    transfer,
    map_high,
    map_low,
    path_map,
    path_high,
    path_low,
    field,
    column,
    leaf_high,
    leaf_low,
    near,
    tile_a,
    tile_b,
    tile_c,
    chain,
    g_chain,
    local,
    edge_send,
    edge_recv,
    g_buf,
    bound_send,
    bound_recv,
    quad_recv,
    rim_recv,
    far_send,
    far_buf,
    part_buf,
    load_sem,
    near_send_sem,
    near_recv_sem,
    edge_send_sem,
    edge_recv_sem,
    g_send_sem,
    g_recv_sem,
    bound_send_sem,
    bound_recv_sem,
    rim_send_sem,
    rim_recv_sem,
    far_send_sem,
    far_recv_sem,
    part_send_sem,
    part_recv_sem,
):
    loading = [
        pltpu.make_async_copy(src, dst, load_sem.at[at])
        for at, (src, dst) in enumerate(
            [
                (coords_hbm, coords),
                (transfer_hbm, transfer),
                (loads_hbm, loads),
                (occ_hbm, occ),
                (basis_hbm, basis),
            ]
        )
    ]
    for copy in loading:
        copy.start()

    device = lax.axis_index("box")
    total = boxes * MEMBERS
    box = device // MEMBERS
    member = device % MEMBERS
    low = low_half((8, 128))
    half = lax.broadcasted_iota(jnp.int32, (8, 128), 1) // 64

    left_device = (device + total - 1) % total
    right_device = (device + 1) % total
    left_box = ((box + boxes - 1) % boxes) * MEMBERS + member
    right_box = ((box + 1) % boxes) * MEMBERS + member
    mates = [box * MEMBERS + (member + r) % MEMBERS for r in range(1, MEMBERS)]
    strides = boxes // MEMBERS
    far_to = [
        (((box // MEMBERS + k) % strides) * MEMBERS + member) * MEMBERS + box % MEMBERS
        for k in range(strides)
    ]
    far_from = [
        ((box // MEMBERS + strides - k) % strides) * MEMBERS + member for k in range(strides)
    ]
    alone = box % MEMBERS == member
    pair = member // 2
    upper = pair // 3
    at_rim = pair % 3 == 0
    rim_box = (box + boxes + 2 * upper - 1) % boxes
    rim_devices = [rim_box * MEMBERS + 6 - 6 * upper + t for t in range(2)]
    quad = member // 4
    early = jnp.where(box // 2 % ahead == 0, 1, 0)
    quad_device = ((box + boxes + 1 - 2 * quad) % boxes) * MEMBERS + member

    barrier = pltpu.get_barrier_semaphore()

    def greet(target):
        pl.semaphore_signal(barrier, inc=1, device_id=(target,), device_id_type=MESH)

    for target in mates + [left_device, right_device, left_box, right_box]:
        greet(target)
    for k in range(1, strides):
        greet(far_from[k] * MEMBERS + box % MEMBERS)

    @pl.when(jnp.logical_not(alone))
    def _():
        greet(far_from[0] * MEMBERS + box % MEMBERS)

    @pl.when(at_rim)
    def _():
        for target in rim_devices:
            greet(target)

    eighths = lax.broadcasted_iota(jnp.int32, (512, 128), 1) % 64 * 8
    every_eighth = (
        (lax.broadcasted_iota(jnp.int32, (512, 128), 0) == eighths).astype(f32).astype(bf16)
    )
    loading[0].wait()
    points = jnp.concatenate([coords[...], jnp.zeros((5, OWN), f32)], axis=0)
    s0 = [
        jnp.concatenate(
            [points[:, 512 * p : 512 * p + 64], points[:, 512 * p + 256 : 512 * p + 320]], axis=1
        )
        for p in range(4)
    ]
    s3 = pick(jnp.concatenate(s0, axis=1), every_eighth)

    loading[1].wait()
    maps = [(map_high.at[level], map_low.at[level]) for level in range(6)]

    def set_map(level):
        once = transfer[level]
        map_high[level], map_low[level] = split(jnp.concatenate([once, once], axis=1))

    for level in range(3):
        set_map(level)
    loading[2].wait()
    loading[3].wait()
    slots = lax.broadcasted_iota(jnp.int32, (COLS, LEAF), 1)
    live = []
    for leaf in range(LEAVES):
        part = loads[:, leaf * LEAF : (leaf + 1) * LEAF].astype(f32)
        live.append(jnp.where(slots < occ[leaf], part, 0.0))
    loading[4].wait()
    c0 = []
    for p in range(4):
        two = jnp.concatenate([live[2 * p], live[2 * p + 1]], axis=0).astype(bf16)
        rows = lax.dot_general(
            two, basis[128 * p : 128 * p + 128, :], NT, preferred_element_type=f32
        )
        c0.append(jnp.where(low, rows[:8], rows[8:]))
    c1 = raise_coef(c0, maps[0])
    c2 = raise_coef(c1, maps[1])
    c3 = raise_coef(c2, maps[2])[0]

    g_buf[member] = jnp.where(half == member % 2, c3, s3)

    def set_field():
        field[0, :, LEAF : LEAF + OWN] = points
        for leaf in range(LEAVES):
            field[1, :, (leaf + 1) * LEAF : (leaf + 2) * LEAF] = live[leaf]
        for at in range(0, OWN, 128):
            column[at : at + 128, :] = points[:, at : at + 128].T
        near[...] = jnp.zeros_like(near)

    def fill_tile(tile, row, col, width):
        sx = field[0, 0:1, pl.ds(col, width)]
        sy = field[0, 1:2, pl.ds(col, width)]
        sz = field[0, 2:3, pl.ds(col, width)]
        for at in range(0, LEAF, 16):
            rows = column[pl.ds(row + at, 16), :]
            tile[at : at + 16, 0:width] = phi(
                rows[:, 0:1], rows[:, 1:2], rows[:, 2:3], sx, sy, sz, near_scale
            ).astype(bf16)

    def near_leaf(tile, row):
        col = row + LEAF
        fill_tile(tile, row, col, 2 * LEAF)
        loads_two = field[1, :, pl.ds(col, 2 * LEAF)].astype(bf16)
        this = lax.dot_general(loads_two, tile[...], NT, preferred_element_type=f32)
        after = lax.dot_general(
            loads_two[:, :LEAF], tile[:, LEAF:], NN, preferred_element_type=f32
        )
        return this, after

    def near_two(row):
        first, second_part = near_leaf(tile_a, row)
        second, third = near_leaf(tile_b, row + LEAF)
        near[:, pl.ds(row, LEAF)] += first
        near[:, pl.ds(row + LEAF, LEAF)] += second_part + second
        near[:, pl.ds(row + 2 * LEAF, LEAF)] += third

    def near_step(pair, carry):
        near_two(pl.multiple_of(pair * (2 * LEAF), 2 * LEAF))
        return carry

    @pl.when(early == 1)
    def _():
        set_field()
        lax.fori_loop(0, 3, near_step, 0)

    pl.semaphore_wait(
        barrier,
        4 + MEMBERS - 1 + strides - alone.astype(jnp.int32) + 2 * at_rim.astype(jnp.int32),
    )

    started = []

    def send(src, dst, send_sem, recv_sem, target):
        copy = pltpu.make_async_remote_copy(
            src_ref=src,
            dst_ref=dst,
            send_sem=send_sem,
            recv_sem=recv_sem,
            device_id=(target,),
            device_id_type=MESH,
        )
        copy.start()
        started.append(copy)
        return copy

    g_copies = []
    for r, mate in enumerate(mates):
        g_copies.append(
            send(g_buf.at[member], g_buf.at[member], g_send_sem.at[r], g_recv_sem.at[r], mate)
        )

    rim_copies = [
        pltpu.make_async_remote_copy(
            src_ref=g_buf.at[member],
            dst_ref=rim_recv.at[member % 2],
            send_sem=rim_send_sem.at[t],
            recv_sem=rim_recv_sem.at[member % 2],
            device_id=(rim_devices[t],),
            device_id_type=MESH,
        )
        for t in range(2)
    ]

    @pl.when(at_rim)
    def _():
        for copy in rim_copies:
            copy.start()

    @pl.when(early == 0)
    def _():
        set_field()

    last = LEAF * LEAVES
    near_copies = [
        send(
            field.at[:, :, last : last + LEAF],
            field.at[:, :, 0:LEAF],
            near_send_sem.at[0],
            near_recv_sem.at[0],
            right_device,
        ),
        send(
            field.at[:, :, LEAF : 2 * LEAF],
            field.at[:, :, last + LEAF : last + 2 * LEAF],
            near_send_sem.at[1],
            near_recv_sem.at[1],
            left_device,
        ),
    ]

    picks = lax.broadcasted_iota(jnp.int32, (128, 128), 1) % 64 * 2
    every_second = (
        (lax.broadcasted_iota(jnp.int32, (128, 128), 0) == picks).astype(f32).astype(bf16)
    )
    s1 = raise_skel(s0, every_second)
    s2 = raise_skel(s1, every_second)

    def set_chain(levels, into):
        for at, (pairs, skels) in enumerate(levels):
            first = (1, 7, 11)[at]
            for p in range(len(pairs)):
                into[first + p, 0] = pairs[p]
                into[first + p, 1] = skels[p]

    set_chain([(c0, s0), (c1, s1), (c2, s2)], chain)
    for at, (pairs, skels) in enumerate([(c0, s0), (c1, s1), (c2, s2)]):
        edge_send[0, at, 0] = pairs[-1]
        edge_send[0, at, 1] = skels[-1]
        edge_send[1, at, 0] = pairs[0]
        edge_send[1, at, 1] = skels[0]
    edge_copies = [
        send(
            edge_send.at[side],
            edge_recv.at[side],
            edge_send_sem.at[side],
            edge_recv_sem.at[side],
            (right_device, left_device)[side],
        )
        for side in range(2)
    ]

    for level in range(3, 6):
        set_map(level)
    paths = lower(lower([transfer[5].T], maps[4]), maps[3])
    for p in range(4):
        path_map[p] = paths[p]
    padded = jnp.concatenate(
        [jnp.concatenate(paths, axis=1), jnp.zeros((64, 512), f32)], axis=0
    )
    path_high[...], path_low[...] = split(padded)

    for copy in g_copies:
        copy.wait_recv()
    c3s, s3s = [], []
    for p in range(4):
        even, odd = g_buf[2 * p], g_buf[2 * p + 1]
        c3s.append(jnp.where(low, even, odd))
        s3s.append(pltpu.roll(jnp.where(low, odd, even), 64, 1))
    c6 = mm(jnp.concatenate(c3s, axis=1), (path_high, path_low), NT)
    s6 = pick(jnp.concatenate(s3s, axis=1), every_eighth)
    far_send[...] = jnp.where(low, c6, s6)

    @pl.when(alone)
    def _():
        far_buf[0] = far_send[...]

    far_copies = []
    for k in range(1, strides):
        far_copies.append(
            send(far_send, far_buf.at[k], far_send_sem.at[k], far_recv_sem.at[k], far_to[k])
        )
    first_far = pltpu.make_async_remote_copy(
        src_ref=far_send,
        dst_ref=far_buf.at[0],
        send_sem=far_send_sem.at[0],
        recv_sem=far_recv_sem.at[0],
        device_id=(far_to[0],),
        device_id_type=MESH,
    )

    @pl.when(jnp.logical_not(alone))
    def _():
        first_far.start()

    c4s, s4s = raise_coef(c3s, maps[3]), raise_skel(s3s, every_second)
    c5s, s5s = raise_coef(c4s, maps[4]), raise_skel(s4s, every_second)
    set_chain([(c3s, s3s), (c4s, s4s), (c5s, s5s)], g_chain)
    for at in range(2):
        bound_send[at, 0] = c5s[0]
        bound_send[at, 1] = s5s[0] + pltpu.roll(s4s[1 - at], 3, 0)
    bound_copies = [
        send(
            bound_send.at[side],
            bound_recv.at[side],
            bound_send_sem.at[side],
            bound_recv_sem.at[side],
            (right_box, left_box)[side],
        )
        for side in range(2)
    ]
    bound_copies.append(
        send(
            g_chain.at[8 - quad, 0],
            quad_recv,
            bound_send_sem.at[2],
            bound_recv_sem.at[2],
            quad_device,
        )
    )

    lax.fori_loop(3 * early, 3, near_step, 0)
    for copy in near_copies:
        copy.wait_recv()

    @pl.when(device == 0)
    def _():
        field[1, :, 0:LEAF] = jnp.zeros((COLS, LEAF), f32)

    @pl.when(device == total - 1)
    def _():
        field[1, :, last + LEAF : last + 2 * LEAF] = jnp.zeros((COLS, LEAF), f32)

    near_two((LEAVES - 2) * LEAF)
    fill_tile(tile_c, 0, 0, LEAF)
    near[:, 0:LEAF] += lax.dot_general(
        field[1, :, 0:LEAF].astype(bf16), tile_c[...], NT, preferred_element_type=f32
    )

    def set_ends(ends, into, at_start, at_end):
        for level in range(3):
            before, after = (0, 6, 10)[level], (5, 9, 12)[level]
            into[before, 0] = jnp.where(at_start, 0.0, ends[0, level, 0])
            into[before, 1] = ends[0, level, 1]
            into[after, 0] = jnp.where(at_end, 0.0, ends[1, level, 0])
            into[after, 1] = ends[1, level, 1]

    for copy in edge_copies:
        copy.wait_recv()
    set_ends(edge_recv, chain, device == 0, device == total - 1)
    for pair, slot in enumerate([1, 2, 3, 4, 7, 8, 11]):
        local[pair] = cousins(chain, slot)

    def side(block, at):
        lanes = lax.broadcasted_iota(jnp.int32, block.shape, 1) // 64
        return jnp.where(lanes == at, block, 0.0)

    x2 = mm(side(path_map[member // 2], member % 2), maps[2], NT)
    x0 = lower(lower([x2], maps[1]), maps[0])
    leaf_high[...], leaf_low[...] = split(jnp.concatenate(x0, axis=1))

    for copy in far_copies:
        copy.wait_recv()

    @pl.when(jnp.logical_not(alone))
    def _():
        first_far.wait_recv()

    top_coef, top_skel = [], []
    for k in range(0, strides, 2):
        halves = []
        for at in (k, k + 1):
            apart = far_from[at] - box
            counts = jnp.logical_or(apart >= 2, apart <= -2)
            halves.append((far_buf[at], counts))
        (one, one_counts), (two, two_counts) = halves
        top_coef.append(
            jnp.where(
                low,
                jnp.where(one_counts, one, 0.0),
                jnp.where(two_counts, pltpu.roll(two, 64, 1), 0.0),
            )
        )
        top_skel.append(jnp.where(low, pltpu.roll(one, 64, 1), two))
    top_column = s6.T[:64]
    tx, ty, tz = top_column[:, 0:1], top_column[:, 1:2], top_column[:, 2:3]
    top_tile = jnp.concatenate(
        [phi(tx, ty, tz, s[0:1], s[1:2], s[2:3], far_scale) for s in top_skel], axis=1
    )
    top = mm(jnp.concatenate(top_coef, axis=1), split(top_tile), NT)
    part_buf[member] = jnp.concatenate([top, jnp.zeros((8, 64), f32)], axis=1)
    part_copies = []
    for r, mate in enumerate(mates):
        part_copies.append(
            send(
                part_buf.at[member],
                part_buf.at[member],
                part_send_sem.at[r],
                part_recv_sem.at[r],
                mate,
            )
        )

    for copy in bound_copies:
        copy.wait_recv()
    at_start, at_end = box == 0, box == boxes - 1
    outside = jnp.logical_or(
        jnp.logical_and(quad == 0, at_start), jnp.logical_and(quad == 1, at_end)
    )
    start_skel, end_skel = bound_recv[0, 1], bound_recv[1, 1]
    g_chain[10, 0] = jnp.where(at_start, 0.0, bound_recv[0, 0])
    g_chain[10, 1] = start_skel
    g_chain[12, 0] = jnp.where(at_end, 0.0, bound_recv[1, 0])
    g_chain[12, 1] = end_skel
    quad_coef = jnp.where(outside, 0.0, quad_recv[...])
    g_chain[6, 0] = quad_coef
    g_chain[6, 1] = pltpu.roll(start_skel, 5, 0)
    g_chain[9, 0] = quad_coef
    g_chain[9, 1] = pltpu.roll(end_skel, 5, 0)

    @pl.when(at_rim)
    def _():
        for copy in rim_copies:
            copy.wait_send()
        for t in range(2):
            pltpu.make_async_remote_copy(
                src_ref=g_buf.at[member],
                dst_ref=rim_recv.at[t],
                send_sem=rim_send_sem.at[t],
                recv_sem=rim_recv_sem.at[t],
                device_id=(rim_devices[t],),
                device_id_type=MESH,
            ).wait_recv()
        even, odd = rim_recv[0], rim_recv[1]
        rim_coef = jnp.where(outside, 0.0, jnp.where(low, even, odd))
        rim_skel = pltpu.roll(jnp.where(low, odd, even), 64, 1)
        for slot in (0, 5):
            g_chain[slot, 0] = rim_coef
            g_chain[slot, 1] = rim_skel

    local3 = cousins(g_chain, 1 + member // 2)
    local4 = cousins(g_chain, 7 + member // 4)
    local5 = cousins(g_chain, 11)
    y4 = local4 + mm(side(local5, member // 4), maps[4], NT)
    y3 = local3 + mm(side(y4, member // 2 % 2), maps[3], NT)
    y2 = local[6] + mm(side(y3, member % 2), maps[2], NT)
    y1 = [y + local[4 + at] for at, y in enumerate(lower([y2], maps[1]))]
    y0 = [y + local[at] for at, y in enumerate(lower(y1, maps[0]))]

    for copy in part_copies:
        copy.wait_recv()
    d6 = part_buf[0]
    for at in range(1, MEMBERS):
        d6 = d6 + part_buf[at]
    d0 = jnp.concatenate(y0, axis=1) + mm(d6[:, :64], (leaf_high, leaf_low), NN)
    for p in range(4):
        pair = d0[:, 128 * p : 128 * p + 128]
        two = jnp.concatenate([jnp.where(low, pair, 0.0), jnp.where(low, 0.0, pair)], axis=0)
        rows = lax.dot_general(
            two.astype(bf16),
            basis[128 * p : 128 * p + 128, :],
            NN,
            preferred_element_type=f32,
        )
        for t in range(2):
            leaf = 2 * p + t
            at = leaf * LEAF
            out_ref[:, at : at + LEAF] = jnp.where(
                slots < occ[leaf], near[:, at : at + LEAF] + rows[8 * t : 8 * t + 8], 0.0
            )

    for copy in started:
        copy.wait_send()

    @pl.when(jnp.logical_not(alone))
    def _():
        first_far.wait_send()


def body(boxes, ahead, coords, loads, occupancy, basis, transfer):
    strides = boxes // MEMBERS
    hbm = pl.BlockSpec(memory_space=pl.ANY)
    dma = pltpu.SemaphoreType.DMA
    return pl.pallas_call(
        functools.partial(kernel, boxes, ahead),
        out_shape=jax.ShapeDtypeStruct((COLS, OWN), f32),
        in_specs=[hbm] * 5,
        out_specs=pl.BlockSpec(memory_space=pltpu.VMEM),
        scratch_shapes=[
            pltpu.VMEM((3, OWN), f32),
            pltpu.VMEM((COLS, OWN), bf16),
            pltpu.SMEM((LEAVES,), jnp.int32),
            pltpu.VMEM((LEAVES * 64, LEAF), bf16),
            pltpu.VMEM((6, 128, 64), f32),
            pltpu.VMEM((6, 128, 128), bf16),
            pltpu.VMEM((6, 128, 128), bf16),
            pltpu.VMEM((4, 64, 128), f32),
            pltpu.VMEM((128, 512), bf16),
            pltpu.VMEM((128, 512), bf16),
            pltpu.VMEM((2, 8, OWN + 2 * LEAF), f32),
            pltpu.VMEM((OWN, 8), f32),
            pltpu.VMEM((64, 512), bf16),
            pltpu.VMEM((64, 512), bf16),
            pltpu.VMEM((COLS, OWN + LEAF), f32),
            pltpu.VMEM((LEAF, 2 * LEAF), bf16),
            pltpu.VMEM((LEAF, 2 * LEAF), bf16),
            pltpu.VMEM((LEAF, LEAF), bf16),
            pltpu.VMEM((13, 2, 8, 128), f32),
            pltpu.VMEM((13, 2, 8, 128), f32),
            pltpu.VMEM((7, 8, 128), f32),
            pltpu.VMEM((2, 3, 2, 8, 128), f32),
            pltpu.VMEM((2, 3, 2, 8, 128), f32),
            pltpu.VMEM((MEMBERS, 8, 128), f32),
            pltpu.VMEM((2, 2, 8, 128), f32),
            pltpu.VMEM((2, 2, 8, 128), f32),
            pltpu.VMEM((8, 128), f32),
            pltpu.VMEM((2, 8, 128), f32),
            pltpu.VMEM((8, 128), f32),
            pltpu.VMEM((strides, 8, 128), f32),
            pltpu.VMEM((MEMBERS, 8, 128), f32),
            dma((5,)),
            dma((2,)),
            dma((2,)),
            dma((2,)),
            dma((2,)),
            dma((MEMBERS - 1,)),
            dma((MEMBERS - 1,)),
            dma((3,)),
            dma((3,)),
            dma((2,)),
            dma((2,)),
            dma((strides,)),
            dma((strides,)),
            dma((MEMBERS - 1,)),
            dma((MEMBERS - 1,)),
        ],
        compiler_params=pltpu.CompilerParams(
            collective_id=0, has_side_effects=True, vmem_limit_bytes=32 * 1024 * 1024
        ),
    )(
        *[
            pltpu.with_memory_space_constraint(x, pltpu.HBM)
            for x in (
                coords,
                loads,
                occupancy,
                basis.reshape(LEAVES * 64, LEAF),
                transfer.reshape(6, 128, 64),
            )
        ]
    )


def solution(mesh):
    boxes = mesh.shape["box"] // MEMBERS
    return jax.shard_map(
        functools.partial(body, boxes, 8),
        mesh=mesh,
        in_specs=(P(None, "box"), P(None, "box"), P("box"), P("box", None, None), P()),
        out_specs=P(None, "box"),
        check_vma=False,
    )
```

```python
import functools

import jax
import jax.numpy as jnp
from jax import lax
from jax.experimental import pallas as pl
from jax.experimental.pallas import tpu as pltpu
from jax.sharding import PartitionSpec as P

LEAF = 256
COLS = 8
LEAVES = 8
MEMBERS = 8
OWN = LEAF * LEAVES

f32 = jnp.float32
bf16 = jnp.bfloat16
soften = 0.0001
near_scale = 0.0625
far_scale = 0.125
NN = (((1,), (0,)), ((), ()))
NT = (((1,), (1,)), ((), ()))
MESH = pl.DeviceIdType.MESH


def phi(tx, ty, tz, sx, sy, sz, scale):
    dx = tx - sx
    dy = ty - sy
    dz = tz - sz
    r2 = dx * dx + dy * dy + dz * dz
    return (r2 * (0.5 * scale)) * jnp.log(r2 + soften)


def split(x):
    high = x.astype(bf16)
    return high, (x - high.astype(f32)).astype(bf16)


def mm(a, b, dims):
    rows = a.shape[0]
    high = a.astype(bf16).astype(f32)
    stacked = jnp.concatenate([high, a - high], axis=0).astype(bf16)
    both = lax.dot_general(stacked, b[0][...], dims, preferred_element_type=f32)
    low = lax.dot_general(stacked[:rows], b[1][...], dims, preferred_element_type=f32)
    return both[:rows] + (both[rows:] + low)


def low_half(shape):
    return lax.broadcasted_iota(jnp.int32, shape, len(shape) - 1) < 64


def merge(rows):
    count = rows.shape[0] // 16
    low = low_half((8, 128))
    return [
        jnp.where(low, rows[16 * i : 16 * i + 8], rows[16 * i + 8 : 16 * i + 16])
        for i in range(count)
    ]


def raise_coef(pairs, level_map):
    rows = mm(jnp.concatenate(pairs, axis=0), level_map, NN)
    return merge(rows) if len(pairs) > 1 else [rows]


def pick(x, entries):
    rows = x.shape[0]
    a = x.astype(bf16).astype(f32)
    b = (x - a).astype(bf16).astype(f32)
    c = (x - a) - b
    stacked = jnp.concatenate([a, b, c], axis=0).astype(bf16)
    picked = lax.dot_general(stacked, entries, NN, preferred_element_type=f32)
    return picked[:rows] + picked[rows : 2 * rows] + picked[2 * rows :]


def raise_skel(pairs, every_second):
    rows_up = pick(jnp.concatenate(pairs, axis=0), every_second)
    return merge(rows_up) if len(pairs) > 1 else [rows_up]


def cousins(chain, slot):
    low = low_half((8, 128))
    column = chain[slot, 1].T
    tx, ty, tz = column[:, 0:1], column[:, 1:2], column[:, 2:3]
    before, after = chain[slot - 1, 0], chain[slot + 1, 0]
    tiles = []
    for skel in (chain[slot - 1, 1], chain[slot + 1, 1]):
        tiles.append(phi(tx, ty, tz, skel[0:1], skel[1:2], skel[2:3], far_scale))
    tile = jnp.concatenate(tiles, axis=1)
    even = jnp.concatenate([jnp.where(low, before, 0.0), after], axis=1)
    odd = jnp.concatenate([before, jnp.where(low, 0.0, after)], axis=1)
    rows = mm(jnp.concatenate([even, odd], axis=0), split(tile), NT)
    return jnp.where(low, rows[:8], rows[8:])


def lower(pairs, level_map):
    height = pairs[0].shape[0]
    low = low_half((height, 128))
    stacked = []
    for pair in pairs:
        stacked += [jnp.where(low, pair, 0.0), jnp.where(low, 0.0, pair)]
    rows = mm(jnp.concatenate(stacked, axis=0), level_map, NT)
    return [rows[height * i : height * (i + 1)] for i in range(2 * len(pairs))]


def kernel(
    boxes,
    across,
    coords_hbm,
    loads_hbm,
    occ_hbm,
    basis_hbm,
    transfer_hbm,
    out_ref,
    coords,
    loads,
    occ,
    basis,
    transfer,
    map_high,
    map_low,
    path_map,
    path_high,
    path_low,
    field,
    column,
    leaf_high,
    leaf_low,
    near,
    tile_a,
    tile_b,
    tile_c,
    chain,
    g_chain,
    local,
    edge_send,
    edge_recv,
    g_buf,
    bound_send,
    bound_recv,
    quad_recv,
    rim_recv,
    far_send,
    far_buf,
    part_buf,
    load_sem,
    near_send_sem,
    near_recv_sem,
    edge_send_sem,
    edge_recv_sem,
    g_send_sem,
    g_recv_sem,
    bound_send_sem,
    bound_recv_sem,
    rim_send_sem,
    rim_recv_sem,
    far_send_sem,
    far_recv_sem,
    part_send_sem,
    part_recv_sem,
):
    loading = [
        pltpu.make_async_copy(src, dst, load_sem.at[at])
        for at, (src, dst) in enumerate(
            [
                (coords_hbm, coords),
                (transfer_hbm, transfer),
                (loads_hbm, loads),
                (occ_hbm, occ),
                (basis_hbm, basis),
            ]
        )
    ]
    for copy in loading:
        copy.start()

    device = lax.axis_index("box")
    total = boxes * MEMBERS
    box = device // MEMBERS
    member = device % MEMBERS
    low = low_half((8, 128))
    half = lax.broadcasted_iota(jnp.int32, (8, 128), 1) // 64

    left_device = (device + total - 1) % total
    right_device = (device + 1) % total
    left_box = ((box + boxes - 1) % boxes) * MEMBERS + member
    right_box = ((box + 1) % boxes) * MEMBERS + member
    mates = [box * MEMBERS + (member + r) % MEMBERS for r in (6, 2, 7, 3, 5, 4, 1)]

    strides = boxes // MEMBERS
    depth = boxes // (2 * across)
    x, z, y_half = box // (2 * depth), box // 2 % depth, box % 2
    y, core = member // 2, member % 2
    outer = jnp.where(y % 3 == 0, 1, 0)
    send_side = outer * (y // 3) + (1 - outer) * (y - 1)
    recv_side = outer * (1 - y // 3) + (1 - outer) * (y - 1)
    far_half = y_half + outer * (1 - 2 * y_half)
    far_member = 2 * (y + outer * (3 - 2 * y)) + z // 2 % 2

    def far_box(side, step, turn):
        other_z = (side + z) % 2 + 2 * core + 4 * ((z // 4 + turn) % 2)
        return ((x + across + step) % across * depth + other_z) * 2 + far_half

    far_steps = [(dx, turn) for dx in range(across) for turn in range(2)]
    far_to = [far_box(send_side, dx, turn) * MEMBERS + far_member for dx, turn in far_steps]
    far_from = [far_box(recv_side, -dx, turn) for dx, turn in far_steps]
    alone = jnp.logical_and(outer == 0, jnp.logical_and(send_side == 0, core == z // 2 % 2))
    pair = member // 2
    upper = pair // 3
    at_rim = pair % 3 == 0
    rim_box = (box + boxes + 2 * upper - 1) % boxes
    rim_devices = [rim_box * MEMBERS + 6 - 6 * upper + t for t in range(2)]
    quad = member // 4
    early = jnp.where(z == 0, 1, 0)
    quad_device = ((box + boxes + 1 - 2 * quad) % boxes) * MEMBERS + member

    barrier = pltpu.get_barrier_semaphore()

    def greet(target):
        pl.semaphore_signal(barrier, inc=1, device_id=(target,), device_id_type=MESH)

    for target in mates + [left_device, right_device, left_box, right_box]:
        greet(target)
    far_order = sorted(range(1, strides), key=lambda k: abs(far_steps[k][0] - across // 2))
    for k in far_order:
        greet(far_from[k] * MEMBERS + far_member)

    @pl.when(jnp.logical_not(alone))
    def _():
        greet(far_from[0] * MEMBERS + far_member)

    @pl.when(at_rim)
    def _():
        for target in rim_devices:
            greet(target)

    eighths = lax.broadcasted_iota(jnp.int32, (512, 128), 1) % 64 * 8
    every_eighth = (
        (lax.broadcasted_iota(jnp.int32, (512, 128), 0) == eighths).astype(f32).astype(bf16)
    )
    loading[0].wait()
    points = jnp.concatenate([coords[...], jnp.zeros((5, OWN), f32)], axis=0)
    s0 = [
        jnp.concatenate(
            [points[:, 512 * p : 512 * p + 64], points[:, 512 * p + 256 : 512 * p + 320]], axis=1
        )
        for p in range(4)
    ]
    s3 = pick(jnp.concatenate(s0, axis=1), every_eighth)

    loading[1].wait()
    maps = [(map_high.at[level], map_low.at[level]) for level in range(6)]

    def set_map(level):
        once = transfer[level]
        map_high[level], map_low[level] = split(jnp.concatenate([once, once], axis=1))

    for level in range(3):
        set_map(level)
    loading[2].wait()
    loading[3].wait()
    slots = lax.broadcasted_iota(jnp.int32, (COLS, LEAF), 1)
    live = []
    for leaf in range(LEAVES):
        part = loads[:, leaf * LEAF : (leaf + 1) * LEAF].astype(f32)
        live.append(jnp.where(slots < occ[leaf], part, 0.0))
    loading[4].wait()
    c0 = []
    for p in range(4):
        two = jnp.concatenate([live[2 * p], live[2 * p + 1]], axis=0).astype(bf16)
        rows = lax.dot_general(
            two, basis[128 * p : 128 * p + 128, :], NT, preferred_element_type=f32
        )
        c0.append(jnp.where(low, rows[:8], rows[8:]))
    c1 = raise_coef(c0, maps[0])
    c2 = raise_coef(c1, maps[1])
    c3 = raise_coef(c2, maps[2])[0]

    g_buf[member] = jnp.where(half == member % 2, c3, s3)

    def set_field():
        field[0, :, LEAF : LEAF + OWN] = points
        for leaf in range(LEAVES):
            field[1, :, (leaf + 1) * LEAF : (leaf + 2) * LEAF] = live[leaf]
        for at in range(0, OWN, 128):
            column[at : at + 128, :] = points[:, at : at + 128].T
        near[...] = jnp.zeros_like(near)

    def fill_tile(tile, row, col, width):
        sx = field[0, 0:1, pl.ds(col, width)]
        sy = field[0, 1:2, pl.ds(col, width)]
        sz = field[0, 2:3, pl.ds(col, width)]
        for at in range(0, LEAF, 16):
            rows = column[pl.ds(row + at, 16), :]
            tile[at : at + 16, 0:width] = phi(
                rows[:, 0:1], rows[:, 1:2], rows[:, 2:3], sx, sy, sz, near_scale
            ).astype(bf16)

    def near_leaf(tile, row):
        col = row + LEAF
        fill_tile(tile, row, col, 2 * LEAF)
        loads_two = field[1, :, pl.ds(col, 2 * LEAF)].astype(bf16)
        this = lax.dot_general(loads_two, tile[...], NT, preferred_element_type=f32)
        after = lax.dot_general(
            loads_two[:, :LEAF], tile[:, LEAF:], NN, preferred_element_type=f32
        )
        return this, after

    def near_two(row):
        first, second_part = near_leaf(tile_a, row)
        second, third = near_leaf(tile_b, row + LEAF)
        near[:, pl.ds(row, LEAF)] += first
        near[:, pl.ds(row + LEAF, LEAF)] += second_part + second
        near[:, pl.ds(row + 2 * LEAF, LEAF)] += third

    def near_step(pair, carry):
        near_two(pl.multiple_of(pair * (2 * LEAF), 2 * LEAF))
        return carry

    @pl.when(early == 1)
    def _():
        set_field()
        lax.fori_loop(0, 3, near_step, 0)

    pl.semaphore_wait(
        barrier,
        4 + MEMBERS - 1 + strides - alone.astype(jnp.int32) + 2 * at_rim.astype(jnp.int32),
    )

    started = []

    def send(src, dst, send_sem, recv_sem, target):
        copy = pltpu.make_async_remote_copy(
            src_ref=src,
            dst_ref=dst,
            send_sem=send_sem,
            recv_sem=recv_sem,
            device_id=(target,),
            device_id_type=MESH,
        )
        copy.start()
        started.append(copy)
        return copy

    g_copies = []
    for r, mate in enumerate(mates):
        g_copies.append(
            send(g_buf.at[member], g_buf.at[member], g_send_sem.at[r], g_recv_sem.at[r], mate)
        )

    rim_copies = [
        pltpu.make_async_remote_copy(
            src_ref=g_buf.at[member],
            dst_ref=rim_recv.at[member % 2],
            send_sem=rim_send_sem.at[t],
            recv_sem=rim_recv_sem.at[member % 2],
            device_id=(rim_devices[t],),
            device_id_type=MESH,
        )
        for t in range(2)
    ]

    @pl.when(at_rim)
    def _():
        for copy in rim_copies:
            copy.start()

    @pl.when(early == 0)
    def _():
        set_field()

    last = LEAF * LEAVES
    near_copies = [
        send(
            field.at[:, :, last : last + LEAF],
            field.at[:, :, 0:LEAF],
            near_send_sem.at[0],
            near_recv_sem.at[0],
            right_device,
        ),
        send(
            field.at[:, :, LEAF : 2 * LEAF],
            field.at[:, :, last + LEAF : last + 2 * LEAF],
            near_send_sem.at[1],
            near_recv_sem.at[1],
            left_device,
        ),
    ]

    picks = lax.broadcasted_iota(jnp.int32, (128, 128), 1) % 64 * 2
    every_second = (
        (lax.broadcasted_iota(jnp.int32, (128, 128), 0) == picks).astype(f32).astype(bf16)
    )
    s1 = raise_skel(s0, every_second)
    s2 = raise_skel(s1, every_second)

    def set_chain(levels, into):
        for at, (pairs, skels) in enumerate(levels):
            first = (1, 7, 11)[at]
            for p in range(len(pairs)):
                into[first + p, 0] = pairs[p]
                into[first + p, 1] = skels[p]

    set_chain([(c0, s0), (c1, s1), (c2, s2)], chain)
    for at, (pairs, skels) in enumerate([(c0, s0), (c1, s1), (c2, s2)]):
        edge_send[0, at, 0] = pairs[-1]
        edge_send[0, at, 1] = skels[-1]
        edge_send[1, at, 0] = pairs[0]
        edge_send[1, at, 1] = skels[0]
    edge_copies = [
        send(
            edge_send.at[side],
            edge_recv.at[side],
            edge_send_sem.at[side],
            edge_recv_sem.at[side],
            (right_device, left_device)[side],
        )
        for side in range(2)
    ]

    for level in range(3, 6):
        set_map(level)
    paths = lower(lower([transfer[5].T], maps[4]), maps[3])
    for p in range(4):
        path_map[p] = paths[p]
    padded = jnp.concatenate(
        [jnp.concatenate(paths, axis=1), jnp.zeros((64, 512), f32)], axis=0
    )
    path_high[...], path_low[...] = split(padded)

    for copy in g_copies:
        copy.wait_recv()
    c3s, s3s = [], []
    for p in range(4):
        even, odd = g_buf[2 * p], g_buf[2 * p + 1]
        c3s.append(jnp.where(low, even, odd))
        s3s.append(pltpu.roll(jnp.where(low, odd, even), 64, 1))
    c6 = mm(jnp.concatenate(c3s, axis=1), (path_high, path_low), NT)
    s6 = pick(jnp.concatenate(s3s, axis=1), every_eighth)
    far_send[...] = jnp.where(low, c6, s6)

    @pl.when(alone)
    def _():
        far_buf[0] = far_send[...]

    far_copies = []
    for k in far_order:
        far_copies.append(
            send(far_send, far_buf.at[k], far_send_sem.at[k], far_recv_sem.at[k], far_to[k])
        )
    first_far = pltpu.make_async_remote_copy(
        src_ref=far_send,
        dst_ref=far_buf.at[0],
        send_sem=far_send_sem.at[0],
        recv_sem=far_recv_sem.at[0],
        device_id=(far_to[0],),
        device_id_type=MESH,
    )

    @pl.when(jnp.logical_not(alone))
    def _():
        first_far.start()

    c4s, s4s = raise_coef(c3s, maps[3]), raise_skel(s3s, every_second)
    c5s, s5s = raise_coef(c4s, maps[4]), raise_skel(s4s, every_second)
    set_chain([(c3s, s3s), (c4s, s4s), (c5s, s5s)], g_chain)
    for at in range(2):
        bound_send[at, 0] = c5s[0]
        bound_send[at, 1] = s5s[0] + pltpu.roll(s4s[1 - at], 3, 0)
    bound_copies = [
        send(
            bound_send.at[side],
            bound_recv.at[side],
            bound_send_sem.at[side],
            bound_recv_sem.at[side],
            (right_box, left_box)[side],
        )
        for side in range(2)
    ]
    bound_copies.append(
        send(
            g_chain.at[8 - quad, 0],
            quad_recv,
            bound_send_sem.at[2],
            bound_recv_sem.at[2],
            quad_device,
        )
    )

    lax.fori_loop(3 * early, 3, near_step, 0)
    for copy in near_copies:
        copy.wait_recv()

    @pl.when(device == 0)
    def _():
        field[1, :, 0:LEAF] = jnp.zeros((COLS, LEAF), f32)

    @pl.when(device == total - 1)
    def _():
        field[1, :, last + LEAF : last + 2 * LEAF] = jnp.zeros((COLS, LEAF), f32)

    near_two((LEAVES - 2) * LEAF)
    fill_tile(tile_c, 0, 0, LEAF)
    near[:, 0:LEAF] += lax.dot_general(
        field[1, :, 0:LEAF].astype(bf16), tile_c[...], NT, preferred_element_type=f32
    )

    def set_ends(ends, into, at_start, at_end):
        for level in range(3):
            before, after = (0, 6, 10)[level], (5, 9, 12)[level]
            into[before, 0] = jnp.where(at_start, 0.0, ends[0, level, 0])
            into[before, 1] = ends[0, level, 1]
            into[after, 0] = jnp.where(at_end, 0.0, ends[1, level, 0])
            into[after, 1] = ends[1, level, 1]

    for copy in edge_copies:
        copy.wait_recv()
    set_ends(edge_recv, chain, device == 0, device == total - 1)
    for pair, slot in enumerate([1, 2, 3, 4, 7, 8, 11]):
        local[pair] = cousins(chain, slot)

    def side(block, at):
        lanes = lax.broadcasted_iota(jnp.int32, block.shape, 1) // 64
        return jnp.where(lanes == at, block, 0.0)

    x2 = mm(side(path_map[member // 2], member % 2), maps[2], NT)
    x0 = lower(lower([x2], maps[1]), maps[0])
    leaf_high[...], leaf_low[...] = split(jnp.concatenate(x0, axis=1))

    for copy in far_copies:
        copy.wait_recv()

    @pl.when(jnp.logical_not(alone))
    def _():
        first_far.wait_recv()

    top_coef, top_skel = [], []
    for k in range(0, strides, 2):
        halves = []
        for at in (k, k + 1):
            apart = far_from[at] - box
            counts = jnp.logical_or(apart >= 2, apart <= -2)
            halves.append((far_buf[at], counts))
        (one, one_counts), (two, two_counts) = halves
        top_coef.append(
            jnp.where(
                low,
                jnp.where(one_counts, one, 0.0),
                jnp.where(two_counts, pltpu.roll(two, 64, 1), 0.0),
            )
        )
        top_skel.append(jnp.where(low, pltpu.roll(one, 64, 1), two))
    top_column = s6.T[:64]
    tx, ty, tz = top_column[:, 0:1], top_column[:, 1:2], top_column[:, 2:3]
    top_tile = jnp.concatenate(
        [phi(tx, ty, tz, s[0:1], s[1:2], s[2:3], far_scale) for s in top_skel], axis=1
    )
    top = mm(jnp.concatenate(top_coef, axis=1), split(top_tile), NT)
    part_buf[member] = jnp.concatenate([top, jnp.zeros((8, 64), f32)], axis=1)
    part_copies = []
    for r, mate in enumerate(mates):
        part_copies.append(
            send(
                part_buf.at[member],
                part_buf.at[member],
                part_send_sem.at[r],
                part_recv_sem.at[r],
                mate,
            )
        )

    for copy in bound_copies:
        copy.wait_recv()
    at_start, at_end = box == 0, box == boxes - 1
    outside = jnp.logical_or(
        jnp.logical_and(quad == 0, at_start), jnp.logical_and(quad == 1, at_end)
    )
    start_skel, end_skel = bound_recv[0, 1], bound_recv[1, 1]
    g_chain[10, 0] = jnp.where(at_start, 0.0, bound_recv[0, 0])
    g_chain[10, 1] = start_skel
    g_chain[12, 0] = jnp.where(at_end, 0.0, bound_recv[1, 0])
    g_chain[12, 1] = end_skel
    quad_coef = jnp.where(outside, 0.0, quad_recv[...])
    g_chain[6, 0] = quad_coef
    g_chain[6, 1] = pltpu.roll(start_skel, 5, 0)
    g_chain[9, 0] = quad_coef
    g_chain[9, 1] = pltpu.roll(end_skel, 5, 0)

    @pl.when(at_rim)
    def _():
        for copy in rim_copies:
            copy.wait_send()
        for t in range(2):
            pltpu.make_async_remote_copy(
                src_ref=g_buf.at[member],
                dst_ref=rim_recv.at[t],
                send_sem=rim_send_sem.at[t],
                recv_sem=rim_recv_sem.at[t],
                device_id=(rim_devices[t],),
                device_id_type=MESH,
            ).wait_recv()
        even, odd = rim_recv[0], rim_recv[1]
        rim_coef = jnp.where(outside, 0.0, jnp.where(low, even, odd))
        rim_skel = pltpu.roll(jnp.where(low, odd, even), 64, 1)
        for slot in (0, 5):
            g_chain[slot, 0] = rim_coef
            g_chain[slot, 1] = rim_skel

    local3 = cousins(g_chain, 1 + member // 2)
    local4 = cousins(g_chain, 7 + member // 4)
    local5 = cousins(g_chain, 11)
    y4 = local4 + mm(side(local5, member // 4), maps[4], NT)
    y3 = local3 + mm(side(y4, member // 2 % 2), maps[3], NT)
    y2 = local[6] + mm(side(y3, member % 2), maps[2], NT)
    y1 = [y + local[4 + at] for at, y in enumerate(lower([y2], maps[1]))]
    y0 = [y + local[at] for at, y in enumerate(lower(y1, maps[0]))]

    for copy in part_copies:
        copy.wait_recv()
    d6 = part_buf[0]
    for at in range(1, MEMBERS):
        d6 = d6 + part_buf[at]
    d0 = jnp.concatenate(y0, axis=1) + mm(d6[:, :64], (leaf_high, leaf_low), NN)
    for p in range(4):
        pair = d0[:, 128 * p : 128 * p + 128]
        two = jnp.concatenate([jnp.where(low, pair, 0.0), jnp.where(low, 0.0, pair)], axis=0)
        rows = lax.dot_general(
            two.astype(bf16),
            basis[128 * p : 128 * p + 128, :],
            NN,
            preferred_element_type=f32,
        )
        for t in range(2):
            leaf = 2 * p + t
            at = leaf * LEAF
            out_ref[:, at : at + LEAF] = jnp.where(
                slots < occ[leaf], near[:, at : at + LEAF] + rows[8 * t : 8 * t + 8], 0.0
            )

    for copy in started:
        copy.wait_send()

    @pl.when(jnp.logical_not(alone))
    def _():
        first_far.wait_send()


def body(boxes, across, coords, loads, occupancy, basis, transfer):
    strides = boxes // MEMBERS
    hbm = pl.BlockSpec(memory_space=pl.ANY)
    dma = pltpu.SemaphoreType.DMA
    return pl.pallas_call(
        functools.partial(kernel, boxes, across),
        out_shape=jax.ShapeDtypeStruct((COLS, OWN), f32),
        in_specs=[hbm] * 5,
        out_specs=pl.BlockSpec(memory_space=pltpu.VMEM),
        scratch_shapes=[
            pltpu.VMEM((3, OWN), f32),
            pltpu.VMEM((COLS, OWN), bf16),
            pltpu.SMEM((LEAVES,), jnp.int32),
            pltpu.VMEM((LEAVES * 64, LEAF), bf16),
            pltpu.VMEM((6, 128, 64), f32),
            pltpu.VMEM((6, 128, 128), bf16),
            pltpu.VMEM((6, 128, 128), bf16),
            pltpu.VMEM((4, 64, 128), f32),
            pltpu.VMEM((128, 512), bf16),
            pltpu.VMEM((128, 512), bf16),
            pltpu.VMEM((2, 8, OWN + 2 * LEAF), f32),
            pltpu.VMEM((OWN, 8), f32),
            pltpu.VMEM((64, 512), bf16),
            pltpu.VMEM((64, 512), bf16),
            pltpu.VMEM((COLS, OWN + LEAF), f32),
            pltpu.VMEM((LEAF, 2 * LEAF), bf16),
            pltpu.VMEM((LEAF, 2 * LEAF), bf16),
            pltpu.VMEM((LEAF, LEAF), bf16),
            pltpu.VMEM((13, 2, 8, 128), f32),
            pltpu.VMEM((13, 2, 8, 128), f32),
            pltpu.VMEM((7, 8, 128), f32),
            pltpu.VMEM((2, 3, 2, 8, 128), f32),
            pltpu.VMEM((2, 3, 2, 8, 128), f32),
            pltpu.VMEM((MEMBERS, 8, 128), f32),
            pltpu.VMEM((2, 2, 8, 128), f32),
            pltpu.VMEM((2, 2, 8, 128), f32),
            pltpu.VMEM((8, 128), f32),
            pltpu.VMEM((2, 8, 128), f32),
            pltpu.VMEM((8, 128), f32),
            pltpu.VMEM((strides, 8, 128), f32),
            pltpu.VMEM((MEMBERS, 8, 128), f32),
            dma((5,)),
            dma((2,)),
            dma((2,)),
            dma((2,)),
            dma((2,)),
            dma((MEMBERS - 1,)),
            dma((MEMBERS - 1,)),
            dma((3,)),
            dma((3,)),
            dma((2,)),
            dma((2,)),
            dma((strides,)),
            dma((strides,)),
            dma((MEMBERS - 1,)),
            dma((MEMBERS - 1,)),
        ],
        compiler_params=pltpu.CompilerParams(
            collective_id=0, has_side_effects=True, vmem_limit_bytes=32 * 1024 * 1024
        ),
    )(
        *[
            pltpu.with_memory_space_constraint(x, pltpu.HBM)
            for x in (
                coords,
                loads,
                occupancy,
                basis.reshape(LEAVES * 64, LEAF),
                transfer.reshape(6, 128, 64),
            )
        ]
    )


def solution(mesh):
    boxes = mesh.shape["box"] // MEMBERS
    return jax.shard_map(
        functools.partial(body, boxes, 4),
        mesh=mesh,
        in_specs=(P(None, "box"), P(None, "box"), P("box"), P("box", None, None), P()),
        out_specs=P(None, "box"),
        check_vma=False,
    )
```

```python
import functools

import jax
import jax.numpy as jnp
from jax import lax
from jax.experimental import pallas as pl
from jax.experimental.pallas import tpu as pltpu
from jax.sharding import PartitionSpec as P

LEAF = 256
COLS = 8
LEAVES = 8
MEMBERS = 8
OWN = LEAF * LEAVES

f32 = jnp.float32
bf16 = jnp.bfloat16
soften = 0.0001
near_scale = 0.0625
far_scale = 0.125
NN = (((1,), (0,)), ((), ()))
NT = (((1,), (1,)), ((), ()))
MESH = pl.DeviceIdType.MESH


def phi(tx, ty, tz, sx, sy, sz, scale):
    dx = tx - sx
    dy = ty - sy
    dz = tz - sz
    r2 = dx * dx + dy * dy + dz * dz
    return (r2 * (0.5 * scale)) * jnp.log(r2 + soften)


def split(x):
    high = x.astype(bf16)
    return high, (x - high.astype(f32)).astype(bf16)


def mm(a, b, dims):
    rows = a.shape[0]
    high = a.astype(bf16).astype(f32)
    stacked = jnp.concatenate([high, a - high], axis=0).astype(bf16)
    both = lax.dot_general(stacked, b[0][...], dims, preferred_element_type=f32)
    low = lax.dot_general(stacked[:rows], b[1][...], dims, preferred_element_type=f32)
    return both[:rows] + (both[rows:] + low)


def low_half(shape):
    return lax.broadcasted_iota(jnp.int32, shape, len(shape) - 1) < 64


def merge(rows):
    count = rows.shape[0] // 16
    low = low_half((8, 128))
    return [
        jnp.where(low, rows[16 * i : 16 * i + 8], rows[16 * i + 8 : 16 * i + 16])
        for i in range(count)
    ]


def raise_coef(pairs, level_map):
    rows = mm(jnp.concatenate(pairs, axis=0), level_map, NN)
    return merge(rows) if len(pairs) > 1 else [rows]


def pick(x, entries):
    rows = x.shape[0]
    a = x.astype(bf16).astype(f32)
    b = (x - a).astype(bf16).astype(f32)
    c = (x - a) - b
    stacked = jnp.concatenate([a, b, c], axis=0).astype(bf16)
    picked = lax.dot_general(stacked, entries, NN, preferred_element_type=f32)
    return picked[:rows] + picked[rows : 2 * rows] + picked[2 * rows :]


def raise_skel(pairs, every_second):
    rows_up = pick(jnp.concatenate(pairs, axis=0), every_second)
    return merge(rows_up) if len(pairs) > 1 else [rows_up]


def cousins(chain, slot):
    low = low_half((8, 128))
    column = chain[slot, 1].T
    tx, ty, tz = column[:, 0:1], column[:, 1:2], column[:, 2:3]
    before, after = chain[slot - 1, 0], chain[slot + 1, 0]
    tiles = []
    for skel in (chain[slot - 1, 1], chain[slot + 1, 1]):
        tiles.append(phi(tx, ty, tz, skel[0:1], skel[1:2], skel[2:3], far_scale))
    tile = jnp.concatenate(tiles, axis=1)
    even = jnp.concatenate([jnp.where(low, before, 0.0), after], axis=1)
    odd = jnp.concatenate([before, jnp.where(low, 0.0, after)], axis=1)
    rows = mm(jnp.concatenate([even, odd], axis=0), split(tile), NT)
    return jnp.where(low, rows[:8], rows[8:])


def lower(pairs, level_map):
    height = pairs[0].shape[0]
    low = low_half((height, 128))
    stacked = []
    for pair in pairs:
        stacked += [jnp.where(low, pair, 0.0), jnp.where(low, 0.0, pair)]
    rows = mm(jnp.concatenate(stacked, axis=0), level_map, NT)
    return [rows[height * i : height * (i + 1)] for i in range(2 * len(pairs))]


def kernel(
    boxes,
    across,
    coords_hbm,
    loads_hbm,
    occ_hbm,
    basis_hbm,
    transfer_hbm,
    out_ref,
    coords,
    loads,
    occ,
    basis,
    transfer,
    map_high,
    map_low,
    path_map,
    path_high,
    path_low,
    field,
    column,
    leaf_high,
    leaf_low,
    near,
    tile_a,
    tile_b,
    tile_c,
    chain,
    g_chain,
    local,
    edge_send,
    edge_recv,
    g_buf,
    bound_send,
    bound_recv,
    quad_recv,
    rim_recv,
    far_send,
    far_buf,
    part_buf,
    load_sem,
    near_send_sem,
    near_recv_sem,
    edge_send_sem,
    edge_recv_sem,
    g_send_sem,
    g_recv_sem,
    bound_send_sem,
    bound_recv_sem,
    rim_send_sem,
    rim_recv_sem,
    far_send_sem,
    far_recv_sem,
    part_send_sem,
    part_recv_sem,
):
    loading = [
        pltpu.make_async_copy(src, dst, load_sem.at[at])
        for at, (src, dst) in enumerate(
            [
                (coords_hbm, coords),
                (transfer_hbm, transfer),
                (loads_hbm, loads),
                (occ_hbm, occ),
                (basis_hbm, basis),
            ]
        )
    ]
    for copy in loading:
        copy.start()

    device = lax.axis_index("box")
    total = boxes * MEMBERS
    box = device // MEMBERS
    member = device % MEMBERS
    low = low_half((8, 128))
    half = lax.broadcasted_iota(jnp.int32, (8, 128), 1) // 64

    left_device = (device + total - 1) % total
    right_device = (device + 1) % total
    left_box = ((box + boxes - 1) % boxes) * MEMBERS + member
    right_box = ((box + 1) % boxes) * MEMBERS + member
    mates = [box * MEMBERS + (member + r) % MEMBERS for r in (6, 2, 7, 3, 5, 4, 1)]

    strides = boxes // MEMBERS
    depth = boxes // (2 * across)
    x, z, y_half = box // (2 * depth), box // 2 % depth, box % 2
    y, core = member // 2, member % 2
    outer = jnp.where(y % 3 == 0, 1, 0)
    send_side = outer * (y // 3) + (1 - outer) * (y - 1)
    recv_side = outer * (1 - y // 3) + (1 - outer) * (y - 1)
    far_half = y_half + outer * (1 - 2 * y_half)
    far_member = 2 * (y + outer * (3 - 2 * y)) + z // 2 % 2

    def far_box(side, step, turn):
        other_z = (side + z) % 2 + 2 * core + 4 * ((z // 4 + turn) % 2)
        return ((x + across + step) % across * depth + other_z) * 2 + far_half

    far_steps = [(dx, turn) for dx in range(across) for turn in range(2)]
    far_to = [far_box(send_side, dx, turn) * MEMBERS + far_member for dx, turn in far_steps]
    far_from = [far_box(recv_side, -dx, turn) for dx, turn in far_steps]
    alone = jnp.logical_and(outer == 0, jnp.logical_and(send_side == 0, core == z // 2 % 2))
    pair = member // 2
    upper = pair // 3
    at_rim = pair % 3 == 0
    rim_box = (box + boxes + 2 * upper - 1) % boxes
    rim_devices = [rim_box * MEMBERS + 6 - 6 * upper + t for t in range(2)]
    quad = member // 4
    early = jnp.where(z == 0, 1, 0)
    quad_device = ((box + boxes + 1 - 2 * quad) % boxes) * MEMBERS + member

    barrier = pltpu.get_barrier_semaphore()

    def greet(target):
        pl.semaphore_signal(barrier, inc=1, device_id=(target,), device_id_type=MESH)

    for target in mates + [left_device, right_device, left_box, right_box]:
        greet(target)
    far_order = sorted(range(1, strides), key=lambda k: abs(far_steps[k][0] - across // 2))
    for k in far_order:
        greet(far_from[k] * MEMBERS + far_member)

    @pl.when(jnp.logical_not(alone))
    def _():
        greet(far_from[0] * MEMBERS + far_member)

    @pl.when(at_rim)
    def _():
        for target in rim_devices:
            greet(target)

    eighths = lax.broadcasted_iota(jnp.int32, (512, 128), 1) % 64 * 8
    rows = lax.broadcasted_iota(jnp.int32, (512, 128), 0)
    every_eighth = (rows == eighths).astype(f32).astype(bf16)
    swapped = rows + 64 - rows // 64 % 2 * 128
    eighth_swapped = (swapped == eighths).astype(f32).astype(bf16)
    loading[0].wait()
    points = jnp.concatenate([coords[...], jnp.zeros((5, OWN), f32)], axis=0)
    s0 = [
        jnp.concatenate(
            [points[:, 512 * p : 512 * p + 64], points[:, 512 * p + 256 : 512 * p + 320]], axis=1
        )
        for p in range(4)
    ]
    s3 = pick(jnp.concatenate(s0, axis=1), every_eighth)

    loading[1].wait()
    maps = [(map_high.at[level], map_low.at[level]) for level in range(6)]

    def set_map(level):
        once = transfer[level]
        map_high[level], map_low[level] = split(jnp.concatenate([once, once], axis=1))

    for level in range(3):
        set_map(level)
    loading[2].wait()
    loading[3].wait()
    slots = lax.broadcasted_iota(jnp.int32, (COLS, LEAF), 1)
    live = []
    for leaf in range(LEAVES):
        part = loads[:, leaf * LEAF : (leaf + 1) * LEAF].astype(f32)
        live.append(jnp.where(slots < occ[leaf], part, 0.0))
    loading[4].wait()
    c0 = []
    for p in range(4):
        two = jnp.concatenate([live[2 * p], live[2 * p + 1]], axis=0).astype(bf16)
        rows = lax.dot_general(
            two, basis[128 * p : 128 * p + 128, :], NT, preferred_element_type=f32
        )
        c0.append(jnp.where(low, rows[:8], rows[8:]))
    c1 = raise_coef(c0, maps[0])
    c2 = raise_coef(c1, maps[1])
    c3 = raise_coef(c2, maps[2])[0]

    g_buf[member] = jnp.where(half == member % 2, c3, s3)

    def set_field():
        field[0, :, LEAF : LEAF + OWN] = points
        for leaf in range(LEAVES):
            field[1, :, (leaf + 1) * LEAF : (leaf + 2) * LEAF] = live[leaf]
        for at in range(0, OWN, 128):
            column[at : at + 128, :] = points[:, at : at + 128].T
        near[...] = jnp.zeros_like(near)

    def fill_tile(tile, row, col, width):
        sx = field[0, 0:1, pl.ds(col, width)]
        sy = field[0, 1:2, pl.ds(col, width)]
        sz = field[0, 2:3, pl.ds(col, width)]
        for at in range(0, LEAF, 16):
            rows = column[pl.ds(row + at, 16), :]
            tile[at : at + 16, 0:width] = phi(
                rows[:, 0:1], rows[:, 1:2], rows[:, 2:3], sx, sy, sz, near_scale
            ).astype(bf16)

    def near_leaf(tile, row):
        col = row + LEAF
        fill_tile(tile, row, col, 2 * LEAF)
        loads_two = field[1, :, pl.ds(col, 2 * LEAF)].astype(bf16)
        this = lax.dot_general(loads_two, tile[...], NT, preferred_element_type=f32)
        after = lax.dot_general(
            loads_two[:, :LEAF], tile[:, LEAF:], NN, preferred_element_type=f32
        )
        return this, after

    def near_two(row):
        first, second_part = near_leaf(tile_a, row)
        second, third = near_leaf(tile_b, row + LEAF)
        near[:, pl.ds(row, LEAF)] += first
        near[:, pl.ds(row + LEAF, LEAF)] += second_part + second
        near[:, pl.ds(row + 2 * LEAF, LEAF)] += third

    def near_step(pair, carry):
        near_two(pl.multiple_of(pair * (2 * LEAF), 2 * LEAF))
        return carry

    def side(block, at):
        lanes = lax.broadcasted_iota(jnp.int32, block.shape, 1) // 64
        return jnp.where(lanes == at, block, 0.0)

    def set_paths():
        for level in range(3, 6):
            set_map(level)
        paths = lower(lower([transfer[5].T], maps[4]), maps[3])
        for p in range(4):
            path_map[p] = paths[p]
        both = jnp.concatenate(paths, axis=1)
        path_high[...], path_low[...] = split(jnp.concatenate([both, both], axis=0))

    def set_leaf_paths():
        x2 = mm(side(path_map[member // 2], member % 2), maps[2], NT)
        x0 = lower(lower([x2], maps[1]), maps[0])
        leaf_high[...], leaf_low[...] = split(jnp.concatenate(x0, axis=1))

    @pl.when(early == 1)
    def _():
        set_field()
        set_paths()
        set_leaf_paths()
        lax.fori_loop(0, 3, near_step, 0)

    pl.semaphore_wait(
        barrier,
        4 + MEMBERS - 1 + strides - alone.astype(jnp.int32) + 2 * at_rim.astype(jnp.int32),
    )

    started = []

    def send(src, dst, send_sem, recv_sem, target):
        copy = pltpu.make_async_remote_copy(
            src_ref=src,
            dst_ref=dst,
            send_sem=send_sem,
            recv_sem=recv_sem,
            device_id=(target,),
            device_id_type=MESH,
        )
        copy.start()
        started.append(copy)
        return copy

    g_copies = []
    for r, mate in enumerate(mates):
        g_copies.append(
            send(g_buf.at[member], g_buf.at[member], g_send_sem.at[r], g_recv_sem.at[r], mate)
        )

    rim_copies = [
        pltpu.make_async_remote_copy(
            src_ref=g_buf.at[member],
            dst_ref=rim_recv.at[member % 2],
            send_sem=rim_send_sem.at[t],
            recv_sem=rim_recv_sem.at[member % 2],
            device_id=(rim_devices[t],),
            device_id_type=MESH,
        )
        for t in range(2)
    ]

    @pl.when(at_rim)
    def _():
        for copy in rim_copies:
            copy.start()

    @pl.when(early == 0)
    def _():
        set_field()

    last = LEAF * LEAVES
    near_copies = [
        send(
            field.at[:, :, last : last + LEAF],
            field.at[:, :, 0:LEAF],
            near_send_sem.at[0],
            near_recv_sem.at[0],
            right_device,
        ),
        send(
            field.at[:, :, LEAF : 2 * LEAF],
            field.at[:, :, last + LEAF : last + 2 * LEAF],
            near_send_sem.at[1],
            near_recv_sem.at[1],
            left_device,
        ),
    ]

    @pl.when(early == 0)
    def _():
        set_paths()

    for copy in g_copies:
        copy.wait_recv()
    c3s, s3s = [], []
    for p in range(4):
        even, odd = g_buf[2 * p], g_buf[2 * p + 1]
        c3s.append(jnp.where(low, even, odd))
        s3s.append(jnp.where(low, odd, even))
    c6 = mm(jnp.concatenate(c3s, axis=1), (path_high, path_low), NT)
    s6 = pick(jnp.concatenate(s3s, axis=1), eighth_swapped)
    far_send[0] = jnp.where(low, c6, s6)
    far_send[1] = jnp.where(low, s6, c6)

    @pl.when(alone)
    def _():
        far_buf[0] = far_send[0]

    far_copies = []
    for k in far_order:
        far_copies.append(
            send(
                far_send.at[k % 2],
                far_buf.at[k],
                far_send_sem.at[k],
                far_recv_sem.at[k],
                far_to[k],
            )
        )
    first_far = pltpu.make_async_remote_copy(
        src_ref=far_send.at[0],
        dst_ref=far_buf.at[0],
        send_sem=far_send_sem.at[0],
        recv_sem=far_recv_sem.at[0],
        device_id=(far_to[0],),
        device_id_type=MESH,
    )

    @pl.when(jnp.logical_not(alone))
    def _():
        first_far.start()

    picks = lax.broadcasted_iota(jnp.int32, (128, 128), 1) % 64 * 2
    every_second = (
        (lax.broadcasted_iota(jnp.int32, (128, 128), 0) == picks).astype(f32).astype(bf16)
    )
    s1 = raise_skel(s0, every_second)
    s2 = raise_skel(s1, every_second)

    def set_chain(levels, into):
        for at, (pairs, skels) in enumerate(levels):
            first = (1, 7, 11)[at]
            for p in range(len(pairs)):
                into[first + p, 0] = pairs[p]
                into[first + p, 1] = skels[p]

    set_chain([(c0, s0), (c1, s1), (c2, s2)], chain)
    for at, (pairs, skels) in enumerate([(c0, s0), (c1, s1), (c2, s2)]):
        edge_send[0, at, 0] = pairs[-1]
        edge_send[0, at, 1] = skels[-1]
        edge_send[1, at, 0] = pairs[0]
        edge_send[1, at, 1] = skels[0]
    edge_copies = [
        send(
            edge_send.at[side],
            edge_recv.at[side],
            edge_send_sem.at[side],
            edge_recv_sem.at[side],
            (right_device, left_device)[side],
        )
        for side in range(2)
    ]

    s3s = [pltpu.roll(skel, 64, 1) for skel in s3s]
    c4s, s4s = raise_coef(c3s, maps[3]), raise_skel(s3s, every_second)
    c5s, s5s = raise_coef(c4s, maps[4]), raise_skel(s4s, every_second)
    set_chain([(c3s, s3s), (c4s, s4s), (c5s, s5s)], g_chain)
    for at in range(2):
        bound_send[at, 0] = c5s[0]
        bound_send[at, 1] = s5s[0] + pltpu.roll(s4s[1 - at], 3, 0)
    bound_copies = [
        send(
            bound_send.at[side],
            bound_recv.at[side],
            bound_send_sem.at[side],
            bound_recv_sem.at[side],
            (right_box, left_box)[side],
        )
        for side in range(2)
    ]
    bound_copies.append(
        send(
            g_chain.at[8 - quad, 0],
            quad_recv,
            bound_send_sem.at[2],
            bound_recv_sem.at[2],
            quad_device,
        )
    )

    lax.fori_loop(3 * early, 3, near_step, 0)

    @pl.when(early == 0)
    def _():
        set_leaf_paths()

    for copy in near_copies:
        copy.wait_recv()

    @pl.when(device == 0)
    def _():
        field[1, :, 0:LEAF] = jnp.zeros((COLS, LEAF), f32)

    @pl.when(device == total - 1)
    def _():
        field[1, :, last + LEAF : last + 2 * LEAF] = jnp.zeros((COLS, LEAF), f32)

    near_two((LEAVES - 2) * LEAF)
    fill_tile(tile_c, 0, 0, LEAF)
    near[:, 0:LEAF] += lax.dot_general(
        field[1, :, 0:LEAF].astype(bf16), tile_c[...], NT, preferred_element_type=f32
    )

    def set_ends(ends, into, at_start, at_end):
        for level in range(3):
            before, after = (0, 6, 10)[level], (5, 9, 12)[level]
            into[before, 0] = jnp.where(at_start, 0.0, ends[0, level, 0])
            into[before, 1] = ends[0, level, 1]
            into[after, 0] = jnp.where(at_end, 0.0, ends[1, level, 0])
            into[after, 1] = ends[1, level, 1]

    for copy in edge_copies:
        copy.wait_recv()
    set_ends(edge_recv, chain, device == 0, device == total - 1)
    for pair, slot in enumerate([1, 2, 3, 4, 7, 8, 11]):
        local[pair] = cousins(chain, slot)

    for copy in bound_copies:
        copy.wait_recv()
    at_start, at_end = box == 0, box == boxes - 1
    outside = jnp.logical_or(
        jnp.logical_and(quad == 0, at_start), jnp.logical_and(quad == 1, at_end)
    )
    start_skel, end_skel = bound_recv[0, 1], bound_recv[1, 1]
    g_chain[10, 0] = jnp.where(at_start, 0.0, bound_recv[0, 0])
    g_chain[10, 1] = start_skel
    g_chain[12, 0] = jnp.where(at_end, 0.0, bound_recv[1, 0])
    g_chain[12, 1] = end_skel
    quad_coef = jnp.where(outside, 0.0, quad_recv[...])
    g_chain[6, 0] = quad_coef
    g_chain[6, 1] = pltpu.roll(start_skel, 5, 0)
    g_chain[9, 0] = quad_coef
    g_chain[9, 1] = pltpu.roll(end_skel, 5, 0)

    @pl.when(at_rim)
    def _():
        for copy in rim_copies:
            copy.wait_send()
        for t in range(2):
            pltpu.make_async_remote_copy(
                src_ref=g_buf.at[member],
                dst_ref=rim_recv.at[t],
                send_sem=rim_send_sem.at[t],
                recv_sem=rim_recv_sem.at[t],
                device_id=(rim_devices[t],),
                device_id_type=MESH,
            ).wait_recv()
        even, odd = rim_recv[0], rim_recv[1]
        rim_coef = jnp.where(outside, 0.0, jnp.where(low, even, odd))
        rim_skel = pltpu.roll(jnp.where(low, odd, even), 64, 1)
        for slot in (0, 5):
            g_chain[slot, 0] = rim_coef
            g_chain[slot, 1] = rim_skel

    local3 = cousins(g_chain, 1 + member // 2)
    local4 = cousins(g_chain, 7 + member // 4)
    local5 = cousins(g_chain, 11)
    y4 = local4 + mm(side(local5, member // 4), maps[4], NT)
    y3 = local3 + mm(side(y4, member // 2 % 2), maps[3], NT)
    y2 = local[6] + mm(side(y3, member % 2), maps[2], NT)
    y1 = [y + local[4 + at] for at, y in enumerate(lower([y2], maps[1]))]
    y0 = [y + local[at] for at, y in enumerate(lower(y1, maps[0]))]

    top_column = s6.T[:64]
    tx, ty, tz = top_column[:, 0:1], top_column[:, 1:2], top_column[:, 2:3]

    for copy in far_copies:
        copy.wait_recv()

    @pl.when(jnp.logical_not(alone))
    def _():
        first_far.wait_recv()

    top_coef, top_skel = [], []
    for k in range(0, strides, 2):
        halves = []
        for at in (k, k + 1):
            apart = far_from[at] - box
            counts = jnp.logical_or(apart >= 2, apart <= -2)
            halves.append((far_buf[at], counts))
        (one, one_counts), (two, two_counts) = halves
        coef = jnp.where(low, jnp.where(one_counts, one, 0.0), jnp.where(two_counts, two, 0.0))
        top_coef.append(pltpu.roll(coef, 64, 1))
        top_skel.append(jnp.where(low, two, one))
    top_tile = jnp.concatenate(
        [phi(tx, ty, tz, s[0:1], s[1:2], s[2:3], far_scale) for s in top_skel], axis=1
    )
    top = mm(jnp.concatenate(top_coef, axis=1), split(top_tile), NT)
    part_buf[member] = jnp.concatenate([top, jnp.zeros((8, 64), f32)], axis=1)
    part_copies = []
    for r, mate in enumerate(mates):
        part_copies.append(
            send(
                part_buf.at[member],
                part_buf.at[member],
                part_send_sem.at[r],
                part_recv_sem.at[r],
                mate,
            )
        )

    for copy in part_copies:
        copy.wait_recv()
    d6 = part_buf[0]
    for at in range(1, MEMBERS):
        d6 = d6 + part_buf[at]
    d0 = jnp.concatenate(y0, axis=1) + mm(d6[:, :64], (leaf_high, leaf_low), NN)
    for p in range(4):
        pair = d0[:, 128 * p : 128 * p + 128]
        two = jnp.concatenate([jnp.where(low, pair, 0.0), jnp.where(low, 0.0, pair)], axis=0)
        rows = lax.dot_general(
            two.astype(bf16),
            basis[128 * p : 128 * p + 128, :],
            NN,
            preferred_element_type=f32,
        )
        for t in range(2):
            leaf = 2 * p + t
            at = leaf * LEAF
            out_ref[:, at : at + LEAF] = jnp.where(
                slots < occ[leaf], near[:, at : at + LEAF] + rows[8 * t : 8 * t + 8], 0.0
            )

    for copy in started:
        copy.wait_send()

    @pl.when(jnp.logical_not(alone))
    def _():
        first_far.wait_send()


def body(boxes, across, coords, loads, occupancy, basis, transfer):
    strides = boxes // MEMBERS
    hbm = pl.BlockSpec(memory_space=pl.ANY)
    dma = pltpu.SemaphoreType.DMA
    return pl.pallas_call(
        functools.partial(kernel, boxes, across),
        out_shape=jax.ShapeDtypeStruct((COLS, OWN), f32),
        in_specs=[hbm] * 5,
        out_specs=pl.BlockSpec(memory_space=pltpu.VMEM),
        scratch_shapes=[
            pltpu.VMEM((3, OWN), f32),
            pltpu.VMEM((COLS, OWN), bf16),
            pltpu.SMEM((LEAVES,), jnp.int32),
            pltpu.VMEM((LEAVES * 64, LEAF), bf16),
            pltpu.VMEM((6, 128, 64), f32),
            pltpu.VMEM((6, 128, 128), bf16),
            pltpu.VMEM((6, 128, 128), bf16),
            pltpu.VMEM((4, 64, 128), f32),
            pltpu.VMEM((128, 512), bf16),
            pltpu.VMEM((128, 512), bf16),
            pltpu.VMEM((2, 8, OWN + 2 * LEAF), f32),
            pltpu.VMEM((OWN, 8), f32),
            pltpu.VMEM((64, 512), bf16),
            pltpu.VMEM((64, 512), bf16),
            pltpu.VMEM((COLS, OWN + LEAF), f32),
            pltpu.VMEM((LEAF, 2 * LEAF), bf16),
            pltpu.VMEM((LEAF, 2 * LEAF), bf16),
            pltpu.VMEM((LEAF, LEAF), bf16),
            pltpu.VMEM((13, 2, 8, 128), f32),
            pltpu.VMEM((13, 2, 8, 128), f32),
            pltpu.VMEM((7, 8, 128), f32),
            pltpu.VMEM((2, 3, 2, 8, 128), f32),
            pltpu.VMEM((2, 3, 2, 8, 128), f32),
            pltpu.VMEM((MEMBERS, 8, 128), f32),
            pltpu.VMEM((2, 2, 8, 128), f32),
            pltpu.VMEM((2, 2, 8, 128), f32),
            pltpu.VMEM((8, 128), f32),
            pltpu.VMEM((2, 8, 128), f32),
            pltpu.VMEM((2, 8, 128), f32),
            pltpu.VMEM((strides, 8, 128), f32),
            pltpu.VMEM((MEMBERS, 8, 128), f32),
            dma((5,)),
            dma((2,)),
            dma((2,)),
            dma((2,)),
            dma((2,)),
            dma((MEMBERS - 1,)),
            dma((MEMBERS - 1,)),
            dma((3,)),
            dma((3,)),
            dma((2,)),
            dma((2,)),
            dma((strides,)),
            dma((strides,)),
            dma((MEMBERS - 1,)),
            dma((MEMBERS - 1,)),
        ],
        compiler_params=pltpu.CompilerParams(
            collective_id=0, has_side_effects=True, vmem_limit_bytes=32 * 1024 * 1024
        ),
    )(
        *[
            pltpu.with_memory_space_constraint(x, pltpu.HBM)
            for x in (
                coords,
                loads,
                occupancy,
                basis.reshape(LEAVES * 64, LEAF),
                transfer.reshape(6, 128, 64),
            )
        ]
    )


def solution(mesh):
    boxes = mesh.shape["box"] // MEMBERS
    return jax.shard_map(
        functools.partial(body, boxes, 4),
        mesh=mesh,
        in_specs=(P(None, "box"), P(None, "box"), P("box"), P("box", None, None), P()),
        out_specs=P(None, "box"),
        check_vma=False,
    )
```

```python
import functools

import jax
import jax.numpy as jnp
from jax import lax
from jax.experimental import pallas as pl
from jax.experimental.pallas import tpu as pltpu
from jax.sharding import PartitionSpec as P

LEAF = 256
COLS = 8
LEAVES = 8
MEMBERS = 8
OWN = LEAF * LEAVES

f32 = jnp.float32
bf16 = jnp.bfloat16
soften = 0.0001
near_scale = 0.0625
far_scale = 0.125
NN = (((1,), (0,)), ((), ()))
NT = (((1,), (1,)), ((), ()))
MESH = pl.DeviceIdType.MESH


def phi(tx, ty, tz, sx, sy, sz, scale):
    dx = tx - sx
    dy = ty - sy
    dz = tz - sz
    r2 = dx * dx + dy * dy + dz * dz
    return (r2 * (0.5 * scale)) * jnp.log(r2 + soften)


def split(x):
    high = x.astype(bf16)
    return high, (x - high.astype(f32)).astype(bf16)


def mm(a, b, dims):
    rows = a.shape[0]
    high = a.astype(bf16).astype(f32)
    stacked = jnp.concatenate([high, a - high], axis=0).astype(bf16)
    both = lax.dot_general(stacked, b[0][...], dims, preferred_element_type=f32)
    low = lax.dot_general(stacked[:rows], b[1][...], dims, preferred_element_type=f32)
    return both[:rows] + (both[rows:] + low)


def low_half(shape):
    return lax.broadcasted_iota(jnp.int32, shape, len(shape) - 1) < 64


def merge(rows):
    count = rows.shape[0] // 16
    low = low_half((8, 128))
    return [
        jnp.where(low, rows[16 * i : 16 * i + 8], rows[16 * i + 8 : 16 * i + 16])
        for i in range(count)
    ]


def raise_coef(pairs, level_map):
    rows = mm(jnp.concatenate(pairs, axis=0), level_map, NN)
    return merge(rows) if len(pairs) > 1 else [rows]


def pick(x, entries):
    rows = x.shape[0]
    a = x.astype(bf16).astype(f32)
    b = (x - a).astype(bf16).astype(f32)
    c = (x - a) - b
    stacked = jnp.concatenate([a, b, c], axis=0).astype(bf16)
    picked = lax.dot_general(stacked, entries, NN, preferred_element_type=f32)
    return picked[:rows] + picked[rows : 2 * rows] + picked[2 * rows :]


def raise_skel(pairs, every_second):
    rows_up = pick(jnp.concatenate(pairs, axis=0), every_second)
    return merge(rows_up) if len(pairs) > 1 else [rows_up]


def cousins(chain, slot):
    low = low_half((8, 128))
    column = chain[slot, 1].T
    tx, ty, tz = column[:, 0:1], column[:, 1:2], column[:, 2:3]
    before, after = chain[slot - 1, 0], chain[slot + 1, 0]
    tiles = []
    for skel in (chain[slot - 1, 1], chain[slot + 1, 1]):
        tiles.append(phi(tx, ty, tz, skel[0:1], skel[1:2], skel[2:3], far_scale))
    tile = jnp.concatenate(tiles, axis=1)
    even = jnp.concatenate([jnp.where(low, before, 0.0), after], axis=1)
    odd = jnp.concatenate([before, jnp.where(low, 0.0, after)], axis=1)
    rows = mm(jnp.concatenate([even, odd], axis=0), split(tile), NT)
    return jnp.where(low, rows[:8], rows[8:])


def lower(pairs, level_map):
    height = pairs[0].shape[0]
    low = low_half((height, 128))
    stacked = []
    for pair in pairs:
        stacked += [jnp.where(low, pair, 0.0), jnp.where(low, 0.0, pair)]
    rows = mm(jnp.concatenate(stacked, axis=0), level_map, NT)
    return [rows[height * i : height * (i + 1)] for i in range(2 * len(pairs))]


def kernel(
    boxes,
    across,
    coords_hbm,
    loads_hbm,
    occ_hbm,
    basis_hbm,
    transfer_hbm,
    out_ref,
    coords,
    loads,
    occ,
    basis,
    transfer,
    map_high,
    map_low,
    path_map,
    path_high,
    path_low,
    field,
    column,
    leaf_high,
    leaf_low,
    near,
    tile_a,
    tile_b,
    tile_c,
    chain,
    g_chain,
    local,
    edge_send,
    edge_recv,
    g_buf,
    bound_send,
    bound_recv,
    quad_recv,
    rim_recv,
    far_send,
    far_buf,
    part_buf,
    load_sem,
    near_send_sem,
    near_recv_sem,
    edge_send_sem,
    edge_recv_sem,
    g_send_sem,
    g_recv_sem,
    bound_send_sem,
    bound_recv_sem,
    rim_send_sem,
    rim_recv_sem,
    far_send_sem,
    far_recv_sem,
    part_send_sem,
    part_recv_sem,
):
    loading = [
        pltpu.make_async_copy(src, dst, load_sem.at[at])
        for at, (src, dst) in enumerate(
            [
                (coords_hbm, coords),
                (transfer_hbm, transfer),
                (loads_hbm, loads),
                (occ_hbm, occ),
                (basis_hbm, basis),
            ]
        )
    ]
    for copy in loading:
        copy.start()

    device = lax.axis_index("box")
    total = boxes * MEMBERS
    box = device // MEMBERS
    member = device % MEMBERS
    low = low_half((8, 128))
    half = lax.broadcasted_iota(jnp.int32, (8, 128), 1) // 64

    left_device = (device + total - 1) % total
    right_device = (device + 1) % total
    left_box = ((box + boxes - 1) % boxes) * MEMBERS + member
    right_box = ((box + 1) % boxes) * MEMBERS + member
    mates = [box * MEMBERS + (member + r) % MEMBERS for r in (6, 2, 7, 3, 5, 4, 1)]

    strides = boxes // MEMBERS
    depth = boxes // (2 * across)
    x, z, y_half = box // (2 * depth), box // 2 % depth, box % 2
    y, core = member // 2, member % 2
    outer = jnp.where(y % 3 == 0, 1, 0)
    send_side = outer * (y // 3) + (1 - outer) * (y - 1)
    recv_side = outer * (1 - y // 3) + (1 - outer) * (y - 1)
    far_half = y_half + outer * (1 - 2 * y_half)
    far_member = 2 * (y + outer * (3 - 2 * y)) + z // 2 % 2

    def far_box(side, step, turn):
        other_z = (side + z) % 2 + 2 * core + 4 * ((z // 4 + turn) % 2)
        return ((x + across + step) % across * depth + other_z) * 2 + far_half

    far_steps = [(dx, turn) for dx in range(across) for turn in range(2)]
    far_to = [far_box(send_side, dx, turn) * MEMBERS + far_member for dx, turn in far_steps]
    far_from = [far_box(recv_side, -dx, turn) for dx, turn in far_steps]
    alone = jnp.logical_and(outer == 0, jnp.logical_and(send_side == 0, core == z // 2 % 2))
    pair = member // 2
    upper = pair // 3
    at_rim = pair % 3 == 0
    rim_box = (box + boxes + 2 * upper - 1) % boxes
    rim_devices = [rim_box * MEMBERS + 6 - 6 * upper + t for t in range(2)]
    quad = member // 4
    early = jnp.where(z == 0, 1, 0)
    quad_device = ((box + boxes + 1 - 2 * quad) % boxes) * MEMBERS + member

    barrier = pltpu.get_barrier_semaphore()

    def greet(target):
        pl.semaphore_signal(barrier, inc=1, device_id=(target,), device_id_type=MESH)

    for target in mates + [left_device, right_device, left_box, right_box]:
        greet(target)
    far_order = sorted(range(1, strides), key=lambda k: abs(far_steps[k][0] - across // 2))
    for k in far_order:
        greet(far_from[k] * MEMBERS + far_member)

    @pl.when(jnp.logical_not(alone))
    def _():
        greet(far_from[0] * MEMBERS + far_member)

    @pl.when(at_rim)
    def _():
        for target in rim_devices:
            greet(target)

    eighths = lax.broadcasted_iota(jnp.int32, (512, 128), 1) % 64 * 8
    rows = lax.broadcasted_iota(jnp.int32, (512, 128), 0)
    every_eighth = (rows == eighths).astype(f32).astype(bf16)
    swapped = rows + 64 - rows // 64 % 2 * 128
    eighth_swapped = (swapped == eighths).astype(f32).astype(bf16)
    picks = lax.broadcasted_iota(jnp.int32, (128, 128), 1) % 64 * 2
    every_second = (
        (lax.broadcasted_iota(jnp.int32, (128, 128), 0) == picks).astype(f32).astype(bf16)
    )
    loading[0].wait()
    points = jnp.concatenate([coords[...], jnp.zeros((5, OWN), f32)], axis=0)
    s0 = [
        jnp.concatenate(
            [points[:, 512 * p : 512 * p + 64], points[:, 512 * p + 256 : 512 * p + 320]], axis=1
        )
        for p in range(4)
    ]
    s3 = pick(jnp.concatenate(s0, axis=1), every_eighth)

    loading[1].wait()
    maps = [(map_high.at[level], map_low.at[level]) for level in range(6)]

    def set_map(level):
        once = transfer[level]
        map_high[level], map_low[level] = split(jnp.concatenate([once, once], axis=1))

    for level in range(3):
        set_map(level)
    loading[2].wait()
    loading[3].wait()
    slots = lax.broadcasted_iota(jnp.int32, (COLS, LEAF), 1)
    live = []
    for leaf in range(LEAVES):
        part = loads[:, leaf * LEAF : (leaf + 1) * LEAF].astype(f32)
        live.append(jnp.where(slots < occ[leaf], part, 0.0))
    loading[4].wait()
    c0 = []
    for p in range(4):
        two = jnp.concatenate([live[2 * p], live[2 * p + 1]], axis=0).astype(bf16)
        rows = lax.dot_general(
            two, basis[128 * p : 128 * p + 128, :], NT, preferred_element_type=f32
        )
        c0.append(jnp.where(low, rows[:8], rows[8:]))
    c1 = raise_coef(c0, maps[0])
    c2 = raise_coef(c1, maps[1])
    c3 = raise_coef(c2, maps[2])[0]

    g_buf[member] = jnp.where(half == member % 2, c3, s3)

    def set_field():
        field[0, :, LEAF : LEAF + OWN] = points
        for leaf in range(LEAVES):
            field[1, :, (leaf + 1) * LEAF : (leaf + 2) * LEAF] = live[leaf]
        for at in range(0, OWN, 128):
            column[at : at + 128, :] = points[:, at : at + 128].T
        near[...] = jnp.zeros_like(near)

    def fill_tile(tile, row, col, width):
        sx = field[0, 0:1, pl.ds(col, width)]
        sy = field[0, 1:2, pl.ds(col, width)]
        sz = field[0, 2:3, pl.ds(col, width)]
        for at in range(0, LEAF, 16):
            rows = column[pl.ds(row + at, 16), :]
            tile[at : at + 16, 0:width] = phi(
                rows[:, 0:1], rows[:, 1:2], rows[:, 2:3], sx, sy, sz, near_scale
            ).astype(bf16)

    def near_leaf(tile, row):
        col = row + LEAF
        fill_tile(tile, row, col, 2 * LEAF)
        loads_two = field[1, :, pl.ds(col, 2 * LEAF)].astype(bf16)
        this = lax.dot_general(loads_two, tile[...], NT, preferred_element_type=f32)
        after = lax.dot_general(
            loads_two[:, :LEAF], tile[:, LEAF:], NN, preferred_element_type=f32
        )
        return this, after

    def near_two(row):
        first, second_part = near_leaf(tile_a, row)
        second, third = near_leaf(tile_b, row + LEAF)
        near[:, pl.ds(row, LEAF)] += first
        near[:, pl.ds(row + LEAF, LEAF)] += second_part + second
        near[:, pl.ds(row + 2 * LEAF, LEAF)] += third

    def near_step(pair, carry):
        near_two(pl.multiple_of(pair * (2 * LEAF), 2 * LEAF))
        return carry

    def side(block, at):
        lanes = lax.broadcasted_iota(jnp.int32, block.shape, 1) // 64
        return jnp.where(lanes == at, block, 0.0)

    def set_chain(levels, into):
        for at, (pairs, skels) in enumerate(levels):
            first = (1, 7, 11)[at]
            for p in range(len(pairs)):
                into[first + p, 0] = pairs[p]
                into[first + p, 1] = skels[p]

    def set_inner():
        lax.fori_loop(0, 3, near_step, 0)
        row = (LEAVES - 2) * LEAF
        this, after = near_leaf(tile_a, row)
        fill_tile(tile_c, row + LEAF, row + 2 * LEAF, LEAF)
        own = field[1, :, row + 2 * LEAF : row + 3 * LEAF].astype(bf16)
        after += lax.dot_general(own, tile_c[...], NT, preferred_element_type=f32)
        near[:, row : row + LEAF] += this
        near[:, row + LEAF : row + 2 * LEAF] += after
        for slot in (2, 3):
            local[slot - 1] = cousins(chain, slot)

    def set_edges():
        s1 = raise_skel(s0, every_second)
        s2 = raise_skel(s1, every_second)

        set_chain([(c0, s0), (c1, s1), (c2, s2)], chain)
        for at, (pairs, skels) in enumerate([(c0, s0), (c1, s1), (c2, s2)]):
            edge_send[0, at, 0] = pairs[-1]
            edge_send[0, at, 1] = skels[-1]
            edge_send[1, at, 0] = pairs[0]
            edge_send[1, at, 1] = skels[0]
    def set_paths():
        for level in range(3, 6):
            set_map(level)
        paths = lower(lower([transfer[5].T], maps[4]), maps[3])
        for p in range(4):
            path_map[p] = paths[p]
        both = jnp.concatenate(paths, axis=1)
        path_high[...], path_low[...] = split(jnp.concatenate([both, both], axis=0))

    def set_leaf_paths():
        from_six = side(path_map[member // 2], member % 2)
        rows = lax.broadcasted_iota(jnp.int32, (64, 128), 0)
        from_three = (rows == lax.broadcasted_iota(jnp.int32, (64, 128), 1)).astype(f32)
        x2 = mm(jnp.concatenate([from_six, from_three], axis=0), maps[2], NT)
        x0 = lower(lower([x2], maps[1]), maps[0])
        leaf_high[...], leaf_low[...] = split(jnp.concatenate(x0, axis=1))

    @pl.when(early == 1)
    def _():
        set_field()
        set_edges()
        set_paths()
        set_leaf_paths()
        set_inner()

    pl.semaphore_wait(
        barrier,
        4 + MEMBERS - 1 + strides - alone.astype(jnp.int32) + 2 * at_rim.astype(jnp.int32),
    )

    started = []

    def remote(src, dst, send_sem, recv_sem, target):
        return pltpu.make_async_remote_copy(
            src_ref=src,
            dst_ref=dst,
            send_sem=send_sem,
            recv_sem=recv_sem,
            device_id=(target,),
            device_id_type=MESH,
        )

    def send(*ends):
        copy = remote(*ends)
        copy.start()
        started.append(copy)
        return copy

    g_copies = []
    for r, mate in enumerate(mates):
        g_copies.append(
            send(g_buf.at[member], g_buf.at[member], g_send_sem.at[r], g_recv_sem.at[r], mate)
        )

    rim_copies = [
        pltpu.make_async_remote_copy(
            src_ref=g_buf.at[member],
            dst_ref=rim_recv.at[member % 2],
            send_sem=rim_send_sem.at[t],
            recv_sem=rim_recv_sem.at[member % 2],
            device_id=(rim_devices[t],),
            device_id_type=MESH,
        )
        for t in range(2)
    ]

    @pl.when(at_rim)
    def _():
        for copy in rim_copies:
            copy.start()

    @pl.when(early == 0)
    def _():
        set_field()

    last = LEAF * LEAVES
    near_copies = [
        send(
            field.at[:, :, last : last + LEAF],
            field.at[:, :, 0:LEAF],
            near_send_sem.at[0],
            near_recv_sem.at[0],
            right_device,
        ),
        send(
            field.at[:, :, LEAF : 2 * LEAF],
            field.at[:, :, last + LEAF : last + 2 * LEAF],
            near_send_sem.at[1],
            near_recv_sem.at[1],
            left_device,
        ),
    ]

    edge_copies = [
        remote(
            edge_send.at[side],
            edge_recv.at[side],
            edge_send_sem.at[side],
            edge_recv_sem.at[side],
            (right_device, left_device)[side],
        )
        for side in range(2)
    ]

    @pl.when(early == 1)
    def _():
        for copy in edge_copies:
            copy.start()

    @pl.when(early == 0)
    def _():
        set_paths()

    for copy in g_copies:
        copy.wait_recv()
    c3s, s3s = [], []
    for p in range(4):
        even, odd = g_buf[2 * p], g_buf[2 * p + 1]
        c3s.append(jnp.where(low, even, odd))
        s3s.append(jnp.where(low, odd, even))
    c6 = mm(jnp.concatenate(c3s, axis=1), (path_high, path_low), NT)
    s6 = pick(jnp.concatenate(s3s, axis=1), eighth_swapped)
    far_send[0] = jnp.where(low, c6, s6)
    far_send[1] = jnp.where(low, s6, c6)

    @pl.when(alone)
    def _():
        far_buf[0] = far_send[0]

    far_copies = []
    for k in far_order:
        far_copies.append(
            send(
                far_send.at[k % 2],
                far_buf.at[k],
                far_send_sem.at[k],
                far_recv_sem.at[k],
                far_to[k],
            )
        )
    first_far = pltpu.make_async_remote_copy(
        src_ref=far_send.at[0],
        dst_ref=far_buf.at[0],
        send_sem=far_send_sem.at[0],
        recv_sem=far_recv_sem.at[0],
        device_id=(far_to[0],),
        device_id_type=MESH,
    )

    @pl.when(jnp.logical_not(alone))
    def _():
        first_far.start()

    @pl.when(early == 0)
    def _():
        set_edges()
        for copy in edge_copies:
            copy.start()

    started.extend(edge_copies)

    s3s = [pltpu.roll(skel, 64, 1) for skel in s3s]
    c4s, s4s = raise_coef(c3s, maps[3]), raise_skel(s3s, every_second)
    c5s, s5s = raise_coef(c4s, maps[4]), raise_skel(s4s, every_second)
    set_chain([(c3s, s3s), (c4s, s4s), (c5s, s5s)], g_chain)
    for at in range(2):
        bound_send[at, 0] = c5s[0]
        bound_send[at, 1] = s5s[0] + pltpu.roll(s4s[1 - at], 3, 0)
    bound_copies = [
        send(
            bound_send.at[side],
            bound_recv.at[side],
            bound_send_sem.at[side],
            bound_recv_sem.at[side],
            (right_box, left_box)[side],
        )
        for side in range(2)
    ]
    bound_copies.append(
        send(
            g_chain.at[8 - quad, 0],
            quad_recv,
            bound_send_sem.at[2],
            bound_recv_sem.at[2],
            quad_device,
        )
    )

    @pl.when(early == 0)
    def _():
        set_inner()
        set_leaf_paths()

    for copy in near_copies:
        copy.wait_recv()

    @pl.when(device == 0)
    def _():
        field[1, :, 0:LEAF] = jnp.zeros((COLS, LEAF), f32)

    @pl.when(device == total - 1)
    def _():
        field[1, :, last + LEAF : last + 2 * LEAF] = jnp.zeros((COLS, LEAF), f32)

    def near_end(tile, row, col):
        fill_tile(tile, row, col, LEAF)
        near[:, row : row + LEAF] += lax.dot_general(
            field[1, :, col : col + LEAF].astype(bf16),
            tile[:, 0:LEAF],
            NT,
            preferred_element_type=f32,
        )

    near_end(tile_c, 0, 0)
    near_end(tile_a, last - LEAF, last + LEAF)

    def set_ends(ends, into, at_start, at_end):
        for level in range(3):
            before, after = (0, 6, 10)[level], (5, 9, 12)[level]
            into[before, 0] = jnp.where(at_start, 0.0, ends[0, level, 0])
            into[before, 1] = ends[0, level, 1]
            into[after, 0] = jnp.where(at_end, 0.0, ends[1, level, 0])
            into[after, 1] = ends[1, level, 1]

    for copy in edge_copies:
        copy.wait_recv()
    set_ends(edge_recv, chain, device == 0, device == total - 1)
    for at, slot in [(0, 1), (3, 4), (4, 7), (5, 8), (6, 11)]:
        local[at] = cousins(chain, slot)

    top_column = s6.T[:64]
    tx, ty, tz = top_column[:, 0:1], top_column[:, 1:2], top_column[:, 2:3]

    for copy in far_copies:
        copy.wait_recv()

    @pl.when(jnp.logical_not(alone))
    def _():
        first_far.wait_recv()

    top_coef, top_skel = [], []
    for k in range(0, strides, 2):
        halves = []
        for at in (k, k + 1):
            apart = far_from[at] - box
            counts = jnp.logical_or(apart >= 2, apart <= -2)
            halves.append((far_buf[at], counts))
        (one, one_counts), (two, two_counts) = halves
        coef = jnp.where(low, jnp.where(one_counts, one, 0.0), jnp.where(two_counts, two, 0.0))
        top_coef.append(pltpu.roll(coef, 64, 1))
        top_skel.append(jnp.where(low, two, one))
    top_tile = jnp.concatenate(
        [phi(tx, ty, tz, s[0:1], s[1:2], s[2:3], far_scale) for s in top_skel], axis=1
    )
    top = mm(jnp.concatenate(top_coef, axis=1), split(top_tile), NT)
    part_buf[member] = jnp.concatenate([top, jnp.zeros((8, 64), f32)], axis=1)
    part_copies = []
    for r, mate in enumerate(mates):
        part_copies.append(
            send(
                part_buf.at[member],
                part_buf.at[member],
                part_send_sem.at[r],
                part_recv_sem.at[r],
                mate,
            )
        )

    for copy in bound_copies:
        copy.wait_recv()
    at_start, at_end = box == 0, box == boxes - 1
    outside = jnp.logical_or(
        jnp.logical_and(quad == 0, at_start), jnp.logical_and(quad == 1, at_end)
    )
    start_skel, end_skel = bound_recv[0, 1], bound_recv[1, 1]
    g_chain[10, 0] = jnp.where(at_start, 0.0, bound_recv[0, 0])
    g_chain[10, 1] = start_skel
    g_chain[12, 0] = jnp.where(at_end, 0.0, bound_recv[1, 0])
    g_chain[12, 1] = end_skel
    quad_coef = jnp.where(outside, 0.0, quad_recv[...])
    g_chain[6, 0] = quad_coef
    g_chain[6, 1] = pltpu.roll(start_skel, 5, 0)
    g_chain[9, 0] = quad_coef
    g_chain[9, 1] = pltpu.roll(end_skel, 5, 0)

    @pl.when(at_rim)
    def _():
        for copy in rim_copies:
            copy.wait_send()
        for t in range(2):
            pltpu.make_async_remote_copy(
                src_ref=g_buf.at[member],
                dst_ref=rim_recv.at[t],
                send_sem=rim_send_sem.at[t],
                recv_sem=rim_recv_sem.at[t],
                device_id=(rim_devices[t],),
                device_id_type=MESH,
            ).wait_recv()
        even, odd = rim_recv[0], rim_recv[1]
        rim_coef = jnp.where(outside, 0.0, jnp.where(low, even, odd))
        rim_skel = pltpu.roll(jnp.where(low, odd, even), 64, 1)
        for slot in (0, 5):
            g_chain[slot, 0] = rim_coef
            g_chain[slot, 1] = rim_skel

    local3 = cousins(g_chain, 1 + member // 2)
    local4 = cousins(g_chain, 7 + member // 4)
    local5 = cousins(g_chain, 11)
    y2 = local[6]
    y1 = [y + local[4 + at] for at, y in enumerate(lower([y2], maps[1]))]
    y0 = [y + local[at] for at, y in enumerate(lower(y1, maps[0]))]
    y4 = local4 + mm(side(local5, member // 4), maps[4], NT)
    y3 = local3 + mm(side(y4, member // 2 % 2), maps[3], NT)
    y3 = jnp.where(member % 2 == 1, y3, pltpu.roll(y3, 64, 1))

    for copy in part_copies:
        copy.wait_recv()
    d6 = part_buf[0]
    for at in range(1, MEMBERS):
        d6 = d6 + part_buf[at]
    d63 = jnp.where(low, d6, y3)
    d0 = jnp.concatenate(y0, axis=1) + mm(d63, (leaf_high, leaf_low), NN)
    for p in range(4):
        pair = d0[:, 128 * p : 128 * p + 128]
        two = jnp.concatenate([jnp.where(low, pair, 0.0), jnp.where(low, 0.0, pair)], axis=0)
        rows = lax.dot_general(
            two.astype(bf16),
            basis[128 * p : 128 * p + 128, :],
            NN,
            preferred_element_type=f32,
        )
        for t in range(2):
            leaf = 2 * p + t
            at = leaf * LEAF
            out_ref[:, at : at + LEAF] = jnp.where(
                slots < occ[leaf], near[:, at : at + LEAF] + rows[8 * t : 8 * t + 8], 0.0
            )

    for copy in started:
        copy.wait_send()

    @pl.when(jnp.logical_not(alone))
    def _():
        first_far.wait_send()


def body(boxes, across, coords, loads, occupancy, basis, transfer):
    strides = boxes // MEMBERS
    hbm = pl.BlockSpec(memory_space=pl.ANY)
    dma = pltpu.SemaphoreType.DMA
    return pl.pallas_call(
        functools.partial(kernel, boxes, across),
        out_shape=jax.ShapeDtypeStruct((COLS, OWN), f32),
        in_specs=[hbm] * 5,
        out_specs=pl.BlockSpec(memory_space=pltpu.VMEM),
        scratch_shapes=[
            pltpu.VMEM((3, OWN), f32),
            pltpu.VMEM((COLS, OWN), bf16),
            pltpu.SMEM((LEAVES,), jnp.int32),
            pltpu.VMEM((LEAVES * 64, LEAF), bf16),
            pltpu.VMEM((6, 128, 64), f32),
            pltpu.VMEM((6, 128, 128), bf16),
            pltpu.VMEM((6, 128, 128), bf16),
            pltpu.VMEM((4, 64, 128), f32),
            pltpu.VMEM((128, 512), bf16),
            pltpu.VMEM((128, 512), bf16),
            pltpu.VMEM((2, 8, OWN + 2 * LEAF), f32),
            pltpu.VMEM((OWN, 8), f32),
            pltpu.VMEM((128, 512), bf16),
            pltpu.VMEM((128, 512), bf16),
            pltpu.VMEM((COLS, OWN + LEAF), f32),
            pltpu.VMEM((LEAF, 2 * LEAF), bf16),
            pltpu.VMEM((LEAF, 2 * LEAF), bf16),
            pltpu.VMEM((LEAF, LEAF), bf16),
            pltpu.VMEM((13, 2, 8, 128), f32),
            pltpu.VMEM((13, 2, 8, 128), f32),
            pltpu.VMEM((7, 8, 128), f32),
            pltpu.VMEM((2, 3, 2, 8, 128), f32),
            pltpu.VMEM((2, 3, 2, 8, 128), f32),
            pltpu.VMEM((MEMBERS, 8, 128), f32),
            pltpu.VMEM((2, 2, 8, 128), f32),
            pltpu.VMEM((2, 2, 8, 128), f32),
            pltpu.VMEM((8, 128), f32),
            pltpu.VMEM((2, 8, 128), f32),
            pltpu.VMEM((2, 8, 128), f32),
            pltpu.VMEM((strides, 8, 128), f32),
            pltpu.VMEM((MEMBERS, 8, 128), f32),
            dma((5,)),
            dma((2,)),
            dma((2,)),
            dma((2,)),
            dma((2,)),
            dma((MEMBERS - 1,)),
            dma((MEMBERS - 1,)),
            dma((3,)),
            dma((3,)),
            dma((2,)),
            dma((2,)),
            dma((strides,)),
            dma((strides,)),
            dma((MEMBERS - 1,)),
            dma((MEMBERS - 1,)),
        ],
        compiler_params=pltpu.CompilerParams(
            collective_id=0, has_side_effects=True, vmem_limit_bytes=32 * 1024 * 1024
        ),
    )(
        *[
            pltpu.with_memory_space_constraint(x, pltpu.HBM)
            for x in (
                coords,
                loads,
                occupancy,
                basis.reshape(LEAVES * 64, LEAF),
                transfer.reshape(6, 128, 64),
            )
        ]
    )


def solution(mesh):
    boxes = mesh.shape["box"] // MEMBERS
    return jax.shard_map(
        functools.partial(body, boxes, 4),
        mesh=mesh,
        in_specs=(P(None, "box"), P(None, "box"), P("box"), P("box", None, None), P()),
        out_specs=P(None, "box"),
        check_vma=False,
    )
```

```python
import functools

import jax
import jax.numpy as jnp
from jax import lax
from jax.experimental import pallas as pl
from jax.experimental.pallas import tpu as pltpu
from jax.sharding import PartitionSpec as P

LEAF = 256
COLS = 8
LEAVES = 8
MEMBERS = 8
OWN = LEAF * LEAVES

f32 = jnp.float32
bf16 = jnp.bfloat16
soften = 0.0001
near_scale = 0.0625
far_scale = 0.125
NN = (((1,), (0,)), ((), ()))
NT = (((1,), (1,)), ((), ()))
MESH = pl.DeviceIdType.MESH


def phi(tx, ty, tz, sx, sy, sz, scale):
    dx = tx - sx
    dy = ty - sy
    dz = tz - sz
    r2 = dx * dx + dy * dy + dz * dz
    return (r2 * (0.5 * scale)) * jnp.log(r2 + soften)


def split(x):
    high = x.astype(bf16)
    return high, (x - high.astype(f32)).astype(bf16)


def mm(a, b, dims):
    rows = a.shape[0]
    high = a.astype(bf16).astype(f32)
    stacked = jnp.concatenate([high, a - high], axis=0).astype(bf16)
    both = lax.dot_general(stacked, b[0][...], dims, preferred_element_type=f32)
    low = lax.dot_general(stacked[:rows], b[1][...], dims, preferred_element_type=f32)
    return both[:rows] + (both[rows:] + low)


def low_half(shape):
    return lax.broadcasted_iota(jnp.int32, shape, len(shape) - 1) < 64


def merge(rows):
    count = rows.shape[0] // 16
    low = low_half((8, 128))
    return [
        jnp.where(low, rows[16 * i : 16 * i + 8], rows[16 * i + 8 : 16 * i + 16])
        for i in range(count)
    ]


def raise_coef(pairs, level_map):
    rows = mm(jnp.concatenate(pairs, axis=0), level_map, NN)
    return merge(rows) if len(pairs) > 1 else [rows]


def pick(x, entries):
    rows = x.shape[0]
    a = x.astype(bf16).astype(f32)
    b = (x - a).astype(bf16).astype(f32)
    c = (x - a) - b
    stacked = jnp.concatenate([a, b, c], axis=0).astype(bf16)
    picked = lax.dot_general(stacked, entries, NN, preferred_element_type=f32)
    return picked[:rows] + picked[rows : 2 * rows] + picked[2 * rows :]


def raise_skel(pairs, every_second):
    rows_up = pick(jnp.concatenate(pairs, axis=0), every_second)
    return merge(rows_up) if len(pairs) > 1 else [rows_up]


def cousins(chain, slot):
    low = low_half((8, 128))
    column = chain[slot, 1].T
    tx, ty, tz = column[:, 0:1], column[:, 1:2], column[:, 2:3]
    before, after = chain[slot - 1, 0], chain[slot + 1, 0]
    tiles = []
    for skel in (chain[slot - 1, 1], chain[slot + 1, 1]):
        tiles.append(phi(tx, ty, tz, skel[0:1], skel[1:2], skel[2:3], far_scale))
    tile = jnp.concatenate(tiles, axis=1)
    even = jnp.concatenate([jnp.where(low, before, 0.0), after], axis=1)
    odd = jnp.concatenate([before, jnp.where(low, 0.0, after)], axis=1)
    rows = mm(jnp.concatenate([even, odd], axis=0), split(tile), NT)
    return jnp.where(low, rows[:8], rows[8:])


def lower(pairs, level_map):
    height = pairs[0].shape[0]
    low = low_half((height, 128))
    stacked = []
    for pair in pairs:
        stacked += [jnp.where(low, pair, 0.0), jnp.where(low, 0.0, pair)]
    rows = mm(jnp.concatenate(stacked, axis=0), level_map, NT)
    return [rows[height * i : height * (i + 1)] for i in range(2 * len(pairs))]


def kernel(
    boxes,
    across,
    coords_hbm,
    loads_hbm,
    occ_hbm,
    basis_hbm,
    transfer_hbm,
    out_ref,
    coords,
    loads,
    occ,
    basis,
    transfer,
    map_high,
    map_low,
    path_map,
    path_high,
    path_low,
    field,
    column,
    leaf_high,
    leaf_low,
    near,
    tile_a,
    tile_b,
    tile_c,
    chain,
    g_chain,
    local,
    edge_send,
    edge_recv,
    g_buf,
    bound_send,
    bound_recv,
    quad_recv,
    rim_recv,
    far_send,
    far_buf,
    part_buf,
    load_sem,
    near_send_sem,
    near_recv_sem,
    edge_send_sem,
    edge_recv_sem,
    g_send_sem,
    g_recv_sem,
    bound_send_sem,
    bound_recv_sem,
    rim_send_sem,
    rim_recv_sem,
    far_send_sem,
    far_recv_sem,
    part_send_sem,
    part_recv_sem,
):
    device = lax.axis_index("box")
    total = boxes * MEMBERS
    box = device // MEMBERS
    member = device % MEMBERS
    low = low_half((8, 128))
    half = lax.broadcasted_iota(jnp.int32, (8, 128), 1) // 64

    left_device = (device + total - 1) % total
    right_device = (device + 1) % total
    left_box = ((box + boxes - 1) % boxes) * MEMBERS + member
    right_box = ((box + 1) % boxes) * MEMBERS + member
    mates = [box * MEMBERS + (member + r) % MEMBERS for r in (6, 2, 7, 3, 5, 4, 1)]

    strides = boxes // MEMBERS
    depth = boxes // (2 * across)
    x, z, y_half = box // (2 * depth), box // 2 % depth, box % 2
    y, core = member // 2, member % 2
    outer = jnp.where(y % 3 == 0, 1, 0)
    send_side = outer * (y // 3) + (1 - outer) * (y - 1)
    recv_side = outer * (1 - y // 3) + (1 - outer) * (y - 1)
    far_half = y_half + outer * (1 - 2 * y_half)
    far_member = 2 * (y + outer * (3 - 2 * y)) + z // 2 % 2

    def far_box(side, step, turn):
        other_z = (side + z) % 2 + 2 * core + 4 * ((z // 4 + turn) % 2)
        return ((x + across + step) % across * depth + other_z) * 2 + far_half

    far_steps = [(dx, turn) for dx in range(across) for turn in range(2)]
    far_to = [far_box(send_side, dx, turn) * MEMBERS + far_member for dx, turn in far_steps]
    far_from = [far_box(recv_side, -dx, turn) for dx, turn in far_steps]
    alone = jnp.logical_and(outer == 0, jnp.logical_and(send_side == 0, core == z // 2 % 2))
    pair = member // 2
    upper = pair // 3
    at_rim = pair % 3 == 0
    rim_box = (box + boxes + 2 * upper - 1) % boxes
    rim_devices = [rim_box * MEMBERS + 6 - 6 * upper + t for t in range(2)]
    quad = member // 4
    early = jnp.where(z == 0, 1, 0)
    quad_device = ((box + boxes + 1 - 2 * quad) % boxes) * MEMBERS + member

    barrier = pltpu.get_barrier_semaphore()

    def greet(target):
        pl.semaphore_signal(barrier, inc=1, device_id=(target,), device_id_type=MESH)

    far_order = sorted(range(1, strides), key=lambda k: abs(far_steps[k][0] - across // 2))
    for k in far_order:
        greet(far_from[k] * MEMBERS + far_member)

    @pl.when(jnp.logical_not(alone))
    def _():
        greet(far_from[0] * MEMBERS + far_member)

    loading = [
        pltpu.make_async_copy(src, dst, load_sem.at[at])
        for at, (src, dst) in enumerate(
            [
                (coords_hbm, coords),
                (transfer_hbm, transfer),
                (loads_hbm, loads),
                (occ_hbm, occ),
                (basis_hbm, basis),
            ]
        )
    ]
    for copy in loading:
        copy.start()

    for target in mates + [left_device, right_device, left_box, right_box]:
        greet(target)
    @pl.when(at_rim)
    def _():
        for target in rim_devices:
            greet(target)

    eighths = lax.broadcasted_iota(jnp.int32, (512, 128), 1) % 64 * 8
    rows = lax.broadcasted_iota(jnp.int32, (512, 128), 0)
    every_eighth = (rows == eighths).astype(f32).astype(bf16)
    swapped = rows + 64 - rows // 64 % 2 * 128
    eighth_swapped = (swapped == eighths).astype(f32).astype(bf16)
    picks = lax.broadcasted_iota(jnp.int32, (128, 128), 1) % 64 * 2
    every_second = (
        (lax.broadcasted_iota(jnp.int32, (128, 128), 0) == picks).astype(f32).astype(bf16)
    )
    loading[0].wait()
    points = jnp.concatenate([coords[...], jnp.zeros((5, OWN), f32)], axis=0)
    s0 = [
        jnp.concatenate(
            [points[:, 512 * p : 512 * p + 64], points[:, 512 * p + 256 : 512 * p + 320]], axis=1
        )
        for p in range(4)
    ]
    s3 = pick(jnp.concatenate(s0, axis=1), every_eighth)

    loading[1].wait()
    maps = [(map_high.at[level], map_low.at[level]) for level in range(6)]

    def set_map(level):
        once = transfer[level]
        map_high[level], map_low[level] = split(jnp.concatenate([once, once], axis=1))

    for level in range(3):
        set_map(level)
    loading[2].wait()
    loading[3].wait()
    slots = lax.broadcasted_iota(jnp.int32, (COLS, LEAF), 1)
    live = []
    for leaf in range(LEAVES):
        part = loads[:, leaf * LEAF : (leaf + 1) * LEAF].astype(f32)
        live.append(jnp.where(slots < occ[leaf], part, 0.0))
    loading[4].wait()
    c0 = []
    for p in range(4):
        two = jnp.concatenate([live[2 * p], live[2 * p + 1]], axis=0).astype(bf16)
        rows = lax.dot_general(
            two, basis[128 * p : 128 * p + 128, :], NT, preferred_element_type=f32
        )
        c0.append(jnp.where(low, rows[:8], rows[8:]))
    c1 = raise_coef(c0, maps[0])
    c2 = raise_coef(c1, maps[1])
    c3 = raise_coef(c2, maps[2])[0]

    g_buf[member] = jnp.where(half == member % 2, c3, s3)

    def set_field():
        field[0, :, LEAF : LEAF + OWN] = points
        for leaf in range(LEAVES):
            field[1, :, (leaf + 1) * LEAF : (leaf + 2) * LEAF] = live[leaf]
        for at in range(0, OWN, 128):
            column[at : at + 128, :] = points[:, at : at + 128].T
        near[...] = jnp.zeros_like(near)

    def fill_tile(tile, row, col, width):
        sx = field[0, 0:1, pl.ds(col, width)]
        sy = field[0, 1:2, pl.ds(col, width)]
        sz = field[0, 2:3, pl.ds(col, width)]
        for at in range(0, LEAF, 16):
            rows = column[pl.ds(row + at, 16), :]
            tile[at : at + 16, 0:width] = phi(
                rows[:, 0:1], rows[:, 1:2], rows[:, 2:3], sx, sy, sz, near_scale
            ).astype(bf16)

    def near_leaf(tile, row):
        col = row + LEAF
        fill_tile(tile, row, col, 2 * LEAF)
        loads_two = field[1, :, pl.ds(col, 2 * LEAF)].astype(bf16)
        this = lax.dot_general(loads_two, tile[...], NT, preferred_element_type=f32)
        after = lax.dot_general(
            loads_two[:, :LEAF], tile[:, LEAF:], NN, preferred_element_type=f32
        )
        return this, after

    def near_two(row):
        first, second_part = near_leaf(tile_a, row)
        second, third = near_leaf(tile_b, row + LEAF)
        near[:, pl.ds(row, LEAF)] += first
        near[:, pl.ds(row + LEAF, LEAF)] += second_part + second
        near[:, pl.ds(row + 2 * LEAF, LEAF)] += third

    def near_step(pair, carry):
        near_two(pl.multiple_of(pair * (2 * LEAF), 2 * LEAF))
        return carry

    def side(block, at):
        lanes = lax.broadcasted_iota(jnp.int32, block.shape, 1) // 64
        return jnp.where(lanes == at, block, 0.0)

    def set_chain(levels, into):
        for at, (pairs, skels) in enumerate(levels):
            first = (1, 7, 11)[at]
            for p in range(len(pairs)):
                into[first + p, 0] = pairs[p]
                into[first + p, 1] = skels[p]

    def set_inner():
        lax.fori_loop(0, 3, near_step, 0)
        row = (LEAVES - 2) * LEAF
        this, after = near_leaf(tile_a, row)
        fill_tile(tile_c, row + LEAF, row + 2 * LEAF, LEAF)
        own = field[1, :, row + 2 * LEAF : row + 3 * LEAF].astype(bf16)
        after += lax.dot_general(own, tile_c[...], NT, preferred_element_type=f32)
        near[:, row : row + LEAF] += this
        near[:, row + LEAF : row + 2 * LEAF] += after
        for slot in (2, 3):
            local[slot - 1] = cousins(chain, slot)

    def set_edges():
        s1 = raise_skel(s0, every_second)
        s2 = raise_skel(s1, every_second)

        set_chain([(c0, s0), (c1, s1), (c2, s2)], chain)
        for at, (pairs, skels) in enumerate([(c0, s0), (c1, s1), (c2, s2)]):
            edge_send[0, at, 0] = pairs[-1]
            edge_send[0, at, 1] = skels[-1]
            edge_send[1, at, 0] = pairs[0]
            edge_send[1, at, 1] = skels[0]
    def set_paths():
        for level in range(3, 6):
            set_map(level)
        paths = lower(lower([transfer[5].T], maps[4]), maps[3])
        for p in range(4):
            path_map[p] = paths[p]
        both = jnp.concatenate(paths, axis=1)
        path_high[...], path_low[...] = split(jnp.concatenate([both, both], axis=0))

    def set_leaf_paths():
        from_six = side(path_map[member // 2], member % 2)
        rows = lax.broadcasted_iota(jnp.int32, (64, 128), 0)
        from_three = (rows == lax.broadcasted_iota(jnp.int32, (64, 128), 1)).astype(f32)
        x2 = mm(jnp.concatenate([from_six, from_three], axis=0), maps[2], NT)
        x0 = lower(lower([x2], maps[1]), maps[0])
        leaf_high[...], leaf_low[...] = split(jnp.concatenate(x0, axis=1))

    @pl.when(early == 1)
    def _():
        set_field()
        set_edges()
        set_paths()
        set_leaf_paths()
        set_inner()

    pl.semaphore_wait(
        barrier,
        4 + MEMBERS - 1 + strides - alone.astype(jnp.int32) + 2 * at_rim.astype(jnp.int32),
    )

    def remote(src, dst, send_sem, recv_sem, target):
        return pltpu.make_async_remote_copy(
            src_ref=src,
            dst_ref=dst,
            send_sem=send_sem,
            recv_sem=recv_sem,
            device_id=(target,),
            device_id_type=MESH,
        )

    def send(*ends):
        copy = remote(*ends)
        copy.start()
        return copy

    def wait_all(ref, semaphore):
        pltpu.make_async_copy(ref, ref, semaphore).wait()

    for mate in mates:
        send(g_buf.at[member], g_buf.at[member], g_send_sem, g_recv_sem, mate)

    rim_copies = [
        pltpu.make_async_remote_copy(
            src_ref=g_buf.at[member],
            dst_ref=rim_recv.at[member % 2],
            send_sem=rim_send_sem.at[t],
            recv_sem=rim_recv_sem.at[member % 2],
            device_id=(rim_devices[t],),
            device_id_type=MESH,
        )
        for t in range(2)
    ]

    @pl.when(at_rim)
    def _():
        for copy in rim_copies:
            copy.start()

    @pl.when(early == 0)
    def _():
        set_field()

    last = LEAF * LEAVES
    near_copies = [
        send(
            field.at[:, :, last : last + LEAF],
            field.at[:, :, 0:LEAF],
            near_send_sem.at[0],
            near_recv_sem.at[0],
            right_device,
        ),
        send(
            field.at[:, :, LEAF : 2 * LEAF],
            field.at[:, :, last + LEAF : last + 2 * LEAF],
            near_send_sem.at[1],
            near_recv_sem.at[1],
            left_device,
        ),
    ]

    edge_copies = [
        remote(
            edge_send.at[side],
            edge_recv.at[side],
            edge_send_sem.at[side],
            edge_recv_sem.at[side],
            (right_device, left_device)[side],
        )
        for side in range(2)
    ]

    @pl.when(early == 1)
    def _():
        for copy in edge_copies:
            copy.start()

    @pl.when(early == 0)
    def _():
        set_paths()

    wait_all(g_buf.at[pl.ds(0, MEMBERS - 1)], g_recv_sem)
    c3s, s3s = [], []
    for p in range(4):
        even, odd = g_buf[2 * p], g_buf[2 * p + 1]
        c3s.append(jnp.where(low, even, odd))
        s3s.append(jnp.where(low, odd, even))
    c6 = mm(jnp.concatenate(c3s, axis=1), (path_high, path_low), NT)
    s6 = pick(jnp.concatenate(s3s, axis=1), eighth_swapped)
    far_send[0] = jnp.where(low, c6, s6)
    far_send[1] = jnp.where(low, s6, c6)

    @pl.when(alone)
    def _():
        far_buf[0] = far_send[0]

    for k in far_order:
        send(
            far_send.at[k % 2], far_buf.at[k], far_send_sem.at[1], far_recv_sem.at[1], far_to[k]
        )
    first_far = pltpu.make_async_remote_copy(
        src_ref=far_send.at[0],
        dst_ref=far_buf.at[0],
        send_sem=far_send_sem.at[0],
        recv_sem=far_recv_sem.at[0],
        device_id=(far_to[0],),
        device_id_type=MESH,
    )

    @pl.when(jnp.logical_not(alone))
    def _():
        first_far.start()

    @pl.when(early == 0)
    def _():
        set_edges()
        for copy in edge_copies:
            copy.start()

    s3s = [pltpu.roll(skel, 64, 1) for skel in s3s]
    c4s, s4s = raise_coef(c3s, maps[3]), raise_skel(s3s, every_second)
    c5s, s5s = raise_coef(c4s, maps[4]), raise_skel(s4s, every_second)
    set_chain([(c3s, s3s), (c4s, s4s), (c5s, s5s)], g_chain)
    for at in range(2):
        bound_send[at, 0] = c5s[0]
        bound_send[at, 1] = s5s[0] + pltpu.roll(s4s[1 - at], 3, 0)
    bound_copies = [
        send(
            bound_send.at[side],
            bound_recv.at[side],
            bound_send_sem.at[side],
            bound_recv_sem.at[side],
            (right_box, left_box)[side],
        )
        for side in range(2)
    ]
    bound_copies.append(
        send(
            g_chain.at[8 - quad, 0],
            quad_recv,
            bound_send_sem.at[2],
            bound_recv_sem.at[2],
            quad_device,
        )
    )

    @pl.when(early == 0)
    def _():
        set_inner()
        set_leaf_paths()

    for copy in near_copies:
        copy.wait_recv()

    @pl.when(device == 0)
    def _():
        field[1, :, 0:LEAF] = jnp.zeros((COLS, LEAF), f32)

    @pl.when(device == total - 1)
    def _():
        field[1, :, last + LEAF : last + 2 * LEAF] = jnp.zeros((COLS, LEAF), f32)

    def near_end(tile, row, col):
        fill_tile(tile, row, col, LEAF)
        near[:, row : row + LEAF] += lax.dot_general(
            field[1, :, col : col + LEAF].astype(bf16),
            tile[:, 0:LEAF],
            NT,
            preferred_element_type=f32,
        )

    near_end(tile_c, 0, 0)
    near_end(tile_a, last - LEAF, last + LEAF)

    def set_ends(ends, into, at_start, at_end):
        for level in range(3):
            before, after = (0, 6, 10)[level], (5, 9, 12)[level]
            into[before, 0] = jnp.where(at_start, 0.0, ends[0, level, 0])
            into[before, 1] = ends[0, level, 1]
            into[after, 0] = jnp.where(at_end, 0.0, ends[1, level, 0])
            into[after, 1] = ends[1, level, 1]

    for copy in edge_copies:
        copy.wait_recv()
    set_ends(edge_recv, chain, device == 0, device == total - 1)
    for at, slot in [(0, 1), (3, 4), (4, 7), (5, 8), (6, 11)]:
        local[at] = cousins(chain, slot)

    top_column = s6.T[:64]
    tx, ty, tz = top_column[:, 0:1], top_column[:, 1:2], top_column[:, 2:3]

    wait_all(far_buf.at[pl.ds(1, strides - 1)], far_recv_sem.at[1])

    @pl.when(jnp.logical_not(alone))
    def _():
        first_far.wait_recv()

    top_coef, top_skel = [], []
    for k in range(0, strides, 2):
        halves = []
        for at in (k, k + 1):
            apart = far_from[at] - box
            counts = jnp.logical_or(apart >= 2, apart <= -2)
            halves.append((far_buf[at], counts))
        (one, one_counts), (two, two_counts) = halves
        coef = jnp.where(low, jnp.where(one_counts, one, 0.0), jnp.where(two_counts, two, 0.0))
        top_coef.append(pltpu.roll(coef, 64, 1))
        top_skel.append(jnp.where(low, two, one))
    top_tile = jnp.concatenate(
        [phi(tx, ty, tz, s[0:1], s[1:2], s[2:3], far_scale) for s in top_skel], axis=1
    )
    top = mm(jnp.concatenate(top_coef, axis=1), split(top_tile), NT)
    part_buf[member] = jnp.concatenate([top, jnp.zeros((8, 64), f32)], axis=1)
    for mate in mates:
        send(part_buf.at[member], part_buf.at[member], part_send_sem, part_recv_sem, mate)

    wait_all(g_buf.at[pl.ds(0, MEMBERS - 1)], g_send_sem)
    wait_all(far_buf.at[pl.ds(1, strides - 1)], far_send_sem.at[1])
    for copy in near_copies + edge_copies + bound_copies:
        copy.wait_send()

    @pl.when(jnp.logical_not(alone))
    def _():
        first_far.wait_send()

    for copy in bound_copies:
        copy.wait_recv()
    at_start, at_end = box == 0, box == boxes - 1
    outside = jnp.logical_or(
        jnp.logical_and(quad == 0, at_start), jnp.logical_and(quad == 1, at_end)
    )
    start_skel, end_skel = bound_recv[0, 1], bound_recv[1, 1]
    g_chain[10, 0] = jnp.where(at_start, 0.0, bound_recv[0, 0])
    g_chain[10, 1] = start_skel
    g_chain[12, 0] = jnp.where(at_end, 0.0, bound_recv[1, 0])
    g_chain[12, 1] = end_skel
    quad_coef = jnp.where(outside, 0.0, quad_recv[...])
    g_chain[6, 0] = quad_coef
    g_chain[6, 1] = pltpu.roll(start_skel, 5, 0)
    g_chain[9, 0] = quad_coef
    g_chain[9, 1] = pltpu.roll(end_skel, 5, 0)

    @pl.when(at_rim)
    def _():
        for copy in rim_copies:
            copy.wait_send()
        for t in range(2):
            pltpu.make_async_remote_copy(
                src_ref=g_buf.at[member],
                dst_ref=rim_recv.at[t],
                send_sem=rim_send_sem.at[t],
                recv_sem=rim_recv_sem.at[t],
                device_id=(rim_devices[t],),
                device_id_type=MESH,
            ).wait_recv()
        even, odd = rim_recv[0], rim_recv[1]
        rim_coef = jnp.where(outside, 0.0, jnp.where(low, even, odd))
        rim_skel = pltpu.roll(jnp.where(low, odd, even), 64, 1)
        for slot in (0, 5):
            g_chain[slot, 0] = rim_coef
            g_chain[slot, 1] = rim_skel

    local3 = cousins(g_chain, 1 + member // 2)
    local4 = cousins(g_chain, 7 + member // 4)
    local5 = cousins(g_chain, 11)
    y2 = local[6]
    y1 = [y + local[4 + at] for at, y in enumerate(lower([y2], maps[1]))]
    y0 = [y + local[at] for at, y in enumerate(lower(y1, maps[0]))]
    y4 = local4 + mm(side(local5, member // 4), maps[4], NT)
    y3 = local3 + mm(side(y4, member // 2 % 2), maps[3], NT)
    y3 = jnp.where(member % 2 == 1, y3, pltpu.roll(y3, 64, 1))

    wait_all(part_buf.at[pl.ds(0, MEMBERS - 1)], part_recv_sem)
    d6 = part_buf[0]
    for at in range(1, MEMBERS):
        d6 = d6 + part_buf[at]
    d63 = jnp.where(low, d6, y3)
    d0 = jnp.concatenate(y0, axis=1) + mm(d63, (leaf_high, leaf_low), NN)
    for p in range(4):
        pair = d0[:, 128 * p : 128 * p + 128]
        two = jnp.concatenate([jnp.where(low, pair, 0.0), jnp.where(low, 0.0, pair)], axis=0)
        rows = lax.dot_general(
            two.astype(bf16),
            basis[128 * p : 128 * p + 128, :],
            NN,
            preferred_element_type=f32,
        )
        for t in range(2):
            leaf = 2 * p + t
            at = leaf * LEAF
            out_ref[:, at : at + LEAF] = jnp.where(
                slots < occ[leaf], near[:, at : at + LEAF] + rows[8 * t : 8 * t + 8], 0.0
            )

    wait_all(part_buf.at[pl.ds(0, MEMBERS - 1)], part_send_sem)


def body(boxes, across, coords, loads, occupancy, basis, transfer):
    strides = boxes // MEMBERS
    hbm = pl.BlockSpec(memory_space=pl.ANY)
    dma = pltpu.SemaphoreType.DMA
    return pl.pallas_call(
        functools.partial(kernel, boxes, across),
        out_shape=jax.ShapeDtypeStruct((COLS, OWN), f32),
        in_specs=[hbm] * 5,
        out_specs=pl.BlockSpec(memory_space=pltpu.VMEM),
        scratch_shapes=[
            pltpu.VMEM((3, OWN), f32),
            pltpu.VMEM((COLS, OWN), bf16),
            pltpu.SMEM((LEAVES,), jnp.int32),
            pltpu.VMEM((LEAVES * 64, LEAF), bf16),
            pltpu.VMEM((6, 128, 64), f32),
            pltpu.VMEM((6, 128, 128), bf16),
            pltpu.VMEM((6, 128, 128), bf16),
            pltpu.VMEM((4, 64, 128), f32),
            pltpu.VMEM((128, 512), bf16),
            pltpu.VMEM((128, 512), bf16),
            pltpu.VMEM((2, 8, OWN + 2 * LEAF), f32),
            pltpu.VMEM((OWN, 8), f32),
            pltpu.VMEM((128, 512), bf16),
            pltpu.VMEM((128, 512), bf16),
            pltpu.VMEM((COLS, OWN + LEAF), f32),
            pltpu.VMEM((LEAF, 2 * LEAF), bf16),
            pltpu.VMEM((LEAF, 2 * LEAF), bf16),
            pltpu.VMEM((LEAF, LEAF), bf16),
            pltpu.VMEM((13, 2, 8, 128), f32),
            pltpu.VMEM((13, 2, 8, 128), f32),
            pltpu.VMEM((7, 8, 128), f32),
            pltpu.VMEM((2, 3, 2, 8, 128), f32),
            pltpu.VMEM((2, 3, 2, 8, 128), f32),
            pltpu.VMEM((MEMBERS, 8, 128), f32),
            pltpu.VMEM((2, 2, 8, 128), f32),
            pltpu.VMEM((2, 2, 8, 128), f32),
            pltpu.VMEM((8, 128), f32),
            pltpu.VMEM((2, 8, 128), f32),
            pltpu.VMEM((2, 8, 128), f32),
            pltpu.VMEM((strides, 8, 128), f32),
            pltpu.VMEM((MEMBERS, 8, 128), f32),
            dma((5,)),
            dma((2,)),
            dma((2,)),
            dma((2,)),
            dma((2,)),
            dma,
            dma,
            dma((3,)),
            dma((3,)),
            dma((2,)),
            dma((2,)),
            dma((2,)),
            dma((2,)),
            dma,
            dma,
        ],
        compiler_params=pltpu.CompilerParams(
            collective_id=0, has_side_effects=True, vmem_limit_bytes=32 * 1024 * 1024
        ),
    )(
        *[
            pltpu.with_memory_space_constraint(x, pltpu.HBM)
            for x in (
                coords,
                loads,
                occupancy,
                basis.reshape(LEAVES * 64, LEAF),
                transfer.reshape(6, 128, 64),
            )
        ]
    )


def solution(mesh):
    boxes = mesh.shape["box"] // MEMBERS
    return jax.shard_map(
        functools.partial(body, boxes, 4),
        mesh=mesh,
        in_specs=(P(None, "box"), P(None, "box"), P("box"), P("box", None, None), P()),
        out_specs=P(None, "box"),
        check_vma=False,
    )
```

```python
import functools

import jax
import jax.numpy as jnp
from jax import lax
from jax.experimental import pallas as pl
from jax.experimental.pallas import tpu as pltpu
from jax.sharding import PartitionSpec as P

LEAF = 256
COLS = 8
LEAVES = 8
MEMBERS = 8
OWN = LEAF * LEAVES

f32 = jnp.float32
bf16 = jnp.bfloat16
soften = 0.0001
near_scale = 0.0625
far_scale = 0.125
NN = (((1,), (0,)), ((), ()))
NT = (((1,), (1,)), ((), ()))
MESH = pl.DeviceIdType.MESH


def div(a, b):
    return lax.div(a, jnp.int32(b))


def rem(a, b):
    return lax.rem(a, jnp.int32(b))


def phi(tx, ty, tz, sx, sy, sz, scale):
    dx = tx - sx
    dy = ty - sy
    dz = tz - sz
    r2 = dx * dx + dy * dy + dz * dz
    return (r2 * (0.5 * scale)) * jnp.log(r2 + soften)


def split(x):
    high = x.astype(bf16)
    return high, (x - high.astype(f32)).astype(bf16)


def mm(a, b, dims):
    rows = a.shape[0]
    high = a.astype(bf16).astype(f32)
    stacked = jnp.concatenate([high, a - high], axis=0).astype(bf16)
    both = lax.dot_general(stacked, b[0][...], dims, preferred_element_type=f32)
    low = lax.dot_general(stacked[:rows], b[1][...], dims, preferred_element_type=f32)
    return both[:rows] + (both[rows:] + low)


def low_half(shape):
    return lax.broadcasted_iota(jnp.int32, shape, len(shape) - 1) < 64


def merge(rows):
    count = rows.shape[0] // 16
    low = low_half((8, 128))
    return [
        jnp.where(low, rows[16 * i : 16 * i + 8], rows[16 * i + 8 : 16 * i + 16])
        for i in range(count)
    ]


def raise_coef(pairs, level_map):
    rows = mm(jnp.concatenate(pairs, axis=0), level_map, NN)
    return merge(rows) if len(pairs) > 1 else [rows]


def pick(x, entries):
    rows = x.shape[0]
    a = x.astype(bf16).astype(f32)
    b = (x - a).astype(bf16).astype(f32)
    c = (x - a) - b
    stacked = jnp.concatenate([a, b, c], axis=0).astype(bf16)
    picked = lax.dot_general(stacked, entries, NN, preferred_element_type=f32)
    return picked[:rows] + picked[rows : 2 * rows] + picked[2 * rows :]


def raise_skel(pairs, every_second):
    rows_up = pick(jnp.concatenate(pairs, axis=0), every_second)
    return merge(rows_up) if len(pairs) > 1 else [rows_up]


def cousins(chain, slot):
    low = low_half((8, 128))
    column = chain[slot, 1].T
    tx, ty, tz = column[:, 0:1], column[:, 1:2], column[:, 2:3]
    before, after = chain[slot - 1, 0], chain[slot + 1, 0]
    tiles = []
    for skel in (chain[slot - 1, 1], chain[slot + 1, 1]):
        tiles.append(phi(tx, ty, tz, skel[0:1], skel[1:2], skel[2:3], far_scale))
    tile = jnp.concatenate(tiles, axis=1)
    even = jnp.concatenate([jnp.where(low, before, 0.0), after], axis=1)
    odd = jnp.concatenate([before, jnp.where(low, 0.0, after)], axis=1)
    rows = mm(jnp.concatenate([even, odd], axis=0), split(tile), NT)
    return jnp.where(low, rows[:8], rows[8:])


def lower(pairs, level_map):
    height = pairs[0].shape[0]
    low = low_half((height, 128))
    stacked = []
    for pair in pairs:
        stacked += [jnp.where(low, pair, 0.0), jnp.where(low, 0.0, pair)]
    rows = mm(jnp.concatenate(stacked, axis=0), level_map, NT)
    return [rows[height * i : height * (i + 1)] for i in range(2 * len(pairs))]


def kernel(
    boxes,
    across,
    coords_hbm,
    loads_hbm,
    occ_hbm,
    basis_hbm,
    transfer_hbm,
    out_ref,
    coords,
    loads,
    occ,
    basis,
    transfer,
    map_high,
    map_low,
    path_map,
    path_high,
    path_low,
    field,
    column,
    leaf_high,
    leaf_low,
    near,
    tile_a,
    tile_b,
    tile_c,
    chain,
    g_chain,
    local,
    edge_send,
    edge_recv,
    g_buf,
    bound_send,
    bound_recv,
    quad_recv,
    rim_recv,
    far_send,
    far_buf,
    part_buf,
    load_sem,
    near_send_sem,
    near_recv_sem,
    edge_send_sem,
    edge_recv_sem,
    g_send_sem,
    g_recv_sem,
    bound_send_sem,
    bound_recv_sem,
    rim_send_sem,
    rim_recv_sem,
    far_send_sem,
    far_recv_sem,
    part_send_sem,
    part_recv_sem,
):
    device = lax.axis_index("box")
    total = boxes * MEMBERS
    strides = boxes // MEMBERS
    depth = boxes // (2 * across)
    box, member = div(device, MEMBERS), rem(device, MEMBERS)
    x, z, y_half = div(box, 2 * depth), rem(div(box, 2), depth), rem(box, 2)
    y, core = div(member, 2), rem(member, 2)
    low = low_half((8, 128))
    half = jnp.where(low, 0, 1)

    top = jnp.where(y == 3, 1, 0)
    outer = jnp.where(y == 0, 1, top)
    side_to = jnp.where(outer == 1, top, y - 1)
    side_from = jnp.where(outer == 1, 1 - top, y - 1)
    far_half = jnp.where(outer == 1, 1 - y_half, y_half)
    z_core = rem(div(z, 2), 2)
    far_member = 2 * jnp.where(outer == 1, 3 - y, y) + z_core
    z_high = div(z, 4)
    far_x = [rem(x + dx, across) for dx in range(across)]
    far_steps = [(dx, turn) for dx in range(across) for turn in range(2)]

    def far_box(side, dx, turn):
        far_z = rem(side + z, 2) + 2 * core + 4 * (1 - z_high if turn else z_high)
        return (far_x[dx % across] * depth + far_z) * 2 + far_half

    far_to = [far_box(side_to, dx, turn) * MEMBERS + far_member for dx, turn in far_steps]
    far_from = [far_box(side_from, -dx, turn) for dx, turn in far_steps]
    alone = jnp.logical_and(jnp.logical_and(outer == 0, side_to == 0), core == z_core)

    barrier = pltpu.get_barrier_semaphore()

    def greet(target):
        pl.semaphore_signal(barrier, inc=1, device_id=(target,), device_id_type=MESH)

    far_order = sorted(range(1, strides), key=lambda k: abs(far_steps[k][0] - across // 2))
    for k in far_order:
        greet(far_from[k] * MEMBERS + far_member)

    @pl.when(jnp.logical_not(alone))
    def _():
        greet(far_from[0] * MEMBERS + far_member)

    loading = [
        pltpu.make_async_copy(src, dst, load_sem.at[at])
        for at, (src, dst) in enumerate(
            [
                (coords_hbm, coords),
                (transfer_hbm, transfer),
                (loads_hbm, loads),
                (occ_hbm, occ),
                (basis_hbm, basis),
            ]
        )
    ]
    for copy in loading:
        copy.start()

    left_device = rem(device + total - 1, total)
    right_device = rem(device + 1, total)
    mirror = 2 * (3 - y) + core
    left_box = rem(box + boxes - 1, boxes) * MEMBERS + mirror
    right_box = rem(box + 1, boxes) * MEMBERS + mirror
    mates = [box * MEMBERS + rem(member + r, MEMBERS) for r in (6, 2, 7, 3, 5, 4, 1)]
    at_rim = outer == 1
    rim_box = rem(box + boxes + 2 * top - 1, boxes)
    rim_devices = [rim_box * MEMBERS + 6 - 6 * top + t for t in range(2)]
    quad = div(member, 4)
    quad_device = rem(box + boxes + 2 * quad - 1, boxes) * MEMBERS + mirror
    early = jnp.where(z == 0, 1, 0)
    for target in mates + [left_device, right_device, left_box, right_box]:
        greet(target)
    @pl.when(at_rim)
    def _():
        for target in rim_devices:
            greet(target)

    eighths = (lax.broadcasted_iota(jnp.int32, (1, 128), 1) & 63) * 8
    rows = lax.broadcasted_iota(jnp.int32, (512, 128), 0)
    every_eighth = (rows == eighths).astype(f32).astype(bf16)
    swapped = rows ^ 64
    eighth_swapped = (swapped == eighths).astype(f32).astype(bf16)
    picks = (lax.broadcasted_iota(jnp.int32, (1, 128), 1) & 63) * 2
    every_second = (
        (lax.broadcasted_iota(jnp.int32, (128, 128), 0) == picks).astype(f32).astype(bf16)
    )
    loading[0].wait()
    points = jnp.concatenate([coords[...], jnp.zeros((5, OWN), f32)], axis=0)
    s0 = [
        jnp.concatenate(
            [points[:, 512 * p : 512 * p + 64], points[:, 512 * p + 256 : 512 * p + 320]], axis=1
        )
        for p in range(4)
    ]
    s3 = pick(jnp.concatenate(s0, axis=1), every_eighth)

    loading[1].wait()
    maps = [(map_high.at[level], map_low.at[level]) for level in range(6)]

    def set_map(level):
        once = transfer[level]
        map_high[level], map_low[level] = split(jnp.concatenate([once, once], axis=1))

    for level in range(3):
        set_map(level)
    loading[2].wait()
    loading[3].wait()
    slots = lax.broadcasted_iota(jnp.int32, (COLS, LEAF), 1)
    live = []
    for leaf in range(LEAVES):
        part = loads[:, leaf * LEAF : (leaf + 1) * LEAF].astype(f32)
        live.append(jnp.where(slots < occ[leaf], part, 0.0))
    loading[4].wait()
    c0 = []
    for p in range(4):
        two = jnp.concatenate([live[2 * p], live[2 * p + 1]], axis=0).astype(bf16)
        rows = lax.dot_general(
            two, basis[128 * p : 128 * p + 128, :], NT, preferred_element_type=f32
        )
        c0.append(jnp.where(low, rows[:8], rows[8:]))
    c1 = raise_coef(c0, maps[0])
    c2 = raise_coef(c1, maps[1])
    c3 = raise_coef(c2, maps[2])[0]

    g_buf[member] = jnp.where(half == core, c3, s3)

    def set_field():
        field[0, :, LEAF : LEAF + OWN] = points
        for leaf in range(LEAVES):
            field[1, :, (leaf + 1) * LEAF : (leaf + 2) * LEAF] = live[leaf]
        for at in range(0, OWN, 128):
            column[at : at + 128, :] = points[:, at : at + 128].T
        near[...] = jnp.zeros_like(near)

    def fill_tile(tile, row, col, width):
        sx = field[0, 0:1, pl.ds(col, width)]
        sy = field[0, 1:2, pl.ds(col, width)]
        sz = field[0, 2:3, pl.ds(col, width)]
        for at in range(0, LEAF, 16):
            rows = column[pl.ds(row + at, 16), :]
            tile[at : at + 16, 0:width] = phi(
                rows[:, 0:1], rows[:, 1:2], rows[:, 2:3], sx, sy, sz, near_scale
            ).astype(bf16)

    def near_leaf(tile, row):
        col = row + LEAF
        fill_tile(tile, row, col, 2 * LEAF)
        loads_two = field[1, :, pl.ds(col, 2 * LEAF)].astype(bf16)
        this = lax.dot_general(loads_two, tile[...], NT, preferred_element_type=f32)
        after = lax.dot_general(
            loads_two[:, :LEAF], tile[:, LEAF:], NN, preferred_element_type=f32
        )
        return this, after

    def near_two(row):
        first, second_part = near_leaf(tile_a, row)
        second, third = near_leaf(tile_b, row + LEAF)
        near[:, pl.ds(row, LEAF)] += first
        near[:, pl.ds(row + LEAF, LEAF)] += second_part + second
        near[:, pl.ds(row + 2 * LEAF, LEAF)] += third

    def near_step(pair, carry):
        near_two(pl.multiple_of(pair * (2 * LEAF), 2 * LEAF))
        return carry

    def side(block, at):
        lanes = jnp.where(low_half((1, 128)), 0, 1)
        return jnp.where(lanes == at, block, 0.0)

    def set_chain(levels, into):
        for at, (pairs, skels) in enumerate(levels):
            first = (1, 7, 11)[at]
            for p in range(len(pairs)):
                into[first + p, 0] = pairs[p]
                into[first + p, 1] = skels[p]

    def set_inner():
        lax.fori_loop(0, 3, near_step, 0)
        row = (LEAVES - 2) * LEAF
        this, after = near_leaf(tile_a, row)
        fill_tile(tile_c, row + LEAF, row + 2 * LEAF, LEAF)
        own = field[1, :, row + 2 * LEAF : row + 3 * LEAF].astype(bf16)
        after += lax.dot_general(own, tile_c[...], NT, preferred_element_type=f32)
        near[:, row : row + LEAF] += this
        near[:, row + LEAF : row + 2 * LEAF] += after
        for slot in (2, 3):
            local[slot - 1] = cousins(chain, slot)

    def set_edges():
        s1 = raise_skel(s0, every_second)
        s2 = raise_skel(s1, every_second)

        set_chain([(c0, s0), (c1, s1), (c2, s2)], chain)
        for at, (pairs, skels) in enumerate([(c0, s0), (c1, s1), (c2, s2)]):
            edge_send[0, at, 0] = pairs[-1]
            edge_send[0, at, 1] = skels[-1]
            edge_send[1, at, 0] = pairs[0]
            edge_send[1, at, 1] = skels[0]
    def set_paths():
        for level in range(3, 6):
            set_map(level)
        paths = lower(lower([transfer[5].T], maps[4]), maps[3])
        for p in range(4):
            path_map[p] = paths[p]
        both = jnp.concatenate(paths, axis=1)
        path_high[...], path_low[...] = split(jnp.concatenate([both, both], axis=0))

    def set_leaf_paths():
        from_six = side(path_map[y], core)
        rows = lax.broadcasted_iota(jnp.int32, (64, 128), 0)
        from_three = (rows == lax.broadcasted_iota(jnp.int32, (64, 128), 1)).astype(f32)
        x2 = mm(jnp.concatenate([from_six, from_three], axis=0), maps[2], NT)
        x0 = lower(lower([x2], maps[1]), maps[0])
        leaf_high[...], leaf_low[...] = split(jnp.concatenate(x0, axis=1))

    @pl.when(early == 1)
    def _():
        set_field()
        set_edges()
        set_paths()
        set_leaf_paths()
        set_inner()

    pl.semaphore_wait(
        barrier,
        4 + MEMBERS - 1 + strides - alone.astype(jnp.int32) + 2 * at_rim.astype(jnp.int32),
    )

    def remote(src, dst, send_sem, recv_sem, target):
        return pltpu.make_async_remote_copy(
            src_ref=src,
            dst_ref=dst,
            send_sem=send_sem,
            recv_sem=recv_sem,
            device_id=(target,),
            device_id_type=MESH,
        )

    def send(*ends):
        copy = remote(*ends)
        copy.start()
        return copy

    def wait_all(ref, semaphore):
        pltpu.make_async_copy(ref, ref, semaphore).wait()

    for mate in mates:
        send(g_buf.at[member], g_buf.at[member], g_send_sem, g_recv_sem, mate)

    rim_copies = [
        pltpu.make_async_remote_copy(
            src_ref=g_buf.at[member],
            dst_ref=rim_recv.at[core],
            send_sem=rim_send_sem.at[t],
            recv_sem=rim_recv_sem.at[core],
            device_id=(rim_devices[t],),
            device_id_type=MESH,
        )
        for t in range(2)
    ]

    @pl.when(at_rim)
    def _():
        for copy in rim_copies:
            copy.start()

    @pl.when(early == 0)
    def _():
        set_field()

    last = LEAF * LEAVES
    near_copies = [
        send(
            field.at[:, :, last : last + LEAF],
            field.at[:, :, 0:LEAF],
            near_send_sem.at[0],
            near_recv_sem.at[0],
            right_device,
        ),
        send(
            field.at[:, :, LEAF : 2 * LEAF],
            field.at[:, :, last + LEAF : last + 2 * LEAF],
            near_send_sem.at[1],
            near_recv_sem.at[1],
            left_device,
        ),
    ]

    edge_copies = [
        remote(
            edge_send.at[side],
            edge_recv.at[side],
            edge_send_sem.at[side],
            edge_recv_sem.at[side],
            (right_device, left_device)[side],
        )
        for side in range(2)
    ]

    @pl.when(early == 1)
    def _():
        for copy in edge_copies:
            copy.start()

    @pl.when(early == 0)
    def _():
        set_paths()

    wait_all(g_buf.at[pl.ds(0, MEMBERS - 1)], g_recv_sem)
    c3s, s3s = [], []
    for p in range(4):
        even, odd = g_buf[2 * p], g_buf[2 * p + 1]
        c3s.append(jnp.where(low, even, odd))
        s3s.append(jnp.where(low, odd, even))
    c6 = mm(jnp.concatenate(c3s, axis=1), (path_high, path_low), NT)
    s6 = pick(jnp.concatenate(s3s, axis=1), eighth_swapped)
    far_send[0] = jnp.where(low, c6, s6)
    far_send[1] = jnp.where(low, s6, c6)

    @pl.when(alone)
    def _():
        far_buf[0] = far_send[0]

    for k in far_order:
        send(
            far_send.at[k % 2], far_buf.at[k], far_send_sem.at[1], far_recv_sem.at[1], far_to[k]
        )
    first_far = pltpu.make_async_remote_copy(
        src_ref=far_send.at[0],
        dst_ref=far_buf.at[0],
        send_sem=far_send_sem.at[0],
        recv_sem=far_recv_sem.at[0],
        device_id=(far_to[0],),
        device_id_type=MESH,
    )

    @pl.when(jnp.logical_not(alone))
    def _():
        first_far.start()

    @pl.when(early == 0)
    def _():
        set_edges()
        for copy in edge_copies:
            copy.start()

    s3s = [pltpu.roll(skel, 64, 1) for skel in s3s]
    c4s, s4s = raise_coef(c3s, maps[3]), raise_skel(s3s, every_second)
    c5s, s5s = raise_coef(c4s, maps[4]), raise_skel(s4s, every_second)
    set_chain([(c3s, s3s), (c4s, s4s), (c5s, s5s)], g_chain)
    for at in range(2):
        bound_send[at, 0] = c5s[0]
        bound_send[at, 1] = s5s[0] + pltpu.roll(s4s[1 - at], 3, 0)
    bound_copies = [
        send(
            bound_send.at[side],
            bound_recv.at[side],
            bound_send_sem.at[side],
            bound_recv_sem.at[side],
            (right_box, left_box)[side],
        )
        for side in range(2)
    ]
    bound_copies.append(
        send(
            g_chain.at[7 + quad, 0],
            quad_recv,
            bound_send_sem.at[2],
            bound_recv_sem.at[2],
            quad_device,
        )
    )

    @pl.when(early == 0)
    def _():
        set_inner()
        set_leaf_paths()

    for copy in near_copies:
        copy.wait_recv()

    @pl.when(device == 0)
    def _():
        field[1, :, 0:LEAF] = jnp.zeros((COLS, LEAF), f32)

    @pl.when(device == total - 1)
    def _():
        field[1, :, last + LEAF : last + 2 * LEAF] = jnp.zeros((COLS, LEAF), f32)

    def near_end(tile, row, col):
        fill_tile(tile, row, col, LEAF)
        near[:, row : row + LEAF] += lax.dot_general(
            field[1, :, col : col + LEAF].astype(bf16),
            tile[:, 0:LEAF],
            NT,
            preferred_element_type=f32,
        )

    near_end(tile_c, 0, 0)
    near_end(tile_a, last - LEAF, last + LEAF)

    def set_ends(ends, into, at_start, at_end):
        for level in range(3):
            before, after = (0, 6, 10)[level], (5, 9, 12)[level]
            into[before, 0] = jnp.where(at_start, 0.0, ends[0, level, 0])
            into[before, 1] = ends[0, level, 1]
            into[after, 0] = jnp.where(at_end, 0.0, ends[1, level, 0])
            into[after, 1] = ends[1, level, 1]

    for copy in edge_copies:
        copy.wait_recv()
    set_ends(edge_recv, chain, device == 0, device == total - 1)
    for at, slot in [(0, 1), (3, 4), (4, 7), (5, 8), (6, 11)]:
        local[at] = cousins(chain, slot)

    top_column = s6.T[:64]
    tx, ty, tz = top_column[:, 0:1], top_column[:, 1:2], top_column[:, 2:3]

    wait_all(far_buf.at[pl.ds(1, strides - 1)], far_recv_sem.at[1])

    @pl.when(jnp.logical_not(alone))
    def _():
        first_far.wait_recv()

    top_coef, top_skel = [], []
    for k in range(0, strides, 2):
        halves = []
        for at in (k, k + 1):
            apart = far_from[at] - box
            counts = jnp.logical_or(apart >= 2, apart <= -2)
            halves.append((far_buf[at], counts))
        (one, one_counts), (two, two_counts) = halves
        coef = jnp.where(low, jnp.where(one_counts, one, 0.0), jnp.where(two_counts, two, 0.0))
        top_coef.append(pltpu.roll(coef, 64, 1))
        top_skel.append(jnp.where(low, two, one))
    top_tile = jnp.concatenate(
        [phi(tx, ty, tz, s[0:1], s[1:2], s[2:3], far_scale) for s in top_skel], axis=1
    )
    top = mm(jnp.concatenate(top_coef, axis=1), split(top_tile), NT)
    part_buf[member] = jnp.concatenate([top, jnp.zeros((8, 64), f32)], axis=1)
    for mate in mates:
        send(part_buf.at[member], part_buf.at[member], part_send_sem, part_recv_sem, mate)

    wait_all(g_buf.at[pl.ds(0, MEMBERS - 1)], g_send_sem)
    wait_all(far_buf.at[pl.ds(1, strides - 1)], far_send_sem.at[1])
    for copy in near_copies + edge_copies + bound_copies:
        copy.wait_send()

    @pl.when(jnp.logical_not(alone))
    def _():
        first_far.wait_send()

    for copy in bound_copies:
        copy.wait_recv()
    at_start, at_end = box == 0, box == boxes - 1
    outside = jnp.logical_or(
        jnp.logical_and(quad == 0, at_start), jnp.logical_and(quad == 1, at_end)
    )
    start_skel, end_skel = bound_recv[0, 1], bound_recv[1, 1]
    g_chain[10, 0] = jnp.where(at_start, 0.0, bound_recv[0, 0])
    g_chain[10, 1] = start_skel
    g_chain[12, 0] = jnp.where(at_end, 0.0, bound_recv[1, 0])
    g_chain[12, 1] = end_skel
    quad_coef = jnp.where(outside, 0.0, quad_recv[...])
    g_chain[6, 0] = quad_coef
    g_chain[6, 1] = pltpu.roll(start_skel, 5, 0)
    g_chain[9, 0] = quad_coef
    g_chain[9, 1] = pltpu.roll(end_skel, 5, 0)

    @pl.when(at_rim)
    def _():
        for copy in rim_copies:
            copy.wait_send()
        for t in range(2):
            pltpu.make_async_remote_copy(
                src_ref=g_buf.at[member],
                dst_ref=rim_recv.at[t],
                send_sem=rim_send_sem.at[t],
                recv_sem=rim_recv_sem.at[t],
                device_id=(rim_devices[t],),
                device_id_type=MESH,
            ).wait_recv()
        even, odd = rim_recv[0], rim_recv[1]
        rim_coef = jnp.where(outside, 0.0, jnp.where(low, even, odd))
        rim_skel = pltpu.roll(jnp.where(low, odd, even), 64, 1)
        for slot in (0, 5):
            g_chain[slot, 0] = rim_coef
            g_chain[slot, 1] = rim_skel

    local3 = cousins(g_chain, 1 + y)
    local4 = cousins(g_chain, 7 + quad)
    local5 = cousins(g_chain, 11)
    y2 = local[6]
    y1 = [x + local[4 + at] for at, x in enumerate(lower([y2], maps[1]))]
    y0 = [x + local[at] for at, x in enumerate(lower(y1, maps[0]))]
    y4 = local4 + mm(side(local5, quad), maps[4], NT)
    y3 = local3 + mm(side(y4, rem(y, 2)), maps[3], NT)
    y3 = jnp.where(core == 1, y3, pltpu.roll(y3, 64, 1))

    wait_all(part_buf.at[pl.ds(0, MEMBERS - 1)], part_recv_sem)
    d6 = part_buf[0]
    for at in range(1, MEMBERS):
        d6 = d6 + part_buf[at]
    d63 = jnp.where(low, d6, y3)
    d0 = jnp.concatenate(y0, axis=1) + mm(d63, (leaf_high, leaf_low), NN)
    for p in range(4):
        pair = d0[:, 128 * p : 128 * p + 128]
        two = jnp.concatenate([jnp.where(low, pair, 0.0), jnp.where(low, 0.0, pair)], axis=0)
        rows = lax.dot_general(
            two.astype(bf16),
            basis[128 * p : 128 * p + 128, :],
            NN,
            preferred_element_type=f32,
        )
        for t in range(2):
            leaf = 2 * p + t
            at = leaf * LEAF
            out_ref[:, at : at + LEAF] = jnp.where(
                slots < occ[leaf], near[:, at : at + LEAF] + rows[8 * t : 8 * t + 8], 0.0
            )

    wait_all(part_buf.at[pl.ds(0, MEMBERS - 1)], part_send_sem)


def body(boxes, across, coords, loads, occupancy, basis, transfer):
    strides = boxes // MEMBERS
    hbm = pl.BlockSpec(memory_space=pl.ANY)
    dma = pltpu.SemaphoreType.DMA
    return pl.pallas_call(
        functools.partial(kernel, boxes, across),
        out_shape=jax.ShapeDtypeStruct((COLS, OWN), f32),
        in_specs=[hbm] * 5,
        out_specs=pl.BlockSpec(memory_space=pltpu.VMEM),
        scratch_shapes=[
            pltpu.VMEM((3, OWN), f32),
            pltpu.VMEM((COLS, OWN), bf16),
            pltpu.SMEM((LEAVES,), jnp.int32),
            pltpu.VMEM((LEAVES * 64, LEAF), bf16),
            pltpu.VMEM((6, 128, 64), f32),
            pltpu.VMEM((6, 128, 128), bf16),
            pltpu.VMEM((6, 128, 128), bf16),
            pltpu.VMEM((4, 64, 128), f32),
            pltpu.VMEM((128, 512), bf16),
            pltpu.VMEM((128, 512), bf16),
            pltpu.VMEM((2, 8, OWN + 2 * LEAF), f32),
            pltpu.VMEM((OWN, 8), f32),
            pltpu.VMEM((128, 512), bf16),
            pltpu.VMEM((128, 512), bf16),
            pltpu.VMEM((COLS, OWN + LEAF), f32),
            pltpu.VMEM((LEAF, 2 * LEAF), bf16),
            pltpu.VMEM((LEAF, 2 * LEAF), bf16),
            pltpu.VMEM((LEAF, LEAF), bf16),
            pltpu.VMEM((13, 2, 8, 128), f32),
            pltpu.VMEM((13, 2, 8, 128), f32),
            pltpu.VMEM((7, 8, 128), f32),
            pltpu.VMEM((2, 3, 2, 8, 128), f32),
            pltpu.VMEM((2, 3, 2, 8, 128), f32),
            pltpu.VMEM((MEMBERS, 8, 128), f32),
            pltpu.VMEM((2, 2, 8, 128), f32),
            pltpu.VMEM((2, 2, 8, 128), f32),
            pltpu.VMEM((8, 128), f32),
            pltpu.VMEM((2, 8, 128), f32),
            pltpu.VMEM((2, 8, 128), f32),
            pltpu.VMEM((strides, 8, 128), f32),
            pltpu.VMEM((MEMBERS, 8, 128), f32),
            dma((5,)),
            dma((2,)),
            dma((2,)),
            dma((2,)),
            dma((2,)),
            dma,
            dma,
            dma((3,)),
            dma((3,)),
            dma((2,)),
            dma((2,)),
            dma((2,)),
            dma((2,)),
            dma,
            dma,
        ],
        compiler_params=pltpu.CompilerParams(
            collective_id=0, has_side_effects=True, vmem_limit_bytes=32 * 1024 * 1024
        ),
    )(
        *[
            pltpu.with_memory_space_constraint(x, pltpu.HBM)
            for x in (
                coords,
                loads,
                occupancy,
                basis.reshape(LEAVES * 64, LEAF),
                transfer.reshape(6, 128, 64),
            )
        ]
    )


def solution(mesh):
    boxes = mesh.shape["box"] // MEMBERS
    return jax.shard_map(
        functools.partial(body, boxes, 4),
        mesh=mesh,
        in_specs=(P(None, "box"), P(None, "box"), P("box"), P("box", None, None), P()),
        out_specs=P(None, "box"),
        check_vma=False,
    )
```

```python
import functools

import jax
import jax.numpy as jnp
from jax import lax
from jax.experimental import pallas as pl
from jax.experimental.pallas import tpu as pltpu
from jax.sharding import PartitionSpec as P

LEAF = 256
COLS = 8
LEAVES = 8
MEMBERS = 8
OWN = LEAF * LEAVES

f32 = jnp.float32
bf16 = jnp.bfloat16
soften = 0.0001
near_scale = 0.0625
far_scale = 0.125
NN = (((1,), (0,)), ((), ()))
NT = (((1,), (1,)), ((), ()))
MESH = pl.DeviceIdType.MESH


def div(a, b):
    return lax.div(a, jnp.int32(b))


def rem(a, b):
    return lax.rem(a, jnp.int32(b))


def phi(tx, ty, tz, sx, sy, sz, scale):
    dx = tx - sx
    dy = ty - sy
    dz = tz - sz
    r2 = dx * dx + dy * dy + dz * dz
    return (r2 * (0.5 * scale)) * jnp.log(r2 + soften)


def split(x):
    high = x.astype(bf16)
    return high, (x - high.astype(f32)).astype(bf16)


def mm(a, b, dims):
    rows = a.shape[0]
    high = a.astype(bf16).astype(f32)
    stacked = jnp.concatenate([high, a - high], axis=0).astype(bf16)
    both = lax.dot_general(stacked, b[0][...], dims, preferred_element_type=f32)
    low = lax.dot_general(stacked[:rows], b[1][...], dims, preferred_element_type=f32)
    return both[:rows] + (both[rows:] + low)


def low_half(shape):
    return lax.broadcasted_iota(jnp.int32, shape, len(shape) - 1) < 64


def merge(rows):
    count = rows.shape[0] // 16
    low = low_half((8, 128))
    return [
        jnp.where(low, rows[16 * i : 16 * i + 8], rows[16 * i + 8 : 16 * i + 16])
        for i in range(count)
    ]


def raise_coef(pairs, level_map):
    rows = mm(jnp.concatenate(pairs, axis=0), level_map, NN)
    return merge(rows) if len(pairs) > 1 else [rows]


def pick(x, entries):
    rows = x.shape[0]
    a = x.astype(bf16).astype(f32)
    b = (x - a).astype(bf16).astype(f32)
    c = (x - a) - b
    stacked = jnp.concatenate([a, b, c], axis=0).astype(bf16)
    picked = lax.dot_general(stacked, entries, NN, preferred_element_type=f32)
    return picked[:rows] + picked[rows : 2 * rows] + picked[2 * rows :]


def raise_skel(pairs, every_second):
    rows_up = pick(jnp.concatenate(pairs, axis=0), every_second)
    return merge(rows_up) if len(pairs) > 1 else [rows_up]


def cousins(chain, slot):
    low = low_half((8, 128))
    column = chain[slot, 1].T
    tx, ty, tz = column[:, 0:1], column[:, 1:2], column[:, 2:3]
    before, after = chain[slot - 1, 0], chain[slot + 1, 0]
    tiles = []
    for skel in (chain[slot - 1, 1], chain[slot + 1, 1]):
        tiles.append(phi(tx, ty, tz, skel[0:1], skel[1:2], skel[2:3], far_scale))
    tile = jnp.concatenate(tiles, axis=1)
    even = jnp.concatenate([jnp.where(low, before, 0.0), after], axis=1)
    odd = jnp.concatenate([before, jnp.where(low, 0.0, after)], axis=1)
    rows = mm(jnp.concatenate([even, odd], axis=0), split(tile), NT)
    return jnp.where(low, rows[:8], rows[8:])


def lower(pairs, level_map):
    height = pairs[0].shape[0]
    low = low_half((height, 128))
    stacked = []
    for pair in pairs:
        stacked += [jnp.where(low, pair, 0.0), jnp.where(low, 0.0, pair)]
    rows = mm(jnp.concatenate(stacked, axis=0), level_map, NT)
    return [rows[height * i : height * (i + 1)] for i in range(2 * len(pairs))]


def kernel(
    boxes,
    across,
    coords_hbm,
    loads_hbm,
    occ_hbm,
    basis_hbm,
    transfer_hbm,
    out_ref,
    coords,
    loads,
    occ,
    basis,
    transfer,
    map_high,
    map_low,
    path_map,
    path_high,
    path_low,
    field,
    column,
    leaf_high,
    leaf_low,
    near,
    tile_a,
    tile_b,
    tile_c,
    chain,
    g_chain,
    local,
    edge_send,
    edge_recv,
    g_buf,
    bound_send,
    bound_recv,
    quad_recv,
    rim_recv,
    far_send,
    far_buf,
    part_buf,
    load_sem,
    near_send_sem,
    near_recv_sem,
    edge_send_sem,
    edge_recv_sem,
    g_send_sem,
    g_recv_sem,
    bound_send_sem,
    bound_recv_sem,
    rim_send_sem,
    rim_recv_sem,
    far_send_sem,
    far_recv_sem,
    part_send_sem,
    part_recv_sem,
    ready,
):
    device = lax.axis_index("box")
    total = boxes * MEMBERS
    strides = boxes // MEMBERS
    depth = boxes // (2 * across)
    box, member = div(device, MEMBERS), rem(device, MEMBERS)
    x, z, y_half = div(box, 2 * depth), rem(div(box, 2), depth), rem(box, 2)
    y, core = div(member, 2), rem(member, 2)
    low = low_half((8, 128))
    half = jnp.where(low, 0, 1)

    top = jnp.where(y == 3, 1, 0)
    outer = jnp.where(y == 0, 1, top)
    side_to = jnp.where(outer == 1, top, y - 1)
    side_from = jnp.where(outer == 1, 1 - top, y - 1)
    far_half = jnp.where(outer == 1, 1 - y_half, y_half)
    z_core = rem(div(z, 2), 2)
    far_member = 2 * jnp.where(outer == 1, 3 - y, y) + z_core
    z_high = div(z, 4)
    far_x = [rem(x + dx, across) for dx in range(across)]
    far_steps = [(dx, turn) for dx in range(across) for turn in range(2)]

    def far_box(side, dx, turn):
        far_z = rem(side + z, 2) + 2 * core + 4 * (1 - z_high if turn else z_high)
        return (far_x[dx % across] * depth + far_z) * 2 + far_half

    far_to = [far_box(side_to, dx, turn) * MEMBERS + far_member for dx, turn in far_steps]
    far_from = [far_box(side_from, -dx, turn) for dx, turn in far_steps]
    alone = jnp.logical_and(jnp.logical_and(outer == 0, side_to == 0), core == z_core)

    barrier = pltpu.get_barrier_semaphore()

    def greet(target):
        pl.semaphore_signal(barrier, inc=1, device_id=(target,), device_id_type=MESH)

    far_order = sorted(range(1, strides), key=lambda k: abs(far_steps[k][0] - across // 2))
    place = 2 * y + z_core
    relay_z = [rem(side_to + z, 2) + 2 * core + 4 * high for high in (z_high, 1 - z_high)]
    to_relay = [((x * depth + at) * 2 + y_half) * MEMBERS + place for at in relay_z]
    sender_z = [rem(side_to + z, 2) + 2 * core + 4 * high for high in (z_high, 1 - z_high)]
    senders = [((x * depth + at) * 2 + y_half) * MEMBERS + place for at in sender_z]
    from_relay = [
        ((at * depth + z) * 2 + far_half) * MEMBERS + far_member - z_core + core for at in far_x
    ]
    own_sender = jnp.logical_and(side_to == 0, core == z_core)

    greet(to_relay[1])
    for dx in (2, 1, 3):
        greet(from_relay[dx])

    @pl.when(jnp.logical_not(own_sender))
    def _():
        greet(to_relay[0])

    @pl.when(outer == 1)
    def _():
        greet(from_relay[0])

    loading = [
        pltpu.make_async_copy(src, dst, load_sem.at[at])
        for at, (src, dst) in enumerate(
            [
                (coords_hbm, coords),
                (transfer_hbm, transfer),
                (loads_hbm, loads),
                (occ_hbm, occ),
                (basis_hbm, basis),
            ]
        )
    ]
    for copy in loading:
        copy.start()

    left_device = rem(device + total - 1, total)
    right_device = rem(device + 1, total)
    mirror = 2 * (3 - y) + core
    left_box = rem(box + boxes - 1, boxes) * MEMBERS + mirror
    right_box = rem(box + 1, boxes) * MEMBERS + mirror
    mates = [box * MEMBERS + rem(member + r, MEMBERS) for r in (6, 2, 7, 3, 5, 4, 1)]
    at_rim = outer == 1
    rim_box = rem(box + boxes + 2 * top - 1, boxes)
    rim_devices = [rim_box * MEMBERS + 6 - 6 * top + t for t in range(2)]
    quad = div(member, 4)
    quad_device = rem(box + boxes + 2 * quad - 1, boxes) * MEMBERS + mirror
    early = jnp.where(z == 0, 1, 0)
    for target in mates + [left_device, right_device, left_box, right_box]:
        greet(target)
    @pl.when(at_rim)
    def _():
        for target in rim_devices:
            greet(target)

    eighths = (lax.broadcasted_iota(jnp.int32, (1, 128), 1) & 63) * 8
    rows = lax.broadcasted_iota(jnp.int32, (512, 128), 0)
    every_eighth = (rows == eighths).astype(f32).astype(bf16)
    swapped = rows ^ 64
    eighth_swapped = (swapped == eighths).astype(f32).astype(bf16)
    picks = (lax.broadcasted_iota(jnp.int32, (1, 128), 1) & 63) * 2
    every_second = (
        (lax.broadcasted_iota(jnp.int32, (128, 128), 0) == picks).astype(f32).astype(bf16)
    )
    loading[0].wait()
    points = jnp.concatenate([coords[...], jnp.zeros((5, OWN), f32)], axis=0)
    s0 = [
        jnp.concatenate(
            [points[:, 512 * p : 512 * p + 64], points[:, 512 * p + 256 : 512 * p + 320]], axis=1
        )
        for p in range(4)
    ]
    s3 = pick(jnp.concatenate(s0, axis=1), every_eighth)

    loading[1].wait()
    maps = [(map_high.at[level], map_low.at[level]) for level in range(6)]

    def set_map(level):
        once = transfer[level]
        map_high[level], map_low[level] = split(jnp.concatenate([once, once], axis=1))

    for level in range(3):
        set_map(level)
    loading[2].wait()
    loading[3].wait()
    slots = lax.broadcasted_iota(jnp.int32, (COLS, LEAF), 1)
    live = []
    for leaf in range(LEAVES):
        part = loads[:, leaf * LEAF : (leaf + 1) * LEAF].astype(f32)
        live.append(jnp.where(slots < occ[leaf], part, 0.0))
    loading[4].wait()
    c0 = []
    for p in range(4):
        two = jnp.concatenate([live[2 * p], live[2 * p + 1]], axis=0).astype(bf16)
        rows = lax.dot_general(
            two, basis[128 * p : 128 * p + 128, :], NT, preferred_element_type=f32
        )
        c0.append(jnp.where(low, rows[:8], rows[8:]))
    c1 = raise_coef(c0, maps[0])
    c2 = raise_coef(c1, maps[1])
    c3 = raise_coef(c2, maps[2])[0]

    g_buf[member] = jnp.where(half == core, c3, s3)

    def set_field():
        field[0, :, LEAF : LEAF + OWN] = points
        for leaf in range(LEAVES):
            field[1, :, (leaf + 1) * LEAF : (leaf + 2) * LEAF] = live[leaf]
        for at in range(0, OWN, 128):
            column[at : at + 128, :] = points[:, at : at + 128].T
        near[...] = jnp.zeros_like(near)

    def fill_tile(tile, row, col, width):
        sx = field[0, 0:1, pl.ds(col, width)]
        sy = field[0, 1:2, pl.ds(col, width)]
        sz = field[0, 2:3, pl.ds(col, width)]
        for at in range(0, LEAF, 16):
            rows = column[pl.ds(row + at, 16), :]
            tile[at : at + 16, 0:width] = phi(
                rows[:, 0:1], rows[:, 1:2], rows[:, 2:3], sx, sy, sz, near_scale
            ).astype(bf16)

    def near_leaf(tile, row):
        col = row + LEAF
        fill_tile(tile, row, col, 2 * LEAF)
        loads_two = field[1, :, pl.ds(col, 2 * LEAF)].astype(bf16)
        this = lax.dot_general(loads_two, tile[...], NT, preferred_element_type=f32)
        after = lax.dot_general(
            loads_two[:, :LEAF], tile[:, LEAF:], NN, preferred_element_type=f32
        )
        return this, after

    def near_two(row):
        first, second_part = near_leaf(tile_a, row)
        second, third = near_leaf(tile_b, row + LEAF)
        near[:, pl.ds(row, LEAF)] += first
        near[:, pl.ds(row + LEAF, LEAF)] += second_part + second
        near[:, pl.ds(row + 2 * LEAF, LEAF)] += third

    def near_step(pair, carry):
        near_two(pl.multiple_of(pair * (2 * LEAF), 2 * LEAF))
        return carry

    def side(block, at):
        lanes = jnp.where(low_half((1, 128)), 0, 1)
        return jnp.where(lanes == at, block, 0.0)

    def set_chain(levels, into):
        for at, (pairs, skels) in enumerate(levels):
            first = (1, 7, 11)[at]
            for p in range(len(pairs)):
                into[first + p, 0] = pairs[p]
                into[first + p, 1] = skels[p]

    def set_inner():
        lax.fori_loop(0, 3, near_step, 0)
        row = (LEAVES - 2) * LEAF
        this, after = near_leaf(tile_a, row)
        fill_tile(tile_c, row + LEAF, row + 2 * LEAF, LEAF)
        own = field[1, :, row + 2 * LEAF : row + 3 * LEAF].astype(bf16)
        after += lax.dot_general(own, tile_c[...], NT, preferred_element_type=f32)
        near[:, row : row + LEAF] += this
        near[:, row + LEAF : row + 2 * LEAF] += after
        for slot in (2, 3):
            local[slot - 1] = cousins(chain, slot)

    def set_edges():
        s1 = raise_skel(s0, every_second)
        s2 = raise_skel(s1, every_second)

        set_chain([(c0, s0), (c1, s1), (c2, s2)], chain)
        for at, (pairs, skels) in enumerate([(c0, s0), (c1, s1), (c2, s2)]):
            edge_send[0, at, 0] = pairs[-1]
            edge_send[0, at, 1] = skels[-1]
            edge_send[1, at, 0] = pairs[0]
            edge_send[1, at, 1] = skels[0]
    def set_paths():
        for level in range(3, 6):
            set_map(level)
        paths = lower(lower([transfer[5].T], maps[4]), maps[3])
        for p in range(4):
            path_map[p] = paths[p]
        both = jnp.concatenate(paths, axis=1)
        path_high[...], path_low[...] = split(jnp.concatenate([both, both], axis=0))

    def set_leaf_paths():
        from_six = side(path_map[y], core)
        rows = lax.broadcasted_iota(jnp.int32, (64, 128), 0)
        from_three = (rows == lax.broadcasted_iota(jnp.int32, (64, 128), 1)).astype(f32)
        x2 = mm(jnp.concatenate([from_six, from_three], axis=0), maps[2], NT)
        x0 = lower(lower([x2], maps[1]), maps[0])
        leaf_high[...], leaf_low[...] = split(jnp.concatenate(x0, axis=1))

    @pl.when(early == 1)
    def _():
        set_field()
        set_edges()
        set_paths()
        set_leaf_paths()
        set_inner()

    pl.semaphore_wait(
        barrier, MEMBERS - 1 + 4 + 3 + outer + 2 - own_sender.astype(jnp.int32) + 2 * outer
    )

    def tell(target):
        pl.semaphore_signal(ready, inc=1, device_id=(target,), device_id_type=MESH)

    tell(senders[1])

    @pl.when(jnp.logical_not(own_sender))
    def _():
        tell(senders[0])

    def remote(src, dst, send_sem, recv_sem, target):
        return pltpu.make_async_remote_copy(
            src_ref=src,
            dst_ref=dst,
            send_sem=send_sem,
            recv_sem=recv_sem,
            device_id=(target,),
            device_id_type=MESH,
        )

    def send(*ends):
        copy = remote(*ends)
        copy.start()
        return copy

    def wait_all(ref, semaphore):
        pltpu.make_async_copy(ref, ref, semaphore).wait()

    for mate in mates:
        send(g_buf.at[member], g_buf.at[member], g_send_sem, g_recv_sem, mate)

    rim_copies = [
        pltpu.make_async_remote_copy(
            src_ref=g_buf.at[member],
            dst_ref=rim_recv.at[core],
            send_sem=rim_send_sem.at[t],
            recv_sem=rim_recv_sem.at[core],
            device_id=(rim_devices[t],),
            device_id_type=MESH,
        )
        for t in range(2)
    ]

    @pl.when(at_rim)
    def _():
        for copy in rim_copies:
            copy.start()

    @pl.when(early == 0)
    def _():
        set_field()

    last = LEAF * LEAVES
    near_copies = [
        send(
            field.at[:, :, last : last + LEAF],
            field.at[:, :, 0:LEAF],
            near_send_sem.at[0],
            near_recv_sem.at[0],
            right_device,
        ),
        send(
            field.at[:, :, LEAF : 2 * LEAF],
            field.at[:, :, last + LEAF : last + 2 * LEAF],
            near_send_sem.at[1],
            near_recv_sem.at[1],
            left_device,
        ),
    ]

    edge_copies = [
        remote(
            edge_send.at[side],
            edge_recv.at[side],
            edge_send_sem.at[side],
            edge_recv_sem.at[side],
            (right_device, left_device)[side],
        )
        for side in range(2)
    ]

    @pl.when(early == 1)
    def _():
        for copy in edge_copies:
            copy.start()

    @pl.when(early == 0)
    def _():
        set_paths()

    wait_all(g_buf.at[pl.ds(0, MEMBERS - 1)], g_recv_sem)
    c3s, s3s = [], []
    for p in range(4):
        even, odd = g_buf[2 * p], g_buf[2 * p + 1]
        c3s.append(jnp.where(low, even, odd))
        s3s.append(jnp.where(low, odd, even))
    c6 = mm(jnp.concatenate(c3s, axis=1), (path_high, path_low), NT)
    s6 = pick(jnp.concatenate(s3s, axis=1), eighth_swapped)
    far_send[0] = jnp.where(low, c6, s6)
    far_send[1] = jnp.where(low, s6, c6)

    @pl.when(alone)
    def _():
        far_buf[0] = far_send[0]

    pl.semaphore_wait(ready, 2 - own_sender.astype(jnp.int32))
    for k in far_order:
        send(
            far_send.at[k % 2], far_buf.at[k], far_send_sem.at[1], far_recv_sem.at[1], far_to[k]
        )
    first_far = pltpu.make_async_remote_copy(
        src_ref=far_send.at[0],
        dst_ref=far_buf.at[0],
        send_sem=far_send_sem.at[0],
        recv_sem=far_recv_sem.at[0],
        device_id=(far_to[0],),
        device_id_type=MESH,
    )

    @pl.when(jnp.logical_not(alone))
    def _():
        first_far.start()

    @pl.when(early == 0)
    def _():
        set_edges()
        for copy in edge_copies:
            copy.start()

    s3s = [pltpu.roll(skel, 64, 1) for skel in s3s]
    c4s, s4s = raise_coef(c3s, maps[3]), raise_skel(s3s, every_second)
    c5s, s5s = raise_coef(c4s, maps[4]), raise_skel(s4s, every_second)
    set_chain([(c3s, s3s), (c4s, s4s), (c5s, s5s)], g_chain)
    for at in range(2):
        bound_send[at, 0] = c5s[0]
        bound_send[at, 1] = s5s[0] + pltpu.roll(s4s[1 - at], 3, 0)
    bound_copies = [
        send(
            bound_send.at[side],
            bound_recv.at[side],
            bound_send_sem.at[side],
            bound_recv_sem.at[side],
            (right_box, left_box)[side],
        )
        for side in range(2)
    ]
    bound_copies.append(
        send(
            g_chain.at[7 + quad, 0],
            quad_recv,
            bound_send_sem.at[2],
            bound_recv_sem.at[2],
            quad_device,
        )
    )

    @pl.when(early == 0)
    def _():
        set_inner()
        set_leaf_paths()

    for copy in near_copies:
        copy.wait_recv()

    @pl.when(device == 0)
    def _():
        field[1, :, 0:LEAF] = jnp.zeros((COLS, LEAF), f32)

    @pl.when(device == total - 1)
    def _():
        field[1, :, last + LEAF : last + 2 * LEAF] = jnp.zeros((COLS, LEAF), f32)

    def near_end(tile, row, col):
        fill_tile(tile, row, col, LEAF)
        near[:, row : row + LEAF] += lax.dot_general(
            field[1, :, col : col + LEAF].astype(bf16),
            tile[:, 0:LEAF],
            NT,
            preferred_element_type=f32,
        )

    near_end(tile_c, 0, 0)
    near_end(tile_a, last - LEAF, last + LEAF)

    def set_ends(ends, into, at_start, at_end):
        for level in range(3):
            before, after = (0, 6, 10)[level], (5, 9, 12)[level]
            into[before, 0] = jnp.where(at_start, 0.0, ends[0, level, 0])
            into[before, 1] = ends[0, level, 1]
            into[after, 0] = jnp.where(at_end, 0.0, ends[1, level, 0])
            into[after, 1] = ends[1, level, 1]

    for copy in edge_copies:
        copy.wait_recv()
    set_ends(edge_recv, chain, device == 0, device == total - 1)
    for at, slot in [(0, 1), (3, 4), (4, 7), (5, 8), (6, 11)]:
        local[at] = cousins(chain, slot)

    top_column = s6.T[:64]
    tx, ty, tz = top_column[:, 0:1], top_column[:, 1:2], top_column[:, 2:3]

    wait_all(far_buf.at[pl.ds(1, strides - 1)], far_recv_sem.at[1])

    @pl.when(jnp.logical_not(alone))
    def _():
        first_far.wait_recv()

    top_coef, top_skel = [], []
    for k in range(0, strides, 2):
        halves = []
        for at in (k, k + 1):
            apart = far_from[at] - box
            counts = jnp.logical_or(apart >= 2, apart <= -2)
            halves.append((far_buf[at], counts))
        (one, one_counts), (two, two_counts) = halves
        coef = jnp.where(low, jnp.where(one_counts, one, 0.0), jnp.where(two_counts, two, 0.0))
        top_coef.append(pltpu.roll(coef, 64, 1))
        top_skel.append(jnp.where(low, two, one))
    top_tile = jnp.concatenate(
        [phi(tx, ty, tz, s[0:1], s[1:2], s[2:3], far_scale) for s in top_skel], axis=1
    )
    top = mm(jnp.concatenate(top_coef, axis=1), split(top_tile), NT)
    part_buf[member] = jnp.concatenate([top, jnp.zeros((8, 64), f32)], axis=1)
    for mate in mates:
        send(part_buf.at[member], part_buf.at[member], part_send_sem, part_recv_sem, mate)

    wait_all(g_buf.at[pl.ds(0, MEMBERS - 1)], g_send_sem)
    wait_all(far_buf.at[pl.ds(1, strides - 1)], far_send_sem.at[1])
    for copy in near_copies + edge_copies + bound_copies:
        copy.wait_send()

    @pl.when(jnp.logical_not(alone))
    def _():
        first_far.wait_send()

    for copy in bound_copies:
        copy.wait_recv()
    at_start, at_end = box == 0, box == boxes - 1
    outside = jnp.logical_or(
        jnp.logical_and(quad == 0, at_start), jnp.logical_and(quad == 1, at_end)
    )
    start_skel, end_skel = bound_recv[0, 1], bound_recv[1, 1]
    g_chain[10, 0] = jnp.where(at_start, 0.0, bound_recv[0, 0])
    g_chain[10, 1] = start_skel
    g_chain[12, 0] = jnp.where(at_end, 0.0, bound_recv[1, 0])
    g_chain[12, 1] = end_skel
    quad_coef = jnp.where(outside, 0.0, quad_recv[...])
    g_chain[6, 0] = quad_coef
    g_chain[6, 1] = pltpu.roll(start_skel, 5, 0)
    g_chain[9, 0] = quad_coef
    g_chain[9, 1] = pltpu.roll(end_skel, 5, 0)

    @pl.when(at_rim)
    def _():
        for copy in rim_copies:
            copy.wait_send()
        for t in range(2):
            pltpu.make_async_remote_copy(
                src_ref=g_buf.at[member],
                dst_ref=rim_recv.at[t],
                send_sem=rim_send_sem.at[t],
                recv_sem=rim_recv_sem.at[t],
                device_id=(rim_devices[t],),
                device_id_type=MESH,
            ).wait_recv()
        even, odd = rim_recv[0], rim_recv[1]
        rim_coef = jnp.where(outside, 0.0, jnp.where(low, even, odd))
        rim_skel = pltpu.roll(jnp.where(low, odd, even), 64, 1)
        for slot in (0, 5):
            g_chain[slot, 0] = rim_coef
            g_chain[slot, 1] = rim_skel

    local3 = cousins(g_chain, 1 + y)
    local4 = cousins(g_chain, 7 + quad)
    local5 = cousins(g_chain, 11)
    y2 = local[6]
    y1 = [x + local[4 + at] for at, x in enumerate(lower([y2], maps[1]))]
    y0 = [x + local[at] for at, x in enumerate(lower(y1, maps[0]))]
    y4 = local4 + mm(side(local5, quad), maps[4], NT)
    y3 = local3 + mm(side(y4, rem(y, 2)), maps[3], NT)
    y3 = jnp.where(core == 1, y3, pltpu.roll(y3, 64, 1))

    wait_all(part_buf.at[pl.ds(0, MEMBERS - 1)], part_recv_sem)
    d6 = part_buf[0]
    for at in range(1, MEMBERS):
        d6 = d6 + part_buf[at]
    d63 = jnp.where(low, d6, y3)
    d0 = jnp.concatenate(y0, axis=1) + mm(d63, (leaf_high, leaf_low), NN)
    for p in range(4):
        pair = d0[:, 128 * p : 128 * p + 128]
        two = jnp.concatenate([jnp.where(low, pair, 0.0), jnp.where(low, 0.0, pair)], axis=0)
        rows = lax.dot_general(
            two.astype(bf16),
            basis[128 * p : 128 * p + 128, :],
            NN,
            preferred_element_type=f32,
        )
        for t in range(2):
            leaf = 2 * p + t
            at = leaf * LEAF
            out_ref[:, at : at + LEAF] = jnp.where(
                slots < occ[leaf], near[:, at : at + LEAF] + rows[8 * t : 8 * t + 8], 0.0
            )

    wait_all(part_buf.at[pl.ds(0, MEMBERS - 1)], part_send_sem)


def body(boxes, across, coords, loads, occupancy, basis, transfer):
    strides = boxes // MEMBERS
    hbm = pl.BlockSpec(memory_space=pl.ANY)
    dma = pltpu.SemaphoreType.DMA
    return pl.pallas_call(
        functools.partial(kernel, boxes, across),
        out_shape=jax.ShapeDtypeStruct((COLS, OWN), f32),
        in_specs=[hbm] * 5,
        out_specs=pl.BlockSpec(memory_space=pltpu.VMEM),
        scratch_shapes=[
            pltpu.VMEM((3, OWN), f32),
            pltpu.VMEM((COLS, OWN), bf16),
            pltpu.SMEM((LEAVES,), jnp.int32),
            pltpu.VMEM((LEAVES * 64, LEAF), bf16),
            pltpu.VMEM((6, 128, 64), f32),
            pltpu.VMEM((6, 128, 128), bf16),
            pltpu.VMEM((6, 128, 128), bf16),
            pltpu.VMEM((4, 64, 128), f32),
            pltpu.VMEM((128, 512), bf16),
            pltpu.VMEM((128, 512), bf16),
            pltpu.VMEM((2, 8, OWN + 2 * LEAF), f32),
            pltpu.VMEM((OWN, 8), f32),
            pltpu.VMEM((128, 512), bf16),
            pltpu.VMEM((128, 512), bf16),
            pltpu.VMEM((COLS, OWN + LEAF), f32),
            pltpu.VMEM((LEAF, 2 * LEAF), bf16),
            pltpu.VMEM((LEAF, 2 * LEAF), bf16),
            pltpu.VMEM((LEAF, LEAF), bf16),
            pltpu.VMEM((13, 2, 8, 128), f32),
            pltpu.VMEM((13, 2, 8, 128), f32),
            pltpu.VMEM((7, 8, 128), f32),
            pltpu.VMEM((2, 3, 2, 8, 128), f32),
            pltpu.VMEM((2, 3, 2, 8, 128), f32),
            pltpu.VMEM((MEMBERS, 8, 128), f32),
            pltpu.VMEM((2, 2, 8, 128), f32),
            pltpu.VMEM((2, 2, 8, 128), f32),
            pltpu.VMEM((8, 128), f32),
            pltpu.VMEM((2, 8, 128), f32),
            pltpu.VMEM((2, 8, 128), f32),
            pltpu.VMEM((strides, 8, 128), f32),
            pltpu.VMEM((MEMBERS, 8, 128), f32),
            dma((5,)),
            dma((2,)),
            dma((2,)),
            dma((2,)),
            dma((2,)),
            dma,
            dma,
            dma((3,)),
            dma((3,)),
            dma((2,)),
            dma((2,)),
            dma((2,)),
            dma((2,)),
            dma,
            dma,
            pltpu.SemaphoreType.REGULAR,
        ],
        compiler_params=pltpu.CompilerParams(
            collective_id=0, has_side_effects=True, vmem_limit_bytes=32 * 1024 * 1024
        ),
    )(
        *[
            pltpu.with_memory_space_constraint(x, pltpu.HBM)
            for x in (
                coords,
                loads,
                occupancy,
                basis.reshape(LEAVES * 64, LEAF),
                transfer.reshape(6, 128, 64),
            )
        ]
    )


def solution(mesh):
    boxes = mesh.shape["box"] // MEMBERS
    return jax.shard_map(
        functools.partial(body, boxes, 4),
        mesh=mesh,
        in_specs=(P(None, "box"), P(None, "box"), P("box"), P("box", None, None), P()),
        out_specs=P(None, "box"),
        check_vma=False,
    )
```

```python
import functools

import jax
import jax.numpy as jnp
from jax import lax
from jax.experimental import pallas as pl
from jax.experimental.pallas import tpu as pltpu
from jax.sharding import PartitionSpec as P

LEAF = 256
COLS = 8
LEAVES = 8
MEMBERS = 8
OWN = LEAF * LEAVES

f32 = jnp.float32
bf16 = jnp.bfloat16
soften = 0.0001
near_scale = 0.0625
far_scale = 0.125
NN = (((1,), (0,)), ((), ()))
NT = (((1,), (1,)), ((), ()))
MESH = pl.DeviceIdType.MESH


def div(a, b):
    return lax.div(a, jnp.int32(b))


def rem(a, b):
    return lax.rem(a, jnp.int32(b))


def phi(tx, ty, tz, sx, sy, sz, scale):
    dx = tx - sx
    dy = ty - sy
    dz = tz - sz
    r2 = dx * dx + dy * dy + dz * dz
    return (r2 * (0.5 * scale)) * jnp.log(r2 + soften)


def split(x):
    high = x.astype(bf16)
    return high, (x - high.astype(f32)).astype(bf16)


def mm(a, b, dims):
    rows = a.shape[0]
    high = a.astype(bf16).astype(f32)
    stacked = jnp.concatenate([high, a - high], axis=0).astype(bf16)
    both = lax.dot_general(stacked, b[0][...], dims, preferred_element_type=f32)
    low = lax.dot_general(stacked[:rows], b[1][...], dims, preferred_element_type=f32)
    return both[:rows] + (both[rows:] + low)


def low_half(shape):
    return lax.broadcasted_iota(jnp.int32, shape, len(shape) - 1) < 64


def merge(rows):
    count = rows.shape[0] // 16
    low = low_half((8, 128))
    return [
        jnp.where(low, rows[16 * i : 16 * i + 8], rows[16 * i + 8 : 16 * i + 16])
        for i in range(count)
    ]


def raise_coef(pairs, level_map):
    rows = mm(jnp.concatenate(pairs, axis=0), level_map, NN)
    return merge(rows) if len(pairs) > 1 else [rows]


def pick(x, entries):
    rows = x.shape[0]
    a = x.astype(bf16).astype(f32)
    b = (x - a).astype(bf16).astype(f32)
    c = (x - a) - b
    stacked = jnp.concatenate([a, b, c], axis=0).astype(bf16)
    picked = lax.dot_general(stacked, entries, NN, preferred_element_type=f32)
    return picked[:rows] + picked[rows : 2 * rows] + picked[2 * rows :]


def raise_skel(pairs, every_second):
    rows_up = pick(jnp.concatenate(pairs, axis=0), every_second)
    return merge(rows_up) if len(pairs) > 1 else [rows_up]


def cousins(chain, slot):
    low = low_half((8, 128))
    column = chain[slot, 1].T
    tx, ty, tz = column[:, 0:1], column[:, 1:2], column[:, 2:3]
    before, after = chain[slot - 1, 0], chain[slot + 1, 0]
    tiles = []
    for skel in (chain[slot - 1, 1], chain[slot + 1, 1]):
        tiles.append(phi(tx, ty, tz, skel[0:1], skel[1:2], skel[2:3], far_scale))
    tile = jnp.concatenate(tiles, axis=1)
    even = jnp.concatenate([jnp.where(low, before, 0.0), after], axis=1)
    odd = jnp.concatenate([before, jnp.where(low, 0.0, after)], axis=1)
    rows = mm(jnp.concatenate([even, odd], axis=0), split(tile), NT)
    return jnp.where(low, rows[:8], rows[8:])


def lower(pairs, level_map):
    height = pairs[0].shape[0]
    low = low_half((height, 128))
    stacked = []
    for pair in pairs:
        stacked += [jnp.where(low, pair, 0.0), jnp.where(low, 0.0, pair)]
    rows = mm(jnp.concatenate(stacked, axis=0), level_map, NT)
    return [rows[height * i : height * (i + 1)] for i in range(2 * len(pairs))]


def kernel(
    boxes,
    across,
    coords_hbm,
    loads_hbm,
    occ_hbm,
    basis_hbm,
    transfer_hbm,
    out_ref,
    coords,
    loads,
    occ,
    basis,
    transfer,
    map_high,
    map_low,
    path_map,
    path_high,
    path_low,
    field,
    column,
    leaf_high,
    leaf_low,
    near,
    tile_a,
    tile_b,
    tile_c,
    chain,
    g_chain,
    local,
    edge_send,
    edge_recv,
    g_buf,
    bound_send,
    bound_recv,
    quad_recv,
    rim_recv,
    far_send,
    far_buf,
    part_buf,
    load_sem,
    near_send_sem,
    near_recv_sem,
    edge_send_sem,
    edge_recv_sem,
    g_send_sem,
    g_recv_sem,
    bound_send_sem,
    bound_recv_sem,
    rim_send_sem,
    rim_recv_sem,
    far_send_sem,
    far_recv_sem,
    part_send_sem,
    part_recv_sem,
    ready,
):
    loading = [
        pltpu.make_async_copy(src, dst, load_sem.at[at])
        for at, (src, dst) in enumerate(
            [
                (coords_hbm, coords),
                (transfer_hbm, transfer),
                (loads_hbm, loads),
                (occ_hbm, occ),
                (basis_hbm, basis),
            ]
        )
    ]
    for copy in loading:
        copy.start()

    device = lax.axis_index("box")
    total = boxes * MEMBERS
    strides = boxes // MEMBERS
    depth = boxes // (2 * across)
    box, member = div(device, MEMBERS), rem(device, MEMBERS)
    x, z, y_half = div(box, 2 * depth), rem(div(box, 2), depth), rem(box, 2)
    y, core = div(member, 2), rem(member, 2)
    low = low_half((8, 128))
    half = jnp.where(low, 0, 1)

    top = jnp.where(y == 3, 1, 0)
    outer = jnp.where(y == 0, 1, top)
    side_to = jnp.where(outer == 1, top, y - 1)
    side_from = jnp.where(outer == 1, 1 - top, y - 1)
    far_half = jnp.where(outer == 1, 1 - y_half, y_half)
    z_core = rem(div(z, 2), 2)
    far_member = 2 * jnp.where(outer == 1, 3 - y, y) + z_core
    z_high = div(z, 4)
    far_x = [rem(x + dx, across) for dx in range(across)]
    far_steps = [(dx, turn) for dx in range(across) for turn in range(2)]

    def far_box(side, dx, turn):
        far_z = rem(side + z, 2) + 2 * core + 4 * (1 - z_high if turn else z_high)
        return (far_x[dx % across] * depth + far_z) * 2 + far_half

    far_to = [far_box(side_to, dx, turn) * MEMBERS + far_member for dx, turn in far_steps]
    far_from = [far_box(side_from, -dx, turn) for dx, turn in far_steps]
    alone = jnp.logical_and(jnp.logical_and(outer == 0, side_to == 0), core == z_core)

    barrier = pltpu.get_barrier_semaphore()

    def greet(target):
        pl.semaphore_signal(barrier, inc=1, device_id=(target,), device_id_type=MESH)

    far_order = sorted(range(1, strides), key=lambda k: abs(far_steps[k][0] - across // 2))
    place = 2 * y + z_core
    relay_z = [rem(side_to + z, 2) + 2 * core + 4 * high for high in (z_high, 1 - z_high)]
    to_relay = [((x * depth + at) * 2 + y_half) * MEMBERS + place for at in relay_z]
    sender_z = [rem(side_to + z, 2) + 2 * core + 4 * high for high in (z_high, 1 - z_high)]
    senders = [((x * depth + at) * 2 + y_half) * MEMBERS + place for at in sender_z]
    from_relay = [
        ((at * depth + z) * 2 + far_half) * MEMBERS + far_member - z_core + core for at in far_x
    ]
    own_sender = jnp.logical_and(side_to == 0, core == z_core)

    greet(to_relay[1])
    for dx in (2, 1, 3):
        greet(from_relay[dx])

    @pl.when(jnp.logical_not(own_sender))
    def _():
        greet(to_relay[0])

    @pl.when(outer == 1)
    def _():
        greet(from_relay[0])

    left_device = rem(device + total - 1, total)
    right_device = rem(device + 1, total)
    mirror = 2 * (3 - y) + core
    left_box = rem(box + boxes - 1, boxes) * MEMBERS + mirror
    right_box = rem(box + 1, boxes) * MEMBERS + mirror
    mates = [box * MEMBERS + rem(member + r, MEMBERS) for r in (6, 2, 7, 3, 5, 4, 1)]
    at_rim = outer == 1
    rim_box = rem(box + boxes + 2 * top - 1, boxes)
    rim_devices = [rim_box * MEMBERS + 6 - 6 * top + t for t in range(2)]
    quad = div(member, 4)
    quad_device = rem(box + boxes + 2 * quad - 1, boxes) * MEMBERS + mirror
    early = jnp.where(z == 0, 1, 0)
    for target in mates + [left_device, right_device, left_box, right_box]:
        greet(target)
    @pl.when(at_rim)
    def _():
        for target in rim_devices:
            greet(target)

    eighths = (lax.broadcasted_iota(jnp.int32, (1, 128), 1) & 63) * 8
    rows = lax.broadcasted_iota(jnp.int32, (512, 128), 0)
    every_eighth = (rows == eighths).astype(f32).astype(bf16)
    swapped = rows ^ 64
    eighth_swapped = (swapped == eighths).astype(f32).astype(bf16)
    picks = (lax.broadcasted_iota(jnp.int32, (1, 128), 1) & 63) * 2
    every_second = (
        (lax.broadcasted_iota(jnp.int32, (128, 128), 0) == picks).astype(f32).astype(bf16)
    )
    for copy in loading:
        copy.wait()
    points = jnp.concatenate([coords[...], jnp.zeros((5, OWN), f32)], axis=0)
    s0 = [
        jnp.concatenate(
            [points[:, 512 * p : 512 * p + 64], points[:, 512 * p + 256 : 512 * p + 320]], axis=1
        )
        for p in range(4)
    ]
    s3 = pick(jnp.concatenate(s0, axis=1), every_eighth)

    maps = [(map_high.at[level], map_low.at[level]) for level in range(6)]

    def set_map(level):
        once = transfer[level]
        map_high[level], map_low[level] = split(jnp.concatenate([once, once], axis=1))

    for level in range(3):
        set_map(level)
    slots = lax.broadcasted_iota(jnp.int32, (COLS, LEAF), 1)
    live = []
    for leaf in range(LEAVES):
        part = loads[:, leaf * LEAF : (leaf + 1) * LEAF].astype(f32)
        live.append(jnp.where(slots < occ[leaf], part, 0.0))
    c0 = []
    for p in range(4):
        two = jnp.concatenate([live[2 * p], live[2 * p + 1]], axis=0).astype(bf16)
        rows = lax.dot_general(
            two, basis[128 * p : 128 * p + 128, :], NT, preferred_element_type=f32
        )
        c0.append(jnp.where(low, rows[:8], rows[8:]))
    c1 = raise_coef(c0, maps[0])
    c2 = raise_coef(c1, maps[1])
    c3 = raise_coef(c2, maps[2])[0]

    g_buf[member] = jnp.where(half == core, c3, s3)

    def set_field():
        field[0, :, LEAF : LEAF + OWN] = points
        for leaf in range(LEAVES):
            field[1, :, (leaf + 1) * LEAF : (leaf + 2) * LEAF] = live[leaf]
        for at in range(0, OWN, 128):
            column[at : at + 128, :] = points[:, at : at + 128].T
        near[...] = jnp.zeros_like(near)

    def fill_tile(tile, row, col, width):
        sx = field[0, 0:1, pl.ds(col, width)]
        sy = field[0, 1:2, pl.ds(col, width)]
        sz = field[0, 2:3, pl.ds(col, width)]
        for at in range(0, LEAF, 16):
            rows = column[pl.ds(row + at, 16), :]
            tile[at : at + 16, 0:width] = phi(
                rows[:, 0:1], rows[:, 1:2], rows[:, 2:3], sx, sy, sz, near_scale
            ).astype(bf16)

    def near_leaf(tile, row):
        col = row + LEAF
        fill_tile(tile, row, col, 2 * LEAF)
        loads_two = field[1, :, pl.ds(col, 2 * LEAF)].astype(bf16)
        this = lax.dot_general(loads_two, tile[...], NT, preferred_element_type=f32)
        after = lax.dot_general(
            loads_two[:, :LEAF], tile[:, LEAF:], NN, preferred_element_type=f32
        )
        return this, after

    def near_two(row):
        first, second_part = near_leaf(tile_a, row)
        second, third = near_leaf(tile_b, row + LEAF)
        near[:, pl.ds(row, LEAF)] += first
        near[:, pl.ds(row + LEAF, LEAF)] += second_part + second
        near[:, pl.ds(row + 2 * LEAF, LEAF)] += third

    def near_step(pair, carry):
        near_two(pl.multiple_of(pair * (2 * LEAF), 2 * LEAF))
        return carry

    def side(block, at):
        lanes = jnp.where(low_half((1, 128)), 0, 1)
        return jnp.where(lanes == at, block, 0.0)

    def set_chain(levels, into):
        for at, (pairs, skels) in enumerate(levels):
            first = (1, 7, 11)[at]
            for p in range(len(pairs)):
                into[first + p, 0] = pairs[p]
                into[first + p, 1] = skels[p]

    def set_inner():
        lax.fori_loop(0, 3, near_step, 0)
        row = (LEAVES - 2) * LEAF
        this, after = near_leaf(tile_a, row)
        fill_tile(tile_c, row + LEAF, row + 2 * LEAF, LEAF)
        own = field[1, :, row + 2 * LEAF : row + 3 * LEAF].astype(bf16)
        after += lax.dot_general(own, tile_c[...], NT, preferred_element_type=f32)
        near[:, row : row + LEAF] += this
        near[:, row + LEAF : row + 2 * LEAF] += after
        for slot in (2, 3):
            local[slot - 1] = cousins(chain, slot)

    def set_edges():
        s1 = raise_skel(s0, every_second)
        s2 = raise_skel(s1, every_second)

        set_chain([(c0, s0), (c1, s1), (c2, s2)], chain)
        for at, (pairs, skels) in enumerate([(c0, s0), (c1, s1), (c2, s2)]):
            edge_send[0, at, 0] = pairs[-1]
            edge_send[0, at, 1] = skels[-1]
            edge_send[1, at, 0] = pairs[0]
            edge_send[1, at, 1] = skels[0]
    def set_paths():
        for level in range(3, 6):
            set_map(level)
        paths = lower(lower([transfer[5].T], maps[4]), maps[3])
        for p in range(4):
            path_map[p] = paths[p]
        both = jnp.concatenate(paths, axis=1)
        path_high[...], path_low[...] = split(jnp.concatenate([both, both], axis=0))

    def set_leaf_paths():
        from_six = side(path_map[y], core)
        rows = lax.broadcasted_iota(jnp.int32, (64, 128), 0)
        from_three = (rows == lax.broadcasted_iota(jnp.int32, (64, 128), 1)).astype(f32)
        x2 = mm(jnp.concatenate([from_six, from_three], axis=0), maps[2], NT)
        x0 = lower(lower([x2], maps[1]), maps[0])
        leaf_high[...], leaf_low[...] = split(jnp.concatenate(x0, axis=1))

    @pl.when(early == 1)
    def _():
        set_field()
        set_edges()
        set_paths()
        set_inner()

    pl.semaphore_wait(
        barrier, MEMBERS - 1 + 4 + 3 + outer + 2 - own_sender.astype(jnp.int32) + 2 * outer
    )

    def tell(target):
        pl.semaphore_signal(ready, inc=1, device_id=(target,), device_id_type=MESH)

    tell(senders[1])

    @pl.when(jnp.logical_not(own_sender))
    def _():
        tell(senders[0])

    def remote(src, dst, send_sem, recv_sem, target):
        return pltpu.make_async_remote_copy(
            src_ref=src,
            dst_ref=dst,
            send_sem=send_sem,
            recv_sem=recv_sem,
            device_id=(target,),
            device_id_type=MESH,
        )

    def send(*ends):
        copy = remote(*ends)
        copy.start()
        return copy

    def wait_all(ref, semaphore):
        pltpu.make_async_copy(ref, ref, semaphore).wait()

    for mate in mates:
        send(g_buf.at[member], g_buf.at[member], g_send_sem, g_recv_sem, mate)

    rim_copies = [
        pltpu.make_async_remote_copy(
            src_ref=g_buf.at[member],
            dst_ref=rim_recv.at[core],
            send_sem=rim_send_sem.at[t],
            recv_sem=rim_recv_sem.at[core],
            device_id=(rim_devices[t],),
            device_id_type=MESH,
        )
        for t in range(2)
    ]

    @pl.when(at_rim)
    def _():
        for copy in rim_copies:
            copy.start()

    @pl.when(early == 0)
    def _():
        set_field()

    last = LEAF * LEAVES
    near_copies = [
        send(
            field.at[:, :, last : last + LEAF],
            field.at[:, :, 0:LEAF],
            near_send_sem.at[0],
            near_recv_sem.at[0],
            right_device,
        ),
        send(
            field.at[:, :, LEAF : 2 * LEAF],
            field.at[:, :, last + LEAF : last + 2 * LEAF],
            near_send_sem.at[1],
            near_recv_sem.at[1],
            left_device,
        ),
    ]

    edge_copies = [
        remote(
            edge_send.at[side],
            edge_recv.at[side],
            edge_send_sem.at[side],
            edge_recv_sem.at[side],
            (right_device, left_device)[side],
        )
        for side in range(2)
    ]

    @pl.when(early == 0)
    def _():
        set_paths()
        set_edges()

    for copy in edge_copies:
        copy.start()

    @pl.when(early == 1)
    def _():
        set_leaf_paths()

    wait_all(g_buf.at[pl.ds(0, MEMBERS - 1)], g_recv_sem)
    c3s, s3s = [], []
    for p in range(4):
        even, odd = g_buf[2 * p], g_buf[2 * p + 1]
        c3s.append(jnp.where(low, even, odd))
        s3s.append(jnp.where(low, odd, even))
    c6 = mm(jnp.concatenate(c3s, axis=1), (path_high, path_low), NT)
    s6 = pick(jnp.concatenate(s3s, axis=1), eighth_swapped)
    far_send[0] = jnp.where(low, c6, s6)
    far_send[1] = jnp.where(low, s6, c6)

    @pl.when(alone)
    def _():
        far_buf[0] = far_send[0]

    pl.semaphore_wait(ready, 2 - own_sender.astype(jnp.int32))
    for k in far_order:
        send(
            far_send.at[k % 2], far_buf.at[k], far_send_sem.at[1], far_recv_sem.at[1], far_to[k]
        )
    first_far = pltpu.make_async_remote_copy(
        src_ref=far_send.at[0],
        dst_ref=far_buf.at[0],
        send_sem=far_send_sem.at[0],
        recv_sem=far_recv_sem.at[0],
        device_id=(far_to[0],),
        device_id_type=MESH,
    )

    @pl.when(jnp.logical_not(alone))
    def _():
        first_far.start()

    s3s = [pltpu.roll(skel, 64, 1) for skel in s3s]
    c4s, s4s = raise_coef(c3s, maps[3]), raise_skel(s3s, every_second)
    c5s, s5s = raise_coef(c4s, maps[4]), raise_skel(s4s, every_second)
    set_chain([(c3s, s3s), (c4s, s4s), (c5s, s5s)], g_chain)
    for at in range(2):
        bound_send[at, 0] = c5s[0]
        bound_send[at, 1] = s5s[0] + pltpu.roll(s4s[1 - at], 3, 0)
    bound_copies = [
        send(
            bound_send.at[side],
            bound_recv.at[side],
            bound_send_sem.at[side],
            bound_recv_sem.at[side],
            (right_box, left_box)[side],
        )
        for side in range(2)
    ]
    bound_copies.append(
        send(
            g_chain.at[7 + quad, 0],
            quad_recv,
            bound_send_sem.at[2],
            bound_recv_sem.at[2],
            quad_device,
        )
    )

    @pl.when(early == 0)
    def _():
        set_inner()
        set_leaf_paths()

    for copy in near_copies:
        copy.wait_recv()

    @pl.when(device == 0)
    def _():
        field[1, :, 0:LEAF] = jnp.zeros((COLS, LEAF), f32)

    @pl.when(device == total - 1)
    def _():
        field[1, :, last + LEAF : last + 2 * LEAF] = jnp.zeros((COLS, LEAF), f32)

    def near_end(tile, row, col):
        fill_tile(tile, row, col, LEAF)
        near[:, row : row + LEAF] += lax.dot_general(
            field[1, :, col : col + LEAF].astype(bf16),
            tile[:, 0:LEAF],
            NT,
            preferred_element_type=f32,
        )

    near_end(tile_c, 0, 0)
    near_end(tile_a, last - LEAF, last + LEAF)

    def set_ends(ends, into, at_start, at_end):
        for level in range(3):
            before, after = (0, 6, 10)[level], (5, 9, 12)[level]
            into[before, 0] = jnp.where(at_start, 0.0, ends[0, level, 0])
            into[before, 1] = ends[0, level, 1]
            into[after, 0] = jnp.where(at_end, 0.0, ends[1, level, 0])
            into[after, 1] = ends[1, level, 1]

    for copy in edge_copies:
        copy.wait_recv()
    set_ends(edge_recv, chain, device == 0, device == total - 1)
    for at, slot in [(0, 1), (3, 4), (4, 7), (5, 8), (6, 11)]:
        local[at] = cousins(chain, slot)

    top_column = s6.T[:64]
    tx, ty, tz = top_column[:, 0:1], top_column[:, 1:2], top_column[:, 2:3]

    wait_all(far_buf.at[pl.ds(1, strides - 1)], far_recv_sem.at[1])

    @pl.when(jnp.logical_not(alone))
    def _():
        first_far.wait_recv()

    top_coef, top_skel = [], []
    for k in range(0, strides, 2):
        halves = []
        for at in (k, k + 1):
            apart = far_from[at] - box
            counts = jnp.logical_or(apart >= 2, apart <= -2)
            halves.append((far_buf[at], counts))
        (one, one_counts), (two, two_counts) = halves
        coef = jnp.where(low, jnp.where(one_counts, one, 0.0), jnp.where(two_counts, two, 0.0))
        top_coef.append(pltpu.roll(coef, 64, 1))
        top_skel.append(jnp.where(low, two, one))
    top_tile = jnp.concatenate(
        [phi(tx, ty, tz, s[0:1], s[1:2], s[2:3], far_scale) for s in top_skel], axis=1
    )
    top = mm(jnp.concatenate(top_coef, axis=1), split(top_tile), NT)
    part_buf[member] = jnp.concatenate([top, jnp.zeros((8, 64), f32)], axis=1)
    for mate in mates:
        send(part_buf.at[member], part_buf.at[member], part_send_sem, part_recv_sem, mate)

    wait_all(g_buf.at[pl.ds(0, MEMBERS - 1)], g_send_sem)
    wait_all(far_buf.at[pl.ds(1, strides - 1)], far_send_sem.at[1])
    for copy in near_copies + edge_copies + bound_copies:
        copy.wait_send()

    @pl.when(jnp.logical_not(alone))
    def _():
        first_far.wait_send()

    for copy in bound_copies:
        copy.wait_recv()
    at_start, at_end = box == 0, box == boxes - 1
    outside = jnp.logical_or(
        jnp.logical_and(quad == 0, at_start), jnp.logical_and(quad == 1, at_end)
    )
    start_skel, end_skel = bound_recv[0, 1], bound_recv[1, 1]
    g_chain[10, 0] = jnp.where(at_start, 0.0, bound_recv[0, 0])
    g_chain[10, 1] = start_skel
    g_chain[12, 0] = jnp.where(at_end, 0.0, bound_recv[1, 0])
    g_chain[12, 1] = end_skel
    quad_coef = jnp.where(outside, 0.0, quad_recv[...])
    g_chain[6, 0] = quad_coef
    g_chain[6, 1] = pltpu.roll(start_skel, 5, 0)
    g_chain[9, 0] = quad_coef
    g_chain[9, 1] = pltpu.roll(end_skel, 5, 0)

    @pl.when(at_rim)
    def _():
        for copy in rim_copies:
            copy.wait_send()
        for t in range(2):
            pltpu.make_async_remote_copy(
                src_ref=g_buf.at[member],
                dst_ref=rim_recv.at[t],
                send_sem=rim_send_sem.at[t],
                recv_sem=rim_recv_sem.at[t],
                device_id=(rim_devices[t],),
                device_id_type=MESH,
            ).wait_recv()
        even, odd = rim_recv[0], rim_recv[1]
        rim_coef = jnp.where(outside, 0.0, jnp.where(low, even, odd))
        rim_skel = pltpu.roll(jnp.where(low, odd, even), 64, 1)
        for slot in (0, 5):
            g_chain[slot, 0] = rim_coef
            g_chain[slot, 1] = rim_skel

    local3 = cousins(g_chain, 1 + y)
    local4 = cousins(g_chain, 7 + quad)
    local5 = cousins(g_chain, 11)
    y2 = local[6]
    y1 = [x + local[4 + at] for at, x in enumerate(lower([y2], maps[1]))]
    y0 = [x + local[at] for at, x in enumerate(lower(y1, maps[0]))]
    y4 = local4 + mm(side(local5, quad), maps[4], NT)
    y3 = local3 + mm(side(y4, rem(y, 2)), maps[3], NT)
    y3 = jnp.where(core == 1, y3, pltpu.roll(y3, 64, 1))

    wait_all(part_buf.at[pl.ds(0, MEMBERS - 1)], part_recv_sem)
    d6 = part_buf[0]
    for at in range(1, MEMBERS):
        d6 = d6 + part_buf[at]
    d63 = jnp.where(low, d6, y3)
    d0 = jnp.concatenate(y0, axis=1) + mm(d63, (leaf_high, leaf_low), NN)
    for p in range(4):
        pair = d0[:, 128 * p : 128 * p + 128]
        two = jnp.concatenate([jnp.where(low, pair, 0.0), jnp.where(low, 0.0, pair)], axis=0)
        rows = lax.dot_general(
            two.astype(bf16),
            basis[128 * p : 128 * p + 128, :],
            NN,
            preferred_element_type=f32,
        )
        for t in range(2):
            leaf = 2 * p + t
            at = leaf * LEAF
            out_ref[:, at : at + LEAF] = jnp.where(
                slots < occ[leaf], near[:, at : at + LEAF] + rows[8 * t : 8 * t + 8], 0.0
            )

    wait_all(part_buf.at[pl.ds(0, MEMBERS - 1)], part_send_sem)


def body(boxes, across, coords, loads, occupancy, basis, transfer):
    strides = boxes // MEMBERS
    hbm = pl.BlockSpec(memory_space=pl.ANY)
    dma = pltpu.SemaphoreType.DMA
    return pl.pallas_call(
        functools.partial(kernel, boxes, across),
        out_shape=jax.ShapeDtypeStruct((COLS, OWN), f32),
        in_specs=[hbm] * 5,
        out_specs=pl.BlockSpec(memory_space=pltpu.VMEM),
        scratch_shapes=[
            pltpu.VMEM((3, OWN), f32),
            pltpu.VMEM((COLS, OWN), bf16),
            pltpu.SMEM((LEAVES,), jnp.int32),
            pltpu.VMEM((LEAVES * 64, LEAF), bf16),
            pltpu.VMEM((6, 128, 64), f32),
            pltpu.VMEM((6, 128, 128), bf16),
            pltpu.VMEM((6, 128, 128), bf16),
            pltpu.VMEM((4, 64, 128), f32),
            pltpu.VMEM((128, 512), bf16),
            pltpu.VMEM((128, 512), bf16),
            pltpu.VMEM((2, 8, OWN + 2 * LEAF), f32),
            pltpu.VMEM((OWN, 8), f32),
            pltpu.VMEM((128, 512), bf16),
            pltpu.VMEM((128, 512), bf16),
            pltpu.VMEM((COLS, OWN + LEAF), f32),
            pltpu.VMEM((LEAF, 2 * LEAF), bf16),
            pltpu.VMEM((LEAF, 2 * LEAF), bf16),
            pltpu.VMEM((LEAF, LEAF), bf16),
            pltpu.VMEM((13, 2, 8, 128), f32),
            pltpu.VMEM((13, 2, 8, 128), f32),
            pltpu.VMEM((7, 8, 128), f32),
            pltpu.VMEM((2, 3, 2, 8, 128), f32),
            pltpu.VMEM((2, 3, 2, 8, 128), f32),
            pltpu.VMEM((MEMBERS, 8, 128), f32),
            pltpu.VMEM((2, 2, 8, 128), f32),
            pltpu.VMEM((2, 2, 8, 128), f32),
            pltpu.VMEM((8, 128), f32),
            pltpu.VMEM((2, 8, 128), f32),
            pltpu.VMEM((2, 8, 128), f32),
            pltpu.VMEM((strides, 8, 128), f32),
            pltpu.VMEM((MEMBERS, 8, 128), f32),
            dma((5,)),
            dma((2,)),
            dma((2,)),
            dma((2,)),
            dma((2,)),
            dma,
            dma,
            dma((3,)),
            dma((3,)),
            dma((2,)),
            dma((2,)),
            dma((2,)),
            dma((2,)),
            dma,
            dma,
            pltpu.SemaphoreType.REGULAR,
        ],
        compiler_params=pltpu.CompilerParams(
            collective_id=0, has_side_effects=True, vmem_limit_bytes=32 * 1024 * 1024
        ),
    )(
        *[
            pltpu.with_memory_space_constraint(x, pltpu.HBM)
            for x in (
                coords,
                loads,
                occupancy,
                basis.reshape(LEAVES * 64, LEAF),
                transfer.reshape(6, 128, 64),
            )
        ]
    )


def solution(mesh):
    boxes = mesh.shape["box"] // MEMBERS
    return jax.shard_map(
        functools.partial(body, boxes, 4),
        mesh=mesh,
        in_specs=(P(None, "box"), P(None, "box"), P("box"), P("box", None, None), P()),
        out_specs=P(None, "box"),
        check_vma=False,
    )
```

```python
import functools

import jax
import jax.numpy as jnp
from jax import lax
from jax.experimental import pallas as pl
from jax.experimental.pallas import tpu as pltpu
from jax.sharding import PartitionSpec as P

LEAF = 256
COLS = 8
LEAVES = 8
MEMBERS = 8
OWN = LEAF * LEAVES

f32 = jnp.float32
bf16 = jnp.bfloat16
soften = 0.0001
near_scale = 0.0625
far_scale = 0.125
NN = (((1,), (0,)), ((), ()))
NT = (((1,), (1,)), ((), ()))
MESH = pl.DeviceIdType.MESH


def div(a, b):
    return lax.div(a, jnp.int32(b))


def rem(a, b):
    return lax.rem(a, jnp.int32(b))


def phi(tx, ty, tz, sx, sy, sz, scale):
    dx = tx - sx
    dy = ty - sy
    dz = tz - sz
    r2 = dx * dx + dy * dy + dz * dz
    return (r2 * (0.5 * scale)) * jnp.log(r2 + soften)


def split(x):
    high = x.astype(bf16)
    return high, (x - high.astype(f32)).astype(bf16)


def mm(a, b, dims):
    rows = a.shape[0]
    high = a.astype(bf16).astype(f32)
    stacked = jnp.concatenate([high, a - high], axis=0).astype(bf16)
    both = lax.dot_general(stacked, b[0][...], dims, preferred_element_type=f32)
    low = lax.dot_general(stacked[:rows], b[1][...], dims, preferred_element_type=f32)
    return both[:rows] + (both[rows:] + low)


def low_half(shape):
    return lax.broadcasted_iota(jnp.int32, shape, len(shape) - 1) < 64


def merge(rows):
    count = rows.shape[0] // 16
    low = low_half((8, 128))
    return [
        jnp.where(low, rows[16 * i : 16 * i + 8], rows[16 * i + 8 : 16 * i + 16])
        for i in range(count)
    ]


def raise_coef(pairs, level_map):
    rows = mm(jnp.concatenate(pairs, axis=0), level_map, NN)
    return merge(rows) if len(pairs) > 1 else [rows]


def pick(x, entries):
    rows = x.shape[0]
    a = x.astype(bf16).astype(f32)
    b = (x - a).astype(bf16).astype(f32)
    c = (x - a) - b
    stacked = jnp.concatenate([a, b, c], axis=0).astype(bf16)
    picked = lax.dot_general(stacked, entries, NN, preferred_element_type=f32)
    return picked[:rows] + picked[rows : 2 * rows] + picked[2 * rows :]


def raise_skel(pairs, every_second):
    rows_up = pick(jnp.concatenate(pairs, axis=0), every_second)
    return merge(rows_up) if len(pairs) > 1 else [rows_up]


def cousins(chain, slot):
    low = low_half((8, 128))
    column = chain[slot, 1].T
    tx, ty, tz = column[:, 0:1], column[:, 1:2], column[:, 2:3]
    before, after = chain[slot - 1, 0], chain[slot + 1, 0]
    tiles = []
    for skel in (chain[slot - 1, 1], chain[slot + 1, 1]):
        tiles.append(phi(tx, ty, tz, skel[0:1], skel[1:2], skel[2:3], far_scale))
    tile = jnp.concatenate(tiles, axis=1)
    even = jnp.concatenate([jnp.where(low, before, 0.0), after], axis=1)
    odd = jnp.concatenate([before, jnp.where(low, 0.0, after)], axis=1)
    rows = mm(jnp.concatenate([even, odd], axis=0), split(tile), NT)
    return jnp.where(low, rows[:8], rows[8:])


def lower(pairs, level_map):
    height = pairs[0].shape[0]
    low = low_half((height, 128))
    stacked = []
    for pair in pairs:
        stacked += [jnp.where(low, pair, 0.0), jnp.where(low, 0.0, pair)]
    rows = mm(jnp.concatenate(stacked, axis=0), level_map, NT)
    return [rows[height * i : height * (i + 1)] for i in range(2 * len(pairs))]


def kernel(
    boxes,
    across,
    coords_hbm,
    loads_hbm,
    occ_hbm,
    basis_hbm,
    transfer_hbm,
    out_ref,
    coords,
    loads,
    occ,
    basis,
    transfer,
    map_high,
    map_low,
    path_map,
    field,
    column,
    leaf_high,
    leaf_low,
    near,
    tile_a,
    tile_b,
    tile_c,
    chain,
    g_chain,
    local,
    edge_send,
    edge_recv,
    u_buf,
    g_buf,
    bound_send,
    bound_recv,
    quad_recv,
    rim_recv,
    far_send,
    far_buf,
    part_buf,
    load_sem,
    near_send_sem,
    near_recv_sem,
    edge_send_sem,
    edge_recv_sem,
    u_send_sem,
    u_recv_sem,
    g_send_sem,
    g_recv_sem,
    bound_send_sem,
    bound_recv_sem,
    rim_send_sem,
    rim_recv_sem,
    far_send_sem,
    far_recv_sem,
    part_send_sem,
    part_recv_sem,
    ready,
):
    loading = [
        pltpu.make_async_copy(src, dst, load_sem.at[at])
        for at, (src, dst) in enumerate(
            [
                (coords_hbm, coords),
                (transfer_hbm, transfer),
                (loads_hbm, loads),
                (occ_hbm, occ),
                (basis_hbm, basis),
            ]
        )
    ]
    for copy in loading:
        copy.start()

    device = lax.axis_index("box")
    total = boxes * MEMBERS
    strides = boxes // MEMBERS
    depth = boxes // (2 * across)
    box, member = div(device, MEMBERS), rem(device, MEMBERS)
    x, z, y_half = div(box, 2 * depth), rem(div(box, 2), depth), rem(box, 2)
    y, core = div(member, 2), rem(member, 2)
    low = low_half((8, 128))
    half = jnp.where(low, 0, 1)

    top = jnp.where(y == 3, 1, 0)
    outer = jnp.where(y == 0, 1, top)
    side_to = jnp.where(outer == 1, top, y - 1)
    side_from = jnp.where(outer == 1, 1 - top, y - 1)
    far_half = jnp.where(outer == 1, 1 - y_half, y_half)
    z_core = rem(div(z, 2), 2)
    far_member = 2 * jnp.where(outer == 1, 3 - y, y) + z_core
    z_high = div(z, 4)
    far_x = [rem(x + dx, across) for dx in range(across)]
    far_steps = [(dx, turn) for dx in range(across) for turn in range(2)]

    def far_box(side, dx, turn):
        far_z = rem(side + z, 2) + 2 * core + 4 * (1 - z_high if turn else z_high)
        return (far_x[dx % across] * depth + far_z) * 2 + far_half

    far_to = [far_box(side_to, dx, turn) * MEMBERS + far_member for dx, turn in far_steps]
    far_from = [far_box(side_from, -dx, turn) for dx, turn in far_steps]
    alone = jnp.logical_and(jnp.logical_and(outer == 0, side_to == 0), core == z_core)

    barrier = pltpu.get_barrier_semaphore()

    def greet(target):
        pl.semaphore_signal(barrier, inc=1, device_id=(target,), device_id_type=MESH)

    far_order = sorted(range(1, strides), key=lambda k: abs(far_steps[k][0] - across // 2))
    place = 2 * y + z_core
    relay_z = [rem(side_to + z, 2) + 2 * core + 4 * high for high in (z_high, 1 - z_high)]
    to_relay = [((x * depth + at) * 2 + y_half) * MEMBERS + place for at in relay_z]
    sender_z = [rem(side_to + z, 2) + 2 * core + 4 * high for high in (z_high, 1 - z_high)]
    senders = [((x * depth + at) * 2 + y_half) * MEMBERS + place for at in sender_z]
    from_relay = [
        ((at * depth + z) * 2 + far_half) * MEMBERS + far_member - z_core + core for at in far_x
    ]
    own_sender = jnp.logical_and(side_to == 0, core == z_core)

    greet(to_relay[1])
    for dx in (2, 1, 3):
        greet(from_relay[dx])

    @pl.when(jnp.logical_not(own_sender))
    def _():
        greet(to_relay[0])

    @pl.when(outer == 1)
    def _():
        greet(from_relay[0])

    left_device = rem(device + total - 1, total)
    right_device = rem(device + 1, total)
    mirror = 2 * (3 - y) + core
    left_box = rem(box + boxes - 1, boxes) * MEMBERS + mirror
    right_box = rem(box + 1, boxes) * MEMBERS + mirror
    mates = [box * MEMBERS + rem(member + r, MEMBERS) for r in (6, 2, 7, 3, 5, 4, 1)]
    at_rim = outer == 1
    rim_box = rem(box + boxes + 2 * top - 1, boxes)
    rim_devices = [rim_box * MEMBERS + 6 - 6 * top + t for t in range(2)]
    quad = div(member, 4)
    quad_device = rem(box + boxes + 2 * quad - 1, boxes) * MEMBERS + mirror
    early = jnp.where(z == 0, 1, 0)
    for target in mates + [left_device, right_device, left_box, right_box]:
        greet(target)
    @pl.when(at_rim)
    def _():
        for target in rim_devices:
            greet(target)

    lanes = lax.broadcasted_iota(jnp.int32, (1, 128), 1)
    index = lax.broadcasted_iota(jnp.int32, (512, 128), 0)
    placed = (index == (lanes - 64 - 8 * member) * 64).astype(f32).astype(bf16)
    picks = (lax.broadcasted_iota(jnp.int32, (1, 128), 1) & 63) * 2
    every_second = (
        (lax.broadcasted_iota(jnp.int32, (128, 128), 0) == picks).astype(f32).astype(bf16)
    )
    for copy in loading:
        copy.wait()
    points = jnp.concatenate([coords[...], jnp.zeros((5, OWN), f32)], axis=0)
    s0 = [
        jnp.concatenate(
            [points[:, 512 * p : 512 * p + 64], points[:, 512 * p + 256 : 512 * p + 320]], axis=1
        )
        for p in range(4)
    ]
    s6 = pick(jnp.concatenate(s0, axis=1), placed)

    maps = [(map_high.at[level], map_low.at[level]) for level in range(6)]

    def set_map(level):
        once = transfer[level]
        map_high[level], map_low[level] = split(jnp.concatenate([once, once], axis=1))

    for level in range(2):
        set_map(level)
    slots = lax.broadcasted_iota(jnp.int32, (COLS, LEAF), 1)
    live = []
    for leaf in range(LEAVES):
        part = loads[:, leaf * LEAF : (leaf + 1) * LEAF].astype(f32)
        live.append(jnp.where(slots < occ[leaf], part, 0.0))
    c0 = []
    for p in range(4):
        two = jnp.concatenate([live[2 * p], live[2 * p + 1]], axis=0).astype(bf16)
        rows = lax.dot_general(
            two, basis[128 * p : 128 * p + 128, :], NT, preferred_element_type=f32
        )
        c0.append(jnp.where(low, rows[:8], rows[8:]))
    c1 = raise_coef(c0, maps[0])
    c2 = raise_coef(c1, maps[1])
    def factor(level, at):
        return transfer[level, pl.ds(pl.multiple_of(64 * at, 64), 64), :]

    map_34 = mm(transfer[2], split(factor(3, core)), NN)
    wide = jnp.concatenate([factor(5, quad), jnp.zeros((64, 64), f32)], axis=1)
    map_56 = mm(factor(4, rem(y, 2)), split(wide), NN)
    map_6 = mm(map_34, split(map_56), NN)
    u_buf[member] = mm(c2[0], split(map_6), NN) + s6
    path_map[...] = map_6

    def set_field():
        field[0, :, LEAF : LEAF + OWN] = points
        for leaf in range(LEAVES):
            field[1, :, (leaf + 1) * LEAF : (leaf + 2) * LEAF] = live[leaf]
        for at in range(0, OWN, 128):
            column[at : at + 128, :] = points[:, at : at + 128].T
        near[...] = jnp.zeros_like(near)

    def fill_tile(tile, row, col, width):
        sx = field[0, 0:1, pl.ds(col, width)]
        sy = field[0, 1:2, pl.ds(col, width)]
        sz = field[0, 2:3, pl.ds(col, width)]
        for at in range(0, LEAF, 16):
            rows = column[pl.ds(row + at, 16), :]
            tile[at : at + 16, 0:width] = phi(
                rows[:, 0:1], rows[:, 1:2], rows[:, 2:3], sx, sy, sz, near_scale
            ).astype(bf16)

    def near_leaf(tile, row):
        col = row + LEAF
        fill_tile(tile, row, col, 2 * LEAF)
        loads_two = field[1, :, pl.ds(col, 2 * LEAF)].astype(bf16)
        this = lax.dot_general(loads_two, tile[...], NT, preferred_element_type=f32)
        after = lax.dot_general(
            loads_two[:, :LEAF], tile[:, LEAF:], NN, preferred_element_type=f32
        )
        return this, after

    def near_two(row):
        first, second_part = near_leaf(tile_a, row)
        second, third = near_leaf(tile_b, row + LEAF)
        near[:, pl.ds(row, LEAF)] += first
        near[:, pl.ds(row + LEAF, LEAF)] += second_part + second
        near[:, pl.ds(row + 2 * LEAF, LEAF)] += third

    def near_step(pair, carry):
        near_two(pl.multiple_of(pair * (2 * LEAF), 2 * LEAF))
        return carry

    def side(block, at):
        lanes = jnp.where(low_half((1, 128)), 0, 1)
        return jnp.where(lanes == at, block, 0.0)

    def set_chain(levels, into):
        for at, (pairs, skels) in enumerate(levels):
            first = (1, 7, 11)[at]
            for p in range(len(pairs)):
                into[first + p, 0] = pairs[p]
                into[first + p, 1] = skels[p]

    def set_inner():
        lax.fori_loop(0, 3, near_step, 0)
        row = (LEAVES - 2) * LEAF
        this, after = near_leaf(tile_a, row)
        fill_tile(tile_c, row + LEAF, row + 2 * LEAF, LEAF)
        own = field[1, :, row + 2 * LEAF : row + 3 * LEAF].astype(bf16)
        after += lax.dot_general(own, tile_c[...], NT, preferred_element_type=f32)
        near[:, row : row + LEAF] += this
        near[:, row + LEAF : row + 2 * LEAF] += after
        for slot in (2, 3):
            local[slot - 1] = cousins(chain, slot)

    def set_edges():
        s1 = raise_skel(s0, every_second)
        s2 = raise_skel(s1, every_second)

        set_chain([(c0, s0), (c1, s1), (c2, s2)], chain)
        for at, (pairs, skels) in enumerate([(c0, s0), (c1, s1), (c2, s2)]):
            edge_send[0, at, 0] = pairs[-1]
            edge_send[0, at, 1] = skels[-1]
            edge_send[1, at, 0] = pairs[0]
            edge_send[1, at, 1] = skels[0]
    def set_leaf_paths():
        x2 = jnp.concatenate([path_map[...].T[:64], transfer[2].T], axis=0)
        x0 = lower(lower([x2], maps[1]), maps[0])
        leaf_high[...], leaf_low[...] = split(jnp.concatenate(x0, axis=1))

    @pl.when(early == 1)
    def _():
        set_field()
        set_edges()
        set_inner()

    pl.semaphore_wait(
        barrier, MEMBERS - 1 + 4 + 3 + outer + 2 - own_sender.astype(jnp.int32) + 2 * outer
    )

    def tell(target):
        pl.semaphore_signal(ready, inc=1, device_id=(target,), device_id_type=MESH)

    tell(senders[1])

    @pl.when(jnp.logical_not(own_sender))
    def _():
        tell(senders[0])

    def remote(src, dst, send_sem, recv_sem, target):
        return pltpu.make_async_remote_copy(
            src_ref=src,
            dst_ref=dst,
            send_sem=send_sem,
            recv_sem=recv_sem,
            device_id=(target,),
            device_id_type=MESH,
        )

    def send(*ends):
        copy = remote(*ends)
        copy.start()
        return copy

    def wait_all(ref, semaphore):
        pltpu.make_async_copy(ref, ref, semaphore).wait()

    for mate in mates:
        send(u_buf.at[member], u_buf.at[member], u_send_sem, u_recv_sem, mate)

    set_map(2)
    every_eighth = (index == (lanes & 63) * 8).astype(f32).astype(bf16)
    s3 = pick(jnp.concatenate(s0, axis=1), every_eighth)
    c3 = raise_coef(c2, maps[2])[0]
    g_buf[member] = jnp.where(half == core, c3, s3)
    for mate in mates:
        send(g_buf.at[member], g_buf.at[member], g_send_sem, g_recv_sem, mate)

    rim_copies = [
        pltpu.make_async_remote_copy(
            src_ref=g_buf.at[member],
            dst_ref=rim_recv.at[core],
            send_sem=rim_send_sem.at[t],
            recv_sem=rim_recv_sem.at[core],
            device_id=(rim_devices[t],),
            device_id_type=MESH,
        )
        for t in range(2)
    ]

    @pl.when(at_rim)
    def _():
        for copy in rim_copies:
            copy.start()

    @pl.when(early == 0)
    def _():
        set_field()

    last = LEAF * LEAVES
    near_copies = [
        send(
            field.at[:, :, last : last + LEAF],
            field.at[:, :, 0:LEAF],
            near_send_sem.at[0],
            near_recv_sem.at[0],
            right_device,
        ),
        send(
            field.at[:, :, LEAF : 2 * LEAF],
            field.at[:, :, last + LEAF : last + 2 * LEAF],
            near_send_sem.at[1],
            near_recv_sem.at[1],
            left_device,
        ),
    ]

    edge_copies = [
        remote(
            edge_send.at[side],
            edge_recv.at[side],
            edge_send_sem.at[side],
            edge_recv_sem.at[side],
            (right_device, left_device)[side],
        )
        for side in range(2)
    ]

    @pl.when(early == 0)
    def _():
        set_edges()

    for copy in edge_copies:
        copy.start()

    set_map(3)
    set_map(4)

    @pl.when(early == 1)
    def _():
        set_leaf_paths()

    wait_all(u_buf.at[pl.ds(0, MEMBERS - 1)], u_recv_sem)
    parts = [u_buf[at] for at in range(MEMBERS)]
    while len(parts) > 1:
        parts = [a + b for a, b in zip(parts[0::2], parts[1::2])]
    top_record = parts[0]
    swapped_record = pltpu.roll(top_record, 64, 1)
    far_send[0] = top_record
    far_send[1] = swapped_record

    @pl.when(alone)
    def _():
        far_buf[0] = far_send[0]

    pl.semaphore_wait(ready, 2 - own_sender.astype(jnp.int32))
    for k in far_order:
        send(
            far_send.at[k % 2], far_buf.at[k], far_send_sem.at[1], far_recv_sem.at[1], far_to[k]
        )
    first_far = pltpu.make_async_remote_copy(
        src_ref=far_send.at[0],
        dst_ref=far_buf.at[0],
        send_sem=far_send_sem.at[0],
        recv_sem=far_recv_sem.at[0],
        device_id=(far_to[0],),
        device_id_type=MESH,
    )

    @pl.when(jnp.logical_not(alone))
    def _():
        first_far.start()

    wait_all(g_buf.at[pl.ds(0, MEMBERS - 1)], g_recv_sem)
    c3s, s3s = [], []
    for p in range(4):
        even, odd = g_buf[2 * p], g_buf[2 * p + 1]
        c3s.append(jnp.where(low, even, odd))
        s3s.append(pltpu.roll(jnp.where(low, odd, even), 64, 1))
    c4s, s4s = raise_coef(c3s, maps[3]), raise_skel(s3s, every_second)
    c5s, s5s = raise_coef(c4s, maps[4]), raise_skel(s4s, every_second)
    set_chain([(c3s, s3s), (c4s, s4s), (c5s, s5s)], g_chain)
    for at in range(2):
        bound_send[at, 0] = c5s[0]
        bound_send[at, 1] = s5s[0] + pltpu.roll(s4s[1 - at], 3, 0)
    bound_copies = [
        send(
            bound_send.at[side],
            bound_recv.at[side],
            bound_send_sem.at[side],
            bound_recv_sem.at[side],
            (right_box, left_box)[side],
        )
        for side in range(2)
    ]
    bound_copies.append(
        send(
            g_chain.at[7 + quad, 0],
            quad_recv,
            bound_send_sem.at[2],
            bound_recv_sem.at[2],
            quad_device,
        )
    )

    @pl.when(early == 0)
    def _():
        set_inner()
        set_leaf_paths()

    for copy in near_copies:
        copy.wait_recv()

    @pl.when(device == 0)
    def _():
        field[1, :, 0:LEAF] = jnp.zeros((COLS, LEAF), f32)

    @pl.when(device == total - 1)
    def _():
        field[1, :, last + LEAF : last + 2 * LEAF] = jnp.zeros((COLS, LEAF), f32)

    def near_end(tile, row, col):
        fill_tile(tile, row, col, LEAF)
        near[:, row : row + LEAF] += lax.dot_general(
            field[1, :, col : col + LEAF].astype(bf16),
            tile[:, 0:LEAF],
            NT,
            preferred_element_type=f32,
        )

    near_end(tile_c, 0, 0)
    near_end(tile_a, last - LEAF, last + LEAF)

    def set_ends(ends, into, at_start, at_end):
        for level in range(3):
            before, after = (0, 6, 10)[level], (5, 9, 12)[level]
            into[before, 0] = jnp.where(at_start, 0.0, ends[0, level, 0])
            into[before, 1] = ends[0, level, 1]
            into[after, 0] = jnp.where(at_end, 0.0, ends[1, level, 0])
            into[after, 1] = ends[1, level, 1]

    for copy in edge_copies:
        copy.wait_recv()
    set_ends(edge_recv, chain, device == 0, device == total - 1)
    for at, slot in [(0, 1), (3, 4), (4, 7), (5, 8), (6, 11)]:
        local[at] = cousins(chain, slot)

    top_column = swapped_record.T[:64]
    tx, ty, tz = top_column[:, 0:1], top_column[:, 1:2], top_column[:, 2:3]

    wait_all(far_buf.at[pl.ds(1, strides - 1)], far_recv_sem.at[1])

    @pl.when(jnp.logical_not(alone))
    def _():
        first_far.wait_recv()

    top_coef, top_skel = [], []
    for k in range(0, strides, 2):
        halves = []
        for at in (k, k + 1):
            apart = far_from[at] - box
            counts = jnp.logical_or(apart >= 2, apart <= -2)
            halves.append((far_buf[at], counts))
        (one, one_counts), (two, two_counts) = halves
        coef = jnp.where(low, jnp.where(one_counts, one, 0.0), jnp.where(two_counts, two, 0.0))
        top_coef.append(pltpu.roll(coef, 64, 1))
        top_skel.append(jnp.where(low, two, one))
    top_tile = jnp.concatenate(
        [phi(tx, ty, tz, s[0:1], s[1:2], s[2:3], far_scale) for s in top_skel], axis=1
    )
    top = mm(jnp.concatenate(top_coef, axis=1), split(top_tile), NT)
    part_buf[member] = jnp.concatenate([top, jnp.zeros((8, 64), f32)], axis=1)
    for mate in mates:
        send(part_buf.at[member], part_buf.at[member], part_send_sem, part_recv_sem, mate)

    wait_all(u_buf.at[pl.ds(0, MEMBERS - 1)], u_send_sem)
    wait_all(g_buf.at[pl.ds(0, MEMBERS - 1)], g_send_sem)
    wait_all(far_buf.at[pl.ds(1, strides - 1)], far_send_sem.at[1])
    for copy in near_copies + edge_copies + bound_copies:
        copy.wait_send()

    @pl.when(jnp.logical_not(alone))
    def _():
        first_far.wait_send()

    for copy in bound_copies:
        copy.wait_recv()
    at_start, at_end = box == 0, box == boxes - 1
    outside = jnp.logical_or(
        jnp.logical_and(quad == 0, at_start), jnp.logical_and(quad == 1, at_end)
    )
    start_skel, end_skel = bound_recv[0, 1], bound_recv[1, 1]
    g_chain[10, 0] = jnp.where(at_start, 0.0, bound_recv[0, 0])
    g_chain[10, 1] = start_skel
    g_chain[12, 0] = jnp.where(at_end, 0.0, bound_recv[1, 0])
    g_chain[12, 1] = end_skel
    quad_coef = jnp.where(outside, 0.0, quad_recv[...])
    g_chain[6, 0] = quad_coef
    g_chain[6, 1] = pltpu.roll(start_skel, 5, 0)
    g_chain[9, 0] = quad_coef
    g_chain[9, 1] = pltpu.roll(end_skel, 5, 0)

    @pl.when(at_rim)
    def _():
        for copy in rim_copies:
            copy.wait_send()
        for t in range(2):
            pltpu.make_async_remote_copy(
                src_ref=g_buf.at[member],
                dst_ref=rim_recv.at[t],
                send_sem=rim_send_sem.at[t],
                recv_sem=rim_recv_sem.at[t],
                device_id=(rim_devices[t],),
                device_id_type=MESH,
            ).wait_recv()
        even, odd = rim_recv[0], rim_recv[1]
        rim_coef = jnp.where(outside, 0.0, jnp.where(low, even, odd))
        rim_skel = pltpu.roll(jnp.where(low, odd, even), 64, 1)
        for slot in (0, 5):
            g_chain[slot, 0] = rim_coef
            g_chain[slot, 1] = rim_skel

    local3 = cousins(g_chain, 1 + y)
    local4 = cousins(g_chain, 7 + quad)
    local5 = cousins(g_chain, 11)
    y2 = local[6]
    y1 = [x + local[4 + at] for at, x in enumerate(lower([y2], maps[1]))]
    y0 = [x + local[at] for at, x in enumerate(lower(y1, maps[0]))]
    y4 = local4 + mm(side(local5, quad), maps[4], NT)
    y3 = local3 + mm(side(y4, rem(y, 2)), maps[3], NT)
    y3 = jnp.where(core == 1, y3, pltpu.roll(y3, 64, 1))

    wait_all(part_buf.at[pl.ds(0, MEMBERS - 1)], part_recv_sem)
    parts = [part_buf[at] for at in range(MEMBERS)]
    while len(parts) > 1:
        parts = [a + b for a, b in zip(parts[0::2], parts[1::2])]
    d6 = parts[0]
    d63 = jnp.where(low, d6, y3)
    d0 = jnp.concatenate(y0, axis=1) + mm(d63, (leaf_high, leaf_low), NN)
    for p in range(4):
        pair = d0[:, 128 * p : 128 * p + 128]
        two = jnp.concatenate([jnp.where(low, pair, 0.0), jnp.where(low, 0.0, pair)], axis=0)
        rows = lax.dot_general(
            two.astype(bf16),
            basis[128 * p : 128 * p + 128, :],
            NN,
            preferred_element_type=f32,
        )
        for t in range(2):
            leaf = 2 * p + t
            at = leaf * LEAF
            out_ref[:, at : at + LEAF] = jnp.where(
                slots < occ[leaf], near[:, at : at + LEAF] + rows[8 * t : 8 * t + 8], 0.0
            )

    wait_all(part_buf.at[pl.ds(0, MEMBERS - 1)], part_send_sem)


def body(boxes, across, coords, loads, occupancy, basis, transfer):
    strides = boxes // MEMBERS
    hbm = pl.BlockSpec(memory_space=pl.ANY)
    dma = pltpu.SemaphoreType.DMA
    return pl.pallas_call(
        functools.partial(kernel, boxes, across),
        out_shape=jax.ShapeDtypeStruct((COLS, OWN), f32),
        in_specs=[hbm] * 5,
        out_specs=pl.BlockSpec(memory_space=pltpu.VMEM),
        scratch_shapes=[
            pltpu.VMEM((3, OWN), f32),
            pltpu.VMEM((COLS, OWN), bf16),
            pltpu.SMEM((LEAVES,), jnp.int32),
            pltpu.VMEM((LEAVES * 64, LEAF), bf16),
            pltpu.VMEM((6, 128, 64), f32),
            pltpu.VMEM((6, 128, 128), bf16),
            pltpu.VMEM((6, 128, 128), bf16),
            pltpu.VMEM((128, 128), f32),
            pltpu.VMEM((2, 8, OWN + 2 * LEAF), f32),
            pltpu.VMEM((OWN, 8), f32),
            pltpu.VMEM((128, 512), bf16),
            pltpu.VMEM((128, 512), bf16),
            pltpu.VMEM((COLS, OWN + LEAF), f32),
            pltpu.VMEM((LEAF, 2 * LEAF), bf16),
            pltpu.VMEM((LEAF, 2 * LEAF), bf16),
            pltpu.VMEM((LEAF, LEAF), bf16),
            pltpu.VMEM((13, 2, 8, 128), f32),
            pltpu.VMEM((13, 2, 8, 128), f32),
            pltpu.VMEM((7, 8, 128), f32),
            pltpu.VMEM((2, 3, 2, 8, 128), f32),
            pltpu.VMEM((2, 3, 2, 8, 128), f32),
            pltpu.VMEM((MEMBERS, 8, 128), f32),
            pltpu.VMEM((MEMBERS, 8, 128), f32),
            pltpu.VMEM((2, 2, 8, 128), f32),
            pltpu.VMEM((2, 2, 8, 128), f32),
            pltpu.VMEM((8, 128), f32),
            pltpu.VMEM((2, 8, 128), f32),
            pltpu.VMEM((2, 8, 128), f32),
            pltpu.VMEM((strides, 8, 128), f32),
            pltpu.VMEM((MEMBERS, 8, 128), f32),
            dma((5,)),
            dma((2,)),
            dma((2,)),
            dma((2,)),
            dma((2,)),
            dma,
            dma,
            dma,
            dma,
            dma((3,)),
            dma((3,)),
            dma((2,)),
            dma((2,)),
            dma((2,)),
            dma((2,)),
            dma,
            dma,
            pltpu.SemaphoreType.REGULAR,
        ],
        compiler_params=pltpu.CompilerParams(
            collective_id=0, has_side_effects=True, vmem_limit_bytes=32 * 1024 * 1024
        ),
    )(
        *[
            pltpu.with_memory_space_constraint(x, pltpu.HBM)
            for x in (
                coords,
                loads,
                occupancy,
                basis.reshape(LEAVES * 64, LEAF),
                transfer.reshape(6, 128, 64),
            )
        ]
    )


def solution(mesh):
    boxes = mesh.shape["box"] // MEMBERS
    return jax.shard_map(
        functools.partial(body, boxes, 4),
        mesh=mesh,
        in_specs=(P(None, "box"), P(None, "box"), P("box"), P("box", None, None), P()),
        out_specs=P(None, "box"),
        check_vma=False,
    )
```

```python
import functools

import jax
import jax.numpy as jnp
from jax import lax
from jax.experimental import pallas as pl
from jax.experimental.pallas import tpu as pltpu
from jax.sharding import PartitionSpec as P

LEAF = 256
COLS = 8
LEAVES = 8
MEMBERS = 8
OWN = LEAF * LEAVES

f32 = jnp.float32
bf16 = jnp.bfloat16
soften = 0.0001
near_scale = 0.0625
far_scale = 0.125
NN = (((1,), (0,)), ((), ()))
NT = (((1,), (1,)), ((), ()))
MESH = pl.DeviceIdType.MESH


def div(a, b):
    return lax.div(a, jnp.int32(b))


def rem(a, b):
    return lax.rem(a, jnp.int32(b))


def phi(tx, ty, tz, sx, sy, sz, scale):
    dx = tx - sx
    dy = ty - sy
    dz = tz - sz
    r2 = dx * dx + dy * dy + dz * dz
    return (r2 * (0.5 * scale)) * jnp.log(r2 + soften)


def split(x):
    high = x.astype(bf16)
    return high, (x - high.astype(f32)).astype(bf16)


def mm(a, b, dims):
    rows = a.shape[0]
    high = a.astype(bf16).astype(f32)
    stacked = jnp.concatenate([high, a - high], axis=0).astype(bf16)
    both = lax.dot_general(stacked, b[0][...], dims, preferred_element_type=f32)
    low = lax.dot_general(stacked[:rows], b[1][...], dims, preferred_element_type=f32)
    return both[:rows] + (both[rows:] + low)


def low_half(shape):
    return lax.broadcasted_iota(jnp.int32, shape, len(shape) - 1) < 64


def merge(rows):
    count = rows.shape[0] // 16
    low = low_half((8, 128))
    return [
        jnp.where(low, rows[16 * i : 16 * i + 8], rows[16 * i + 8 : 16 * i + 16])
        for i in range(count)
    ]


def raise_coef(pairs, level_map):
    rows = mm(jnp.concatenate(pairs, axis=0), level_map, NN)
    return merge(rows) if len(pairs) > 1 else [rows]


def pick(x, entries):
    rows = x.shape[0]
    a = x.astype(bf16).astype(f32)
    b = (x - a).astype(bf16).astype(f32)
    c = (x - a) - b
    stacked = jnp.concatenate([a, b, c], axis=0).astype(bf16)
    picked = lax.dot_general(stacked, entries, NN, preferred_element_type=f32)
    return picked[:rows] + picked[rows : 2 * rows] + picked[2 * rows :]


def raise_skel(pairs, every_second):
    rows_up = pick(jnp.concatenate(pairs, axis=0), every_second)
    return merge(rows_up) if len(pairs) > 1 else [rows_up]


def cousins(chain, slot):
    low = low_half((8, 128))
    column = chain[slot, 1].T
    tx, ty, tz = column[:, 0:1], column[:, 1:2], column[:, 2:3]
    before, after = chain[slot - 1, 0], chain[slot + 1, 0]
    tiles = []
    for skel in (chain[slot - 1, 1], chain[slot + 1, 1]):
        tiles.append(phi(tx, ty, tz, skel[0:1], skel[1:2], skel[2:3], far_scale))
    tile = jnp.concatenate(tiles, axis=1)
    even = jnp.concatenate([jnp.where(low, before, 0.0), after], axis=1)
    odd = jnp.concatenate([before, jnp.where(low, 0.0, after)], axis=1)
    rows = mm(jnp.concatenate([even, odd], axis=0), split(tile), NT)
    return jnp.where(low, rows[:8], rows[8:])


def lower(pairs, level_map):
    height = pairs[0].shape[0]
    low = low_half((height, 128))
    stacked = []
    for pair in pairs:
        stacked += [jnp.where(low, pair, 0.0), jnp.where(low, 0.0, pair)]
    rows = mm(jnp.concatenate(stacked, axis=0), level_map, NT)
    return [rows[height * i : height * (i + 1)] for i in range(2 * len(pairs))]


def kernel(
    boxes,
    across,
    coords_hbm,
    loads_hbm,
    occ_hbm,
    basis_hbm,
    transfer_hbm,
    out_ref,
    coords,
    loads,
    occ,
    basis,
    transfer,
    map_high,
    map_low,
    path_map,
    field,
    column,
    leaf_high,
    leaf_low,
    near,
    tile_a,
    tile_b,
    tile_c,
    chain,
    g_chain,
    local,
    edge_send,
    edge_recv,
    u_buf,
    g_buf,
    bound_send,
    bound_recv,
    quad_recv,
    rim_recv,
    far_send,
    far_buf,
    part_buf,
    load_sem,
    near_send_sem,
    near_recv_sem,
    edge_send_sem,
    edge_recv_sem,
    u_send_sem,
    u_recv_sem,
    g_send_sem,
    g_recv_sem,
    bound_send_sem,
    bound_recv_sem,
    rim_send_sem,
    rim_recv_sem,
    far_send_sem,
    far_recv_sem,
    part_send_sem,
    part_recv_sem,
    ready,
):
    loading = [
        pltpu.make_async_copy(src, dst, load_sem.at[at])
        for at, (src, dst) in enumerate(
            [
                (coords_hbm, coords),
                (transfer_hbm, transfer),
                (loads_hbm, loads),
                (occ_hbm, occ),
                (basis_hbm, basis),
            ]
        )
    ]
    for copy in loading:
        copy.start()

    device = lax.axis_index("box")
    total = boxes * MEMBERS
    strides = boxes // MEMBERS
    depth = boxes // (2 * across)
    box, member = div(device, MEMBERS), rem(device, MEMBERS)
    x, z, y_half = div(box, 2 * depth), rem(div(box, 2), depth), rem(box, 2)
    y, core = div(member, 2), rem(member, 2)
    low = low_half((8, 128))
    half = jnp.where(low, 0, 1)

    top = jnp.where(y == 3, 1, 0)
    outer = jnp.where(y == 0, 1, top)
    side_to = jnp.where(outer == 1, top, 2 - y)
    side_from = jnp.where(outer == 1, 1 - top, 2 - y)
    far_half = jnp.where(outer == 1, 1 - y_half, y_half)
    z_core = rem(div(z, 2), 2)
    far_member = 2 * jnp.where(outer == 1, 3 - y, y) + z_core
    z_high, z_low = div(z, 4), rem(z, 2)
    far_x = [rem(x + dx, across) for dx in range(across)]
    far_steps = [(dx, turn) for dx in range(across) for turn in range(2)]

    def far_box(side, dx, turn):
        far_z = 4 * rem(side + z_high, 2) + 2 * core + (1 - z_low if turn else z_low)
        return (far_x[dx % across] * depth + far_z) * 2 + far_half

    far_to = [far_box(side_to, dx, turn) * MEMBERS + far_member for dx, turn in far_steps]
    far_from = [far_box(side_from, -dx, turn) for dx, turn in far_steps]
    alone = jnp.logical_and(jnp.logical_and(outer == 0, side_to == 0), core == z_core)

    barrier = pltpu.get_barrier_semaphore()

    def greet(target):
        pl.semaphore_signal(barrier, inc=1, device_id=(target,), device_id_type=MESH)

    far_order = sorted(range(1, strides), key=lambda k: abs(far_steps[k][0] - across // 2))
    place = 2 * y + z_core
    relay_z = [4 * rem(side_to + z_high, 2) + 2 * core + at for at in (z_low, 1 - z_low)]
    to_relay = [((x * depth + at) * 2 + y_half) * MEMBERS + place for at in relay_z]
    senders = to_relay
    from_relay = [
        ((at * depth + z) * 2 + far_half) * MEMBERS + far_member - z_core + core for at in far_x
    ]
    own_sender = jnp.logical_and(side_to == 0, core == z_core)

    greet(to_relay[1])
    for dx in (2, 1, 3):
        greet(from_relay[dx])

    @pl.when(jnp.logical_not(own_sender))
    def _():
        greet(to_relay[0])

    @pl.when(outer == 1)
    def _():
        greet(from_relay[0])

    left_device = rem(device + total - 1, total)
    right_device = rem(device + 1, total)
    mirror = 2 * (3 - y) + core
    left_box = rem(box + boxes - 1, boxes) * MEMBERS + mirror
    right_box = rem(box + 1, boxes) * MEMBERS + mirror
    mates = [box * MEMBERS + rem(member + r, MEMBERS) for r in (6, 2, 7, 3, 5, 4, 1)]
    at_rim = outer == 1
    rim_box = rem(box + boxes + 2 * top - 1, boxes)
    rim_devices = [rim_box * MEMBERS + 6 - 6 * top + t for t in range(2)]
    quad = div(member, 4)
    quad_device = rem(box + boxes + 2 * quad - 1, boxes) * MEMBERS + mirror
    early = jnp.where(z == 0, 1, 0)
    for target in mates + [left_device, right_device, left_box, right_box]:
        greet(target)
    @pl.when(at_rim)
    def _():
        for target in rim_devices:
            greet(target)

    lanes = lax.broadcasted_iota(jnp.int32, (1, 128), 1)
    index = lax.broadcasted_iota(jnp.int32, (512, 128), 0)
    placed = (index == (lanes - 64 - 8 * member) * 64).astype(f32).astype(bf16)
    picks = (lax.broadcasted_iota(jnp.int32, (1, 128), 1) & 63) * 2
    every_second = (
        (lax.broadcasted_iota(jnp.int32, (128, 128), 0) == picks).astype(f32).astype(bf16)
    )
    for copy in loading:
        copy.wait()
    points = jnp.concatenate([coords[...], jnp.zeros((5, OWN), f32)], axis=0)
    s0 = [
        jnp.concatenate(
            [points[:, 512 * p : 512 * p + 64], points[:, 512 * p + 256 : 512 * p + 320]], axis=1
        )
        for p in range(4)
    ]
    s6 = pick(jnp.concatenate(s0, axis=1), placed)

    maps = [(map_high.at[level], map_low.at[level]) for level in range(6)]

    def set_map(level):
        once = transfer[level]
        map_high[level], map_low[level] = split(jnp.concatenate([once, once], axis=1))

    for level in range(2):
        set_map(level)
    slots = lax.broadcasted_iota(jnp.int32, (COLS, LEAF), 1)
    live = []
    for leaf in range(LEAVES):
        part = loads[:, leaf * LEAF : (leaf + 1) * LEAF].astype(f32)
        live.append(jnp.where(slots < occ[leaf], part, 0.0))
    c0 = []
    for p in range(4):
        two = jnp.concatenate([live[2 * p], live[2 * p + 1]], axis=0).astype(bf16)
        rows = lax.dot_general(
            two, basis[128 * p : 128 * p + 128, :], NT, preferred_element_type=f32
        )
        c0.append(jnp.where(low, rows[:8], rows[8:]))
    c1 = raise_coef(c0, maps[0])
    c2 = raise_coef(c1, maps[1])
    def factor(level, at):
        return transfer[level, pl.ds(pl.multiple_of(64 * at, 64), 64), :]

    map_34 = mm(transfer[2], split(factor(3, core)), NN)
    wide = jnp.concatenate([factor(5, quad), jnp.zeros((64, 64), f32)], axis=1)
    map_56 = mm(factor(4, rem(y, 2)), split(wide), NN)
    map_6 = mm(map_34, split(map_56), NN)
    u_buf[member] = mm(c2[0], split(map_6), NN) + s6
    path_map[...] = map_6

    def set_field():
        field[0, :, LEAF : LEAF + OWN] = points
        for leaf in range(LEAVES):
            field[1, :, (leaf + 1) * LEAF : (leaf + 2) * LEAF] = live[leaf]
        for at in range(0, OWN, 128):
            column[at : at + 128, :] = points[:, at : at + 128].T
        near[...] = jnp.zeros_like(near)

    def fill_tile(tile, row, col, width):
        sx = field[0, 0:1, pl.ds(col, width)]
        sy = field[0, 1:2, pl.ds(col, width)]
        sz = field[0, 2:3, pl.ds(col, width)]
        for at in range(0, LEAF, 16):
            rows = column[pl.ds(row + at, 16), :]
            tile[at : at + 16, 0:width] = phi(
                rows[:, 0:1], rows[:, 1:2], rows[:, 2:3], sx, sy, sz, near_scale
            ).astype(bf16)

    def near_leaf(tile, row):
        col = row + LEAF
        fill_tile(tile, row, col, 2 * LEAF)
        loads_two = field[1, :, pl.ds(col, 2 * LEAF)].astype(bf16)
        this = lax.dot_general(loads_two, tile[...], NT, preferred_element_type=f32)
        after = lax.dot_general(
            loads_two[:, :LEAF], tile[:, LEAF:], NN, preferred_element_type=f32
        )
        return this, after

    def near_two(row):
        first, second_part = near_leaf(tile_a, row)
        second, third = near_leaf(tile_b, row + LEAF)
        near[:, pl.ds(row, LEAF)] += first
        near[:, pl.ds(row + LEAF, LEAF)] += second_part + second
        near[:, pl.ds(row + 2 * LEAF, LEAF)] += third

    def near_step(pair, carry):
        near_two(pl.multiple_of(pair * (2 * LEAF), 2 * LEAF))
        return carry

    def side(block, at):
        lanes = jnp.where(low_half((1, 128)), 0, 1)
        return jnp.where(lanes == at, block, 0.0)

    def set_chain(levels, into):
        for at, (pairs, skels) in enumerate(levels):
            first = (1, 7, 11)[at]
            for p in range(len(pairs)):
                into[first + p, 0] = pairs[p]
                into[first + p, 1] = skels[p]

    def set_inner():
        lax.fori_loop(0, 3, near_step, 0)
        row = (LEAVES - 2) * LEAF
        this, after = near_leaf(tile_a, row)
        fill_tile(tile_c, row + LEAF, row + 2 * LEAF, LEAF)
        own = field[1, :, row + 2 * LEAF : row + 3 * LEAF].astype(bf16)
        after += lax.dot_general(own, tile_c[...], NT, preferred_element_type=f32)
        near[:, row : row + LEAF] += this
        near[:, row + LEAF : row + 2 * LEAF] += after
        for slot in (2, 3):
            local[slot - 1] = cousins(chain, slot)

    def set_edges():
        s1 = raise_skel(s0, every_second)
        s2 = raise_skel(s1, every_second)

        set_chain([(c0, s0), (c1, s1), (c2, s2)], chain)
        for at, (pairs, skels) in enumerate([(c0, s0), (c1, s1), (c2, s2)]):
            edge_send[0, at, 0] = pairs[-1]
            edge_send[0, at, 1] = skels[-1]
            edge_send[1, at, 0] = pairs[0]
            edge_send[1, at, 1] = skels[0]
    def set_leaf_paths():
        x2 = jnp.concatenate([path_map[...].T[:64], transfer[2].T], axis=0)
        x0 = lower(lower([x2], maps[1]), maps[0])
        leaf_high[...], leaf_low[...] = split(jnp.concatenate(x0, axis=1))

    @pl.when(early == 1)
    def _():
        set_field()
        set_edges()
        set_inner()

    pl.semaphore_wait(
        barrier, MEMBERS - 1 + 4 + 3 + outer + 2 - own_sender.astype(jnp.int32) + 2 * outer
    )

    def tell(target):
        pl.semaphore_signal(ready, inc=1, device_id=(target,), device_id_type=MESH)

    tell(senders[1])

    @pl.when(jnp.logical_not(own_sender))
    def _():
        tell(senders[0])

    def remote(src, dst, send_sem, recv_sem, target):
        return pltpu.make_async_remote_copy(
            src_ref=src,
            dst_ref=dst,
            send_sem=send_sem,
            recv_sem=recv_sem,
            device_id=(target,),
            device_id_type=MESH,
        )

    def send(*ends):
        copy = remote(*ends)
        copy.start()
        return copy

    def wait_all(ref, semaphore):
        pltpu.make_async_copy(ref, ref, semaphore).wait()

    for mate in mates:
        send(u_buf.at[member], u_buf.at[member], u_send_sem, u_recv_sem, mate)

    set_map(2)
    every_eighth = (index == (lanes & 63) * 8).astype(f32).astype(bf16)
    s3 = pick(jnp.concatenate(s0, axis=1), every_eighth)
    c3 = raise_coef(c2, maps[2])[0]
    g_buf[member] = jnp.where(half == core, c3, s3)
    for mate in mates:
        send(g_buf.at[member], g_buf.at[member], g_send_sem, g_recv_sem, mate)

    rim_copies = [
        pltpu.make_async_remote_copy(
            src_ref=g_buf.at[member],
            dst_ref=rim_recv.at[core],
            send_sem=rim_send_sem.at[t],
            recv_sem=rim_recv_sem.at[core],
            device_id=(rim_devices[t],),
            device_id_type=MESH,
        )
        for t in range(2)
    ]

    @pl.when(at_rim)
    def _():
        for copy in rim_copies:
            copy.start()

    @pl.when(early == 0)
    def _():
        set_field()

    last = LEAF * LEAVES
    near_copies = [
        send(
            field.at[:, :, last : last + LEAF],
            field.at[:, :, 0:LEAF],
            near_send_sem.at[0],
            near_recv_sem.at[0],
            right_device,
        ),
        send(
            field.at[:, :, LEAF : 2 * LEAF],
            field.at[:, :, last + LEAF : last + 2 * LEAF],
            near_send_sem.at[1],
            near_recv_sem.at[1],
            left_device,
        ),
    ]

    edge_copies = [
        remote(
            edge_send.at[side],
            edge_recv.at[side],
            edge_send_sem.at[side],
            edge_recv_sem.at[side],
            (right_device, left_device)[side],
        )
        for side in range(2)
    ]

    @pl.when(early == 0)
    def _():
        set_edges()

    for copy in edge_copies:
        copy.start()

    set_map(3)
    set_map(4)

    @pl.when(early == 1)
    def _():
        set_leaf_paths()

    wait_all(u_buf.at[pl.ds(0, MEMBERS - 1)], u_recv_sem)
    parts = [u_buf[at] for at in range(MEMBERS)]
    while len(parts) > 1:
        parts = [a + b for a, b in zip(parts[0::2], parts[1::2])]
    top_record = parts[0]
    swapped_record = pltpu.roll(top_record, 64, 1)
    far_send[0] = top_record
    far_send[1] = swapped_record

    @pl.when(alone)
    def _():
        far_buf[0] = far_send[0]

    pl.semaphore_wait(ready, 2 - own_sender.astype(jnp.int32))
    for k in far_order:
        send(
            far_send.at[k % 2], far_buf.at[k], far_send_sem.at[1], far_recv_sem.at[1], far_to[k]
        )
    first_far = pltpu.make_async_remote_copy(
        src_ref=far_send.at[0],
        dst_ref=far_buf.at[0],
        send_sem=far_send_sem.at[0],
        recv_sem=far_recv_sem.at[0],
        device_id=(far_to[0],),
        device_id_type=MESH,
    )

    @pl.when(jnp.logical_not(alone))
    def _():
        first_far.start()

    wait_all(g_buf.at[pl.ds(0, MEMBERS - 1)], g_recv_sem)
    c3s, s3s = [], []
    for p in range(4):
        even, odd = g_buf[2 * p], g_buf[2 * p + 1]
        c3s.append(jnp.where(low, even, odd))
        s3s.append(pltpu.roll(jnp.where(low, odd, even), 64, 1))
    c4s, s4s = raise_coef(c3s, maps[3]), raise_skel(s3s, every_second)
    c5s, s5s = raise_coef(c4s, maps[4]), raise_skel(s4s, every_second)
    set_chain([(c3s, s3s), (c4s, s4s), (c5s, s5s)], g_chain)
    for at in range(2):
        bound_send[at, 0] = c5s[0]
        bound_send[at, 1] = s5s[0] + pltpu.roll(s4s[1 - at], 3, 0)
    bound_copies = [
        send(
            bound_send.at[side],
            bound_recv.at[side],
            bound_send_sem.at[side],
            bound_recv_sem.at[side],
            (right_box, left_box)[side],
        )
        for side in range(2)
    ]
    bound_copies.append(
        send(
            g_chain.at[7 + quad, 0],
            quad_recv,
            bound_send_sem.at[2],
            bound_recv_sem.at[2],
            quad_device,
        )
    )

    @pl.when(early == 0)
    def _():
        set_inner()
        set_leaf_paths()

    for copy in near_copies:
        copy.wait_recv()

    @pl.when(device == 0)
    def _():
        field[1, :, 0:LEAF] = jnp.zeros((COLS, LEAF), f32)

    @pl.when(device == total - 1)
    def _():
        field[1, :, last + LEAF : last + 2 * LEAF] = jnp.zeros((COLS, LEAF), f32)

    def near_end(tile, row, col):
        fill_tile(tile, row, col, LEAF)
        near[:, row : row + LEAF] += lax.dot_general(
            field[1, :, col : col + LEAF].astype(bf16),
            tile[:, 0:LEAF],
            NT,
            preferred_element_type=f32,
        )

    near_end(tile_c, 0, 0)
    near_end(tile_a, last - LEAF, last + LEAF)

    def set_ends(ends, into, at_start, at_end):
        for level in range(3):
            before, after = (0, 6, 10)[level], (5, 9, 12)[level]
            into[before, 0] = jnp.where(at_start, 0.0, ends[0, level, 0])
            into[before, 1] = ends[0, level, 1]
            into[after, 0] = jnp.where(at_end, 0.0, ends[1, level, 0])
            into[after, 1] = ends[1, level, 1]

    for copy in edge_copies:
        copy.wait_recv()
    set_ends(edge_recv, chain, device == 0, device == total - 1)
    for at, slot in [(0, 1), (3, 4), (4, 7), (5, 8), (6, 11)]:
        local[at] = cousins(chain, slot)

    top_column = swapped_record.T[:64]
    tx, ty, tz = top_column[:, 0:1], top_column[:, 1:2], top_column[:, 2:3]

    wait_all(far_buf.at[pl.ds(1, strides - 1)], far_recv_sem.at[1])

    @pl.when(jnp.logical_not(alone))
    def _():
        first_far.wait_recv()

    top_coef, top_skel = [], []
    for k in range(0, strides, 2):
        halves = []
        for at in (k, k + 1):
            apart = far_from[at] - box
            counts = jnp.logical_or(apart >= 2, apart <= -2)
            halves.append((far_buf[at], counts))
        (one, one_counts), (two, two_counts) = halves
        coef = jnp.where(low, jnp.where(one_counts, one, 0.0), jnp.where(two_counts, two, 0.0))
        top_coef.append(pltpu.roll(coef, 64, 1))
        top_skel.append(jnp.where(low, two, one))
    top_tile = jnp.concatenate(
        [phi(tx, ty, tz, s[0:1], s[1:2], s[2:3], far_scale) for s in top_skel], axis=1
    )
    top = mm(jnp.concatenate(top_coef, axis=1), split(top_tile), NT)
    part_buf[member] = jnp.concatenate([top, jnp.zeros((8, 64), f32)], axis=1)
    for at in range(MEMBERS - 1):
        mate = box * MEMBERS + at + jnp.where(member <= at, 1, 0)
        send(part_buf.at[member], part_buf.at[member], part_send_sem, part_recv_sem, mate)

    wait_all(u_buf.at[pl.ds(0, MEMBERS - 1)], u_send_sem)
    wait_all(g_buf.at[pl.ds(0, MEMBERS - 1)], g_send_sem)
    wait_all(far_buf.at[pl.ds(1, strides - 1)], far_send_sem.at[1])
    for copy in near_copies + edge_copies + bound_copies:
        copy.wait_send()

    @pl.when(jnp.logical_not(alone))
    def _():
        first_far.wait_send()

    for copy in bound_copies:
        copy.wait_recv()
    at_start, at_end = box == 0, box == boxes - 1
    outside = jnp.logical_or(
        jnp.logical_and(quad == 0, at_start), jnp.logical_and(quad == 1, at_end)
    )
    start_skel, end_skel = bound_recv[0, 1], bound_recv[1, 1]
    g_chain[10, 0] = jnp.where(at_start, 0.0, bound_recv[0, 0])
    g_chain[10, 1] = start_skel
    g_chain[12, 0] = jnp.where(at_end, 0.0, bound_recv[1, 0])
    g_chain[12, 1] = end_skel
    quad_coef = jnp.where(outside, 0.0, quad_recv[...])
    g_chain[6, 0] = quad_coef
    g_chain[6, 1] = pltpu.roll(start_skel, 5, 0)
    g_chain[9, 0] = quad_coef
    g_chain[9, 1] = pltpu.roll(end_skel, 5, 0)

    @pl.when(at_rim)
    def _():
        for copy in rim_copies:
            copy.wait_send()
        for t in range(2):
            pltpu.make_async_remote_copy(
                src_ref=g_buf.at[member],
                dst_ref=rim_recv.at[t],
                send_sem=rim_send_sem.at[t],
                recv_sem=rim_recv_sem.at[t],
                device_id=(rim_devices[t],),
                device_id_type=MESH,
            ).wait_recv()
        even, odd = rim_recv[0], rim_recv[1]
        rim_coef = jnp.where(outside, 0.0, jnp.where(low, even, odd))
        rim_skel = pltpu.roll(jnp.where(low, odd, even), 64, 1)
        for slot in (0, 5):
            g_chain[slot, 0] = rim_coef
            g_chain[slot, 1] = rim_skel

    local3 = cousins(g_chain, 1 + y)
    local4 = cousins(g_chain, 7 + quad)
    local5 = cousins(g_chain, 11)
    y2 = local[6]
    y1 = [x + local[4 + at] for at, x in enumerate(lower([y2], maps[1]))]
    y0 = [x + local[at] for at, x in enumerate(lower(y1, maps[0]))]
    y4 = local4 + mm(side(local5, quad), maps[4], NT)
    y3 = local3 + mm(side(y4, rem(y, 2)), maps[3], NT)
    y3 = jnp.where(core == 1, y3, pltpu.roll(y3, 64, 1))

    wait_all(part_buf.at[pl.ds(0, MEMBERS - 1)], part_recv_sem)
    parts = [part_buf[at] for at in range(MEMBERS)]
    while len(parts) > 1:
        parts = [a + b for a, b in zip(parts[0::2], parts[1::2])]
    d6 = parts[0]
    d63 = jnp.where(low, d6, y3)
    d0 = jnp.concatenate(y0, axis=1) + mm(d63, (leaf_high, leaf_low), NN)
    for p in range(4):
        pair = d0[:, 128 * p : 128 * p + 128]
        two = jnp.concatenate([jnp.where(low, pair, 0.0), jnp.where(low, 0.0, pair)], axis=0)
        rows = lax.dot_general(
            two.astype(bf16),
            basis[128 * p : 128 * p + 128, :],
            NN,
            preferred_element_type=f32,
        )
        for t in range(2):
            leaf = 2 * p + t
            at = leaf * LEAF
            out_ref[:, at : at + LEAF] = jnp.where(
                slots < occ[leaf], near[:, at : at + LEAF] + rows[8 * t : 8 * t + 8], 0.0
            )

    wait_all(part_buf.at[pl.ds(0, MEMBERS - 1)], part_send_sem)


def body(boxes, across, coords, loads, occupancy, basis, transfer):
    strides = boxes // MEMBERS
    hbm = pl.BlockSpec(memory_space=pl.ANY)
    dma = pltpu.SemaphoreType.DMA
    return pl.pallas_call(
        functools.partial(kernel, boxes, across),
        out_shape=jax.ShapeDtypeStruct((COLS, OWN), f32),
        in_specs=[hbm] * 5,
        out_specs=pl.BlockSpec(memory_space=pltpu.VMEM),
        scratch_shapes=[
            pltpu.VMEM((3, OWN), f32),
            pltpu.VMEM((COLS, OWN), bf16),
            pltpu.SMEM((LEAVES,), jnp.int32),
            pltpu.VMEM((LEAVES * 64, LEAF), bf16),
            pltpu.VMEM((6, 128, 64), f32),
            pltpu.VMEM((6, 128, 128), bf16),
            pltpu.VMEM((6, 128, 128), bf16),
            pltpu.VMEM((128, 128), f32),
            pltpu.VMEM((2, 8, OWN + 2 * LEAF), f32),
            pltpu.VMEM((OWN, 8), f32),
            pltpu.VMEM((128, 512), bf16),
            pltpu.VMEM((128, 512), bf16),
            pltpu.VMEM((COLS, OWN + LEAF), f32),
            pltpu.VMEM((LEAF, 2 * LEAF), bf16),
            pltpu.VMEM((LEAF, 2 * LEAF), bf16),
            pltpu.VMEM((LEAF, LEAF), bf16),
            pltpu.VMEM((13, 2, 8, 128), f32),
            pltpu.VMEM((13, 2, 8, 128), f32),
            pltpu.VMEM((7, 8, 128), f32),
            pltpu.VMEM((2, 3, 2, 8, 128), f32),
            pltpu.VMEM((2, 3, 2, 8, 128), f32),
            pltpu.VMEM((MEMBERS, 8, 128), f32),
            pltpu.VMEM((MEMBERS, 8, 128), f32),
            pltpu.VMEM((2, 2, 8, 128), f32),
            pltpu.VMEM((2, 2, 8, 128), f32),
            pltpu.VMEM((8, 128), f32),
            pltpu.VMEM((2, 8, 128), f32),
            pltpu.VMEM((2, 8, 128), f32),
            pltpu.VMEM((strides, 8, 128), f32),
            pltpu.VMEM((MEMBERS, 8, 128), f32),
            dma((5,)),
            dma((2,)),
            dma((2,)),
            dma((2,)),
            dma((2,)),
            dma,
            dma,
            dma,
            dma,
            dma((3,)),
            dma((3,)),
            dma((2,)),
            dma((2,)),
            dma((2,)),
            dma((2,)),
            dma,
            dma,
            pltpu.SemaphoreType.REGULAR,
        ],
        compiler_params=pltpu.CompilerParams(
            collective_id=0, has_side_effects=True, vmem_limit_bytes=32 * 1024 * 1024
        ),
    )(
        *[
            pltpu.with_memory_space_constraint(x, pltpu.HBM)
            for x in (
                coords,
                loads,
                occupancy,
                basis.reshape(LEAVES * 64, LEAF),
                transfer.reshape(6, 128, 64),
            )
        ]
    )


def solution(mesh):
    boxes = mesh.shape["box"] // MEMBERS
    return jax.shard_map(
        functools.partial(body, boxes, 4),
        mesh=mesh,
        in_specs=(P(None, "box"), P(None, "box"), P("box"), P("box", None, None), P()),
        out_specs=P(None, "box"),
        check_vma=False,
    )
```

```python
import functools

import jax
import jax.numpy as jnp
from jax import lax
from jax.experimental import pallas as pl
from jax.experimental.pallas import tpu as pltpu
from jax.sharding import PartitionSpec as P

LEAF = 256
COLS = 8
LEAVES = 8
MEMBERS = 8
OWN = LEAF * LEAVES

f32 = jnp.float32
bf16 = jnp.bfloat16
soften = 0.0001
near_scale = 0.0625
far_scale = 0.125
NN = (((1,), (0,)), ((), ()))
NT = (((1,), (1,)), ((), ()))
MESH = pl.DeviceIdType.MESH


def div(a, b):
    return lax.div(a, jnp.int32(b))


def rem(a, b):
    return lax.rem(a, jnp.int32(b))


def phi(tx, ty, tz, sx, sy, sz, scale):
    dx = tx - sx
    dy = ty - sy
    dz = tz - sz
    r2 = dx * dx + dy * dy + dz * dz
    return (r2 * (0.5 * scale)) * jnp.log(r2 + soften)


def split(x):
    high = x.astype(bf16)
    return high, (x - high.astype(f32)).astype(bf16)


def mm(a, b, dims):
    rows = a.shape[0]
    high = a.astype(bf16).astype(f32)
    stacked = jnp.concatenate([high, a - high], axis=0).astype(bf16)
    both = lax.dot_general(stacked, b[0][...], dims, preferred_element_type=f32)
    low = lax.dot_general(stacked[:rows], b[1][...], dims, preferred_element_type=f32)
    return both[:rows] + (both[rows:] + low)


def low_half(shape):
    return lax.broadcasted_iota(jnp.int32, shape, len(shape) - 1) < 64


def merge(rows):
    count = rows.shape[0] // 16
    low = low_half((8, 128))
    return [
        jnp.where(low, rows[16 * i : 16 * i + 8], rows[16 * i + 8 : 16 * i + 16])
        for i in range(count)
    ]


def raise_coef(pairs, level_map):
    rows = mm(jnp.concatenate(pairs, axis=0), level_map, NN)
    return merge(rows) if len(pairs) > 1 else [rows]


def pick(x, entries):
    rows = x.shape[0]
    a = x.astype(bf16).astype(f32)
    b = (x - a).astype(bf16).astype(f32)
    c = (x - a) - b
    stacked = jnp.concatenate([a, b, c], axis=0).astype(bf16)
    picked = lax.dot_general(stacked, entries, NN, preferred_element_type=f32)
    return picked[:rows] + picked[rows : 2 * rows] + picked[2 * rows :]


def raise_skel(pairs, every_second):
    rows_up = pick(jnp.concatenate(pairs, axis=0), every_second)
    return merge(rows_up) if len(pairs) > 1 else [rows_up]


def cousins(chain, slot):
    low = low_half((8, 128))
    column = chain[slot, 1].T
    tx, ty, tz = column[:, 0:1], column[:, 1:2], column[:, 2:3]
    before, after = chain[slot - 1, 0], chain[slot + 1, 0]
    tiles = []
    for skel in (chain[slot - 1, 1], chain[slot + 1, 1]):
        tiles.append(phi(tx, ty, tz, skel[0:1], skel[1:2], skel[2:3], far_scale))
    tile = jnp.concatenate(tiles, axis=1)
    even = jnp.concatenate([jnp.where(low, before, 0.0), after], axis=1)
    odd = jnp.concatenate([before, jnp.where(low, 0.0, after)], axis=1)
    rows = mm(jnp.concatenate([even, odd], axis=0), split(tile), NT)
    return jnp.where(low, rows[:8], rows[8:])


def lower(pairs, level_map):
    height = pairs[0].shape[0]
    low = low_half((height, 128))
    stacked = []
    for pair in pairs:
        stacked += [jnp.where(low, pair, 0.0), jnp.where(low, 0.0, pair)]
    rows = mm(jnp.concatenate(stacked, axis=0), level_map, NT)
    return [rows[height * i : height * (i + 1)] for i in range(2 * len(pairs))]


def kernel(
    boxes,
    across,
    coords_hbm,
    loads_hbm,
    occ_hbm,
    basis_hbm,
    transfer_hbm,
    out_ref,
    coords,
    loads,
    occ,
    basis,
    transfer,
    map_high,
    map_low,
    path_map,
    field,
    column,
    point_high,
    point_low,
    near,
    tile_a,
    tile_b,
    tile_c,
    chain,
    g_chain,
    local,
    edge_send,
    edge_recv,
    u_buf,
    g_buf,
    bound_send,
    bound_recv,
    quad_recv,
    rim_recv,
    far_send,
    far_buf,
    part_buf,
    load_sem,
    near_send_sem,
    near_recv_sem,
    edge_send_sem,
    edge_recv_sem,
    u_send_sem,
    u_recv_sem,
    g_send_sem,
    g_recv_sem,
    bound_send_sem,
    bound_recv_sem,
    rim_send_sem,
    rim_recv_sem,
    far_send_sem,
    far_recv_sem,
    part_send_sem,
    part_recv_sem,
    ready,
):
    loading = [
        pltpu.make_async_copy(src, dst, load_sem.at[at])
        for at, (src, dst) in enumerate(
            [
                (coords_hbm, coords),
                (transfer_hbm, transfer),
                (loads_hbm, loads),
                (occ_hbm, occ),
                (basis_hbm, basis),
            ]
        )
    ]
    for copy in loading:
        copy.start()

    device = lax.axis_index("box")
    total = boxes * MEMBERS
    strides = boxes // MEMBERS
    depth = boxes // (2 * across)
    box, member = div(device, MEMBERS), rem(device, MEMBERS)
    x, z, y_half = div(box, 2 * depth), rem(div(box, 2), depth), rem(box, 2)
    y, core = div(member, 2), rem(member, 2)
    low = low_half((8, 128))
    half = jnp.where(low, 0, 1)

    top = jnp.where(y == 3, 1, 0)
    outer = jnp.where(y == 0, 1, top)
    side_to = jnp.where(outer == 1, top, 2 - y)
    side_from = jnp.where(outer == 1, 1 - top, 2 - y)
    far_half = jnp.where(outer == 1, 1 - y_half, y_half)
    z_core = rem(div(z, 2), 2)
    far_member = 2 * jnp.where(outer == 1, 3 - y, y) + z_core
    z_high, z_low = div(z, 4), rem(z, 2)
    far_x = [rem(x + dx, across) for dx in range(across)]
    far_steps = [(dx, turn) for dx in range(across) for turn in range(2)]

    def far_box(side, dx, turn):
        far_z = 4 * rem(side + z_high, 2) + 2 * core + (1 - z_low if turn else z_low)
        return (far_x[dx % across] * depth + far_z) * 2 + far_half

    far_to = [far_box(side_to, dx, turn) * MEMBERS + far_member for dx, turn in far_steps]
    far_from = [far_box(side_from, -dx, turn) for dx, turn in far_steps]
    alone = jnp.logical_and(jnp.logical_and(outer == 0, side_to == 0), core == z_core)

    barrier = pltpu.get_barrier_semaphore()

    def greet(target):
        pl.semaphore_signal(barrier, inc=1, device_id=(target,), device_id_type=MESH)

    far_order = sorted(range(1, strides), key=lambda k: abs(far_steps[k][0] - across // 2))
    place = 2 * y + z_core
    relay_z = [4 * rem(side_to + z_high, 2) + 2 * core + at for at in (z_low, 1 - z_low)]
    to_relay = [((x * depth + at) * 2 + y_half) * MEMBERS + place for at in relay_z]
    senders = to_relay
    from_relay = [
        ((at * depth + z) * 2 + far_half) * MEMBERS + far_member - z_core + core for at in far_x
    ]
    own_sender = jnp.logical_and(side_to == 0, core == z_core)

    greet(to_relay[1])
    for dx in (2, 1, 3):
        greet(from_relay[dx])

    @pl.when(jnp.logical_not(own_sender))
    def _():
        greet(to_relay[0])

    @pl.when(outer == 1)
    def _():
        greet(from_relay[0])

    left_device = rem(device + total - 1, total)
    right_device = rem(device + 1, total)
    mirror = 2 * (3 - y) + core
    left_box = rem(box + boxes - 1, boxes) * MEMBERS + mirror
    right_box = rem(box + 1, boxes) * MEMBERS + mirror
    mates = [box * MEMBERS + rem(member + r, MEMBERS) for r in (6, 2, 7, 3, 5, 4, 1)]
    at_rim = outer == 1
    rim_box = rem(box + boxes + 2 * top - 1, boxes)
    rim_devices = [rim_box * MEMBERS + 6 - 6 * top + t for t in range(2)]
    quad = div(member, 4)
    quad_device = rem(box + boxes + 2 * quad - 1, boxes) * MEMBERS + mirror
    early = jnp.where(z == 0, 1, 0)
    for target in mates + [left_device, right_device, left_box, right_box]:
        greet(target)
    @pl.when(at_rim)
    def _():
        for target in rim_devices:
            greet(target)

    lanes = lax.broadcasted_iota(jnp.int32, (1, 128), 1)
    index = lax.broadcasted_iota(jnp.int32, (512, 128), 0)
    placed = (index == (lanes - 64 - 8 * member) * 64).astype(f32).astype(bf16)
    picks = (lax.broadcasted_iota(jnp.int32, (1, 128), 1) & 63) * 2
    every_second = (
        (lax.broadcasted_iota(jnp.int32, (128, 128), 0) == picks).astype(f32).astype(bf16)
    )
    for copy in loading:
        copy.wait()
    points = jnp.concatenate([coords[...], jnp.zeros((5, OWN), f32)], axis=0)
    s0 = [
        jnp.concatenate(
            [points[:, 512 * p : 512 * p + 64], points[:, 512 * p + 256 : 512 * p + 320]], axis=1
        )
        for p in range(4)
    ]
    s6 = pick(jnp.concatenate(s0, axis=1), placed)

    maps = [(map_high.at[level], map_low.at[level]) for level in range(6)]

    def set_map(level):
        once = transfer[level]
        map_high[level], map_low[level] = split(jnp.concatenate([once, once], axis=1))

    for level in range(2):
        set_map(level)
    slots = lax.broadcasted_iota(jnp.int32, (COLS, LEAF), 1)
    live = []
    for leaf in range(LEAVES):
        part = loads[:, leaf * LEAF : (leaf + 1) * LEAF].astype(f32)
        live.append(jnp.where(slots < occ[leaf], part, 0.0))
    c0 = []
    for p in range(4):
        two = jnp.concatenate([live[2 * p], live[2 * p + 1]], axis=0).astype(bf16)
        rows = lax.dot_general(
            two, basis[128 * p : 128 * p + 128, :], NT, preferred_element_type=f32
        )
        c0.append(jnp.where(low, rows[:8], rows[8:]))
    c1 = raise_coef(c0, maps[0])
    c2 = raise_coef(c1, maps[1])
    def factor(level, at):
        return transfer[level, pl.ds(pl.multiple_of(64 * at, 64), 64), :]

    map_34 = mm(transfer[2], split(factor(3, core)), NN)
    wide = jnp.concatenate([factor(5, quad), jnp.zeros((64, 64), f32)], axis=1)
    map_56 = mm(factor(4, rem(y, 2)), split(wide), NN)
    map_6 = mm(map_34, split(map_56), NN)
    u_buf[member] = mm(c2[0], split(map_6), NN) + s6
    path_map[...] = map_6

    def set_field():
        field[0, :, LEAF : LEAF + OWN] = points
        for leaf in range(LEAVES):
            field[1, :, (leaf + 1) * LEAF : (leaf + 2) * LEAF] = live[leaf]
        for at in range(0, OWN, 128):
            column[at : at + 128, :] = points[:, at : at + 128].T
        near[...] = jnp.zeros_like(near)

    def fill_tile(tile, row, col, width):
        sx = field[0, 0:1, pl.ds(col, width)]
        sy = field[0, 1:2, pl.ds(col, width)]
        sz = field[0, 2:3, pl.ds(col, width)]
        for at in range(0, LEAF, 16):
            rows = column[pl.ds(row + at, 16), :]
            tile[at : at + 16, 0:width] = phi(
                rows[:, 0:1], rows[:, 1:2], rows[:, 2:3], sx, sy, sz, near_scale
            ).astype(bf16)

    def near_leaf(tile, row):
        col = row + LEAF
        fill_tile(tile, row, col, 2 * LEAF)
        loads_two = field[1, :, pl.ds(col, 2 * LEAF)].astype(bf16)
        this = lax.dot_general(loads_two, tile[...], NT, preferred_element_type=f32)
        after = lax.dot_general(
            loads_two[:, :LEAF], tile[:, LEAF:], NN, preferred_element_type=f32
        )
        return this, after

    def near_two(row):
        first, second_part = near_leaf(tile_a, row)
        second, third = near_leaf(tile_b, row + LEAF)
        near[:, pl.ds(row, LEAF)] += first
        near[:, pl.ds(row + LEAF, LEAF)] += second_part + second
        near[:, pl.ds(row + 2 * LEAF, LEAF)] += third

    def near_step(pair, carry):
        near_two(pl.multiple_of(pair * (2 * LEAF), 2 * LEAF))
        return carry

    def side(block, at):
        lanes = jnp.where(low_half((1, 128)), 0, 1)
        return jnp.where(lanes == at, block, 0.0)

    def set_chain(levels, into):
        for at, (pairs, skels) in enumerate(levels):
            first = (1, 7, 11)[at]
            for p in range(len(pairs)):
                into[first + p, 0] = pairs[p]
                into[first + p, 1] = skels[p]

    def set_inner():
        lax.fori_loop(0, 3, near_step, 0)
        row = (LEAVES - 2) * LEAF
        this, after = near_leaf(tile_a, row)
        fill_tile(tile_c, row + LEAF, row + 2 * LEAF, LEAF)
        own = field[1, :, row + 2 * LEAF : row + 3 * LEAF].astype(bf16)
        after += lax.dot_general(own, tile_c[...], NT, preferred_element_type=f32)
        near[:, row : row + LEAF] += this
        near[:, row + LEAF : row + 2 * LEAF] += after
        for slot in (2, 3):
            local[slot - 1] = cousins(chain, slot)

    def set_edges():
        s1 = raise_skel(s0, every_second)
        s2 = raise_skel(s1, every_second)

        set_chain([(c0, s0), (c1, s1), (c2, s2)], chain)
        for at, (pairs, skels) in enumerate([(c0, s0), (c1, s1), (c2, s2)]):
            edge_send[0, at, 0] = pairs[-1]
            edge_send[0, at, 1] = skels[-1]
            edge_send[1, at, 0] = pairs[0]
            edge_send[1, at, 1] = skels[0]
    def mm_basis(block, p):
        high, rest = split(block)
        rows = block.shape[0]
        both = lax.dot_general(
            jnp.concatenate([high.astype(f32), rest.astype(f32)], axis=0).astype(bf16),
            basis[128 * p : 128 * p + 128, :],
            NN,
            preferred_element_type=f32,
        )
        return both[:rows] + both[rows:]

    def set_leaf_paths():
        x2 = jnp.concatenate([path_map[...].T[:64], transfer[2].T], axis=0)
        x0 = lower(lower([x2], maps[1]), maps[0])
        for p in range(4):
            two = jnp.concatenate([side(x0[p], 0), side(x0[p], 1)], axis=0)
            to_points = mm_basis(two, p)
            for t in range(2):
                at = (2 * p + t) * LEAF
                high, rest = split(to_points[128 * t : 128 * t + 128])
                point_high[:, at : at + LEAF] = high
                point_low[:, at : at + LEAF] = rest

    @pl.when(early == 1)
    def _():
        set_field()
        set_edges()
        set_inner()

    pl.semaphore_wait(
        barrier, MEMBERS - 1 + 4 + 3 + outer + 2 - own_sender.astype(jnp.int32) + 2 * outer
    )

    def tell(target):
        pl.semaphore_signal(ready, inc=1, device_id=(target,), device_id_type=MESH)

    tell(senders[1])

    @pl.when(jnp.logical_not(own_sender))
    def _():
        tell(senders[0])

    def remote(src, dst, send_sem, recv_sem, target):
        return pltpu.make_async_remote_copy(
            src_ref=src,
            dst_ref=dst,
            send_sem=send_sem,
            recv_sem=recv_sem,
            device_id=(target,),
            device_id_type=MESH,
        )

    def send(*ends):
        copy = remote(*ends)
        copy.start()
        return copy

    def wait_all(ref, semaphore):
        pltpu.make_async_copy(ref, ref, semaphore).wait()

    for mate in mates:
        send(u_buf.at[member], u_buf.at[member], u_send_sem, u_recv_sem, mate)

    set_map(2)
    every_eighth = (index == (lanes & 63) * 8).astype(f32).astype(bf16)
    s3 = pick(jnp.concatenate(s0, axis=1), every_eighth)
    c3 = raise_coef(c2, maps[2])[0]
    g_buf[member] = jnp.where(half == core, c3, s3)
    for mate in mates:
        send(g_buf.at[member], g_buf.at[member], g_send_sem, g_recv_sem, mate)

    rim_copies = [
        pltpu.make_async_remote_copy(
            src_ref=g_buf.at[member],
            dst_ref=rim_recv.at[core],
            send_sem=rim_send_sem.at[t],
            recv_sem=rim_recv_sem.at[core],
            device_id=(rim_devices[t],),
            device_id_type=MESH,
        )
        for t in range(2)
    ]

    @pl.when(at_rim)
    def _():
        for copy in rim_copies:
            copy.start()

    @pl.when(early == 0)
    def _():
        set_field()

    last = LEAF * LEAVES
    near_copies = [
        send(
            field.at[:, :, last : last + LEAF],
            field.at[:, :, 0:LEAF],
            near_send_sem.at[0],
            near_recv_sem.at[0],
            right_device,
        ),
        send(
            field.at[:, :, LEAF : 2 * LEAF],
            field.at[:, :, last + LEAF : last + 2 * LEAF],
            near_send_sem.at[1],
            near_recv_sem.at[1],
            left_device,
        ),
    ]

    edge_copies = [
        remote(
            edge_send.at[side],
            edge_recv.at[side],
            edge_send_sem.at[side],
            edge_recv_sem.at[side],
            (right_device, left_device)[side],
        )
        for side in range(2)
    ]

    @pl.when(early == 0)
    def _():
        set_edges()

    for copy in edge_copies:
        copy.start()

    set_map(3)
    set_map(4)

    @pl.when(early == 1)
    def _():
        set_leaf_paths()

    wait_all(u_buf.at[pl.ds(0, MEMBERS - 1)], u_recv_sem)
    parts = [u_buf[at] for at in range(MEMBERS)]
    while len(parts) > 1:
        parts = [a + b for a, b in zip(parts[0::2], parts[1::2])]
    top_record = parts[0]
    swapped_record = pltpu.roll(top_record, 64, 1)
    far_send[0] = top_record
    far_send[1] = swapped_record

    @pl.when(alone)
    def _():
        far_buf[0] = far_send[0]

    def set_ends(ends, into, at_start, at_end):
        for level in range(3):
            before, after = (0, 6, 10)[level], (5, 9, 12)[level]
            into[before, 0] = jnp.where(at_start, 0.0, ends[0, level, 0])
            into[before, 1] = ends[0, level, 1]
            into[after, 0] = jnp.where(at_end, 0.0, ends[1, level, 0])
            into[after, 1] = ends[1, level, 1]

    def near_end(tile, row, col):
        fill_tile(tile, row, col, LEAF)
        near[:, row : row + LEAF] += lax.dot_general(
            field[1, :, col : col + LEAF].astype(bf16),
            tile[:, 0:LEAF],
            NT,
            preferred_element_type=f32,
        )

    def finish_ends():
        for copy in near_copies:
            copy.wait_recv()

        @pl.when(device == 0)
        def _():
            field[1, :, 0:LEAF] = jnp.zeros((COLS, LEAF), f32)

        @pl.when(device == total - 1)
        def _():
            field[1, :, last + LEAF : last + 2 * LEAF] = jnp.zeros((COLS, LEAF), f32)

        near_end(tile_c, 0, 0)
        near_end(tile_a, last - LEAF, last + LEAF)

        for copy in edge_copies:
            copy.wait_recv()
        set_ends(edge_recv, chain, device == 0, device == total - 1)
        for at, slot in [(0, 1), (3, 4), (4, 7), (5, 8), (6, 11)]:
            local[at] = cousins(chain, slot)

    @pl.when(early == 1)
    def _():
        finish_ends()

    pl.semaphore_wait(ready, 2 - own_sender.astype(jnp.int32))
    for k in far_order:
        send(
            far_send.at[k % 2], far_buf.at[k], far_send_sem.at[1], far_recv_sem.at[1], far_to[k]
        )
    first_far = pltpu.make_async_remote_copy(
        src_ref=far_send.at[0],
        dst_ref=far_buf.at[0],
        send_sem=far_send_sem.at[0],
        recv_sem=far_recv_sem.at[0],
        device_id=(far_to[0],),
        device_id_type=MESH,
    )

    @pl.when(jnp.logical_not(alone))
    def _():
        first_far.start()

    wait_all(g_buf.at[pl.ds(0, MEMBERS - 1)], g_recv_sem)
    c3s, s3s = [], []
    for p in range(4):
        even, odd = g_buf[2 * p], g_buf[2 * p + 1]
        c3s.append(jnp.where(low, even, odd))
        s3s.append(pltpu.roll(jnp.where(low, odd, even), 64, 1))
    c4s, s4s = raise_coef(c3s, maps[3]), raise_skel(s3s, every_second)
    c5s, s5s = raise_coef(c4s, maps[4]), raise_skel(s4s, every_second)
    set_chain([(c3s, s3s), (c4s, s4s), (c5s, s5s)], g_chain)
    for at in range(2):
        bound_send[at, 0] = c5s[0]
        bound_send[at, 1] = s5s[0] + pltpu.roll(s4s[1 - at], 3, 0)
    bound_copies = [
        send(
            bound_send.at[side],
            bound_recv.at[side],
            bound_send_sem.at[side],
            bound_recv_sem.at[side],
            (right_box, left_box)[side],
        )
        for side in range(2)
    ]
    bound_copies.append(
        send(
            g_chain.at[7 + quad, 0],
            quad_recv,
            bound_send_sem.at[2],
            bound_recv_sem.at[2],
            quad_device,
        )
    )

    @pl.when(early == 0)
    def _():
        set_inner()
        set_leaf_paths()
        finish_ends()

    top_column = swapped_record.T[:64]
    tx, ty, tz = top_column[:, 0:1], top_column[:, 1:2], top_column[:, 2:3]

    wait_all(far_buf.at[pl.ds(1, strides - 1)], far_recv_sem.at[1])

    @pl.when(jnp.logical_not(alone))
    def _():
        first_far.wait_recv()

    top_coef, top_skel = [], []
    for k in range(0, strides, 2):
        halves = []
        for at in (k, k + 1):
            apart = far_from[at] - box
            counts = jnp.logical_or(apart >= 2, apart <= -2)
            halves.append((far_buf[at], counts))
        (one, one_counts), (two, two_counts) = halves
        coef = jnp.where(low, jnp.where(one_counts, one, 0.0), jnp.where(two_counts, two, 0.0))
        top_coef.append(pltpu.roll(coef, 64, 1))
        top_skel.append(jnp.where(low, two, one))
    top_tile = jnp.concatenate(
        [phi(tx, ty, tz, s[0:1], s[1:2], s[2:3], far_scale) for s in top_skel], axis=1
    )
    top = mm(jnp.concatenate(top_coef, axis=1), split(top_tile), NT)
    part_buf[member] = jnp.concatenate([top, jnp.zeros((8, 64), f32)], axis=1)
    for at in range(MEMBERS - 1):
        mate = box * MEMBERS + at + jnp.where(member <= at, 1, 0)
        send(part_buf.at[member], part_buf.at[member], part_send_sem, part_recv_sem, mate)

    wait_all(u_buf.at[pl.ds(0, MEMBERS - 1)], u_send_sem)
    wait_all(g_buf.at[pl.ds(0, MEMBERS - 1)], g_send_sem)
    wait_all(far_buf.at[pl.ds(1, strides - 1)], far_send_sem.at[1])
    for copy in near_copies + edge_copies + bound_copies:
        copy.wait_send()

    @pl.when(jnp.logical_not(alone))
    def _():
        first_far.wait_send()

    for copy in bound_copies:
        copy.wait_recv()
    at_start, at_end = box == 0, box == boxes - 1
    outside = jnp.logical_or(
        jnp.logical_and(quad == 0, at_start), jnp.logical_and(quad == 1, at_end)
    )
    start_skel, end_skel = bound_recv[0, 1], bound_recv[1, 1]
    g_chain[10, 0] = jnp.where(at_start, 0.0, bound_recv[0, 0])
    g_chain[10, 1] = start_skel
    g_chain[12, 0] = jnp.where(at_end, 0.0, bound_recv[1, 0])
    g_chain[12, 1] = end_skel
    quad_coef = jnp.where(outside, 0.0, quad_recv[...])
    g_chain[6, 0] = quad_coef
    g_chain[6, 1] = pltpu.roll(start_skel, 5, 0)
    g_chain[9, 0] = quad_coef
    g_chain[9, 1] = pltpu.roll(end_skel, 5, 0)

    @pl.when(at_rim)
    def _():
        for copy in rim_copies:
            copy.wait_send()
        for t in range(2):
            pltpu.make_async_remote_copy(
                src_ref=g_buf.at[member],
                dst_ref=rim_recv.at[t],
                send_sem=rim_send_sem.at[t],
                recv_sem=rim_recv_sem.at[t],
                device_id=(rim_devices[t],),
                device_id_type=MESH,
            ).wait_recv()
        even, odd = rim_recv[0], rim_recv[1]
        rim_coef = jnp.where(outside, 0.0, jnp.where(low, even, odd))
        rim_skel = pltpu.roll(jnp.where(low, odd, even), 64, 1)
        for slot in (0, 5):
            g_chain[slot, 0] = rim_coef
            g_chain[slot, 1] = rim_skel

    local3 = cousins(g_chain, 1 + y)
    local4 = cousins(g_chain, 7 + quad)
    local5 = cousins(g_chain, 11)
    y2 = local[6]
    y1 = [x + local[4 + at] for at, x in enumerate(lower([y2], maps[1]))]
    y0 = [x + local[at] for at, x in enumerate(lower(y1, maps[0]))]
    for p in range(4):
        rows = mm_basis(jnp.concatenate([side(y0[p], 0), side(y0[p], 1)], axis=0), p)
        for t in range(2):
            at = (2 * p + t) * LEAF
            near[:, at : at + LEAF] += rows[8 * t : 8 * t + 8]
    y4 = local4 + mm(side(local5, quad), maps[4], NT)
    y3 = local3 + mm(side(y4, rem(y, 2)), maps[3], NT)
    y3 = jnp.where(core == 1, y3, pltpu.roll(y3, 64, 1))

    wait_all(part_buf.at[pl.ds(0, MEMBERS - 1)], part_recv_sem)
    parts = [part_buf[at] for at in range(MEMBERS)]
    while len(parts) > 1:
        parts = [a + b for a, b in zip(parts[0::2], parts[1::2])]
    d6 = parts[0]
    d63 = jnp.where(low, d6, y3)
    total_field = near[:, 0:OWN] + mm(d63, (point_high, point_low), NN)
    for leaf in range(LEAVES):
        at = leaf * LEAF
        out_ref[:, at : at + LEAF] = jnp.where(
            slots < occ[leaf], total_field[:, at : at + LEAF], 0.0
        )

    wait_all(part_buf.at[pl.ds(0, MEMBERS - 1)], part_send_sem)


def body(boxes, across, coords, loads, occupancy, basis, transfer):
    strides = boxes // MEMBERS
    hbm = pl.BlockSpec(memory_space=pl.ANY)
    dma = pltpu.SemaphoreType.DMA
    return pl.pallas_call(
        functools.partial(kernel, boxes, across),
        out_shape=jax.ShapeDtypeStruct((COLS, OWN), f32),
        in_specs=[hbm] * 5,
        out_specs=pl.BlockSpec(memory_space=pltpu.VMEM),
        scratch_shapes=[
            pltpu.VMEM((3, OWN), f32),
            pltpu.VMEM((COLS, OWN), bf16),
            pltpu.SMEM((LEAVES,), jnp.int32),
            pltpu.VMEM((LEAVES * 64, LEAF), bf16),
            pltpu.VMEM((6, 128, 64), f32),
            pltpu.VMEM((6, 128, 128), bf16),
            pltpu.VMEM((6, 128, 128), bf16),
            pltpu.VMEM((128, 128), f32),
            pltpu.VMEM((2, 8, OWN + 2 * LEAF), f32),
            pltpu.VMEM((OWN, 8), f32),
            pltpu.VMEM((128, OWN), bf16),
            pltpu.VMEM((128, OWN), bf16),
            pltpu.VMEM((COLS, OWN + LEAF), f32),
            pltpu.VMEM((LEAF, 2 * LEAF), bf16),
            pltpu.VMEM((LEAF, 2 * LEAF), bf16),
            pltpu.VMEM((LEAF, LEAF), bf16),
            pltpu.VMEM((13, 2, 8, 128), f32),
            pltpu.VMEM((13, 2, 8, 128), f32),
            pltpu.VMEM((7, 8, 128), f32),
            pltpu.VMEM((2, 3, 2, 8, 128), f32),
            pltpu.VMEM((2, 3, 2, 8, 128), f32),
            pltpu.VMEM((MEMBERS, 8, 128), f32),
            pltpu.VMEM((MEMBERS, 8, 128), f32),
            pltpu.VMEM((2, 2, 8, 128), f32),
            pltpu.VMEM((2, 2, 8, 128), f32),
            pltpu.VMEM((8, 128), f32),
            pltpu.VMEM((2, 8, 128), f32),
            pltpu.VMEM((2, 8, 128), f32),
            pltpu.VMEM((strides, 8, 128), f32),
            pltpu.VMEM((MEMBERS, 8, 128), f32),
            dma((5,)),
            dma((2,)),
            dma((2,)),
            dma((2,)),
            dma((2,)),
            dma,
            dma,
            dma,
            dma,
            dma((3,)),
            dma((3,)),
            dma((2,)),
            dma((2,)),
            dma((2,)),
            dma((2,)),
            dma,
            dma,
            pltpu.SemaphoreType.REGULAR,
        ],
        compiler_params=pltpu.CompilerParams(
            collective_id=0, has_side_effects=True, vmem_limit_bytes=32 * 1024 * 1024
        ),
    )(
        *[
            pltpu.with_memory_space_constraint(x, pltpu.HBM)
            for x in (
                coords,
                loads,
                occupancy,
                basis.reshape(LEAVES * 64, LEAF),
                transfer.reshape(6, 128, 64),
            )
        ]
    )


def solution(mesh):
    boxes = mesh.shape["box"] // MEMBERS
    return jax.shard_map(
        functools.partial(body, boxes, 4),
        mesh=mesh,
        in_specs=(P(None, "box"), P(None, "box"), P("box"), P("box", None, None), P()),
        out_specs=P(None, "box"),
        check_vma=False,
    )
```

```python
import functools

import jax
import jax.numpy as jnp
from jax import lax
from jax.experimental import pallas as pl
from jax.experimental.pallas import tpu as pltpu
from jax.sharding import PartitionSpec as P

LEAF = 256
COLS = 8
LEAVES = 8
MEMBERS = 8
OWN = LEAF * LEAVES

f32 = jnp.float32
bf16 = jnp.bfloat16
soften = 0.0001
near_scale = 0.0625
far_scale = 0.125
NN = (((1,), (0,)), ((), ()))
NT = (((1,), (1,)), ((), ()))
MESH = pl.DeviceIdType.MESH


def div(a, b):
    return lax.div(a, jnp.int32(b))


def rem(a, b):
    return lax.rem(a, jnp.int32(b))


def phi(tx, ty, tz, sx, sy, sz, scale):
    dx = tx - sx
    dy = ty - sy
    dz = tz - sz
    r2 = dx * dx + dy * dy + dz * dz
    return (r2 * (0.5 * scale)) * jnp.log(r2 + soften)


def split(x):
    high = x.astype(bf16)
    return high, (x - high.astype(f32)).astype(bf16)


def mm(a, b, dims):
    rows = a.shape[0]
    high = a.astype(bf16).astype(f32)
    stacked = jnp.concatenate([high, a - high], axis=0).astype(bf16)
    both = lax.dot_general(stacked, b[0][...], dims, preferred_element_type=f32)
    low = lax.dot_general(stacked[:rows], b[1][...], dims, preferred_element_type=f32)
    return both[:rows] + (both[rows:] + low)


def low_half(shape):
    return lax.broadcasted_iota(jnp.int32, shape, len(shape) - 1) < 64


def merge(rows):
    count = rows.shape[0] // 16
    low = low_half((8, 128))
    return [
        jnp.where(low, rows[16 * i : 16 * i + 8], rows[16 * i + 8 : 16 * i + 16])
        for i in range(count)
    ]


def raise_coef(pairs, level_map):
    rows = mm(jnp.concatenate(pairs, axis=0), level_map, NN)
    return merge(rows) if len(pairs) > 1 else [rows]


def pick(x, entries):
    rows = x.shape[0]
    a = x.astype(bf16).astype(f32)
    b = (x - a).astype(bf16).astype(f32)
    c = (x - a) - b
    stacked = jnp.concatenate([a, b, c], axis=0).astype(bf16)
    picked = lax.dot_general(stacked, entries, NN, preferred_element_type=f32)
    return picked[:rows] + picked[rows : 2 * rows] + picked[2 * rows :]


def raise_skel(pairs, every_second):
    rows_up = pick(jnp.concatenate(pairs, axis=0), every_second)
    return merge(rows_up) if len(pairs) > 1 else [rows_up]


def cousins(chain, slot):
    low = low_half((8, 128))
    column = chain[slot, 1].T
    tx, ty, tz = column[:, 0:1], column[:, 1:2], column[:, 2:3]
    before, after = chain[slot - 1, 0], chain[slot + 1, 0]
    tiles = []
    for skel in (chain[slot - 1, 1], chain[slot + 1, 1]):
        tiles.append(phi(tx, ty, tz, skel[0:1], skel[1:2], skel[2:3], far_scale))
    tile = jnp.concatenate(tiles, axis=1)
    even = jnp.concatenate([jnp.where(low, before, 0.0), after], axis=1)
    odd = jnp.concatenate([before, jnp.where(low, 0.0, after)], axis=1)
    rows = mm(jnp.concatenate([even, odd], axis=0), split(tile), NT)
    return jnp.where(low, rows[:8], rows[8:])


def lower(pairs, level_map):
    height = pairs[0].shape[0]
    low = low_half((height, 128))
    stacked = []
    for pair in pairs:
        stacked += [jnp.where(low, pair, 0.0), jnp.where(low, 0.0, pair)]
    rows = mm(jnp.concatenate(stacked, axis=0), level_map, NT)
    return [rows[height * i : height * (i + 1)] for i in range(2 * len(pairs))]


def kernel(
    boxes,
    across,
    coords_hbm,
    loads_hbm,
    occ_hbm,
    basis_hbm,
    transfer_hbm,
    out_ref,
    coords,
    loads,
    occ,
    basis,
    transfer,
    map_high,
    map_low,
    path_map,
    field,
    column,
    leaf_high,
    leaf_low,
    near,
    tile_a,
    tile_b,
    tile_c,
    chain,
    g_chain,
    local,
    edge_send,
    edge_recv,
    u_buf,
    g_buf,
    bound_send,
    bound_recv,
    quad_recv,
    rim_recv,
    far_send,
    far_buf,
    part_buf,
    load_sem,
    near_send_sem,
    near_recv_sem,
    edge_send_sem,
    edge_recv_sem,
    u_send_sem,
    u_recv_sem,
    g_send_sem,
    g_recv_sem,
    bound_send_sem,
    bound_recv_sem,
    rim_send_sem,
    rim_recv_sem,
    far_send_sem,
    far_recv_sem,
    part_send_sem,
    part_recv_sem,
    ready,
):
    loading = [
        pltpu.make_async_copy(src, dst, load_sem.at[at])
        for at, (src, dst) in enumerate(
            [
                (coords_hbm, coords),
                (transfer_hbm, transfer),
                (loads_hbm, loads),
                (occ_hbm, occ),
                (basis_hbm, basis),
            ]
        )
    ]
    for copy in loading:
        copy.start()

    device = lax.axis_index("box")
    total = boxes * MEMBERS
    strides = boxes // MEMBERS
    depth = boxes // (2 * across)
    box, member = div(device, MEMBERS), rem(device, MEMBERS)
    x, z, y_half = div(box, 2 * depth), rem(div(box, 2), depth), rem(box, 2)
    y, core = div(member, 2), rem(member, 2)
    low = low_half((8, 128))
    half = jnp.where(low, 0, 1)

    top = jnp.where(y == 3, 1, 0)
    outer = jnp.where(y == 0, 1, top)
    side_to = jnp.where(outer == 1, top, 2 - y)
    side_from = jnp.where(outer == 1, 1 - top, 2 - y)
    far_half = jnp.where(outer == 1, 1 - y_half, y_half)
    z_core = rem(div(z, 2), 2)
    far_member = 2 * jnp.where(outer == 1, 3 - y, y) + z_core
    z_high, z_low = div(z, 4), rem(z, 2)
    far_x = [rem(x + dx, across) for dx in range(across)]
    far_steps = [(dx, turn) for dx in range(across) for turn in range(2)]

    def far_box(side, dx, turn):
        far_z = 4 * rem(side + z_high, 2) + 2 * core + (1 - z_low if turn else z_low)
        return (far_x[dx % across] * depth + far_z) * 2 + far_half

    far_to = [far_box(side_to, dx, turn) * MEMBERS + far_member for dx, turn in far_steps]
    far_from = [far_box(side_from, -dx, turn) for dx, turn in far_steps]
    alone = jnp.logical_and(jnp.logical_and(outer == 0, side_to == 0), core == z_core)

    barrier = pltpu.get_barrier_semaphore()

    def greet(target):
        pl.semaphore_signal(barrier, inc=1, device_id=(target,), device_id_type=MESH)

    far_order = sorted(range(1, strides), key=lambda k: abs(far_steps[k][0] - across // 2))
    place = 2 * y + z_core
    relay_z = [4 * rem(side_to + z_high, 2) + 2 * core + at for at in (z_low, 1 - z_low)]
    to_relay = [((x * depth + at) * 2 + y_half) * MEMBERS + place for at in relay_z]
    senders = to_relay
    from_relay = [
        ((at * depth + z) * 2 + far_half) * MEMBERS + far_member - z_core + core for at in far_x
    ]
    own_sender = jnp.logical_and(side_to == 0, core == z_core)

    greet(to_relay[1])
    for dx in (2, 1, 3):
        greet(from_relay[dx])

    @pl.when(jnp.logical_not(own_sender))
    def _():
        greet(to_relay[0])

    @pl.when(outer == 1)
    def _():
        greet(from_relay[0])

    left_device = rem(device + total - 1, total)
    right_device = rem(device + 1, total)
    mirror = 2 * (3 - y) + core
    left_box = rem(box + boxes - 1, boxes) * MEMBERS + mirror
    right_box = rem(box + 1, boxes) * MEMBERS + mirror
    mates = [box * MEMBERS + rem(member + r, MEMBERS) for r in (6, 2, 7, 3, 5, 4, 1)]
    at_rim = outer == 1
    rim_box = rem(box + boxes + 2 * top - 1, boxes)
    rim_devices = [rim_box * MEMBERS + 6 - 6 * top + t for t in range(2)]
    quad = div(member, 4)
    quad_device = rem(box + boxes + 2 * quad - 1, boxes) * MEMBERS + mirror
    early = jnp.where(z == 0, 1, 0)
    ahead = 2
    for target in mates + [left_device, right_device, left_box, right_box]:
        greet(target)
    @pl.when(at_rim)
    def _():
        for target in rim_devices:
            greet(target)

    lanes = lax.broadcasted_iota(jnp.int32, (1, 128), 1)
    index = lax.broadcasted_iota(jnp.int32, (512, 128), 0)
    placed = (index == (lanes - 64 - 8 * member) * 64).astype(f32).astype(bf16)
    picks = (lax.broadcasted_iota(jnp.int32, (1, 128), 1) & 63) * 2
    every_second = (
        (lax.broadcasted_iota(jnp.int32, (128, 128), 0) == picks).astype(f32).astype(bf16)
    )
    for copy in loading:
        copy.wait()
    points = jnp.concatenate([coords[...], jnp.zeros((5, OWN), f32)], axis=0)
    s0 = [
        jnp.concatenate(
            [points[:, 512 * p : 512 * p + 64], points[:, 512 * p + 256 : 512 * p + 320]], axis=1
        )
        for p in range(4)
    ]
    s6 = pick(jnp.concatenate(s0, axis=1), placed)

    maps = [(map_high.at[level], map_low.at[level]) for level in range(6)]

    def set_map(level):
        once = transfer[level]
        map_high[level], map_low[level] = split(jnp.concatenate([once, once], axis=1))

    for level in range(2):
        set_map(level)
    slots = lax.broadcasted_iota(jnp.int32, (COLS, LEAF), 1)
    live = []
    for leaf in range(LEAVES):
        part = loads[:, leaf * LEAF : (leaf + 1) * LEAF].astype(f32)
        live.append(jnp.where(slots < occ[leaf], part, 0.0))
    c0 = []
    for p in range(4):
        two = jnp.concatenate([live[2 * p], live[2 * p + 1]], axis=0).astype(bf16)
        rows = lax.dot_general(
            two, basis[128 * p : 128 * p + 128, :], NT, preferred_element_type=f32
        )
        c0.append(jnp.where(low, rows[:8], rows[8:]))
    c1 = raise_coef(c0, maps[0])
    c2 = raise_coef(c1, maps[1])
    def factor(level, at):
        return transfer[level, pl.ds(pl.multiple_of(64 * at, 64), 64), :]

    map_34 = mm(transfer[2], split(factor(3, core)), NN)
    wide = jnp.concatenate([factor(5, quad), jnp.zeros((64, 64), f32)], axis=1)
    map_56 = mm(factor(4, rem(y, 2)), split(wide), NN)
    map_6 = mm(map_34, split(map_56), NN)
    u_buf[member] = mm(c2[0], split(map_6), NN) + s6
    path_map[...] = map_6

    def set_field():
        field[0, :, LEAF : LEAF + OWN] = points
        for leaf in range(LEAVES):
            field[1, :, (leaf + 1) * LEAF : (leaf + 2) * LEAF] = live[leaf]
        for at in range(0, OWN, 128):
            column[at : at + 128, :] = points[:, at : at + 128].T
        near[...] = jnp.zeros_like(near)

    def fill_tile(tile, row, col, width):
        sx = field[0, 0:1, pl.ds(col, width)]
        sy = field[0, 1:2, pl.ds(col, width)]
        sz = field[0, 2:3, pl.ds(col, width)]
        for at in range(0, LEAF, 16):
            rows = column[pl.ds(row + at, 16), :]
            tile[at : at + 16, 0:width] = phi(
                rows[:, 0:1], rows[:, 1:2], rows[:, 2:3], sx, sy, sz, near_scale
            ).astype(bf16)

    def near_leaf(tile, row):
        col = row + LEAF
        fill_tile(tile, row, col, 2 * LEAF)
        loads_two = field[1, :, pl.ds(col, 2 * LEAF)].astype(bf16)
        this = lax.dot_general(loads_two, tile[...], NT, preferred_element_type=f32)
        after = lax.dot_general(
            loads_two[:, :LEAF], tile[:, LEAF:], NN, preferred_element_type=f32
        )
        return this, after

    def near_two(row):
        first, second_part = near_leaf(tile_a, row)
        second, third = near_leaf(tile_b, row + LEAF)
        near[:, pl.ds(row, LEAF)] += first
        near[:, pl.ds(row + LEAF, LEAF)] += second_part + second
        near[:, pl.ds(row + 2 * LEAF, LEAF)] += third

    def near_step(pair, carry):
        near_two(pl.multiple_of(pair * (2 * LEAF), 2 * LEAF))
        return carry

    def side(block, at):
        lanes = jnp.where(low_half((1, 128)), 0, 1)
        return jnp.where(lanes == at, block, 0.0)

    def set_chain(levels, into):
        for at, (pairs, skels) in enumerate(levels):
            first = (1, 7, 11)[at]
            for p in range(len(pairs)):
                into[first + p, 0] = pairs[p]
                into[first + p, 1] = skels[p]

    def set_inner():
        row = (LEAVES - 2) * LEAF
        this, after = near_leaf(tile_a, row)
        fill_tile(tile_c, row + LEAF, row + 2 * LEAF, LEAF)
        own = field[1, :, row + 2 * LEAF : row + 3 * LEAF].astype(bf16)
        after += lax.dot_general(own, tile_c[...], NT, preferred_element_type=f32)
        near[:, row : row + LEAF] += this
        near[:, row + LEAF : row + 2 * LEAF] += after
        for slot in (2, 3):
            local[slot - 1] = cousins(chain, slot)

    def set_edges():
        s1 = raise_skel(s0, every_second)
        s2 = raise_skel(s1, every_second)

        set_chain([(c0, s0), (c1, s1), (c2, s2)], chain)
        for at, (pairs, skels) in enumerate([(c0, s0), (c1, s1), (c2, s2)]):
            edge_send[0, at, 0] = pairs[-1]
            edge_send[0, at, 1] = skels[-1]
            edge_send[1, at, 0] = pairs[0]
            edge_send[1, at, 1] = skels[0]
    def set_leaf_paths():
        x2 = jnp.concatenate([path_map[...].T[:64], transfer[2].T], axis=0)
        x0 = lower(lower([x2], maps[1]), maps[0])
        leaf_high[...], leaf_low[...] = split(jnp.concatenate(x0, axis=1))

    @pl.when(early == 1)
    def _():
        set_field()
        lax.fori_loop(0, ahead, near_step, 0)

    pl.semaphore_wait(
        barrier, MEMBERS - 1 + 4 + 3 + outer + 2 - own_sender.astype(jnp.int32) + 2 * outer
    )

    def tell(target):
        pl.semaphore_signal(ready, inc=1, device_id=(target,), device_id_type=MESH)

    tell(senders[1])

    @pl.when(jnp.logical_not(own_sender))
    def _():
        tell(senders[0])

    def remote(src, dst, send_sem, recv_sem, target):
        return pltpu.make_async_remote_copy(
            src_ref=src,
            dst_ref=dst,
            send_sem=send_sem,
            recv_sem=recv_sem,
            device_id=(target,),
            device_id_type=MESH,
        )

    def send(*ends):
        copy = remote(*ends)
        copy.start()
        return copy

    def wait_all(ref, semaphore):
        pltpu.make_async_copy(ref, ref, semaphore).wait()

    for mate in mates:
        send(u_buf.at[member], u_buf.at[member], u_send_sem, u_recv_sem, mate)

    set_map(2)
    every_eighth = (index == (lanes & 63) * 8).astype(f32).astype(bf16)
    s3 = pick(jnp.concatenate(s0, axis=1), every_eighth)
    c3 = raise_coef(c2, maps[2])[0]
    g_buf[member] = jnp.where(half == core, c3, s3)
    for mate in mates:
        send(g_buf.at[member], g_buf.at[member], g_send_sem, g_recv_sem, mate)

    rim_copies = [
        pltpu.make_async_remote_copy(
            src_ref=g_buf.at[member],
            dst_ref=rim_recv.at[core],
            send_sem=rim_send_sem.at[t],
            recv_sem=rim_recv_sem.at[core],
            device_id=(rim_devices[t],),
            device_id_type=MESH,
        )
        for t in range(2)
    ]

    @pl.when(at_rim)
    def _():
        for copy in rim_copies:
            copy.start()

    @pl.when(early == 0)
    def _():
        set_field()

    last = LEAF * LEAVES
    near_copies = [
        send(
            field.at[:, :, last : last + LEAF],
            field.at[:, :, 0:LEAF],
            near_send_sem.at[0],
            near_recv_sem.at[0],
            right_device,
        ),
        send(
            field.at[:, :, LEAF : 2 * LEAF],
            field.at[:, :, last + LEAF : last + 2 * LEAF],
            near_send_sem.at[1],
            near_recv_sem.at[1],
            left_device,
        ),
    ]

    edge_copies = [
        remote(
            edge_send.at[side],
            edge_recv.at[side],
            edge_send_sem.at[side],
            edge_recv_sem.at[side],
            (right_device, left_device)[side],
        )
        for side in range(2)
    ]

    set_edges()
    for copy in edge_copies:
        copy.start()

    set_map(3)
    set_map(4)

    @pl.when(early == 1)
    def _():
        set_leaf_paths()

    wait_all(u_buf.at[pl.ds(0, MEMBERS - 1)], u_recv_sem)
    parts = [u_buf[at] for at in range(MEMBERS)]
    while len(parts) > 1:
        parts = [a + b for a, b in zip(parts[0::2], parts[1::2])]
    top_record = parts[0]
    swapped_record = pltpu.roll(top_record, 64, 1)
    far_send[0] = top_record
    far_send[1] = swapped_record

    @pl.when(alone)
    def _():
        far_buf[0] = far_send[0]

    @pl.when(early == 1)
    def _():
        lax.fori_loop(ahead, 3, near_step, 0)
        set_inner()

    pl.semaphore_wait(ready, 2 - own_sender.astype(jnp.int32))
    for k in far_order:
        send(
            far_send.at[k % 2], far_buf.at[k], far_send_sem.at[1], far_recv_sem.at[1], far_to[k]
        )
    first_far = pltpu.make_async_remote_copy(
        src_ref=far_send.at[0],
        dst_ref=far_buf.at[0],
        send_sem=far_send_sem.at[0],
        recv_sem=far_recv_sem.at[0],
        device_id=(far_to[0],),
        device_id_type=MESH,
    )

    @pl.when(jnp.logical_not(alone))
    def _():
        first_far.start()

    wait_all(g_buf.at[pl.ds(0, MEMBERS - 1)], g_recv_sem)
    c3s, s3s = [], []
    for p in range(4):
        even, odd = g_buf[2 * p], g_buf[2 * p + 1]
        c3s.append(jnp.where(low, even, odd))
        s3s.append(pltpu.roll(jnp.where(low, odd, even), 64, 1))
    c4s, s4s = raise_coef(c3s, maps[3]), raise_skel(s3s, every_second)
    c5s, s5s = raise_coef(c4s, maps[4]), raise_skel(s4s, every_second)
    set_chain([(c3s, s3s), (c4s, s4s), (c5s, s5s)], g_chain)
    for at in range(2):
        bound_send[at, 0] = c5s[0]
        bound_send[at, 1] = s5s[0] + pltpu.roll(s4s[1 - at], 3, 0)
    bound_copies = [
        send(
            bound_send.at[side],
            bound_recv.at[side],
            bound_send_sem.at[side],
            bound_recv_sem.at[side],
            (right_box, left_box)[side],
        )
        for side in range(2)
    ]
    bound_copies.append(
        send(
            g_chain.at[7 + quad, 0],
            quad_recv,
            bound_send_sem.at[2],
            bound_recv_sem.at[2],
            quad_device,
        )
    )

    @pl.when(early == 0)
    def _():
        lax.fori_loop(0, 3, near_step, 0)
        set_inner()
        set_leaf_paths()

    for copy in near_copies:
        copy.wait_recv()

    @pl.when(device == 0)
    def _():
        field[1, :, 0:LEAF] = jnp.zeros((COLS, LEAF), f32)

    @pl.when(device == total - 1)
    def _():
        field[1, :, last + LEAF : last + 2 * LEAF] = jnp.zeros((COLS, LEAF), f32)

    def near_end(tile, row, col):
        fill_tile(tile, row, col, LEAF)
        near[:, row : row + LEAF] += lax.dot_general(
            field[1, :, col : col + LEAF].astype(bf16),
            tile[:, 0:LEAF],
            NT,
            preferred_element_type=f32,
        )

    near_end(tile_c, 0, 0)
    near_end(tile_a, last - LEAF, last + LEAF)

    def set_ends(ends, into, at_start, at_end):
        for level in range(3):
            before, after = (0, 6, 10)[level], (5, 9, 12)[level]
            into[before, 0] = jnp.where(at_start, 0.0, ends[0, level, 0])
            into[before, 1] = ends[0, level, 1]
            into[after, 0] = jnp.where(at_end, 0.0, ends[1, level, 0])
            into[after, 1] = ends[1, level, 1]

    for copy in edge_copies:
        copy.wait_recv()
    set_ends(edge_recv, chain, device == 0, device == total - 1)
    for at, slot in [(0, 1), (3, 4), (4, 7), (5, 8), (6, 11)]:
        local[at] = cousins(chain, slot)

    top_column = swapped_record.T[:64]
    tx, ty, tz = top_column[:, 0:1], top_column[:, 1:2], top_column[:, 2:3]

    wait_all(far_buf.at[pl.ds(1, strides - 1)], far_recv_sem.at[1])

    @pl.when(jnp.logical_not(alone))
    def _():
        first_far.wait_recv()

    top_coef, top_skel = [], []
    for k in range(0, strides, 2):
        halves = []
        for at in (k, k + 1):
            apart = far_from[at] - box
            counts = jnp.logical_or(apart >= 2, apart <= -2)
            halves.append((far_buf[at], counts))
        (one, one_counts), (two, two_counts) = halves
        coef = jnp.where(low, jnp.where(one_counts, one, 0.0), jnp.where(two_counts, two, 0.0))
        top_coef.append(pltpu.roll(coef, 64, 1))
        top_skel.append(jnp.where(low, two, one))
    top_tile = jnp.concatenate(
        [phi(tx, ty, tz, s[0:1], s[1:2], s[2:3], far_scale) for s in top_skel], axis=1
    )
    top = mm(jnp.concatenate(top_coef, axis=1), split(top_tile), NT)
    part_buf[member] = jnp.concatenate([top, jnp.zeros((8, 64), f32)], axis=1)
    for at in range(MEMBERS - 1):
        mate = box * MEMBERS + at + jnp.where(member <= at, 1, 0)
        send(part_buf.at[member], part_buf.at[member], part_send_sem, part_recv_sem, mate)

    wait_all(u_buf.at[pl.ds(0, MEMBERS - 1)], u_send_sem)
    wait_all(g_buf.at[pl.ds(0, MEMBERS - 1)], g_send_sem)
    wait_all(far_buf.at[pl.ds(1, strides - 1)], far_send_sem.at[1])
    for copy in near_copies + edge_copies + bound_copies:
        copy.wait_send()

    @pl.when(jnp.logical_not(alone))
    def _():
        first_far.wait_send()

    for copy in bound_copies:
        copy.wait_recv()
    at_start, at_end = box == 0, box == boxes - 1
    outside = jnp.logical_or(
        jnp.logical_and(quad == 0, at_start), jnp.logical_and(quad == 1, at_end)
    )
    start_skel, end_skel = bound_recv[0, 1], bound_recv[1, 1]
    g_chain[10, 0] = jnp.where(at_start, 0.0, bound_recv[0, 0])
    g_chain[10, 1] = start_skel
    g_chain[12, 0] = jnp.where(at_end, 0.0, bound_recv[1, 0])
    g_chain[12, 1] = end_skel
    quad_coef = jnp.where(outside, 0.0, quad_recv[...])
    g_chain[6, 0] = quad_coef
    g_chain[6, 1] = pltpu.roll(start_skel, 5, 0)
    g_chain[9, 0] = quad_coef
    g_chain[9, 1] = pltpu.roll(end_skel, 5, 0)

    @pl.when(at_rim)
    def _():
        for copy in rim_copies:
            copy.wait_send()
        for t in range(2):
            pltpu.make_async_remote_copy(
                src_ref=g_buf.at[member],
                dst_ref=rim_recv.at[t],
                send_sem=rim_send_sem.at[t],
                recv_sem=rim_recv_sem.at[t],
                device_id=(rim_devices[t],),
                device_id_type=MESH,
            ).wait_recv()
        even, odd = rim_recv[0], rim_recv[1]
        rim_coef = jnp.where(outside, 0.0, jnp.where(low, even, odd))
        rim_skel = pltpu.roll(jnp.where(low, odd, even), 64, 1)
        for slot in (0, 5):
            g_chain[slot, 0] = rim_coef
            g_chain[slot, 1] = rim_skel

    local3 = cousins(g_chain, 1 + y)
    local4 = cousins(g_chain, 7 + quad)
    local5 = cousins(g_chain, 11)
    y2 = local[6]
    y1 = [x + local[4 + at] for at, x in enumerate(lower([y2], maps[1]))]
    y0 = [x + local[at] for at, x in enumerate(lower(y1, maps[0]))]
    y4 = local4 + mm(side(local5, quad), maps[4], NT)
    y3 = local3 + mm(side(y4, rem(y, 2)), maps[3], NT)
    y3 = jnp.where(core == 1, y3, pltpu.roll(y3, 64, 1))

    wait_all(part_buf.at[pl.ds(0, MEMBERS - 1)], part_recv_sem)
    parts = [part_buf[at] for at in range(MEMBERS)]
    while len(parts) > 1:
        parts = [a + b for a, b in zip(parts[0::2], parts[1::2])]
    d6 = parts[0]
    d63 = jnp.where(low, d6, y3)
    d0 = jnp.concatenate(y0, axis=1) + mm(d63, (leaf_high, leaf_low), NN)
    for p in range(4):
        pair = d0[:, 128 * p : 128 * p + 128]
        two = jnp.concatenate([jnp.where(low, pair, 0.0), jnp.where(low, 0.0, pair)], axis=0)
        rows = lax.dot_general(
            two.astype(bf16),
            basis[128 * p : 128 * p + 128, :],
            NN,
            preferred_element_type=f32,
        )
        for t in range(2):
            leaf = 2 * p + t
            at = leaf * LEAF
            out_ref[:, at : at + LEAF] = jnp.where(
                slots < occ[leaf], near[:, at : at + LEAF] + rows[8 * t : 8 * t + 8], 0.0
            )

    wait_all(part_buf.at[pl.ds(0, MEMBERS - 1)], part_send_sem)


def body(boxes, across, coords, loads, occupancy, basis, transfer):
    strides = boxes // MEMBERS
    hbm = pl.BlockSpec(memory_space=pl.ANY)
    dma = pltpu.SemaphoreType.DMA
    return pl.pallas_call(
        functools.partial(kernel, boxes, across),
        out_shape=jax.ShapeDtypeStruct((COLS, OWN), f32),
        in_specs=[hbm] * 5,
        out_specs=pl.BlockSpec(memory_space=pltpu.VMEM),
        scratch_shapes=[
            pltpu.VMEM((3, OWN), f32),
            pltpu.VMEM((COLS, OWN), bf16),
            pltpu.SMEM((LEAVES,), jnp.int32),
            pltpu.VMEM((LEAVES * 64, LEAF), bf16),
            pltpu.VMEM((6, 128, 64), f32),
            pltpu.VMEM((6, 128, 128), bf16),
            pltpu.VMEM((6, 128, 128), bf16),
            pltpu.VMEM((128, 128), f32),
            pltpu.VMEM((2, 8, OWN + 2 * LEAF), f32),
            pltpu.VMEM((OWN, 8), f32),
            pltpu.VMEM((128, 512), bf16),
            pltpu.VMEM((128, 512), bf16),
            pltpu.VMEM((COLS, OWN + LEAF), f32),
            pltpu.VMEM((LEAF, 2 * LEAF), bf16),
            pltpu.VMEM((LEAF, 2 * LEAF), bf16),
            pltpu.VMEM((LEAF, LEAF), bf16),
            pltpu.VMEM((13, 2, 8, 128), f32),
            pltpu.VMEM((13, 2, 8, 128), f32),
            pltpu.VMEM((7, 8, 128), f32),
            pltpu.VMEM((2, 3, 2, 8, 128), f32),
            pltpu.VMEM((2, 3, 2, 8, 128), f32),
            pltpu.VMEM((MEMBERS, 8, 128), f32),
            pltpu.VMEM((MEMBERS, 8, 128), f32),
            pltpu.VMEM((2, 2, 8, 128), f32),
            pltpu.VMEM((2, 2, 8, 128), f32),
            pltpu.VMEM((8, 128), f32),
            pltpu.VMEM((2, 8, 128), f32),
            pltpu.VMEM((2, 8, 128), f32),
            pltpu.VMEM((strides, 8, 128), f32),
            pltpu.VMEM((MEMBERS, 8, 128), f32),
            dma((5,)),
            dma((2,)),
            dma((2,)),
            dma((2,)),
            dma((2,)),
            dma,
            dma,
            dma,
            dma,
            dma((3,)),
            dma((3,)),
            dma((2,)),
            dma((2,)),
            dma((2,)),
            dma((2,)),
            dma,
            dma,
            pltpu.SemaphoreType.REGULAR,
        ],
        compiler_params=pltpu.CompilerParams(
            collective_id=0, has_side_effects=True, vmem_limit_bytes=32 * 1024 * 1024
        ),
    )(
        *[
            pltpu.with_memory_space_constraint(x, pltpu.HBM)
            for x in (
                coords,
                loads,
                occupancy,
                basis.reshape(LEAVES * 64, LEAF),
                transfer.reshape(6, 128, 64),
            )
        ]
    )


def solution(mesh):
    boxes = mesh.shape["box"] // MEMBERS
    return jax.shard_map(
        functools.partial(body, boxes, 4),
        mesh=mesh,
        in_specs=(P(None, "box"), P(None, "box"), P("box"), P("box", None, None), P()),
        out_specs=P(None, "box"),
        check_vma=False,
    )
```

```python
import functools

import jax
import jax.numpy as jnp
from jax import lax
from jax.experimental import pallas as pl
from jax.experimental.pallas import tpu as pltpu
from jax.sharding import PartitionSpec as P

LEAF = 256
COLS = 8
LEAVES = 8
MEMBERS = 8
OWN = LEAF * LEAVES

f32 = jnp.float32
bf16 = jnp.bfloat16
soften = 0.0001
near_scale = 0.0625
far_scale = 0.125
NN = (((1,), (0,)), ((), ()))
NT = (((1,), (1,)), ((), ()))
MESH = pl.DeviceIdType.MESH


def div(a, b):
    return lax.div(a, jnp.int32(b))


def rem(a, b):
    return lax.rem(a, jnp.int32(b))


def phi(tx, ty, tz, sx, sy, sz, scale):
    dx = tx - sx
    dy = ty - sy
    dz = tz - sz
    r2 = dx * dx + dy * dy + dz * dz
    return (r2 * (0.5 * scale)) * jnp.log(r2 + soften)


def split(x):
    high = x.astype(bf16)
    return high, (x - high.astype(f32)).astype(bf16)


def mm(a, b, dims):
    rows = a.shape[0]
    high = a.astype(bf16).astype(f32)
    stacked = jnp.concatenate([high, a - high], axis=0).astype(bf16)
    both = lax.dot_general(stacked, b[0][...], dims, preferred_element_type=f32)
    low = lax.dot_general(stacked[:rows], b[1][...], dims, preferred_element_type=f32)
    return both[:rows] + (both[rows:] + low)


def low_half(shape):
    return lax.broadcasted_iota(jnp.int32, shape, len(shape) - 1) < 64


def merge(rows):
    count = rows.shape[0] // 16
    low = low_half((8, 128))
    return [
        jnp.where(low, rows[16 * i : 16 * i + 8], rows[16 * i + 8 : 16 * i + 16])
        for i in range(count)
    ]


def raise_coef(pairs, level_map):
    rows = mm(jnp.concatenate(pairs, axis=0), level_map, NN)
    return merge(rows) if len(pairs) > 1 else [rows]


def pick(x, entries):
    rows = x.shape[0]
    a = x.astype(bf16).astype(f32)
    b = (x - a).astype(bf16).astype(f32)
    c = (x - a) - b
    stacked = jnp.concatenate([a, b, c], axis=0).astype(bf16)
    picked = lax.dot_general(stacked, entries, NN, preferred_element_type=f32)
    return picked[:rows] + picked[rows : 2 * rows] + picked[2 * rows :]


def raise_skel(pairs, every_second):
    rows_up = pick(jnp.concatenate(pairs, axis=0), every_second)
    return merge(rows_up) if len(pairs) > 1 else [rows_up]


def cousins(chain, slot):
    low = low_half((8, 128))
    column = chain[slot, 1].T
    tx, ty, tz = column[:, 0:1], column[:, 1:2], column[:, 2:3]
    before, after = chain[slot - 1, 0], chain[slot + 1, 0]
    tiles = []
    for skel in (chain[slot - 1, 1], chain[slot + 1, 1]):
        tiles.append(phi(tx, ty, tz, skel[0:1], skel[1:2], skel[2:3], far_scale))
    tile = jnp.concatenate(tiles, axis=1)
    even = jnp.concatenate([jnp.where(low, before, 0.0), after], axis=1)
    odd = jnp.concatenate([before, jnp.where(low, 0.0, after)], axis=1)
    rows = mm(jnp.concatenate([even, odd], axis=0), split(tile), NT)
    return jnp.where(low, rows[:8], rows[8:])


def lower(pairs, level_map):
    height = pairs[0].shape[0]
    low = low_half((height, 128))
    stacked = []
    for pair in pairs:
        stacked += [jnp.where(low, pair, 0.0), jnp.where(low, 0.0, pair)]
    rows = mm(jnp.concatenate(stacked, axis=0), level_map, NT)
    return [rows[height * i : height * (i + 1)] for i in range(2 * len(pairs))]


def kernel(
    boxes,
    across,
    coords_hbm,
    loads_hbm,
    occ_hbm,
    basis_hbm,
    transfer_hbm,
    out_ref,
    coords,
    loads,
    occ,
    basis,
    transfer,
    map_high,
    map_low,
    path_map,
    field,
    column,
    leaf_high,
    leaf_low,
    near,
    tile_a,
    tile_b,
    tile_c,
    chain,
    g_chain,
    local,
    edge_send,
    edge_recv,
    u_buf,
    g_buf,
    bound_send,
    bound_recv,
    quad_recv,
    rim_recv,
    far_send,
    far_buf,
    part_buf,
    load_sem,
    near_send_sem,
    near_recv_sem,
    edge_send_sem,
    edge_recv_sem,
    u_send_sem,
    u_recv_sem,
    g_send_sem,
    g_recv_sem,
    bound_send_sem,
    bound_recv_sem,
    rim_send_sem,
    rim_recv_sem,
    far_send_sem,
    far_recv_sem,
    part_send_sem,
    part_recv_sem,
    ready,
):
    loading = [
        pltpu.make_async_copy(src, dst, load_sem.at[at])
        for at, (src, dst) in enumerate(
            [
                (coords_hbm, coords),
                (transfer_hbm, transfer),
                (loads_hbm, loads),
                (occ_hbm, occ),
                (basis_hbm, basis),
            ]
        )
    ]
    for copy in loading:
        copy.start()

    device = lax.axis_index("box")
    total = boxes * MEMBERS
    strides = boxes // MEMBERS
    depth = boxes // (2 * across)
    box, member = div(device, MEMBERS), rem(device, MEMBERS)
    x, z, y_half = div(box, 2 * depth), rem(div(box, 2), depth), rem(box, 2)
    y, core = div(member, 2), rem(member, 2)
    low = low_half((8, 128))
    half = jnp.where(low, 0, 1)

    top = jnp.where(y == 3, 1, 0)
    outer = jnp.where(y == 0, 1, top)
    side_to = jnp.where(outer == 1, top, 2 - y)
    side_from = jnp.where(outer == 1, 1 - top, 2 - y)
    far_half = jnp.where(outer == 1, 1 - y_half, y_half)
    z_core = rem(div(z, 2), 2)
    far_member = 2 * jnp.where(outer == 1, 3 - y, y) + z_core
    z_high, z_low = div(z, 4), rem(z, 2)
    far_x = [rem(x + dx, across) for dx in range(across)]
    far_steps = [(dx, turn) for dx in range(across) for turn in range(2)]

    def far_depths(side):
        first = 4 * rem(side + z_high, 2) + 2 * core
        return [first + z_low, first + 1 - z_low]

    to_z, from_z = far_depths(side_to), far_depths(side_from)

    def far_box(depths, dx, turn):
        return (far_x[dx % across] * depth + depths[turn]) * 2 + far_half

    far_to = [far_box(to_z, dx, turn) * MEMBERS + far_member for dx, turn in far_steps]
    far_from = [far_box(from_z, -dx, turn) for dx, turn in far_steps]
    alone = jnp.logical_and(jnp.logical_and(outer == 0, side_to == 0), core == z_core)

    barrier = pltpu.get_barrier_semaphore()

    def greet(target):
        pl.semaphore_signal(barrier, inc=1, device_id=(target,), device_id_type=MESH)

    def order(at):
        return jnp.where(at == 0, 0, jnp.where(at >= 6, 2, 1))

    mine = order(z)
    to_later = [jnp.where(order(at) > mine, 1, 0) for at in to_z]
    from_earlier = [jnp.where(order(at) < mine, 1, 0) for at in from_z]
    far_order = [(2 * dx + turn) for turn in range(2) for dx in (2, 1, 3, 0)]

    def far_each(turn, act):
        for k in far_order[4 * turn : 4 * turn + 4]:
            if k:
                act(k)
            else:
                pl.when(jnp.logical_not(alone))(functools.partial(act, 0))

    for turn in range(2):

        @pl.when(from_earlier[turn] == 0)
        def _(turn=turn):
            far_each(turn, lambda k: greet(far_from[k] * MEMBERS + far_member))

        @pl.when(to_later[turn] == 1)
        def _(turn=turn):
            far_each(turn, lambda k: greet(far_to[k]))

    left_device = rem(device + total - 1, total)
    right_device = rem(device + 1, total)
    mirror = 2 * (3 - y) + core
    left_box = rem(box + boxes - 1, boxes) * MEMBERS + mirror
    right_box = rem(box + 1, boxes) * MEMBERS + mirror
    mates = [box * MEMBERS + rem(member + r, MEMBERS) for r in (6, 2, 7, 3, 5, 4, 1)]
    at_rim = outer == 1
    rim_box = rem(box + boxes + 2 * top - 1, boxes)
    rim_devices = [rim_box * MEMBERS + 6 - 6 * top + t for t in range(2)]
    quad = div(member, 4)
    quad_device = rem(box + boxes + 2 * quad - 1, boxes) * MEMBERS + mirror
    early = jnp.where(z == 0, 1, 0)
    ahead = 2
    for target in mates + [left_device, right_device, left_box, right_box]:
        greet(target)
    @pl.when(at_rim)
    def _():
        for target in rim_devices:
            greet(target)

    lanes = lax.broadcasted_iota(jnp.int32, (1, 128), 1)
    index = lax.broadcasted_iota(jnp.int32, (512, 128), 0)
    placed = (index == (lanes - 64 - 8 * member) * 64).astype(f32).astype(bf16)
    picks = (lax.broadcasted_iota(jnp.int32, (1, 128), 1) & 63) * 2
    every_second = (
        (lax.broadcasted_iota(jnp.int32, (128, 128), 0) == picks).astype(f32).astype(bf16)
    )
    for copy in loading:
        copy.wait()
    points = jnp.concatenate([coords[...], jnp.zeros((5, OWN), f32)], axis=0)
    s0 = [
        jnp.concatenate(
            [points[:, 512 * p : 512 * p + 64], points[:, 512 * p + 256 : 512 * p + 320]], axis=1
        )
        for p in range(4)
    ]
    s6 = pick(jnp.concatenate(s0, axis=1), placed)

    maps = [(map_high.at[level], map_low.at[level]) for level in range(6)]

    def set_map(level):
        once = transfer[level]
        map_high[level], map_low[level] = split(jnp.concatenate([once, once], axis=1))

    for level in range(2):
        set_map(level)
    slots = lax.broadcasted_iota(jnp.int32, (COLS, LEAF), 1)
    live = []
    for leaf in range(LEAVES):
        part = loads[:, leaf * LEAF : (leaf + 1) * LEAF].astype(f32)
        live.append(jnp.where(slots < occ[leaf], part, 0.0))
    c0 = []
    for p in range(4):
        two = jnp.concatenate([live[2 * p], live[2 * p + 1]], axis=0).astype(bf16)
        rows = lax.dot_general(
            two, basis[128 * p : 128 * p + 128, :], NT, preferred_element_type=f32
        )
        c0.append(jnp.where(low, rows[:8], rows[8:]))
    c1 = raise_coef(c0, maps[0])
    c2 = raise_coef(c1, maps[1])
    def factor(level, at):
        return transfer[level, pl.ds(pl.multiple_of(64 * at, 64), 64), :]

    map_34 = mm(transfer[2], split(factor(3, core)), NN)
    wide = jnp.concatenate([factor(5, quad), jnp.zeros((64, 64), f32)], axis=1)
    map_56 = mm(factor(4, rem(y, 2)), split(wide), NN)
    map_6 = mm(map_34, split(map_56), NN)
    u_buf[member] = mm(c2[0], split(map_6), NN) + s6
    path_map[...] = map_6

    def set_field():
        field[0, :, LEAF : LEAF + OWN] = points
        for leaf in range(LEAVES):
            field[1, :, (leaf + 1) * LEAF : (leaf + 2) * LEAF] = live[leaf]
        for at in range(0, OWN, 128):
            column[at : at + 128, :] = points[:, at : at + 128].T
        near[...] = jnp.zeros_like(near)

    def fill_tile(tile, row, col, width):
        sx = field[0, 0:1, pl.ds(col, width)]
        sy = field[0, 1:2, pl.ds(col, width)]
        sz = field[0, 2:3, pl.ds(col, width)]
        for at in range(0, LEAF, 16):
            rows = column[pl.ds(row + at, 16), :]
            tile[at : at + 16, 0:width] = phi(
                rows[:, 0:1], rows[:, 1:2], rows[:, 2:3], sx, sy, sz, near_scale
            ).astype(bf16)

    def near_leaf(tile, row):
        col = row + LEAF
        fill_tile(tile, row, col, 2 * LEAF)
        loads_two = field[1, :, pl.ds(col, 2 * LEAF)].astype(bf16)
        this = lax.dot_general(loads_two, tile[...], NT, preferred_element_type=f32)
        after = lax.dot_general(
            loads_two[:, :LEAF], tile[:, LEAF:], NN, preferred_element_type=f32
        )
        return this, after

    def near_two(row):
        first, second_part = near_leaf(tile_a, row)
        second, third = near_leaf(tile_b, row + LEAF)
        near[:, pl.ds(row, LEAF)] += first
        near[:, pl.ds(row + LEAF, LEAF)] += second_part + second
        near[:, pl.ds(row + 2 * LEAF, LEAF)] += third

    def near_step(pair, carry):
        near_two(pl.multiple_of(pair * (2 * LEAF), 2 * LEAF))
        return carry

    def side(block, at):
        lanes = jnp.where(low_half((1, 128)), 0, 1)
        return jnp.where(lanes == at, block, 0.0)

    def set_chain(levels, into):
        for at, (pairs, skels) in enumerate(levels):
            first = (1, 7, 11)[at]
            for p in range(len(pairs)):
                into[first + p, 0] = pairs[p]
                into[first + p, 1] = skels[p]

    def set_inner():
        row = (LEAVES - 2) * LEAF
        this, after = near_leaf(tile_a, row)
        fill_tile(tile_c, row + LEAF, row + 2 * LEAF, LEAF)
        own = field[1, :, row + 2 * LEAF : row + 3 * LEAF].astype(bf16)
        after += lax.dot_general(own, tile_c[...], NT, preferred_element_type=f32)
        near[:, row : row + LEAF] += this
        near[:, row + LEAF : row + 2 * LEAF] += after
        for slot in (2, 3):
            local[slot - 1] = cousins(chain, slot)

    def set_edges():
        s1 = raise_skel(s0, every_second)
        s2 = raise_skel(s1, every_second)

        set_chain([(c0, s0), (c1, s1), (c2, s2)], chain)
        for at, (pairs, skels) in enumerate([(c0, s0), (c1, s1), (c2, s2)]):
            edge_send[0, at, 0] = pairs[-1]
            edge_send[0, at, 1] = skels[-1]
            edge_send[1, at, 0] = pairs[0]
            edge_send[1, at, 1] = skels[0]
    def set_leaf_paths():
        x2 = jnp.concatenate([path_map[...].T[:64], transfer[2].T], axis=0)
        x0 = lower(lower([x2], maps[1]), maps[0])
        leaf_high[...], leaf_low[...] = split(jnp.concatenate(x0, axis=1))

    @pl.when(early == 1)
    def _():
        set_field()
        lax.fori_loop(0, ahead, near_step, 0)

    pl.semaphore_wait(
        barrier,
        MEMBERS - 1
        + 4
        + 2 * outer
        + 4 * (2 - to_later[0] - to_later[1])
        - alone.astype(jnp.int32)
        + 4 * (from_earlier[0] + from_earlier[1]),
    )

    def tell(target):
        pl.semaphore_signal(ready, inc=1, device_id=(target,), device_id_type=MESH)

    for turn in range(2):

        @pl.when(from_earlier[turn] == 1)
        def _(turn=turn):
            far_each(turn, lambda k: tell(far_from[k] * MEMBERS + far_member))

    def remote(src, dst, send_sem, recv_sem, target):
        return pltpu.make_async_remote_copy(
            src_ref=src,
            dst_ref=dst,
            send_sem=send_sem,
            recv_sem=recv_sem,
            device_id=(target,),
            device_id_type=MESH,
        )

    def send(*ends):
        copy = remote(*ends)
        copy.start()
        return copy

    def wait_all(ref, semaphore):
        pltpu.make_async_copy(ref, ref, semaphore).wait()

    for mate in mates:
        send(u_buf.at[member], u_buf.at[member], u_send_sem, u_recv_sem, mate)

    set_map(2)
    every_eighth = (index == (lanes & 63) * 8).astype(f32).astype(bf16)
    s3 = pick(jnp.concatenate(s0, axis=1), every_eighth)
    c3 = raise_coef(c2, maps[2])[0]
    g_buf[member] = jnp.where(half == core, c3, s3)
    for mate in mates:
        send(g_buf.at[member], g_buf.at[member], g_send_sem, g_recv_sem, mate)

    rim_copies = [
        pltpu.make_async_remote_copy(
            src_ref=g_buf.at[member],
            dst_ref=rim_recv.at[core],
            send_sem=rim_send_sem.at[t],
            recv_sem=rim_recv_sem.at[core],
            device_id=(rim_devices[t],),
            device_id_type=MESH,
        )
        for t in range(2)
    ]

    @pl.when(at_rim)
    def _():
        for copy in rim_copies:
            copy.start()

    @pl.when(early == 0)
    def _():
        set_field()

    last = LEAF * LEAVES
    near_copies = [
        send(
            field.at[:, :, last : last + LEAF],
            field.at[:, :, 0:LEAF],
            near_send_sem.at[0],
            near_recv_sem.at[0],
            right_device,
        ),
        send(
            field.at[:, :, LEAF : 2 * LEAF],
            field.at[:, :, last + LEAF : last + 2 * LEAF],
            near_send_sem.at[1],
            near_recv_sem.at[1],
            left_device,
        ),
    ]

    edge_copies = [
        remote(
            edge_send.at[side],
            edge_recv.at[side],
            edge_send_sem.at[side],
            edge_recv_sem.at[side],
            (right_device, left_device)[side],
        )
        for side in range(2)
    ]

    set_edges()
    for copy in edge_copies:
        copy.start()

    set_map(3)
    set_map(4)

    @pl.when(early == 1)
    def _():
        set_leaf_paths()

    wait_all(u_buf.at[pl.ds(0, MEMBERS - 1)], u_recv_sem)
    parts = [u_buf[at] for at in range(MEMBERS)]
    while len(parts) > 1:
        parts = [a + b for a, b in zip(parts[0::2], parts[1::2])]
    top_record = parts[0]
    swapped_record = pltpu.roll(top_record, 64, 1)
    far_send[0] = top_record
    far_send[1] = swapped_record

    @pl.when(alone)
    def _():
        far_buf[0] = far_send[0]

    def far_copy(k):
        return remote(
            far_send.at[k % 2],
            far_buf.at[k],
            far_send_sem.at[min(k, 1)],
            far_recv_sem.at[min(k, 1)],
            far_to[k],
        )

    first_far = far_copy(0)
    for turn in range(2):

        @pl.when(to_later[turn] == 0)
        def _(turn=turn):
            far_each(turn, lambda k: far_copy(k).start())

    wait_all(g_buf.at[pl.ds(0, MEMBERS - 1)], g_recv_sem)
    c3s, s3s = [], []
    for p in range(4):
        even, odd = g_buf[2 * p], g_buf[2 * p + 1]
        c3s.append(jnp.where(low, even, odd))
        s3s.append(pltpu.roll(jnp.where(low, odd, even), 64, 1))
    c4s, s4s = raise_coef(c3s, maps[3]), raise_skel(s3s, every_second)
    c5s, s5s = raise_coef(c4s, maps[4]), raise_skel(s4s, every_second)
    set_chain([(c3s, s3s), (c4s, s4s), (c5s, s5s)], g_chain)
    for at in range(2):
        bound_send[at, 0] = c5s[0]
        bound_send[at, 1] = s5s[0] + pltpu.roll(s4s[1 - at], 3, 0)
    bound_copies = [
        send(
            bound_send.at[side],
            bound_recv.at[side],
            bound_send_sem.at[side],
            bound_recv_sem.at[side],
            (right_box, left_box)[side],
        )
        for side in range(2)
    ]
    bound_copies.append(
        send(
            g_chain.at[7 + quad, 0],
            quad_recv,
            bound_send_sem.at[2],
            bound_recv_sem.at[2],
            quad_device,
        )
    )

    def set_ends(ends, into, at_start, at_end):
        for level in range(3):
            before, after = (0, 6, 10)[level], (5, 9, 12)[level]
            into[before, 0] = jnp.where(at_start, 0.0, ends[0, level, 0])
            into[before, 1] = ends[0, level, 1]
            into[after, 0] = jnp.where(at_end, 0.0, ends[1, level, 0])
            into[after, 1] = ends[1, level, 1]

    def near_end(tile, row, col):
        fill_tile(tile, row, col, LEAF)
        near[:, row : row + LEAF] += lax.dot_general(
            field[1, :, col : col + LEAF].astype(bf16),
            tile[:, 0:LEAF],
            NT,
            preferred_element_type=f32,
        )

    def finish_ends():
        for copy in near_copies:
            copy.wait_recv()

        @pl.when(device == 0)
        def _():
            field[1, :, 0:LEAF] = jnp.zeros((COLS, LEAF), f32)

        @pl.when(device == total - 1)
        def _():
            field[1, :, last + LEAF : last + 2 * LEAF] = jnp.zeros((COLS, LEAF), f32)

        near_end(tile_c, 0, 0)
        near_end(tile_a, last - LEAF, last + LEAF)

        for copy in edge_copies:
            copy.wait_recv()
        set_ends(edge_recv, chain, device == 0, device == total - 1)
        for at, slot in [(0, 1), (3, 4), (4, 7), (5, 8), (6, 11)]:
            local[at] = cousins(chain, slot)

    @pl.when(early == 1)
    def _():
        lax.fori_loop(ahead, 3, near_step, 0)
        set_inner()
        finish_ends()

    later = to_later[0] + to_later[1]

    @pl.when(later > 0)
    def _():
        pl.semaphore_wait(ready, 4 * later)

    for turn in range(2):

        @pl.when(to_later[turn] == 1)
        def _(turn=turn):
            far_each(turn, lambda k: far_copy(k).start())

    @pl.when(early == 0)
    def _():
        lax.fori_loop(0, 3, near_step, 0)
        set_inner()
        set_leaf_paths()
        finish_ends()

    top_column = swapped_record.T[:64]
    tx, ty, tz = top_column[:, 0:1], top_column[:, 1:2], top_column[:, 2:3]

    wait_all(far_buf.at[pl.ds(1, strides - 1)], far_recv_sem.at[1])

    @pl.when(jnp.logical_not(alone))
    def _():
        first_far.wait_recv()

    top_coef, top_skel = [], []
    for k in range(0, strides, 2):
        halves = []
        for at in (k, k + 1):
            apart = far_from[at] - box
            counts = jnp.logical_or(apart >= 2, apart <= -2)
            halves.append((far_buf[at], counts))
        (one, one_counts), (two, two_counts) = halves
        coef = jnp.where(low, jnp.where(one_counts, one, 0.0), jnp.where(two_counts, two, 0.0))
        top_coef.append(pltpu.roll(coef, 64, 1))
        top_skel.append(jnp.where(low, two, one))
    top_tile = jnp.concatenate(
        [phi(tx, ty, tz, s[0:1], s[1:2], s[2:3], far_scale) for s in top_skel], axis=1
    )
    top = mm(jnp.concatenate(top_coef, axis=1), split(top_tile), NT)
    part_buf[member] = jnp.concatenate([top, jnp.zeros((8, 64), f32)], axis=1)
    for at in range(MEMBERS - 1):
        mate = box * MEMBERS + at + jnp.where(member <= at, 1, 0)
        send(part_buf.at[member], part_buf.at[member], part_send_sem, part_recv_sem, mate)

    wait_all(u_buf.at[pl.ds(0, MEMBERS - 1)], u_send_sem)
    wait_all(g_buf.at[pl.ds(0, MEMBERS - 1)], g_send_sem)
    wait_all(far_buf.at[pl.ds(1, strides - 1)], far_send_sem.at[1])
    for copy in near_copies + edge_copies + bound_copies:
        copy.wait_send()

    @pl.when(jnp.logical_not(alone))
    def _():
        first_far.wait_send()

    for copy in bound_copies:
        copy.wait_recv()
    at_start, at_end = box == 0, box == boxes - 1
    outside = jnp.logical_or(
        jnp.logical_and(quad == 0, at_start), jnp.logical_and(quad == 1, at_end)
    )
    start_skel, end_skel = bound_recv[0, 1], bound_recv[1, 1]
    g_chain[10, 0] = jnp.where(at_start, 0.0, bound_recv[0, 0])
    g_chain[10, 1] = start_skel
    g_chain[12, 0] = jnp.where(at_end, 0.0, bound_recv[1, 0])
    g_chain[12, 1] = end_skel
    quad_coef = jnp.where(outside, 0.0, quad_recv[...])
    g_chain[6, 0] = quad_coef
    g_chain[6, 1] = pltpu.roll(start_skel, 5, 0)
    g_chain[9, 0] = quad_coef
    g_chain[9, 1] = pltpu.roll(end_skel, 5, 0)

    @pl.when(at_rim)
    def _():
        for copy in rim_copies:
            copy.wait_send()
        for t in range(2):
            pltpu.make_async_remote_copy(
                src_ref=g_buf.at[member],
                dst_ref=rim_recv.at[t],
                send_sem=rim_send_sem.at[t],
                recv_sem=rim_recv_sem.at[t],
                device_id=(rim_devices[t],),
                device_id_type=MESH,
            ).wait_recv()
        even, odd = rim_recv[0], rim_recv[1]
        rim_coef = jnp.where(outside, 0.0, jnp.where(low, even, odd))
        rim_skel = pltpu.roll(jnp.where(low, odd, even), 64, 1)
        for slot in (0, 5):
            g_chain[slot, 0] = rim_coef
            g_chain[slot, 1] = rim_skel

    local3 = cousins(g_chain, 1 + y)
    local4 = cousins(g_chain, 7 + quad)
    local5 = cousins(g_chain, 11)
    y2 = local[6]
    y1 = [x + local[4 + at] for at, x in enumerate(lower([y2], maps[1]))]
    y0 = [x + local[at] for at, x in enumerate(lower(y1, maps[0]))]
    y4 = local4 + mm(side(local5, quad), maps[4], NT)
    y3 = local3 + mm(side(y4, rem(y, 2)), maps[3], NT)
    y3 = jnp.where(core == 1, y3, pltpu.roll(y3, 64, 1))

    wait_all(part_buf.at[pl.ds(0, MEMBERS - 1)], part_recv_sem)
    parts = [part_buf[at] for at in range(MEMBERS)]
    while len(parts) > 1:
        parts = [a + b for a, b in zip(parts[0::2], parts[1::2])]
    d6 = parts[0]
    d63 = jnp.where(low, d6, y3)
    d0 = jnp.concatenate(y0, axis=1) + mm(d63, (leaf_high, leaf_low), NN)
    for p in range(4):
        pair = d0[:, 128 * p : 128 * p + 128]
        two = jnp.concatenate([jnp.where(low, pair, 0.0), jnp.where(low, 0.0, pair)], axis=0)
        rows = lax.dot_general(
            two.astype(bf16),
            basis[128 * p : 128 * p + 128, :],
            NN,
            preferred_element_type=f32,
        )
        for t in range(2):
            leaf = 2 * p + t
            at = leaf * LEAF
            out_ref[:, at : at + LEAF] = jnp.where(
                slots < occ[leaf], near[:, at : at + LEAF] + rows[8 * t : 8 * t + 8], 0.0
            )

    wait_all(part_buf.at[pl.ds(0, MEMBERS - 1)], part_send_sem)


def body(boxes, across, coords, loads, occupancy, basis, transfer):
    strides = boxes // MEMBERS
    hbm = pl.BlockSpec(memory_space=pl.ANY)
    dma = pltpu.SemaphoreType.DMA
    return pl.pallas_call(
        functools.partial(kernel, boxes, across),
        out_shape=jax.ShapeDtypeStruct((COLS, OWN), f32),
        in_specs=[hbm] * 5,
        out_specs=pl.BlockSpec(memory_space=pltpu.VMEM),
        scratch_shapes=[
            pltpu.VMEM((3, OWN), f32),
            pltpu.VMEM((COLS, OWN), bf16),
            pltpu.SMEM((LEAVES,), jnp.int32),
            pltpu.VMEM((LEAVES * 64, LEAF), bf16),
            pltpu.VMEM((6, 128, 64), f32),
            pltpu.VMEM((6, 128, 128), bf16),
            pltpu.VMEM((6, 128, 128), bf16),
            pltpu.VMEM((128, 128), f32),
            pltpu.VMEM((2, 8, OWN + 2 * LEAF), f32),
            pltpu.VMEM((OWN, 8), f32),
            pltpu.VMEM((128, 512), bf16),
            pltpu.VMEM((128, 512), bf16),
            pltpu.VMEM((COLS, OWN + LEAF), f32),
            pltpu.VMEM((LEAF, 2 * LEAF), bf16),
            pltpu.VMEM((LEAF, 2 * LEAF), bf16),
            pltpu.VMEM((LEAF, LEAF), bf16),
            pltpu.VMEM((13, 2, 8, 128), f32),
            pltpu.VMEM((13, 2, 8, 128), f32),
            pltpu.VMEM((7, 8, 128), f32),
            pltpu.VMEM((2, 3, 2, 8, 128), f32),
            pltpu.VMEM((2, 3, 2, 8, 128), f32),
            pltpu.VMEM((MEMBERS, 8, 128), f32),
            pltpu.VMEM((MEMBERS, 8, 128), f32),
            pltpu.VMEM((2, 2, 8, 128), f32),
            pltpu.VMEM((2, 2, 8, 128), f32),
            pltpu.VMEM((8, 128), f32),
            pltpu.VMEM((2, 8, 128), f32),
            pltpu.VMEM((2, 8, 128), f32),
            pltpu.VMEM((strides, 8, 128), f32),
            pltpu.VMEM((MEMBERS, 8, 128), f32),
            dma((5,)),
            dma((2,)),
            dma((2,)),
            dma((2,)),
            dma((2,)),
            dma,
            dma,
            dma,
            dma,
            dma((3,)),
            dma((3,)),
            dma((2,)),
            dma((2,)),
            dma((2,)),
            dma((2,)),
            dma,
            dma,
            pltpu.SemaphoreType.REGULAR,
        ],
        compiler_params=pltpu.CompilerParams(
            collective_id=0, has_side_effects=True, vmem_limit_bytes=32 * 1024 * 1024
        ),
    )(
        *[
            pltpu.with_memory_space_constraint(x, pltpu.HBM)
            for x in (
                coords,
                loads,
                occupancy,
                basis.reshape(LEAVES * 64, LEAF),
                transfer.reshape(6, 128, 64),
            )
        ]
    )


def solution(mesh):
    boxes = mesh.shape["box"] // MEMBERS
    return jax.shard_map(
        functools.partial(body, boxes, 4),
        mesh=mesh,
        in_specs=(P(None, "box"), P(None, "box"), P("box"), P("box", None, None), P()),
        out_specs=P(None, "box"),
        check_vma=False,
    )
```

```python
import functools

import jax
import jax.numpy as jnp
from jax import lax
from jax.experimental import pallas as pl
from jax.experimental.pallas import tpu as pltpu
from jax.sharding import PartitionSpec as P

LEAF = 256
COLS = 8
LEAVES = 8
MEMBERS = 8
OWN = LEAF * LEAVES

f32 = jnp.float32
bf16 = jnp.bfloat16
soften = 0.0001
near_scale = 0.0625
far_scale = 0.125
NN = (((1,), (0,)), ((), ()))
NT = (((1,), (1,)), ((), ()))
MESH = pl.DeviceIdType.MESH


def div(a, b):
    return lax.div(a, jnp.int32(b))


def rem(a, b):
    return lax.rem(a, jnp.int32(b))


def phi(tx, ty, tz, sx, sy, sz, scale):
    dx = tx - sx
    dy = ty - sy
    dz = tz - sz
    r2 = dx * dx + dy * dy + dz * dz
    return (r2 * (0.5 * scale)) * jnp.log(r2 + soften)


def split(x):
    high = x.astype(bf16)
    return high, (x - high.astype(f32)).astype(bf16)


def mm(a, b, dims):
    rows = a.shape[0]
    high = a.astype(bf16).astype(f32)
    stacked = jnp.concatenate([high, a - high], axis=0).astype(bf16)
    both = lax.dot_general(stacked, b[0][...], dims, preferred_element_type=f32)
    low = lax.dot_general(stacked[:rows], b[1][...], dims, preferred_element_type=f32)
    return both[:rows] + (both[rows:] + low)


def low_half(shape):
    return lax.broadcasted_iota(jnp.int32, shape, len(shape) - 1) < 64


def merge(rows):
    count = rows.shape[0] // 16
    low = low_half((8, 128))
    return [
        jnp.where(low, rows[16 * i : 16 * i + 8], rows[16 * i + 8 : 16 * i + 16])
        for i in range(count)
    ]


def raise_coef(pairs, level_map):
    rows = mm(jnp.concatenate(pairs, axis=0), level_map, NN)
    return merge(rows) if len(pairs) > 1 else [rows]


def pick(x, entries):
    rows = x.shape[0]
    a = x.astype(bf16).astype(f32)
    b = (x - a).astype(bf16).astype(f32)
    c = (x - a) - b
    stacked = jnp.concatenate([a, b, c], axis=0).astype(bf16)
    picked = lax.dot_general(stacked, entries, NN, preferred_element_type=f32)
    return picked[:rows] + picked[rows : 2 * rows] + picked[2 * rows :]


def raise_skel(pairs, every_second):
    rows_up = pick(jnp.concatenate(pairs, axis=0), every_second)
    return merge(rows_up) if len(pairs) > 1 else [rows_up]


def cousins(chain, slot):
    low = low_half((8, 128))
    column = chain[slot, 1].T
    tx, ty, tz = column[:, 0:1], column[:, 1:2], column[:, 2:3]
    before, after = chain[slot - 1, 0], chain[slot + 1, 0]
    tiles = []
    for skel in (chain[slot - 1, 1], chain[slot + 1, 1]):
        tiles.append(phi(tx, ty, tz, skel[0:1], skel[1:2], skel[2:3], far_scale))
    tile = jnp.concatenate(tiles, axis=1)
    even = jnp.concatenate([jnp.where(low, before, 0.0), after], axis=1)
    odd = jnp.concatenate([before, jnp.where(low, 0.0, after)], axis=1)
    rows = mm(jnp.concatenate([even, odd], axis=0), split(tile), NT)
    return jnp.where(low, rows[:8], rows[8:])


def lower(pairs, level_map):
    height = pairs[0].shape[0]
    low = low_half((height, 128))
    stacked = []
    for pair in pairs:
        stacked += [jnp.where(low, pair, 0.0), jnp.where(low, 0.0, pair)]
    rows = mm(jnp.concatenate(stacked, axis=0), level_map, NT)
    return [rows[height * i : height * (i + 1)] for i in range(2 * len(pairs))]


def kernel(
    boxes,
    across,
    coords_hbm,
    loads_hbm,
    occ_hbm,
    basis_hbm,
    transfer_hbm,
    out_ref,
    coords,
    loads,
    occ,
    basis,
    transfer,
    map_high,
    map_low,
    path_map,
    field,
    column,
    leaf_high,
    leaf_low,
    near,
    tile_a,
    tile_b,
    tile_c,
    chain,
    g_chain,
    local,
    edge_send,
    edge_recv,
    u_buf,
    g_buf,
    bound_send,
    bound_recv,
    quad_recv,
    rim_recv,
    far_send,
    far_buf,
    part_buf,
    load_sem,
    near_send_sem,
    near_recv_sem,
    edge_send_sem,
    edge_recv_sem,
    u_send_sem,
    u_recv_sem,
    g_send_sem,
    g_recv_sem,
    bound_send_sem,
    bound_recv_sem,
    rim_send_sem,
    rim_recv_sem,
    far_send_sem,
    far_recv_sem,
    part_send_sem,
    part_recv_sem,
    ready,
):
    loading = [
        pltpu.make_async_copy(src, dst, load_sem.at[at])
        for at, (src, dst) in enumerate(
            [
                (coords_hbm, coords),
                (transfer_hbm, transfer),
                (loads_hbm, loads),
                (occ_hbm, occ),
                (basis_hbm, basis),
            ]
        )
    ]
    for copy in loading:
        copy.start()

    device = lax.axis_index("box")
    total = boxes * MEMBERS
    strides = boxes // MEMBERS
    depth = boxes // (2 * across)
    box, member = div(device, MEMBERS), rem(device, MEMBERS)
    x, z, y_half = div(box, 2 * depth), rem(div(box, 2), depth), rem(box, 2)
    y, core = div(member, 2), rem(member, 2)
    low = low_half((8, 128))
    half = jnp.where(low, 0, 1)

    top = jnp.where(y == 3, 1, 0)
    outer = jnp.where(y == 0, 1, top)
    side_to = jnp.where(outer == 1, top, 2 - y)
    side_from = jnp.where(outer == 1, 1 - top, 2 - y)
    far_half = jnp.where(outer == 1, 1 - y_half, y_half)
    z_core = rem(div(z, 2), 2)
    far_member = 2 * jnp.where(outer == 1, 3 - y, y) + z_core
    z_high, z_low = div(z, 4), rem(z, 2)
    far_x = [rem(x + dx, across) for dx in range(across)]
    far_steps = [(dx, turn) for dx in range(across) for turn in range(2)]

    def far_depths(side):
        first = 4 * rem(side + z_high, 2) + 2 * core
        return [first + z_low, first + 1 - z_low]

    to_z, from_z = far_depths(side_to), far_depths(side_from)

    def far_box(depths, dx, turn):
        return (far_x[dx % across] * depth + depths[turn]) * 2 + far_half

    far_to = [far_box(to_z, dx, turn) * MEMBERS + far_member for dx, turn in far_steps]
    far_from = [far_box(from_z, -dx, turn) for dx, turn in far_steps]
    alone = jnp.logical_and(jnp.logical_and(outer == 0, side_to == 0), core == z_core)

    barrier = pltpu.get_barrier_semaphore()

    def greet(target):
        pl.semaphore_signal(barrier, inc=1, device_id=(target,), device_id_type=MESH)

    def order(at):
        return jnp.where(at == 0, 0, jnp.where(at >= 6, 2, 1))

    mine = order(z)
    to_later = [jnp.where(order(at) > mine, 1, 0) for at in to_z]
    from_earlier = [jnp.where(order(at) < mine, 1, 0) for at in from_z]
    far_order = [(2 * dx + turn) for turn in range(2) for dx in (2, 1, 3, 0)]

    def far_each(turn, act):
        for k in far_order[4 * turn : 4 * turn + 4]:
            if k:
                act(k)
            else:
                pl.when(jnp.logical_not(alone))(functools.partial(act, 0))

    for turn in range(2):

        @pl.when(from_earlier[turn] == 0)
        def _(turn=turn):
            far_each(turn, lambda k: greet(far_from[k] * MEMBERS + far_member))

        @pl.when(to_later[turn] == 1)
        def _(turn=turn):
            far_each(turn, lambda k: greet(far_to[k]))

    left_device = rem(device + total - 1, total)
    right_device = rem(device + 1, total)
    mirror = 2 * (3 - y) + core
    left_box = rem(box + boxes - 1, boxes) * MEMBERS + mirror
    right_box = rem(box + 1, boxes) * MEMBERS + mirror
    mates = [box * MEMBERS + rem(member + r, MEMBERS) for r in (6, 2, 7, 3, 5, 4, 1)]
    at_rim = outer == 1
    rim_box = rem(box + boxes + 2 * top - 1, boxes)
    rim_devices = [rim_box * MEMBERS + 6 - 6 * top + t for t in range(2)]
    quad = div(member, 4)
    quad_device = rem(box + boxes + 2 * quad - 1, boxes) * MEMBERS + mirror
    early = jnp.where(z == 0, 1, 0)
    ahead = 2
    before = [device > 0, box > 0]
    after = [device < total - 1, box < boxes - 1]
    inside = jnp.where(quad == 0, box, boxes - 1 - box) > 0
    open_rim = jnp.logical_and(at_rim, inside)

    for target in mates:
        greet(target)
    for has, targets in ((before, (left_device, left_box)), (after, (right_device, right_box))):
        for at in range(2):
            pl.when(has[at])(functools.partial(greet, targets[at]))

    @pl.when(open_rim)
    def _():
        for target in rim_devices:
            greet(target)

    lanes = lax.broadcasted_iota(jnp.int32, (1, 128), 1)
    index = lax.broadcasted_iota(jnp.int32, (512, 128), 0)
    placed = (index == (lanes - 64 - 8 * member) * 64).astype(f32).astype(bf16)
    picks = (lax.broadcasted_iota(jnp.int32, (1, 128), 1) & 63) * 2
    every_second = (
        (lax.broadcasted_iota(jnp.int32, (128, 128), 0) == picks).astype(f32).astype(bf16)
    )
    for copy in loading:
        copy.wait()
    points = jnp.concatenate([coords[...], jnp.zeros((5, OWN), f32)], axis=0)
    s0 = [
        jnp.concatenate(
            [points[:, 512 * p : 512 * p + 64], points[:, 512 * p + 256 : 512 * p + 320]], axis=1
        )
        for p in range(4)
    ]
    s6 = pick(jnp.concatenate(s0, axis=1), placed)

    maps = [(map_high.at[level], map_low.at[level]) for level in range(6)]

    def set_map(level):
        once = transfer[level]
        map_high[level], map_low[level] = split(jnp.concatenate([once, once], axis=1))

    for level in range(2):
        set_map(level)
    slots = lax.broadcasted_iota(jnp.int32, (COLS, LEAF), 1)
    live = []
    for leaf in range(LEAVES):
        part = loads[:, leaf * LEAF : (leaf + 1) * LEAF].astype(f32)
        live.append(jnp.where(slots < occ[leaf], part, 0.0))
    c0 = []
    for p in range(4):
        two = jnp.concatenate([live[2 * p], live[2 * p + 1]], axis=0).astype(bf16)
        rows = lax.dot_general(
            two, basis[128 * p : 128 * p + 128, :], NT, preferred_element_type=f32
        )
        c0.append(jnp.where(low, rows[:8], rows[8:]))
    c1 = raise_coef(c0, maps[0])
    c2 = raise_coef(c1, maps[1])
    def factor(level, at):
        return transfer[level, pl.ds(pl.multiple_of(64 * at, 64), 64), :]

    map_34 = mm(transfer[2], split(factor(3, core)), NN)
    wide = jnp.concatenate([factor(5, quad), jnp.zeros((64, 64), f32)], axis=1)
    map_56 = mm(factor(4, rem(y, 2)), split(wide), NN)
    map_6 = mm(map_34, split(map_56), NN)
    u_buf[member] = mm(c2[0], split(map_6), NN) + s6
    path_map[...] = map_6

    def set_field():
        field[0, :, LEAF : LEAF + OWN] = points
        for leaf in range(LEAVES):
            field[1, :, (leaf + 1) * LEAF : (leaf + 2) * LEAF] = live[leaf]
        for at in range(0, OWN, 128):
            column[at : at + 128, :] = points[:, at : at + 128].T
        near[...] = jnp.zeros_like(near)

    def fill_tile(tile, row, col, width):
        sx = field[0, 0:1, pl.ds(col, width)]
        sy = field[0, 1:2, pl.ds(col, width)]
        sz = field[0, 2:3, pl.ds(col, width)]
        for at in range(0, LEAF, 16):
            rows = column[pl.ds(row + at, 16), :]
            tile[at : at + 16, 0:width] = phi(
                rows[:, 0:1], rows[:, 1:2], rows[:, 2:3], sx, sy, sz, near_scale
            ).astype(bf16)

    def near_leaf(tile, row):
        col = row + LEAF
        fill_tile(tile, row, col, 2 * LEAF)
        loads_two = field[1, :, pl.ds(col, 2 * LEAF)].astype(bf16)
        this = lax.dot_general(loads_two, tile[...], NT, preferred_element_type=f32)
        after = lax.dot_general(
            loads_two[:, :LEAF], tile[:, LEAF:], NN, preferred_element_type=f32
        )
        return this, after

    def near_two(row):
        first, second_part = near_leaf(tile_a, row)
        second, third = near_leaf(tile_b, row + LEAF)
        near[:, pl.ds(row, LEAF)] += first
        near[:, pl.ds(row + LEAF, LEAF)] += second_part + second
        near[:, pl.ds(row + 2 * LEAF, LEAF)] += third

    def near_step(pair, carry):
        near_two(pl.multiple_of(pair * (2 * LEAF), 2 * LEAF))
        return carry

    def side(block, at):
        lanes = jnp.where(low_half((1, 128)), 0, 1)
        return jnp.where(lanes == at, block, 0.0)

    def set_chain(levels, into):
        for at, (pairs, skels) in enumerate(levels):
            first = (1, 7, 11)[at]
            for p in range(len(pairs)):
                into[first + p, 0] = pairs[p]
                into[first + p, 1] = skels[p]

    def set_inner():
        row = (LEAVES - 2) * LEAF
        this, after = near_leaf(tile_a, row)
        fill_tile(tile_c, row + LEAF, row + 2 * LEAF, LEAF)
        own = field[1, :, row + 2 * LEAF : row + 3 * LEAF].astype(bf16)
        after += lax.dot_general(own, tile_c[...], NT, preferred_element_type=f32)
        near[:, row : row + LEAF] += this
        near[:, row + LEAF : row + 2 * LEAF] += after
        for slot in (2, 3):
            local[slot - 1] = cousins(chain, slot)

    def set_edges():
        s1 = raise_skel(s0, every_second)
        s2 = raise_skel(s1, every_second)

        set_chain([(c0, s0), (c1, s1), (c2, s2)], chain)
        for at, (pairs, skels) in enumerate([(c0, s0), (c1, s1), (c2, s2)]):
            edge_send[0, at, 0] = pairs[-1]
            edge_send[0, at, 1] = skels[-1]
            edge_send[1, at, 0] = pairs[0]
            edge_send[1, at, 1] = skels[0]
    def set_leaf_paths():
        x2 = jnp.concatenate([path_map[...].T[:64], transfer[2].T], axis=0)
        x0 = lower(lower([x2], maps[1]), maps[0])
        leaf_high[...], leaf_low[...] = split(jnp.concatenate(x0, axis=1))

    @pl.when(early == 1)
    def _():
        set_field()
        lax.fori_loop(0, ahead, near_step, 0)

    pl.semaphore_wait(
        barrier,
        MEMBERS - 1
        + sum(has.astype(jnp.int32) for has in before + after)
        + 2 * open_rim.astype(jnp.int32)
        + 4 * (2 - to_later[0] - to_later[1])
        - alone.astype(jnp.int32)
        + 4 * (from_earlier[0] + from_earlier[1]),
    )

    def tell(target):
        pl.semaphore_signal(ready, inc=1, device_id=(target,), device_id_type=MESH)

    for turn in range(2):

        @pl.when(from_earlier[turn] == 1)
        def _(turn=turn):
            far_each(turn, lambda k: tell(far_from[k] * MEMBERS + far_member))

    def remote(src, dst, send_sem, recv_sem, target):
        return pltpu.make_async_remote_copy(
            src_ref=src,
            dst_ref=dst,
            send_sem=send_sem,
            recv_sem=recv_sem,
            device_id=(target,),
            device_id_type=MESH,
        )

    def send(*ends):
        copy = remote(*ends)
        copy.start()
        return copy

    def wait_all(ref, semaphore):
        pltpu.make_async_copy(ref, ref, semaphore).wait()

    for mate in mates:
        send(u_buf.at[member], u_buf.at[member], u_send_sem, u_recv_sem, mate)

    set_map(2)
    every_eighth = (index == (lanes & 63) * 8).astype(f32).astype(bf16)
    s3 = pick(jnp.concatenate(s0, axis=1), every_eighth)
    c3 = raise_coef(c2, maps[2])[0]
    g_buf[member] = jnp.where(half == core, c3, s3)
    for mate in mates:
        send(g_buf.at[member], g_buf.at[member], g_send_sem, g_recv_sem, mate)

    rim_copies = [
        pltpu.make_async_remote_copy(
            src_ref=g_buf.at[member],
            dst_ref=rim_recv.at[core],
            send_sem=rim_send_sem.at[t],
            recv_sem=rim_recv_sem.at[core],
            device_id=(rim_devices[t],),
            device_id_type=MESH,
        )
        for t in range(2)
    ]

    @pl.when(open_rim)
    def _():
        for copy in rim_copies:
            copy.start()

    @pl.when(early == 0)
    def _():
        set_field()

    last = LEAF * LEAVES
    near_copies = [
        remote(
            field.at[:, :, last : last + LEAF],
            field.at[:, :, 0:LEAF],
            near_send_sem.at[0],
            near_recv_sem.at[0],
            right_device,
        ),
        remote(
            field.at[:, :, LEAF : 2 * LEAF],
            field.at[:, :, last + LEAF : last + 2 * LEAF],
            near_send_sem.at[1],
            near_recv_sem.at[1],
            left_device,
        ),
    ]

    def start(copies, at=0):
        for copy, has in zip(copies, (after[at], before[at])):
            pl.when(has)(copy.start)

    def receive(copies, at=0):
        for copy, has in zip(copies, (before[at], after[at])):
            pl.when(has)(copy.wait_recv)

    start(near_copies)

    edge_copies = [
        remote(
            edge_send.at[side],
            edge_recv.at[side],
            edge_send_sem.at[side],
            edge_recv_sem.at[side],
            (right_device, left_device)[side],
        )
        for side in range(2)
    ]

    set_edges()
    start(edge_copies)

    set_map(3)
    set_map(4)

    @pl.when(early == 1)
    def _():
        set_leaf_paths()

    wait_all(u_buf.at[pl.ds(0, MEMBERS - 1)], u_recv_sem)
    parts = [u_buf[at] for at in range(MEMBERS)]
    while len(parts) > 1:
        parts = [a + b for a, b in zip(parts[0::2], parts[1::2])]
    top_record = parts[0]
    swapped_record = pltpu.roll(top_record, 64, 1)
    far_send[0] = top_record
    far_send[1] = swapped_record

    @pl.when(alone)
    def _():
        far_buf[0] = far_send[0]

    def far_copy(k):
        return remote(
            far_send.at[k % 2],
            far_buf.at[k],
            far_send_sem.at[min(k, 1)],
            far_recv_sem.at[min(k, 1)],
            far_to[k],
        )

    first_far = far_copy(0)
    for turn in range(2):

        @pl.when(to_later[turn] == 0)
        def _(turn=turn):
            far_each(turn, lambda k: far_copy(k).start())

    wait_all(g_buf.at[pl.ds(0, MEMBERS - 1)], g_recv_sem)
    c3s, s3s = [], []
    for p in range(4):
        even, odd = g_buf[2 * p], g_buf[2 * p + 1]
        c3s.append(jnp.where(low, even, odd))
        s3s.append(pltpu.roll(jnp.where(low, odd, even), 64, 1))
    c4s, s4s = raise_coef(c3s, maps[3]), raise_skel(s3s, every_second)
    c5s, s5s = raise_coef(c4s, maps[4]), raise_skel(s4s, every_second)
    set_chain([(c3s, s3s), (c4s, s4s), (c5s, s5s)], g_chain)
    for at in range(2):
        bound_send[at, 0] = c5s[0]
        bound_send[at, 1] = s5s[0] + pltpu.roll(s4s[1 - at], 3, 0)
    bound_copies = [
        remote(
            bound_send.at[side],
            bound_recv.at[side],
            bound_send_sem.at[side],
            bound_recv_sem.at[side],
            (right_box, left_box)[side],
        )
        for side in range(2)
    ]
    quad_copy = remote(
        g_chain.at[7 + quad, 0],
        quad_recv,
        bound_send_sem.at[2],
        bound_recv_sem.at[2],
        quad_device,
    )
    start(bound_copies, 1)
    pl.when(inside)(quad_copy.start)

    def set_ends(ends, into):
        for level in range(3):
            into[(0, 6, 10)[level]] = ends[0, level]
            into[(5, 9, 12)[level]] = ends[1, level]

    def near_end(tile, row, col):
        fill_tile(tile, row, col, LEAF)
        near[:, row : row + LEAF] += lax.dot_general(
            field[1, :, col : col + LEAF].astype(bf16),
            tile[:, 0:LEAF],
            NT,
            preferred_element_type=f32,
        )

    def finish_ends():
        receive(near_copies)

        @pl.when(device == 0)
        def _():
            field[:, :, 0:LEAF] = jnp.zeros((2, 8, LEAF), f32)
            edge_recv[0] = jnp.zeros((3, 2, 8, 128), f32)

        @pl.when(device == total - 1)
        def _():
            field[:, :, last + LEAF : last + 2 * LEAF] = jnp.zeros((2, 8, LEAF), f32)
            edge_recv[1] = jnp.zeros((3, 2, 8, 128), f32)

        near_end(tile_c, 0, 0)
        near_end(tile_a, last - LEAF, last + LEAF)

        receive(edge_copies)
        set_ends(edge_recv, chain)
        for at, slot in [(0, 1), (3, 4), (4, 7), (5, 8), (6, 11)]:
            local[at] = cousins(chain, slot)

    @pl.when(early == 1)
    def _():
        lax.fori_loop(ahead, 3, near_step, 0)
        set_inner()
        finish_ends()

    later = to_later[0] + to_later[1]

    @pl.when(later > 0)
    def _():
        pl.semaphore_wait(ready, 4 * later)

    for turn in range(2):

        @pl.when(to_later[turn] == 1)
        def _(turn=turn):
            far_each(turn, lambda k: far_copy(k).start())

    @pl.when(early == 0)
    def _():
        lax.fori_loop(0, 3, near_step, 0)
        set_inner()
        set_leaf_paths()
        finish_ends()

    top_column = swapped_record.T[:64]
    tx, ty, tz = top_column[:, 0:1], top_column[:, 1:2], top_column[:, 2:3]

    wait_all(far_buf.at[pl.ds(1, strides - 1)], far_recv_sem.at[1])

    @pl.when(jnp.logical_not(alone))
    def _():
        first_far.wait_recv()

    top_coef, top_skel = [], []
    for k in range(0, strides, 2):
        halves = []
        for at in (k, k + 1):
            apart = far_from[at] - box
            counts = jnp.logical_or(apart >= 2, apart <= -2)
            halves.append((far_buf[at], counts))
        (one, one_counts), (two, two_counts) = halves
        coef = jnp.where(low, jnp.where(one_counts, one, 0.0), jnp.where(two_counts, two, 0.0))
        top_coef.append(pltpu.roll(coef, 64, 1))
        top_skel.append(jnp.where(low, two, one))
    top_tile = jnp.concatenate(
        [phi(tx, ty, tz, s[0:1], s[1:2], s[2:3], far_scale) for s in top_skel], axis=1
    )
    top = mm(jnp.concatenate(top_coef, axis=1), split(top_tile), NT)
    part_buf[member] = jnp.concatenate([top, jnp.zeros((8, 64), f32)], axis=1)
    for at in range(MEMBERS - 1):
        mate = box * MEMBERS + at + jnp.where(member <= at, 1, 0)
        send(part_buf.at[member], part_buf.at[member], part_send_sem, part_recv_sem, mate)

    wait_all(u_buf.at[pl.ds(0, MEMBERS - 1)], u_send_sem)
    wait_all(g_buf.at[pl.ds(0, MEMBERS - 1)], g_send_sem)
    wait_all(far_buf.at[pl.ds(1, strides - 1)], far_send_sem.at[1])
    for copies, at in ((near_copies, 0), (edge_copies, 0), (bound_copies, 1)):
        for copy, has in zip(copies, (after[at], before[at])):
            pl.when(has)(copy.wait_send)
    pl.when(inside)(quad_copy.wait_send)

    @pl.when(jnp.logical_not(alone))
    def _():
        first_far.wait_send()

    receive(bound_copies, 1)
    pl.when(inside)(quad_copy.wait_recv)
    start_skel = jnp.where(before[1], bound_recv[0, 1], 0.0)
    end_skel = jnp.where(after[1], bound_recv[1, 1], 0.0)
    g_chain[10, 0] = jnp.where(before[1], bound_recv[0, 0], 0.0)
    g_chain[10, 1] = start_skel
    g_chain[12, 0] = jnp.where(after[1], bound_recv[1, 0], 0.0)
    g_chain[12, 1] = end_skel
    quad_coef = jnp.where(inside, quad_recv[...], 0.0)
    g_chain[6, 0] = quad_coef
    g_chain[6, 1] = pltpu.roll(start_skel, 5, 0)
    g_chain[9, 0] = quad_coef
    g_chain[9, 1] = pltpu.roll(end_skel, 5, 0)

    @pl.when(jnp.logical_not(inside))
    def _():
        for slot in (0, 5):
            g_chain[slot] = jnp.zeros((2, 8, 128), f32)

    @pl.when(open_rim)
    def _():
        for copy in rim_copies:
            copy.wait_send()
        for t in range(2):
            pltpu.make_async_remote_copy(
                src_ref=g_buf.at[member],
                dst_ref=rim_recv.at[t],
                send_sem=rim_send_sem.at[t],
                recv_sem=rim_recv_sem.at[t],
                device_id=(rim_devices[t],),
                device_id_type=MESH,
            ).wait_recv()
        even, odd = rim_recv[0], rim_recv[1]
        rim_coef = jnp.where(low, even, odd)
        rim_skel = pltpu.roll(jnp.where(low, odd, even), 64, 1)
        for slot in (0, 5):
            g_chain[slot, 0] = rim_coef
            g_chain[slot, 1] = rim_skel

    local3 = cousins(g_chain, 1 + y)
    local4 = cousins(g_chain, 7 + quad)
    local5 = cousins(g_chain, 11)
    y2 = local[6]
    y1 = [x + local[4 + at] for at, x in enumerate(lower([y2], maps[1]))]
    y0 = [x + local[at] for at, x in enumerate(lower(y1, maps[0]))]
    y4 = local4 + mm(side(local5, quad), maps[4], NT)
    y3 = local3 + mm(side(y4, rem(y, 2)), maps[3], NT)
    y3 = jnp.where(core == 1, y3, pltpu.roll(y3, 64, 1))

    wait_all(part_buf.at[pl.ds(0, MEMBERS - 1)], part_recv_sem)
    parts = [part_buf[at] for at in range(MEMBERS)]
    while len(parts) > 1:
        parts = [a + b for a, b in zip(parts[0::2], parts[1::2])]
    d6 = parts[0]
    d63 = jnp.where(low, d6, y3)
    d0 = jnp.concatenate(y0, axis=1) + mm(d63, (leaf_high, leaf_low), NN)
    for p in range(4):
        pair = d0[:, 128 * p : 128 * p + 128]
        two = jnp.concatenate([jnp.where(low, pair, 0.0), jnp.where(low, 0.0, pair)], axis=0)
        rows = lax.dot_general(
            two.astype(bf16),
            basis[128 * p : 128 * p + 128, :],
            NN,
            preferred_element_type=f32,
        )
        for t in range(2):
            leaf = 2 * p + t
            at = leaf * LEAF
            out_ref[:, at : at + LEAF] = jnp.where(
                slots < occ[leaf], near[:, at : at + LEAF] + rows[8 * t : 8 * t + 8], 0.0
            )

    wait_all(part_buf.at[pl.ds(0, MEMBERS - 1)], part_send_sem)


def body(boxes, across, coords, loads, occupancy, basis, transfer):
    strides = boxes // MEMBERS
    hbm = pl.BlockSpec(memory_space=pl.ANY)
    dma = pltpu.SemaphoreType.DMA
    return pl.pallas_call(
        functools.partial(kernel, boxes, across),
        out_shape=jax.ShapeDtypeStruct((COLS, OWN), f32),
        in_specs=[hbm] * 5,
        out_specs=pl.BlockSpec(memory_space=pltpu.VMEM),
        scratch_shapes=[
            pltpu.VMEM((3, OWN), f32),
            pltpu.VMEM((COLS, OWN), bf16),
            pltpu.SMEM((LEAVES,), jnp.int32),
            pltpu.VMEM((LEAVES * 64, LEAF), bf16),
            pltpu.VMEM((6, 128, 64), f32),
            pltpu.VMEM((6, 128, 128), bf16),
            pltpu.VMEM((6, 128, 128), bf16),
            pltpu.VMEM((128, 128), f32),
            pltpu.VMEM((2, 8, OWN + 2 * LEAF), f32),
            pltpu.VMEM((OWN, 8), f32),
            pltpu.VMEM((128, 512), bf16),
            pltpu.VMEM((128, 512), bf16),
            pltpu.VMEM((COLS, OWN + LEAF), f32),
            pltpu.VMEM((LEAF, 2 * LEAF), bf16),
            pltpu.VMEM((LEAF, 2 * LEAF), bf16),
            pltpu.VMEM((LEAF, LEAF), bf16),
            pltpu.VMEM((13, 2, 8, 128), f32),
            pltpu.VMEM((13, 2, 8, 128), f32),
            pltpu.VMEM((7, 8, 128), f32),
            pltpu.VMEM((2, 3, 2, 8, 128), f32),
            pltpu.VMEM((2, 3, 2, 8, 128), f32),
            pltpu.VMEM((MEMBERS, 8, 128), f32),
            pltpu.VMEM((MEMBERS, 8, 128), f32),
            pltpu.VMEM((2, 2, 8, 128), f32),
            pltpu.VMEM((2, 2, 8, 128), f32),
            pltpu.VMEM((8, 128), f32),
            pltpu.VMEM((2, 8, 128), f32),
            pltpu.VMEM((2, 8, 128), f32),
            pltpu.VMEM((strides, 8, 128), f32),
            pltpu.VMEM((MEMBERS, 8, 128), f32),
            dma((5,)),
            dma((2,)),
            dma((2,)),
            dma((2,)),
            dma((2,)),
            dma,
            dma,
            dma,
            dma,
            dma((3,)),
            dma((3,)),
            dma((2,)),
            dma((2,)),
            dma((2,)),
            dma((2,)),
            dma,
            dma,
            pltpu.SemaphoreType.REGULAR,
        ],
        compiler_params=pltpu.CompilerParams(
            collective_id=0, has_side_effects=True, vmem_limit_bytes=32 * 1024 * 1024
        ),
    )(
        *[
            pltpu.with_memory_space_constraint(x, pltpu.HBM)
            for x in (
                coords,
                loads,
                occupancy,
                basis.reshape(LEAVES * 64, LEAF),
                transfer.reshape(6, 128, 64),
            )
        ]
    )


def solution(mesh):
    boxes = mesh.shape["box"] // MEMBERS
    return jax.shard_map(
        functools.partial(body, boxes, 4),
        mesh=mesh,
        in_specs=(P(None, "box"), P(None, "box"), P("box"), P("box", None, None), P()),
        out_specs=P(None, "box"),
        check_vma=False,
    )
```

```python
import functools

import jax
import jax.numpy as jnp
from jax import lax
from jax.experimental import pallas as pl
from jax.experimental.pallas import tpu as pltpu
from jax.sharding import PartitionSpec as P

LEAF = 256
COLS = 8
LEAVES = 8
MEMBERS = 8
OWN = LEAF * LEAVES

f32 = jnp.float32
bf16 = jnp.bfloat16
soften = 0.0001
near_scale = 0.0625
far_scale = 0.125
NN = (((1,), (0,)), ((), ()))
NT = (((1,), (1,)), ((), ()))
MESH = pl.DeviceIdType.MESH


def div(a, b):
    return lax.div(a, jnp.int32(b))


def rem(a, b):
    return lax.rem(a, jnp.int32(b))


def phi(tx, ty, tz, sx, sy, sz, scale):
    dx = tx - sx
    dy = ty - sy
    dz = tz - sz
    r2 = dx * dx + dy * dy + dz * dz
    return (r2 * (0.5 * scale)) * jnp.log(r2 + soften)


def split(x):
    high = x.astype(bf16)
    return high, (x - high.astype(f32)).astype(bf16)


def mm(a, b, dims):
    rows = a.shape[0]
    high = a.astype(bf16).astype(f32)
    stacked = jnp.concatenate([high, a - high], axis=0).astype(bf16)
    both = lax.dot_general(stacked, b[0][...], dims, preferred_element_type=f32)
    low = lax.dot_general(stacked[:rows], b[1][...], dims, preferred_element_type=f32)
    return both[:rows] + (both[rows:] + low)


def low_half(shape):
    return lax.broadcasted_iota(jnp.int32, shape, len(shape) - 1) < 64


def merge(rows):
    count = rows.shape[0] // 16
    low = low_half((8, 128))
    return [
        jnp.where(low, rows[16 * i : 16 * i + 8], rows[16 * i + 8 : 16 * i + 16])
        for i in range(count)
    ]


def raise_coef(pairs, level_map):
    rows = mm(jnp.concatenate(pairs, axis=0), level_map, NN)
    return merge(rows) if len(pairs) > 1 else [rows]


def pick(x, entries):
    rows = x.shape[0]
    a = x.astype(bf16).astype(f32)
    b = (x - a).astype(bf16).astype(f32)
    c = (x - a) - b
    stacked = jnp.concatenate([a, b, c], axis=0).astype(bf16)
    picked = lax.dot_general(stacked, entries, NN, preferred_element_type=f32)
    return picked[:rows] + picked[rows : 2 * rows] + picked[2 * rows :]


def raise_skel(pairs, every_second):
    rows_up = pick(jnp.concatenate(pairs, axis=0), every_second)
    return merge(rows_up) if len(pairs) > 1 else [rows_up]


def cousins(chain, slot):
    low = low_half((8, 128))
    column = chain[slot, 1].T
    tx, ty, tz = column[:, 0:1], column[:, 1:2], column[:, 2:3]
    before, after = chain[slot - 1, 0], chain[slot + 1, 0]
    tiles = []
    for skel in (chain[slot - 1, 1], chain[slot + 1, 1]):
        tiles.append(phi(tx, ty, tz, skel[0:1], skel[1:2], skel[2:3], far_scale))
    tile = jnp.concatenate(tiles, axis=1)
    even = jnp.concatenate([jnp.where(low, before, 0.0), after], axis=1)
    odd = jnp.concatenate([before, jnp.where(low, 0.0, after)], axis=1)
    rows = mm(jnp.concatenate([even, odd], axis=0), split(tile), NT)
    return jnp.where(low, rows[:8], rows[8:])


def lower(pairs, level_map):
    height = pairs[0].shape[0]
    low = low_half((height, 128))
    stacked = []
    for pair in pairs:
        stacked += [jnp.where(low, pair, 0.0), jnp.where(low, 0.0, pair)]
    rows = mm(jnp.concatenate(stacked, axis=0), level_map, NT)
    return [rows[height * i : height * (i + 1)] for i in range(2 * len(pairs))]


def kernel(
    boxes,
    across,
    coords_hbm,
    loads_hbm,
    occ_hbm,
    basis_hbm,
    transfer_hbm,
    out_ref,
    coords,
    loads,
    occ,
    basis,
    transfer,
    map_high,
    map_low,
    path_map,
    field,
    column,
    leaf_high,
    leaf_low,
    near,
    tile_a,
    tile_b,
    tile_c,
    chain,
    g_chain,
    local,
    edge_send,
    edge_recv,
    u_buf,
    g_buf,
    bound_send,
    bound_recv,
    quad_recv,
    rim_recv,
    far_send,
    far_buf,
    part_buf,
    load_sem,
    near_send_sem,
    near_recv_sem,
    edge_send_sem,
    edge_recv_sem,
    u_send_sem,
    u_recv_sem,
    g_send_sem,
    g_recv_sem,
    bound_send_sem,
    bound_recv_sem,
    rim_send_sem,
    rim_recv_sem,
    far_send_sem,
    far_recv_sem,
    part_send_sem,
    part_recv_sem,
    ready,
):
    loading = [
        pltpu.make_async_copy(src, dst, load_sem.at[at])
        for at, (src, dst) in enumerate(
            [
                (coords_hbm, coords),
                (transfer_hbm, transfer),
                (loads_hbm, loads),
                (occ_hbm, occ),
                (basis_hbm, basis),
            ]
        )
    ]
    for copy in loading:
        copy.start()

    device = lax.axis_index("box")
    total = boxes * MEMBERS
    strides = boxes // MEMBERS
    depth = boxes // (2 * across)
    box, member = div(device, MEMBERS), rem(device, MEMBERS)
    x, z, y_half = div(box, 2 * depth), rem(div(box, 2), depth), rem(box, 2)
    y, core = div(member, 2), rem(member, 2)
    low = low_half((8, 128))
    half = jnp.where(low, 0, 1)

    top = jnp.where(y == 3, 1, 0)
    outer = jnp.where(y == 0, 1, top)
    side_to = jnp.where(outer == 1, top, 2 - y)
    side_from = jnp.where(outer == 1, 1 - top, 2 - y)
    far_half = jnp.where(outer == 1, 1 - y_half, y_half)
    z_core = rem(div(z, 2), 2)
    far_member = 2 * jnp.where(outer == 1, 3 - y, y) + z_core
    z_high, z_low = div(z, 4), rem(z, 2)
    far_x = [rem(x + dx, across) for dx in range(across)]
    far_steps = [(dx, turn) for dx in range(across) for turn in range(2)]

    def far_depths(side):
        first = 4 * rem(side + z_high, 2) + 2 * core
        return [first, first + 1]

    to_z, from_z = far_depths(side_to), far_depths(side_from)

    def far_box(depths, dx, turn):
        return (far_x[dx % across] * depth + depths[turn]) * 2 + far_half

    far_to = [far_box(to_z, dx, turn) * MEMBERS + far_member for dx, turn in far_steps]
    far_from = [far_box(from_z, -dx, turn) for dx, turn in far_steps]
    alone = jnp.logical_and(jnp.logical_and(outer == 0, side_to == 0), core == z_core)

    barrier = pltpu.get_barrier_semaphore()

    def greet(target):
        pl.semaphore_signal(barrier, inc=1, device_id=(target,), device_id_type=MESH)

    def order(at):
        return jnp.where(at == 0, 0, jnp.where(at >= 6, 2, 1))

    mine = order(z)
    to_later = [jnp.where(order(at) > mine, 1, 0) for at in to_z]
    from_earlier = [jnp.where(order(at) < mine, 1, 0) for at in from_z]
    far_order = [(2 * dx + turn) for turn in range(2) for dx in (2, 1, 3, 0)]

    def far_each(turn, act):
        for k in far_order[4 * turn : 4 * turn + 4]:
            if k == turn:
                pl.when(jnp.logical_not(jnp.logical_and(alone, z_low == turn)))(
                    functools.partial(act, k)
                )
            else:
                act(k)

    for turn in range(2):

        @pl.when(from_earlier[turn] == 0)
        def _(turn=turn):
            far_each(turn, lambda k: greet(far_from[k] * MEMBERS + far_member))

        @pl.when(to_later[turn] == 1)
        def _(turn=turn):
            far_each(turn, lambda k: greet(far_to[k]))

    left_device = rem(device + total - 1, total)
    right_device = rem(device + 1, total)
    mirror = 2 * (3 - y) + core
    left_box = rem(box + boxes - 1, boxes) * MEMBERS + mirror
    right_box = rem(box + 1, boxes) * MEMBERS + mirror
    mates = [box * MEMBERS + rem(member + r, MEMBERS) for r in (6, 2, 7, 3, 5, 4, 1)]
    at_rim = outer == 1
    rim_box = rem(box + boxes + 2 * top - 1, boxes)
    rim_devices = [rim_box * MEMBERS + 6 - 6 * top + t for t in range(2)]
    quad = div(member, 4)
    quad_device = rem(box + boxes + 2 * quad - 1, boxes) * MEMBERS + mirror
    early = jnp.where(z == 0, 1, 0)
    ahead = 2
    before = [device > 0, box > 0]
    after = [device < total - 1, box < boxes - 1]
    inside = jnp.where(quad == 0, box, boxes - 1 - box) > 0
    open_rim = jnp.logical_and(at_rim, inside)

    for target in mates:
        greet(target)
    for has, targets in ((before, (left_device, left_box)), (after, (right_device, right_box))):
        for at in range(2):
            pl.when(has[at])(functools.partial(greet, targets[at]))

    @pl.when(open_rim)
    def _():
        for target in rim_devices:
            greet(target)

    lanes = lax.broadcasted_iota(jnp.int32, (1, 128), 1)
    index = lax.broadcasted_iota(jnp.int32, (512, 128), 0)
    placed = (index == (lanes - 64 - 8 * member) * 64).astype(f32).astype(bf16)
    picks = (lax.broadcasted_iota(jnp.int32, (1, 128), 1) & 63) * 2
    every_second = (
        (lax.broadcasted_iota(jnp.int32, (128, 128), 0) == picks).astype(f32).astype(bf16)
    )
    for copy in loading:
        copy.wait()
    points = jnp.concatenate([coords[...], jnp.zeros((5, OWN), f32)], axis=0)
    s0 = [
        jnp.concatenate(
            [points[:, 512 * p : 512 * p + 64], points[:, 512 * p + 256 : 512 * p + 320]], axis=1
        )
        for p in range(4)
    ]
    s6 = pick(jnp.concatenate(s0, axis=1), placed)

    maps = [(map_high.at[level], map_low.at[level]) for level in range(6)]

    def set_map(level):
        once = transfer[level]
        map_high[level], map_low[level] = split(jnp.concatenate([once, once], axis=1))

    for level in range(2):
        set_map(level)
    slots = lax.broadcasted_iota(jnp.int32, (COLS, LEAF), 1)
    live = []
    for leaf in range(LEAVES):
        part = loads[:, leaf * LEAF : (leaf + 1) * LEAF].astype(f32)
        live.append(jnp.where(slots < occ[leaf], part, 0.0))
    c0 = []
    for p in range(4):
        two = jnp.concatenate([live[2 * p], live[2 * p + 1]], axis=0).astype(bf16)
        rows = lax.dot_general(
            two, basis[128 * p : 128 * p + 128, :], NT, preferred_element_type=f32
        )
        c0.append(jnp.where(low, rows[:8], rows[8:]))
    c1 = raise_coef(c0, maps[0])
    c2 = raise_coef(c1, maps[1])
    def factor(level, at):
        return transfer[level, pl.ds(pl.multiple_of(64 * at, 64), 64), :]

    map_34 = mm(transfer[2], split(factor(3, core)), NN)
    wide = jnp.concatenate([factor(5, quad), jnp.zeros((64, 64), f32)], axis=1)
    map_56 = mm(factor(4, rem(y, 2)), split(wide), NN)
    map_6 = mm(map_34, split(map_56), NN)
    u_buf[member] = mm(c2[0], split(map_6), NN) + s6
    path_map[...] = map_6

    set_map(2)
    every_eighth = (index == (lanes & 63) * 8).astype(f32).astype(bf16)
    s3 = pick(jnp.concatenate(s0, axis=1), every_eighth)
    c3 = raise_coef(c2, maps[2])[0]
    g_buf[member] = jnp.where(half == core, c3, s3)

    def set_field():
        field[0, :, LEAF : LEAF + OWN] = points
        for leaf in range(LEAVES):
            field[1, :, (leaf + 1) * LEAF : (leaf + 2) * LEAF] = live[leaf]
        for at in range(0, OWN, 128):
            column[at : at + 128, :] = points[:, at : at + 128].T
        near[...] = jnp.zeros_like(near)

    def fill_tile(tile, row, col, width):
        sx = field[0, 0:1, pl.ds(col, width)]
        sy = field[0, 1:2, pl.ds(col, width)]
        sz = field[0, 2:3, pl.ds(col, width)]
        for at in range(0, LEAF, 16):
            rows = column[pl.ds(row + at, 16), :]
            tile[at : at + 16, 0:width] = phi(
                rows[:, 0:1], rows[:, 1:2], rows[:, 2:3], sx, sy, sz, near_scale
            ).astype(bf16)

    def near_leaf(tile, row):
        col = row + LEAF
        fill_tile(tile, row, col, 2 * LEAF)
        loads_two = field[1, :, pl.ds(col, 2 * LEAF)].astype(bf16)
        this = lax.dot_general(loads_two, tile[...], NT, preferred_element_type=f32)
        after = lax.dot_general(
            loads_two[:, :LEAF], tile[:, LEAF:], NN, preferred_element_type=f32
        )
        return this, after

    def near_two(row):
        first, second_part = near_leaf(tile_a, row)
        second, third = near_leaf(tile_b, row + LEAF)
        near[:, pl.ds(row, LEAF)] += first
        near[:, pl.ds(row + LEAF, LEAF)] += second_part + second
        near[:, pl.ds(row + 2 * LEAF, LEAF)] += third

    def near_step(pair, carry):
        near_two(pl.multiple_of(pair * (2 * LEAF), 2 * LEAF))
        return carry

    def side(block, at):
        lanes = jnp.where(low_half((1, 128)), 0, 1)
        return jnp.where(lanes == at, block, 0.0)

    def set_chain(levels, into):
        for at, (pairs, skels) in enumerate(levels):
            first = (1, 7, 11)[at]
            for p in range(len(pairs)):
                into[first + p, 0] = pairs[p]
                into[first + p, 1] = skels[p]

    def set_inner():
        row = (LEAVES - 2) * LEAF
        this, after = near_leaf(tile_a, row)
        fill_tile(tile_c, row + LEAF, row + 2 * LEAF, LEAF)
        own = field[1, :, row + 2 * LEAF : row + 3 * LEAF].astype(bf16)
        after += lax.dot_general(own, tile_c[...], NT, preferred_element_type=f32)
        near[:, row : row + LEAF] += this
        near[:, row + LEAF : row + 2 * LEAF] += after
        for slot in (2, 3):
            local[slot - 1] = cousins(chain, slot)

    def set_edges():
        s1 = raise_skel(s0, every_second)
        s2 = raise_skel(s1, every_second)

        set_chain([(c0, s0), (c1, s1), (c2, s2)], chain)
        for at, (pairs, skels) in enumerate([(c0, s0), (c1, s1), (c2, s2)]):
            edge_send[0, at, 0] = pairs[-1]
            edge_send[0, at, 1] = skels[-1]
            edge_send[1, at, 0] = pairs[0]
            edge_send[1, at, 1] = skels[0]
    def set_leaf_paths():
        x2 = jnp.concatenate([path_map[...].T[:64], transfer[2].T], axis=0)
        x0 = lower(lower([x2], maps[1]), maps[0])
        leaf_high[...], leaf_low[...] = split(jnp.concatenate(x0, axis=1))

    @pl.when(early == 1)
    def _():
        set_field()
        lax.fori_loop(0, ahead, near_step, 0)

    pl.semaphore_wait(
        barrier,
        MEMBERS - 1
        + sum(has.astype(jnp.int32) for has in before + after)
        + 2 * open_rim.astype(jnp.int32)
        + 4 * (2 - to_later[0] - to_later[1])
        - alone.astype(jnp.int32)
        + 4 * (from_earlier[0] + from_earlier[1]),
    )

    def tell(target):
        pl.semaphore_signal(ready, inc=1, device_id=(target,), device_id_type=MESH)

    for turn in range(2):

        @pl.when(from_earlier[turn] == 1)
        def _(turn=turn):
            far_each(turn, lambda k: tell(far_from[k] * MEMBERS + far_member))

    def remote(src, dst, send_sem, recv_sem, target):
        return pltpu.make_async_remote_copy(
            src_ref=src,
            dst_ref=dst,
            send_sem=send_sem,
            recv_sem=recv_sem,
            device_id=(target,),
            device_id_type=MESH,
        )

    def send(*ends):
        copy = remote(*ends)
        copy.start()
        return copy

    def wait_all(ref, semaphore):
        pltpu.make_async_copy(ref, ref, semaphore).wait()

    first = (6, 2, 7, 3, 0, 4, 1, 5)
    place = sum(jnp.where(member == at, rank, 0) for rank, at in enumerate(first))
    for rank in range(MEMBERS - 1):
        mate = box * MEMBERS + jnp.where(place <= rank, first[rank + 1], first[rank])
        send(u_buf.at[member], u_buf.at[member], u_send_sem, u_recv_sem, mate)

    for mate in mates:
        send(g_buf.at[member], g_buf.at[member], g_send_sem, g_recv_sem, mate)

    rim_copies = [
        pltpu.make_async_remote_copy(
            src_ref=g_buf.at[member],
            dst_ref=rim_recv.at[core],
            send_sem=rim_send_sem.at[t],
            recv_sem=rim_recv_sem.at[core],
            device_id=(rim_devices[t],),
            device_id_type=MESH,
        )
        for t in range(2)
    ]

    @pl.when(open_rim)
    def _():
        for copy in rim_copies:
            copy.start()

    @pl.when(early == 0)
    def _():
        set_field()

    last = LEAF * LEAVES
    near_copies = [
        remote(
            field.at[:, :, last : last + LEAF],
            field.at[:, :, 0:LEAF],
            near_send_sem.at[0],
            near_recv_sem.at[0],
            right_device,
        ),
        remote(
            field.at[:, :, LEAF : 2 * LEAF],
            field.at[:, :, last + LEAF : last + 2 * LEAF],
            near_send_sem.at[1],
            near_recv_sem.at[1],
            left_device,
        ),
    ]

    def start(copies, at=0):
        for copy, has in zip(copies, (after[at], before[at])):
            pl.when(has)(copy.start)

    def receive(copies, at=0):
        for copy, has in zip(copies, (before[at], after[at])):
            pl.when(has)(copy.wait_recv)

    start(near_copies)

    edge_copies = [
        remote(
            edge_send.at[side],
            edge_recv.at[side],
            edge_send_sem.at[side],
            edge_recv_sem.at[side],
            (right_device, left_device)[side],
        )
        for side in range(2)
    ]

    set_edges()
    start(edge_copies)

    set_map(3)
    set_map(4)

    @pl.when(early == 1)
    def _():
        set_leaf_paths()

    wait_all(u_buf.at[pl.ds(0, MEMBERS - 1)], u_recv_sem)
    parts = [u_buf[at] for at in range(MEMBERS)]
    while len(parts) > 1:
        parts = [a + b for a, b in zip(parts[0::2], parts[1::2])]
    top_record = parts[0]
    swapped_record = pltpu.roll(top_record, 64, 1)
    far_send[...] = jnp.where(z_low == 0, top_record, swapped_record)

    @pl.when(alone)
    def _():
        far_buf[z_low] = far_send[...]

    def far_copy(k):
        slot = k - k % 2 + z_low
        return remote(far_send, far_buf.at[slot], far_send_sem, far_recv_sem, far_to[k])

    def far_wait(semaphore):
        @pl.when(alone)
        def _():
            wait_all(far_buf.at[pl.ds(1, strides - 1)], semaphore)

        @pl.when(jnp.logical_not(alone))
        def _():
            wait_all(far_buf, semaphore)

    for turn in range(2):

        @pl.when(to_later[turn] == 0)
        def _(turn=turn):
            far_each(turn, lambda k: far_copy(k).start())

    wait_all(g_buf.at[pl.ds(0, MEMBERS - 1)], g_recv_sem)
    c3s, s3s = [], []
    for p in range(4):
        even, odd = g_buf[2 * p], g_buf[2 * p + 1]
        c3s.append(jnp.where(low, even, odd))
        s3s.append(pltpu.roll(jnp.where(low, odd, even), 64, 1))
    c4s, s4s = raise_coef(c3s, maps[3]), raise_skel(s3s, every_second)
    c5s, s5s = raise_coef(c4s, maps[4]), raise_skel(s4s, every_second)
    set_chain([(c3s, s3s), (c4s, s4s), (c5s, s5s)], g_chain)
    for at in range(2):
        bound_send[at, 0] = c5s[0]
        bound_send[at, 1] = s5s[0] + pltpu.roll(s4s[1 - at], 3, 0)
    bound_copies = [
        remote(
            bound_send.at[side],
            bound_recv.at[side],
            bound_send_sem.at[side],
            bound_recv_sem.at[side],
            (right_box, left_box)[side],
        )
        for side in range(2)
    ]
    quad_copy = remote(
        g_chain.at[7 + quad, 0],
        quad_recv,
        bound_send_sem.at[2],
        bound_recv_sem.at[2],
        quad_device,
    )
    start(bound_copies, 1)
    pl.when(inside)(quad_copy.start)

    def set_ends(ends, into):
        for level in range(3):
            into[(0, 6, 10)[level]] = ends[0, level]
            into[(5, 9, 12)[level]] = ends[1, level]

    def near_end(tile, row, col):
        fill_tile(tile, row, col, LEAF)
        near[:, row : row + LEAF] += lax.dot_general(
            field[1, :, col : col + LEAF].astype(bf16),
            tile[:, 0:LEAF],
            NT,
            preferred_element_type=f32,
        )

    def finish_ends():
        receive(near_copies)

        @pl.when(device == 0)
        def _():
            field[:, :, 0:LEAF] = jnp.zeros((2, 8, LEAF), f32)
            edge_recv[0] = jnp.zeros((3, 2, 8, 128), f32)

        @pl.when(device == total - 1)
        def _():
            field[:, :, last + LEAF : last + 2 * LEAF] = jnp.zeros((2, 8, LEAF), f32)
            edge_recv[1] = jnp.zeros((3, 2, 8, 128), f32)

        near_end(tile_c, 0, 0)
        near_end(tile_a, last - LEAF, last + LEAF)

        receive(edge_copies)
        set_ends(edge_recv, chain)
        for at, slot in [(0, 1), (3, 4), (4, 7), (5, 8), (6, 11)]:
            local[at] = cousins(chain, slot)

    @pl.when(early == 1)
    def _():
        lax.fori_loop(ahead, 3, near_step, 0)
        set_inner()
        finish_ends()

    later = to_later[0] + to_later[1]

    @pl.when(later > 0)
    def _():
        pl.semaphore_wait(ready, 4 * later)

    for turn in range(2):

        @pl.when(to_later[turn] == 1)
        def _(turn=turn):
            far_each(turn, lambda k: far_copy(k).start())

    @pl.when(early == 0)
    def _():
        lax.fori_loop(0, 3, near_step, 0)
        set_inner()
        set_leaf_paths()
        finish_ends()

    top_column = swapped_record.T[:64]
    tx, ty, tz = top_column[:, 0:1], top_column[:, 1:2], top_column[:, 2:3]

    far_wait(far_recv_sem)

    top_coef, top_skel = [], []
    for k in range(0, strides, 2):
        halves = []
        for at in (k, k + 1):
            apart = far_from[at] - box
            counts = jnp.logical_or(apart >= 2, apart <= -2)
            halves.append((far_buf[at], counts))
        (one, one_counts), (two, two_counts) = halves
        coef = jnp.where(low, jnp.where(one_counts, one, 0.0), jnp.where(two_counts, two, 0.0))
        top_coef.append(pltpu.roll(coef, 64, 1))
        top_skel.append(jnp.where(low, two, one))
    top_tile = jnp.concatenate(
        [phi(tx, ty, tz, s[0:1], s[1:2], s[2:3], far_scale) for s in top_skel], axis=1
    )
    top = mm(jnp.concatenate(top_coef, axis=1), split(top_tile), NT)
    part_buf[member] = jnp.concatenate([top, jnp.zeros((8, 64), f32)], axis=1)
    for at in range(MEMBERS - 1):
        mate = box * MEMBERS + at + jnp.where(member <= at, 1, 0)
        send(part_buf.at[member], part_buf.at[member], part_send_sem, part_recv_sem, mate)

    wait_all(u_buf.at[pl.ds(0, MEMBERS - 1)], u_send_sem)
    wait_all(g_buf.at[pl.ds(0, MEMBERS - 1)], g_send_sem)
    far_wait(far_send_sem)
    for copies, at in ((near_copies, 0), (edge_copies, 0), (bound_copies, 1)):
        for copy, has in zip(copies, (after[at], before[at])):
            pl.when(has)(copy.wait_send)
    pl.when(inside)(quad_copy.wait_send)

    receive(bound_copies, 1)
    pl.when(inside)(quad_copy.wait_recv)
    start_skel = jnp.where(before[1], bound_recv[0, 1], 0.0)
    end_skel = jnp.where(after[1], bound_recv[1, 1], 0.0)
    g_chain[10, 0] = jnp.where(before[1], bound_recv[0, 0], 0.0)
    g_chain[10, 1] = start_skel
    g_chain[12, 0] = jnp.where(after[1], bound_recv[1, 0], 0.0)
    g_chain[12, 1] = end_skel
    quad_coef = jnp.where(inside, quad_recv[...], 0.0)
    g_chain[6, 0] = quad_coef
    g_chain[6, 1] = pltpu.roll(start_skel, 5, 0)
    g_chain[9, 0] = quad_coef
    g_chain[9, 1] = pltpu.roll(end_skel, 5, 0)

    @pl.when(jnp.logical_not(inside))
    def _():
        for slot in (0, 5):
            g_chain[slot] = jnp.zeros((2, 8, 128), f32)

    @pl.when(open_rim)
    def _():
        for copy in rim_copies:
            copy.wait_send()
        for t in range(2):
            pltpu.make_async_remote_copy(
                src_ref=g_buf.at[member],
                dst_ref=rim_recv.at[t],
                send_sem=rim_send_sem.at[t],
                recv_sem=rim_recv_sem.at[t],
                device_id=(rim_devices[t],),
                device_id_type=MESH,
            ).wait_recv()
        even, odd = rim_recv[0], rim_recv[1]
        rim_coef = jnp.where(low, even, odd)
        rim_skel = pltpu.roll(jnp.where(low, odd, even), 64, 1)
        for slot in (0, 5):
            g_chain[slot, 0] = rim_coef
            g_chain[slot, 1] = rim_skel

    local3 = cousins(g_chain, 1 + y)
    local4 = cousins(g_chain, 7 + quad)
    local5 = cousins(g_chain, 11)
    y2 = local[6]
    y1 = [x + local[4 + at] for at, x in enumerate(lower([y2], maps[1]))]
    y0 = [x + local[at] for at, x in enumerate(lower(y1, maps[0]))]
    y4 = local4 + mm(side(local5, quad), maps[4], NT)
    y3 = local3 + mm(side(y4, rem(y, 2)), maps[3], NT)
    y3 = jnp.where(core == 1, y3, pltpu.roll(y3, 64, 1))

    wait_all(part_buf.at[pl.ds(0, MEMBERS - 1)], part_recv_sem)
    parts = [part_buf[at] for at in range(MEMBERS)]
    while len(parts) > 1:
        parts = [a + b for a, b in zip(parts[0::2], parts[1::2])]
    d6 = parts[0]
    d63 = jnp.where(low, d6, y3)
    d0 = jnp.concatenate(y0, axis=1) + mm(d63, (leaf_high, leaf_low), NN)
    for p in range(4):
        pair = d0[:, 128 * p : 128 * p + 128]
        two = jnp.concatenate([jnp.where(low, pair, 0.0), jnp.where(low, 0.0, pair)], axis=0)
        rows = lax.dot_general(
            two.astype(bf16),
            basis[128 * p : 128 * p + 128, :],
            NN,
            preferred_element_type=f32,
        )
        for t in range(2):
            leaf = 2 * p + t
            at = leaf * LEAF
            out_ref[:, at : at + LEAF] = jnp.where(
                slots < occ[leaf], near[:, at : at + LEAF] + rows[8 * t : 8 * t + 8], 0.0
            )

    wait_all(part_buf.at[pl.ds(0, MEMBERS - 1)], part_send_sem)


def body(boxes, across, coords, loads, occupancy, basis, transfer):
    strides = boxes // MEMBERS
    hbm = pl.BlockSpec(memory_space=pl.ANY)
    dma = pltpu.SemaphoreType.DMA
    return pl.pallas_call(
        functools.partial(kernel, boxes, across),
        out_shape=jax.ShapeDtypeStruct((COLS, OWN), f32),
        in_specs=[hbm] * 5,
        out_specs=pl.BlockSpec(memory_space=pltpu.VMEM),
        scratch_shapes=[
            pltpu.VMEM((3, OWN), f32),
            pltpu.VMEM((COLS, OWN), bf16),
            pltpu.SMEM((LEAVES,), jnp.int32),
            pltpu.VMEM((LEAVES * 64, LEAF), bf16),
            pltpu.VMEM((6, 128, 64), f32),
            pltpu.VMEM((6, 128, 128), bf16),
            pltpu.VMEM((6, 128, 128), bf16),
            pltpu.VMEM((128, 128), f32),
            pltpu.VMEM((2, 8, OWN + 2 * LEAF), f32),
            pltpu.VMEM((OWN, 8), f32),
            pltpu.VMEM((128, 512), bf16),
            pltpu.VMEM((128, 512), bf16),
            pltpu.VMEM((COLS, OWN + LEAF), f32),
            pltpu.VMEM((LEAF, 2 * LEAF), bf16),
            pltpu.VMEM((LEAF, 2 * LEAF), bf16),
            pltpu.VMEM((LEAF, LEAF), bf16),
            pltpu.VMEM((13, 2, 8, 128), f32),
            pltpu.VMEM((13, 2, 8, 128), f32),
            pltpu.VMEM((7, 8, 128), f32),
            pltpu.VMEM((2, 3, 2, 8, 128), f32),
            pltpu.VMEM((2, 3, 2, 8, 128), f32),
            pltpu.VMEM((MEMBERS, 8, 128), f32),
            pltpu.VMEM((MEMBERS, 8, 128), f32),
            pltpu.VMEM((2, 2, 8, 128), f32),
            pltpu.VMEM((2, 2, 8, 128), f32),
            pltpu.VMEM((8, 128), f32),
            pltpu.VMEM((2, 8, 128), f32),
            pltpu.VMEM((8, 128), f32),
            pltpu.VMEM((strides, 8, 128), f32),
            pltpu.VMEM((MEMBERS, 8, 128), f32),
            dma((5,)),
            dma((2,)),
            dma((2,)),
            dma((2,)),
            dma((2,)),
            dma,
            dma,
            dma,
            dma,
            dma((3,)),
            dma((3,)),
            dma((2,)),
            dma((2,)),
            dma,
            dma,
            dma,
            dma,
            pltpu.SemaphoreType.REGULAR,
        ],
        compiler_params=pltpu.CompilerParams(
            collective_id=0, has_side_effects=True, vmem_limit_bytes=32 * 1024 * 1024
        ),
    )(
        *[
            pltpu.with_memory_space_constraint(x, pltpu.HBM)
            for x in (
                coords,
                loads,
                occupancy,
                basis.reshape(LEAVES * 64, LEAF),
                transfer.reshape(6, 128, 64),
            )
        ]
    )


def solution(mesh):
    boxes = mesh.shape["box"] // MEMBERS
    return jax.shard_map(
        functools.partial(body, boxes, 4),
        mesh=mesh,
        in_specs=(P(None, "box"), P(None, "box"), P("box"), P("box", None, None), P()),
        out_specs=P(None, "box"),
        check_vma=False,
    )
```

```python
import functools

import jax
import jax.numpy as jnp
from jax import lax
from jax.experimental import pallas as pl
from jax.experimental.pallas import tpu as pltpu
from jax.sharding import PartitionSpec as P

LEAF = 256
COLS = 8
LEAVES = 8
MEMBERS = 8
OWN = LEAF * LEAVES

f32 = jnp.float32
bf16 = jnp.bfloat16
soften = 0.0001
near_scale = 0.0625
far_scale = 0.125
NN = (((1,), (0,)), ((), ()))
NT = (((1,), (1,)), ((), ()))
MESH = pl.DeviceIdType.MESH


def div(a, b):
    return lax.div(a, jnp.int32(b))


def rem(a, b):
    return lax.rem(a, jnp.int32(b))


def phi(tx, ty, tz, sx, sy, sz, scale):
    dx = tx - sx
    dy = ty - sy
    dz = tz - sz
    r2 = dx * dx + dy * dy + dz * dz
    return (r2 * (0.5 * scale)) * jnp.log(r2 + soften)


def split(x):
    high = x.astype(bf16)
    return high, (x - high.astype(f32)).astype(bf16)


def mm(a, b, dims):
    rows = a.shape[0]
    high = a.astype(bf16).astype(f32)
    stacked = jnp.concatenate([high, a - high], axis=0).astype(bf16)
    both = lax.dot_general(stacked, b[0][...], dims, preferred_element_type=f32)
    low = lax.dot_general(stacked[:rows], b[1][...], dims, preferred_element_type=f32)
    return both[:rows] + (both[rows:] + low)


def low_half(shape):
    return lax.broadcasted_iota(jnp.int32, shape, len(shape) - 1) < 64


def merge(rows):
    count = rows.shape[0] // 16
    low = low_half((8, 128))
    return [
        jnp.where(low, rows[16 * i : 16 * i + 8], rows[16 * i + 8 : 16 * i + 16])
        for i in range(count)
    ]


def raise_coef(pairs, level_map):
    rows = mm(jnp.concatenate(pairs, axis=0), level_map, NN)
    return merge(rows) if len(pairs) > 1 else [rows]


def pick(x, entries):
    rows = x.shape[0]
    a = x.astype(bf16).astype(f32)
    b = (x - a).astype(bf16).astype(f32)
    c = (x - a) - b
    stacked = jnp.concatenate([a, b, c], axis=0).astype(bf16)
    picked = lax.dot_general(stacked, entries, NN, preferred_element_type=f32)
    return picked[:rows] + picked[rows : 2 * rows] + picked[2 * rows :]


def raise_skel(pairs, every_second):
    rows_up = pick(jnp.concatenate(pairs, axis=0), every_second)
    return merge(rows_up) if len(pairs) > 1 else [rows_up]


def cousins(chain, slot):
    low = low_half((8, 128))
    column = chain[slot, 1].T
    tx, ty, tz = column[:, 0:1], column[:, 1:2], column[:, 2:3]
    before, after = chain[slot - 1, 0], chain[slot + 1, 0]
    tiles = []
    for skel in (chain[slot - 1, 1], chain[slot + 1, 1]):
        tiles.append(phi(tx, ty, tz, skel[0:1], skel[1:2], skel[2:3], far_scale))
    tile = jnp.concatenate(tiles, axis=1)
    even = jnp.concatenate([jnp.where(low, before, 0.0), after], axis=1)
    odd = jnp.concatenate([before, jnp.where(low, 0.0, after)], axis=1)
    rows = mm(jnp.concatenate([even, odd], axis=0), split(tile), NT)
    return jnp.where(low, rows[:8], rows[8:])


def lower(pairs, level_map):
    height = pairs[0].shape[0]
    low = low_half((height, 128))
    stacked = []
    for pair in pairs:
        stacked += [jnp.where(low, pair, 0.0), jnp.where(low, 0.0, pair)]
    rows = mm(jnp.concatenate(stacked, axis=0), level_map, NT)
    return [rows[height * i : height * (i + 1)] for i in range(2 * len(pairs))]


def kernel(
    boxes,
    across,
    coords_hbm,
    loads_hbm,
    occ_hbm,
    basis_hbm,
    transfer_hbm,
    out_ref,
    coords,
    loads,
    occ,
    basis,
    transfer,
    map_high,
    map_low,
    path_map,
    field,
    column,
    leaf_high,
    leaf_low,
    near,
    tile_a,
    tile_b,
    tile_c,
    chain,
    g_chain,
    local,
    edge_send,
    edge_recv,
    u_buf,
    g_buf,
    bound_send,
    bound_recv,
    quad_recv,
    rim_recv,
    far_send,
    far_buf,
    part_buf,
    load_sem,
    near_send_sem,
    near_recv_sem,
    edge_send_sem,
    edge_recv_sem,
    u_send_sem,
    u_recv_sem,
    g_send_sem,
    g_recv_sem,
    bound_send_sem,
    bound_recv_sem,
    rim_send_sem,
    rim_recv_sem,
    far_send_sem,
    far_recv_sem,
    part_send_sem,
    part_recv_sem,
    ready,
):
    loading = [
        pltpu.make_async_copy(src, dst, load_sem.at[at])
        for at, (src, dst) in enumerate(
            [
                (coords_hbm, coords),
                (transfer_hbm, transfer),
                (loads_hbm, loads),
                (occ_hbm, occ),
                (basis_hbm, basis),
            ]
        )
    ]
    for copy in loading:
        copy.start()

    device = lax.axis_index("box")
    total = boxes * MEMBERS
    strides = boxes // MEMBERS
    depth = boxes // (2 * across)
    box, member = div(device, MEMBERS), rem(device, MEMBERS)
    x, z, y_half = div(box, 2 * depth), rem(div(box, 2), depth), rem(box, 2)
    y, core = div(member, 2), rem(member, 2)
    low = low_half((8, 128))
    half = jnp.where(low, 0, 1)

    top = jnp.where(y == 3, 1, 0)
    outer = jnp.where(y == 0, 1, top)
    side_to = jnp.where(outer == 1, top, 2 - y)
    side_from = jnp.where(outer == 1, 1 - top, 2 - y)
    far_half = jnp.where(outer == 1, 1 - y_half, y_half)
    z_core = rem(div(z, 2), 2)
    far_member = 2 * jnp.where(outer == 1, 3 - y, y) + z_core
    z_high, z_low = div(z, 4), rem(z, 2)
    far_x = [rem(x + dx, across) for dx in range(across)]
    far_steps = [(dx, turn) for dx in range(across) for turn in range(2)]

    def far_depths(side):
        first = 4 * rem(side + z_high, 2) + 2 * core
        return [first, first + 1]

    to_z, from_z = far_depths(side_to), far_depths(side_from)

    def far_box(depths, dx, turn):
        return (far_x[dx % across] * depth + depths[turn]) * 2 + far_half

    far_to = [far_box(to_z, dx, turn) * MEMBERS + far_member for dx, turn in far_steps]
    far_from = [far_box(from_z, -dx, turn) for dx, turn in far_steps]
    alone = jnp.logical_and(jnp.logical_and(outer == 0, side_to == 0), core == z_core)

    barrier = pltpu.get_barrier_semaphore()

    def greet(target):
        pl.semaphore_signal(barrier, inc=1, device_id=(target,), device_id_type=MESH)

    def order(at):
        return jnp.where(at == 0, 0, jnp.where(at >= 6, 2, 1))

    mine = order(z)
    to_later = [jnp.where(order(at) > mine, 1, 0) for at in to_z]
    from_earlier = [jnp.where(order(at) < mine, 1, 0) for at in from_z]
    far_order = [(2 * dx + turn) for turn in range(2) for dx in (2, 1, 3, 0)]

    def far_each(turn, act):
        for k in far_order[4 * turn : 4 * turn + 4]:
            if k == turn:
                pl.when(jnp.logical_not(jnp.logical_and(alone, z_low == turn)))(
                    functools.partial(act, k)
                )
            else:
                act(k)

    for turn in range(2):

        @pl.when(from_earlier[turn] == 0)
        def _(turn=turn):
            far_each(turn, lambda k: greet(far_from[k] * MEMBERS + far_member))

        @pl.when(to_later[turn] == 1)
        def _(turn=turn):
            far_each(turn, lambda k: greet(far_to[k]))

    left_device = rem(device + total - 1, total)
    right_device = rem(device + 1, total)
    mirror = 2 * (3 - y) + core
    left_box = rem(box + boxes - 1, boxes) * MEMBERS + mirror
    right_box = rem(box + 1, boxes) * MEMBERS + mirror
    mates = [box * MEMBERS + rem(member + r, MEMBERS) for r in (6, 2, 7, 3, 5, 4, 1)]
    at_rim = outer == 1
    rim_box = rem(box + boxes + 2 * top - 1, boxes)
    rim_devices = [rim_box * MEMBERS + 6 - 6 * top + t for t in range(2)]
    quad = div(member, 4)
    quad_device = rem(box + boxes + 2 * quad - 1, boxes) * MEMBERS + mirror
    early = jnp.where(z <= 1, 1, 0)
    ahead = 2
    before = [device > 0, box > 0]
    after = [device < total - 1, box < boxes - 1]
    inside = jnp.where(quad == 0, box, boxes - 1 - box) > 0
    open_rim = jnp.logical_and(at_rim, inside)

    for target in mates:
        greet(target)
    for has, targets in ((before, (left_device, left_box)), (after, (right_device, right_box))):
        for at in range(2):
            pl.when(has[at])(functools.partial(greet, targets[at]))

    @pl.when(open_rim)
    def _():
        for target in rim_devices:
            greet(target)

    lanes = lax.broadcasted_iota(jnp.int32, (1, 128), 1)
    index = lax.broadcasted_iota(jnp.int32, (512, 128), 0)
    placed = (index == (lanes - 64 - 8 * member) * 64).astype(f32).astype(bf16)
    picks = (lax.broadcasted_iota(jnp.int32, (1, 128), 1) & 63) * 2
    every_second = (
        (lax.broadcasted_iota(jnp.int32, (128, 128), 0) == picks).astype(f32).astype(bf16)
    )
    for copy in loading:
        copy.wait()
    points = jnp.concatenate([coords[...], jnp.zeros((5, OWN), f32)], axis=0)
    s0 = [
        jnp.concatenate(
            [points[:, 512 * p : 512 * p + 64], points[:, 512 * p + 256 : 512 * p + 320]], axis=1
        )
        for p in range(4)
    ]
    s6 = pick(jnp.concatenate(s0, axis=1), placed)

    maps = [(map_high.at[level], map_low.at[level]) for level in range(6)]

    def set_map(level):
        once = transfer[level]
        map_high[level], map_low[level] = split(jnp.concatenate([once, once], axis=1))

    for level in range(2):
        set_map(level)
    slots = lax.broadcasted_iota(jnp.int32, (COLS, LEAF), 1)
    live = []
    for leaf in range(LEAVES):
        part = loads[:, leaf * LEAF : (leaf + 1) * LEAF].astype(f32)
        live.append(jnp.where(slots < occ[leaf], part, 0.0))
    c0 = []
    for p in range(4):
        two = jnp.concatenate([live[2 * p], live[2 * p + 1]], axis=0).astype(bf16)
        rows = lax.dot_general(
            two, basis[128 * p : 128 * p + 128, :], NT, preferred_element_type=f32
        )
        c0.append(jnp.where(low, rows[:8], rows[8:]))
    c1 = raise_coef(c0, maps[0])
    c2 = raise_coef(c1, maps[1])
    def factor(level, at):
        return transfer[level, pl.ds(pl.multiple_of(64 * at, 64), 64), :]

    map_34 = mm(transfer[2], split(factor(3, core)), NN)
    wide = jnp.concatenate([factor(5, quad), jnp.zeros((64, 64), f32)], axis=1)
    map_56 = mm(factor(4, rem(y, 2)), split(wide), NN)
    map_6 = mm(map_34, split(map_56), NN)
    u_buf[member] = mm(c2[0], split(map_6), NN) + s6
    path_map[...] = map_6

    set_map(2)
    every_eighth = (index == (lanes & 63) * 8).astype(f32).astype(bf16)
    s3 = pick(jnp.concatenate(s0, axis=1), every_eighth)
    c3 = raise_coef(c2, maps[2])[0]
    g_buf[member] = jnp.where(half == core, c3, s3)

    def set_field():
        field[0, :, LEAF : LEAF + OWN] = points
        for leaf in range(LEAVES):
            field[1, :, (leaf + 1) * LEAF : (leaf + 2) * LEAF] = live[leaf]
        for at in range(0, OWN, 128):
            column[at : at + 128, :] = points[:, at : at + 128].T
        near[...] = jnp.zeros_like(near)

    def fill_tile(tile, row, col, width):
        sx = field[0, 0:1, pl.ds(col, width)]
        sy = field[0, 1:2, pl.ds(col, width)]
        sz = field[0, 2:3, pl.ds(col, width)]
        for at in range(0, LEAF, 16):
            rows = column[pl.ds(row + at, 16), :]
            tile[at : at + 16, 0:width] = phi(
                rows[:, 0:1], rows[:, 1:2], rows[:, 2:3], sx, sy, sz, near_scale
            ).astype(bf16)

    def near_leaf(tile, row):
        col = row + LEAF
        fill_tile(tile, row, col, 2 * LEAF)
        loads_two = field[1, :, pl.ds(col, 2 * LEAF)].astype(bf16)
        this = lax.dot_general(loads_two, tile[...], NT, preferred_element_type=f32)
        after = lax.dot_general(
            loads_two[:, :LEAF], tile[:, LEAF:], NN, preferred_element_type=f32
        )
        return this, after

    def near_two(row):
        first, second_part = near_leaf(tile_a, row)
        second, third = near_leaf(tile_b, row + LEAF)
        near[:, pl.ds(row, LEAF)] += first
        near[:, pl.ds(row + LEAF, LEAF)] += second_part + second
        near[:, pl.ds(row + 2 * LEAF, LEAF)] += third

    def near_step(pair, carry):
        near_two(pl.multiple_of(pair * (2 * LEAF), 2 * LEAF))
        return carry

    def side(block, at):
        lanes = jnp.where(low_half((1, 128)), 0, 1)
        return jnp.where(lanes == at, block, 0.0)

    def set_chain(levels, into):
        for at, (pairs, skels) in enumerate(levels):
            first = (1, 7, 11)[at]
            for p in range(len(pairs)):
                into[first + p, 0] = pairs[p]
                into[first + p, 1] = skels[p]

    def set_inner():
        row = (LEAVES - 2) * LEAF
        this, after = near_leaf(tile_a, row)
        fill_tile(tile_c, row + LEAF, row + 2 * LEAF, LEAF)
        own = field[1, :, row + 2 * LEAF : row + 3 * LEAF].astype(bf16)
        after += lax.dot_general(own, tile_c[...], NT, preferred_element_type=f32)
        near[:, row : row + LEAF] += this
        near[:, row + LEAF : row + 2 * LEAF] += after
        for slot in (2, 3):
            local[slot - 1] = cousins(chain, slot)

    def set_edges():
        s1 = raise_skel(s0, every_second)
        s2 = raise_skel(s1, every_second)

        set_chain([(c0, s0), (c1, s1), (c2, s2)], chain)
        for at, (pairs, skels) in enumerate([(c0, s0), (c1, s1), (c2, s2)]):
            edge_send[0, at, 0] = pairs[-1]
            edge_send[0, at, 1] = skels[-1]
            edge_send[1, at, 0] = pairs[0]
            edge_send[1, at, 1] = skels[0]
    def set_leaf_paths():
        x2 = jnp.concatenate([path_map[...].T[:64], transfer[2].T], axis=0)
        x0 = lower(lower([x2], maps[1]), maps[0])
        leaf_high[...], leaf_low[...] = split(jnp.concatenate(x0, axis=1))

    @pl.when(early == 1)
    def _():
        set_field()
        lax.fori_loop(0, ahead, near_step, 0)

    pl.semaphore_wait(
        barrier,
        MEMBERS - 1
        + sum(has.astype(jnp.int32) for has in before + after)
        + 2 * open_rim.astype(jnp.int32)
        + 4 * (2 - to_later[0] - to_later[1])
        - alone.astype(jnp.int32)
        + 4 * (from_earlier[0] + from_earlier[1]),
    )

    def tell(target):
        pl.semaphore_signal(ready, inc=1, device_id=(target,), device_id_type=MESH)

    for turn in range(2):

        @pl.when(from_earlier[turn] == 1)
        def _(turn=turn):
            far_each(turn, lambda k: tell(far_from[k] * MEMBERS + far_member))

    def remote(src, dst, send_sem, recv_sem, target):
        return pltpu.make_async_remote_copy(
            src_ref=src,
            dst_ref=dst,
            send_sem=send_sem,
            recv_sem=recv_sem,
            device_id=(target,),
            device_id_type=MESH,
        )

    def send(*ends):
        copy = remote(*ends)
        copy.start()
        return copy

    def wait_all(ref, semaphore):
        pltpu.make_async_copy(ref, ref, semaphore).wait()

    first = (6, 2, 7, 3, 0, 4, 1, 5)
    place = sum(jnp.where(member == at, rank, 0) for rank, at in enumerate(first))
    for rank in range(MEMBERS - 1):
        mate = box * MEMBERS + jnp.where(place <= rank, first[rank + 1], first[rank])
        send(u_buf.at[member], u_buf.at[member], u_send_sem, u_recv_sem, mate)

    for mate in mates:
        send(g_buf.at[member], g_buf.at[member], g_send_sem, g_recv_sem, mate)

    rim_copies = [
        pltpu.make_async_remote_copy(
            src_ref=g_buf.at[member],
            dst_ref=rim_recv.at[core],
            send_sem=rim_send_sem.at[t],
            recv_sem=rim_recv_sem.at[core],
            device_id=(rim_devices[t],),
            device_id_type=MESH,
        )
        for t in range(2)
    ]

    @pl.when(open_rim)
    def _():
        for copy in rim_copies:
            copy.start()

    @pl.when(early == 0)
    def _():
        set_field()

    last = LEAF * LEAVES
    near_copies = [
        remote(
            field.at[:, :, last : last + LEAF],
            field.at[:, :, 0:LEAF],
            near_send_sem.at[0],
            near_recv_sem.at[0],
            right_device,
        ),
        remote(
            field.at[:, :, LEAF : 2 * LEAF],
            field.at[:, :, last + LEAF : last + 2 * LEAF],
            near_send_sem.at[1],
            near_recv_sem.at[1],
            left_device,
        ),
    ]

    def start(copies, at=0):
        for copy, has in zip(copies, (after[at], before[at])):
            pl.when(has)(copy.start)

    def receive(copies, at=0):
        for copy, has in zip(copies, (before[at], after[at])):
            pl.when(has)(copy.wait_recv)

    start(near_copies)

    edge_copies = [
        remote(
            edge_send.at[side],
            edge_recv.at[side],
            edge_send_sem.at[side],
            edge_recv_sem.at[side],
            (right_device, left_device)[side],
        )
        for side in range(2)
    ]

    set_edges()
    start(edge_copies)

    set_map(3)
    set_map(4)

    @pl.when(early == 1)
    def _():
        set_leaf_paths()

    wait_all(u_buf.at[pl.ds(0, MEMBERS - 1)], u_recv_sem)
    parts = [u_buf[at] for at in range(MEMBERS)]
    while len(parts) > 1:
        parts = [a + b for a, b in zip(parts[0::2], parts[1::2])]
    top_record = parts[0]
    swapped_record = pltpu.roll(top_record, 64, 1)
    far_send[...] = jnp.where(z_low == 0, top_record, swapped_record)

    @pl.when(alone)
    def _():
        far_buf[z_low] = far_send[...]

    def far_copy(k):
        slot = k - k % 2 + z_low
        return remote(far_send, far_buf.at[slot], far_send_sem, far_recv_sem, far_to[k])

    def far_wait(semaphore):
        @pl.when(alone)
        def _():
            wait_all(far_buf.at[pl.ds(1, strides - 1)], semaphore)

        @pl.when(jnp.logical_not(alone))
        def _():
            wait_all(far_buf, semaphore)

    for turn in range(2):

        @pl.when(to_later[turn] == 0)
        def _(turn=turn):
            far_each(turn, lambda k: far_copy(k).start())

    wait_all(g_buf.at[pl.ds(0, MEMBERS - 1)], g_recv_sem)
    c3s, s3s = [], []
    for p in range(4):
        even, odd = g_buf[2 * p], g_buf[2 * p + 1]
        c3s.append(jnp.where(low, even, odd))
        s3s.append(pltpu.roll(jnp.where(low, odd, even), 64, 1))
    c4s, s4s = raise_coef(c3s, maps[3]), raise_skel(s3s, every_second)
    c5s, s5s = raise_coef(c4s, maps[4]), raise_skel(s4s, every_second)
    set_chain([(c3s, s3s), (c4s, s4s), (c5s, s5s)], g_chain)
    for at in range(2):
        bound_send[at, 0] = c5s[0]
        bound_send[at, 1] = s5s[0] + pltpu.roll(s4s[1 - at], 3, 0)
    bound_copies = [
        remote(
            bound_send.at[side],
            bound_recv.at[side],
            bound_send_sem.at[side],
            bound_recv_sem.at[side],
            (right_box, left_box)[side],
        )
        for side in range(2)
    ]
    quad_copy = remote(
        g_chain.at[7 + quad, 0],
        quad_recv,
        bound_send_sem.at[2],
        bound_recv_sem.at[2],
        quad_device,
    )
    start(bound_copies, 1)
    pl.when(inside)(quad_copy.start)

    def set_ends(ends, into):
        for level in range(3):
            into[(0, 6, 10)[level]] = ends[0, level]
            into[(5, 9, 12)[level]] = ends[1, level]

    def near_end(tile, row, col):
        fill_tile(tile, row, col, LEAF)
        near[:, row : row + LEAF] += lax.dot_general(
            field[1, :, col : col + LEAF].astype(bf16),
            tile[:, 0:LEAF],
            NT,
            preferred_element_type=f32,
        )

    def finish_ends():
        receive(near_copies)

        @pl.when(device == 0)
        def _():
            field[:, :, 0:LEAF] = jnp.zeros((2, 8, LEAF), f32)
            edge_recv[0] = jnp.zeros((3, 2, 8, 128), f32)

        @pl.when(device == total - 1)
        def _():
            field[:, :, last + LEAF : last + 2 * LEAF] = jnp.zeros((2, 8, LEAF), f32)
            edge_recv[1] = jnp.zeros((3, 2, 8, 128), f32)

        near_end(tile_c, 0, 0)
        near_end(tile_a, last - LEAF, last + LEAF)

        receive(edge_copies)
        set_ends(edge_recv, chain)
        for at, slot in [(0, 1), (3, 4), (4, 7), (5, 8), (6, 11)]:
            local[at] = cousins(chain, slot)

    @pl.when(early == 1)
    def _():
        lax.fori_loop(ahead, 3, near_step, 0)
        set_inner()
        finish_ends()

    later = to_later[0] + to_later[1]

    @pl.when(later > 0)
    def _():
        pl.semaphore_wait(ready, 4 * later)

    for turn in range(2):

        @pl.when(to_later[turn] == 1)
        def _(turn=turn):
            far_each(turn, lambda k: far_copy(k).start())

    @pl.when(early == 0)
    def _():
        lax.fori_loop(0, 3, near_step, 0)
        set_inner()
        set_leaf_paths()
        finish_ends()

    top_column = swapped_record.T[:64]
    tx, ty, tz = top_column[:, 0:1], top_column[:, 1:2], top_column[:, 2:3]

    far_wait(far_recv_sem)

    top_coef, top_skel = [], []
    for k in range(0, strides, 2):
        halves = []
        for at in (k, k + 1):
            apart = far_from[at] - box
            counts = jnp.logical_or(apart >= 2, apart <= -2)
            halves.append((far_buf[at], counts))
        (one, one_counts), (two, two_counts) = halves
        coef = jnp.where(low, jnp.where(one_counts, one, 0.0), jnp.where(two_counts, two, 0.0))
        top_coef.append(pltpu.roll(coef, 64, 1))
        top_skel.append(jnp.where(low, two, one))
    top_tile = jnp.concatenate(
        [phi(tx, ty, tz, s[0:1], s[1:2], s[2:3], far_scale) for s in top_skel], axis=1
    )
    top = mm(jnp.concatenate(top_coef, axis=1), split(top_tile), NT)
    part_buf[member] = jnp.concatenate([top, jnp.zeros((8, 64), f32)], axis=1)
    for at in range(MEMBERS - 1):
        mate = box * MEMBERS + at + jnp.where(member <= at, 1, 0)
        send(part_buf.at[member], part_buf.at[member], part_send_sem, part_recv_sem, mate)

    wait_all(u_buf.at[pl.ds(0, MEMBERS - 1)], u_send_sem)
    wait_all(g_buf.at[pl.ds(0, MEMBERS - 1)], g_send_sem)
    far_wait(far_send_sem)
    for copies, at in ((near_copies, 0), (edge_copies, 0), (bound_copies, 1)):
        for copy, has in zip(copies, (after[at], before[at])):
            pl.when(has)(copy.wait_send)
    pl.when(inside)(quad_copy.wait_send)

    receive(bound_copies, 1)
    pl.when(inside)(quad_copy.wait_recv)
    start_skel = jnp.where(before[1], bound_recv[0, 1], 0.0)
    end_skel = jnp.where(after[1], bound_recv[1, 1], 0.0)
    g_chain[10, 0] = jnp.where(before[1], bound_recv[0, 0], 0.0)
    g_chain[10, 1] = start_skel
    g_chain[12, 0] = jnp.where(after[1], bound_recv[1, 0], 0.0)
    g_chain[12, 1] = end_skel
    quad_coef = jnp.where(inside, quad_recv[...], 0.0)
    g_chain[6, 0] = quad_coef
    g_chain[6, 1] = pltpu.roll(start_skel, 5, 0)
    g_chain[9, 0] = quad_coef
    g_chain[9, 1] = pltpu.roll(end_skel, 5, 0)

    @pl.when(jnp.logical_not(inside))
    def _():
        for slot in (0, 5):
            g_chain[slot] = jnp.zeros((2, 8, 128), f32)

    @pl.when(open_rim)
    def _():
        for copy in rim_copies:
            copy.wait_send()
        for t in range(2):
            pltpu.make_async_remote_copy(
                src_ref=g_buf.at[member],
                dst_ref=rim_recv.at[t],
                send_sem=rim_send_sem.at[t],
                recv_sem=rim_recv_sem.at[t],
                device_id=(rim_devices[t],),
                device_id_type=MESH,
            ).wait_recv()
        even, odd = rim_recv[0], rim_recv[1]
        rim_coef = jnp.where(low, even, odd)
        rim_skel = pltpu.roll(jnp.where(low, odd, even), 64, 1)
        for slot in (0, 5):
            g_chain[slot, 0] = rim_coef
            g_chain[slot, 1] = rim_skel

    local3 = cousins(g_chain, 1 + y)
    local4 = cousins(g_chain, 7 + quad)
    local5 = cousins(g_chain, 11)
    y2 = local[6]
    y1 = [x + local[4 + at] for at, x in enumerate(lower([y2], maps[1]))]
    y0 = [x + local[at] for at, x in enumerate(lower(y1, maps[0]))]
    y4 = local4 + mm(side(local5, quad), maps[4], NT)
    y3 = local3 + mm(side(y4, rem(y, 2)), maps[3], NT)
    y3 = jnp.where(core == 1, y3, pltpu.roll(y3, 64, 1))

    wait_all(part_buf.at[pl.ds(0, MEMBERS - 1)], part_recv_sem)
    parts = [part_buf[at] for at in range(MEMBERS)]
    while len(parts) > 1:
        parts = [a + b for a, b in zip(parts[0::2], parts[1::2])]
    d6 = parts[0]
    d63 = jnp.where(low, d6, y3)
    d0 = jnp.concatenate(y0, axis=1) + mm(d63, (leaf_high, leaf_low), NN)
    for p in range(4):
        pair = d0[:, 128 * p : 128 * p + 128]
        two = jnp.concatenate([jnp.where(low, pair, 0.0), jnp.where(low, 0.0, pair)], axis=0)
        rows = lax.dot_general(
            two.astype(bf16),
            basis[128 * p : 128 * p + 128, :],
            NN,
            preferred_element_type=f32,
        )
        for t in range(2):
            leaf = 2 * p + t
            at = leaf * LEAF
            out_ref[:, at : at + LEAF] = jnp.where(
                slots < occ[leaf], near[:, at : at + LEAF] + rows[8 * t : 8 * t + 8], 0.0
            )

    wait_all(part_buf.at[pl.ds(0, MEMBERS - 1)], part_send_sem)


def body(boxes, across, coords, loads, occupancy, basis, transfer):
    strides = boxes // MEMBERS
    hbm = pl.BlockSpec(memory_space=pl.ANY)
    dma = pltpu.SemaphoreType.DMA
    return pl.pallas_call(
        functools.partial(kernel, boxes, across),
        out_shape=jax.ShapeDtypeStruct((COLS, OWN), f32),
        in_specs=[hbm] * 5,
        out_specs=pl.BlockSpec(memory_space=pltpu.VMEM),
        scratch_shapes=[
            pltpu.VMEM((3, OWN), f32),
            pltpu.VMEM((COLS, OWN), bf16),
            pltpu.SMEM((LEAVES,), jnp.int32),
            pltpu.VMEM((LEAVES * 64, LEAF), bf16),
            pltpu.VMEM((6, 128, 64), f32),
            pltpu.VMEM((6, 128, 128), bf16),
            pltpu.VMEM((6, 128, 128), bf16),
            pltpu.VMEM((128, 128), f32),
            pltpu.VMEM((2, 8, OWN + 2 * LEAF), f32),
            pltpu.VMEM((OWN, 8), f32),
            pltpu.VMEM((128, 512), bf16),
            pltpu.VMEM((128, 512), bf16),
            pltpu.VMEM((COLS, OWN + LEAF), f32),
            pltpu.VMEM((LEAF, 2 * LEAF), bf16),
            pltpu.VMEM((LEAF, 2 * LEAF), bf16),
            pltpu.VMEM((LEAF, LEAF), bf16),
            pltpu.VMEM((13, 2, 8, 128), f32),
            pltpu.VMEM((13, 2, 8, 128), f32),
            pltpu.VMEM((7, 8, 128), f32),
            pltpu.VMEM((2, 3, 2, 8, 128), f32),
            pltpu.VMEM((2, 3, 2, 8, 128), f32),
            pltpu.VMEM((MEMBERS, 8, 128), f32),
            pltpu.VMEM((MEMBERS, 8, 128), f32),
            pltpu.VMEM((2, 2, 8, 128), f32),
            pltpu.VMEM((2, 2, 8, 128), f32),
            pltpu.VMEM((8, 128), f32),
            pltpu.VMEM((2, 8, 128), f32),
            pltpu.VMEM((8, 128), f32),
            pltpu.VMEM((strides, 8, 128), f32),
            pltpu.VMEM((MEMBERS, 8, 128), f32),
            dma((5,)),
            dma((2,)),
            dma((2,)),
            dma((2,)),
            dma((2,)),
            dma,
            dma,
            dma,
            dma,
            dma((3,)),
            dma((3,)),
            dma((2,)),
            dma((2,)),
            dma,
            dma,
            dma,
            dma,
            pltpu.SemaphoreType.REGULAR,
        ],
        compiler_params=pltpu.CompilerParams(
            collective_id=0, has_side_effects=True, vmem_limit_bytes=32 * 1024 * 1024
        ),
    )(
        *[
            pltpu.with_memory_space_constraint(x, pltpu.HBM)
            for x in (
                coords,
                loads,
                occupancy,
                basis.reshape(LEAVES * 64, LEAF),
                transfer.reshape(6, 128, 64),
            )
        ]
    )


def solution(mesh):
    boxes = mesh.shape["box"] // MEMBERS
    return jax.shard_map(
        functools.partial(body, boxes, 4),
        mesh=mesh,
        in_specs=(P(None, "box"), P(None, "box"), P("box"), P("box", None, None), P()),
        out_specs=P(None, "box"),
        check_vma=False,
    )
```

```python
import functools

import jax
import jax.numpy as jnp
from jax import lax
from jax.experimental import pallas as pl
from jax.experimental.pallas import tpu as pltpu
from jax.sharding import PartitionSpec as P

LEAF = 256
COLS = 8
LEAVES = 8
MEMBERS = 8
OWN = LEAF * LEAVES

f32 = jnp.float32
bf16 = jnp.bfloat16
soften = 0.0001
near_scale = 0.0625
far_scale = 0.125
NN = (((1,), (0,)), ((), ()))
NT = (((1,), (1,)), ((), ()))
MESH = pl.DeviceIdType.MESH


def div(a, b):
    return lax.div(a, jnp.int32(b))


def rem(a, b):
    return lax.rem(a, jnp.int32(b))


def phi(tx, ty, tz, sx, sy, sz, scale):
    dx = tx - sx
    dy = ty - sy
    dz = tz - sz
    r2 = dx * dx + dy * dy + dz * dz
    return (r2 * (0.5 * scale)) * jnp.log(r2 + soften)


def split(x):
    high = x.astype(bf16)
    return high, (x - high.astype(f32)).astype(bf16)


def mm(a, b, dims):
    rows = a.shape[0]
    high = a.astype(bf16).astype(f32)
    stacked = jnp.concatenate([high, a - high], axis=0).astype(bf16)
    both = lax.dot_general(stacked, b[0][...], dims, preferred_element_type=f32)
    low = lax.dot_general(stacked[:rows], b[1][...], dims, preferred_element_type=f32)
    return both[:rows] + (both[rows:] + low)


def low_half(shape):
    return lax.broadcasted_iota(jnp.int32, shape, len(shape) - 1) < 64


def merge(rows):
    count = rows.shape[0] // 16
    low = low_half((8, 128))
    return [
        jnp.where(low, rows[16 * i : 16 * i + 8], rows[16 * i + 8 : 16 * i + 16])
        for i in range(count)
    ]


def raise_coef(pairs, level_map):
    rows = mm(jnp.concatenate(pairs, axis=0), level_map, NN)
    return merge(rows) if len(pairs) > 1 else [rows]


def pick(x, entries):
    rows = x.shape[0]
    a = x.astype(bf16).astype(f32)
    b = (x - a).astype(bf16).astype(f32)
    c = (x - a) - b
    stacked = jnp.concatenate([a, b, c], axis=0).astype(bf16)
    picked = lax.dot_general(stacked, entries, NN, preferred_element_type=f32)
    return picked[:rows] + picked[rows : 2 * rows] + picked[2 * rows :]


def raise_skel(pairs, every_second):
    rows_up = pick(jnp.concatenate(pairs, axis=0), every_second)
    return merge(rows_up) if len(pairs) > 1 else [rows_up]


def cousins(chain, slot):
    low = low_half((8, 128))
    column = chain[slot, 1].T
    tx, ty, tz = column[:, 0:1], column[:, 1:2], column[:, 2:3]
    before, after = chain[slot - 1, 0], chain[slot + 1, 0]
    tiles = []
    for skel in (chain[slot - 1, 1], chain[slot + 1, 1]):
        tiles.append(phi(tx, ty, tz, skel[0:1], skel[1:2], skel[2:3], far_scale))
    tile = jnp.concatenate(tiles, axis=1)
    even = jnp.concatenate([jnp.where(low, before, 0.0), after], axis=1)
    odd = jnp.concatenate([before, jnp.where(low, 0.0, after)], axis=1)
    rows = mm(jnp.concatenate([even, odd], axis=0), split(tile), NT)
    return jnp.where(low, rows[:8], rows[8:])


def lower(pairs, level_map):
    height = pairs[0].shape[0]
    low = low_half((height, 128))
    stacked = []
    for pair in pairs:
        stacked += [jnp.where(low, pair, 0.0), jnp.where(low, 0.0, pair)]
    rows = mm(jnp.concatenate(stacked, axis=0), level_map, NT)
    return [rows[height * i : height * (i + 1)] for i in range(2 * len(pairs))]


def kernel(
    boxes,
    across,
    coords_hbm,
    loads_hbm,
    occ_hbm,
    basis_hbm,
    transfer_hbm,
    out_ref,
    coords,
    loads,
    occ,
    basis,
    transfer,
    map_high,
    map_low,
    path_map,
    field,
    column,
    leaf_high,
    leaf_low,
    near,
    tile_a,
    tile_b,
    tile_c,
    chain,
    g_chain,
    local,
    edge_send,
    edge_recv,
    u_buf,
    g_buf,
    bound_send,
    bound_recv,
    quad_recv,
    rim_recv,
    far_send,
    far_buf,
    part_buf,
    load_sem,
    near_send_sem,
    near_recv_sem,
    edge_send_sem,
    edge_recv_sem,
    u_send_sem,
    u_recv_sem,
    g_send_sem,
    g_recv_sem,
    bound_send_sem,
    bound_recv_sem,
    rim_send_sem,
    rim_recv_sem,
    far_send_sem,
    far_recv_sem,
    part_send_sem,
    part_recv_sem,
    ready,
):
    loading = [
        pltpu.make_async_copy(src, dst, load_sem.at[at])
        for at, (src, dst) in enumerate(
            [
                (coords_hbm, coords),
                (transfer_hbm, transfer),
                (loads_hbm, loads),
                (occ_hbm, occ),
                (basis_hbm, basis),
            ]
        )
    ]
    for copy in loading:
        copy.start()

    device = lax.axis_index("box")
    total = boxes * MEMBERS
    strides = boxes // MEMBERS
    depth = boxes // (2 * across)
    box, member = div(device, MEMBERS), rem(device, MEMBERS)
    x, z, y_half = div(box, 2 * depth), rem(div(box, 2), depth), rem(box, 2)
    y, core = div(member, 2), rem(member, 2)
    low = low_half((8, 128))
    half = jnp.where(low, 0, 1)

    top = jnp.where(y == 3, 1, 0)
    outer = jnp.where(y == 0, 1, top)
    side_to = jnp.where(outer == 1, top, 2 - y)
    side_from = jnp.where(outer == 1, 1 - top, 2 - y)
    far_half = jnp.where(outer == 1, 1 - y_half, y_half)
    z_core = rem(div(z, 2), 2)
    far_member = 2 * jnp.where(outer == 1, 3 - y, y) + z_core
    z_high, z_low = div(z, 4), rem(z, 2)
    far_x = [rem(x + dx, across) for dx in range(across)]
    far_steps = [(dx, turn) for dx in range(across) for turn in range(2)]

    def far_depths(side):
        first = 4 * rem(side + z_high, 2) + 2 * core
        return [first, first + 1]

    to_z, from_z = far_depths(side_to), far_depths(side_from)

    def far_box(depths, dx, turn):
        return (far_x[dx % across] * depth + depths[turn]) * 2 + far_half

    far_to = [far_box(to_z, dx, turn) * MEMBERS + far_member for dx, turn in far_steps]
    far_from = [far_box(from_z, -dx, turn) for dx, turn in far_steps]
    alone = jnp.logical_and(jnp.logical_and(outer == 0, side_to == 0), core == z_core)

    barrier = pltpu.get_barrier_semaphore()

    def greet(target):
        pl.semaphore_signal(barrier, inc=1, device_id=(target,), device_id_type=MESH)

    def order(at):
        return jnp.where(at == 0, 0, jnp.where(at >= 6, 2, 1))

    mine = order(z)
    to_later = [jnp.where(order(at) > mine, 1, 0) for at in to_z]
    from_earlier = [jnp.where(order(at) < mine, 1, 0) for at in from_z]
    far_order = [(2 * dx + turn) for turn in range(2) for dx in (2, 1, 3, 0)]

    def far_each(turn, act):
        for k in far_order[4 * turn : 4 * turn + 4]:
            if k == turn:
                pl.when(jnp.logical_not(jnp.logical_and(alone, z_low == turn)))(
                    functools.partial(act, k)
                )
            else:
                act(k)

    for turn in range(2):

        @pl.when(from_earlier[turn] == 0)
        def _(turn=turn):
            far_each(turn, lambda k: greet(far_from[k] * MEMBERS + far_member))

        @pl.when(to_later[turn] == 1)
        def _(turn=turn):
            far_each(turn, lambda k: greet(far_to[k]))

    left_device = rem(device + total - 1, total)
    right_device = rem(device + 1, total)
    mirror = 2 * (3 - y) + core
    left_box = rem(box + boxes - 1, boxes) * MEMBERS + mirror
    right_box = rem(box + 1, boxes) * MEMBERS + mirror
    mates = [box * MEMBERS + rem(member + r, MEMBERS) for r in (6, 2, 7, 3, 5, 4, 1)]
    at_rim = outer == 1
    rim_box = rem(box + boxes + 2 * top - 1, boxes)
    rim_devices = [rim_box * MEMBERS + 6 - 6 * top + t for t in range(2)]
    quad = div(member, 4)
    quad_device = rem(box + boxes + 2 * quad - 1, boxes) * MEMBERS + mirror
    early = jnp.where(z == 0, 1, 0)
    ahead = 2
    before = [device > 0, box > 0]
    after = [device < total - 1, box < boxes - 1]
    inside = jnp.where(quad == 0, box, boxes - 1 - box) > 0
    open_rim = jnp.logical_and(at_rim, inside)

    for target in mates:
        greet(target)
    for has, targets in ((before, (left_device, left_box)), (after, (right_device, right_box))):
        for at in range(2):
            pl.when(has[at])(functools.partial(greet, targets[at]))

    @pl.when(open_rim)
    def _():
        for target in rim_devices:
            greet(target)

    lanes = lax.broadcasted_iota(jnp.int32, (1, 128), 1)
    index = lax.broadcasted_iota(jnp.int32, (512, 128), 0)
    placed = (index == (lanes - 64 - 8 * member) * 64).astype(f32).astype(bf16)
    picks = (lax.broadcasted_iota(jnp.int32, (1, 128), 1) & 63) * 2
    every_second = (
        (lax.broadcasted_iota(jnp.int32, (128, 128), 0) == picks).astype(f32).astype(bf16)
    )
    for copy in loading:
        copy.wait()
    points = jnp.concatenate([coords[...], jnp.zeros((5, OWN), f32)], axis=0)
    s0 = [
        jnp.concatenate(
            [points[:, 512 * p : 512 * p + 64], points[:, 512 * p + 256 : 512 * p + 320]], axis=1
        )
        for p in range(4)
    ]
    s6 = pick(jnp.concatenate(s0, axis=1), placed)

    maps = [(map_high.at[level], map_low.at[level]) for level in range(6)]

    def set_map(level):
        once = transfer[level]
        map_high[level], map_low[level] = split(jnp.concatenate([once, once], axis=1))

    for level in range(2):
        set_map(level)
    slots = lax.broadcasted_iota(jnp.int32, (COLS, LEAF), 1)
    live = []
    for leaf in range(LEAVES):
        part = loads[:, leaf * LEAF : (leaf + 1) * LEAF].astype(f32)
        live.append(jnp.where(slots < occ[leaf], part, 0.0))
    c0 = []
    for p in range(4):
        two = jnp.concatenate([live[2 * p], live[2 * p + 1]], axis=0).astype(bf16)
        rows = lax.dot_general(
            two, basis[128 * p : 128 * p + 128, :], NT, preferred_element_type=f32
        )
        c0.append(jnp.where(low, rows[:8], rows[8:]))
    c1 = raise_coef(c0, maps[0])
    c2 = raise_coef(c1, maps[1])
    def factor(level, at):
        return transfer[level, pl.ds(pl.multiple_of(64 * at, 64), 64), :]

    map_34 = mm(transfer[2], split(factor(3, core)), NN)
    wide = jnp.concatenate([factor(5, quad), jnp.zeros((64, 64), f32)], axis=1)
    map_56 = mm(factor(4, rem(y, 2)), split(wide), NN)
    map_6 = mm(map_34, split(map_56), NN)
    u_buf[member] = mm(c2[0], split(map_6), NN) + s6
    path_map[...] = map_6

    set_map(2)
    every_eighth = (index == (lanes & 63) * 8).astype(f32).astype(bf16)
    s3 = pick(jnp.concatenate(s0, axis=1), every_eighth)
    c3 = raise_coef(c2, maps[2])[0]
    g_buf[member] = jnp.where(half == core, c3, s3)

    def set_field():
        field[0, :, LEAF : LEAF + OWN] = points
        for leaf in range(LEAVES):
            field[1, :, (leaf + 1) * LEAF : (leaf + 2) * LEAF] = live[leaf]
        for at in range(0, OWN, 128):
            column[at : at + 128, :] = points[:, at : at + 128].T
        near[...] = jnp.zeros_like(near)

    def fill_tile(tile, row, col, width):
        sx = field[0, 0:1, pl.ds(col, width)]
        sy = field[0, 1:2, pl.ds(col, width)]
        sz = field[0, 2:3, pl.ds(col, width)]
        for at in range(0, LEAF, 16):
            rows = column[pl.ds(row + at, 16), :]
            tile[at : at + 16, 0:width] = phi(
                rows[:, 0:1], rows[:, 1:2], rows[:, 2:3], sx, sy, sz, near_scale
            ).astype(bf16)

    def near_leaf(tile, row):
        col = row + LEAF
        fill_tile(tile, row, col, 2 * LEAF)
        loads_two = field[1, :, pl.ds(col, 2 * LEAF)].astype(bf16)
        this = lax.dot_general(loads_two, tile[...], NT, preferred_element_type=f32)
        after = lax.dot_general(
            loads_two[:, :LEAF], tile[:, LEAF:], NN, preferred_element_type=f32
        )
        return this, after

    def near_two(row):
        first, second_part = near_leaf(tile_a, row)
        second, third = near_leaf(tile_b, row + LEAF)
        near[:, pl.ds(row, LEAF)] += first
        near[:, pl.ds(row + LEAF, LEAF)] += second_part + second
        near[:, pl.ds(row + 2 * LEAF, LEAF)] += third

    def near_step(pair, carry):
        near_two(pl.multiple_of(pair * (2 * LEAF), 2 * LEAF))
        return carry

    def side(block, at):
        lanes = jnp.where(low_half((1, 128)), 0, 1)
        return jnp.where(lanes == at, block, 0.0)

    def set_chain(levels, into):
        for at, (pairs, skels) in enumerate(levels):
            first = (1, 7, 11)[at]
            for p in range(len(pairs)):
                into[first + p, 0] = pairs[p]
                into[first + p, 1] = skels[p]

    def set_inner():
        row = (LEAVES - 2) * LEAF
        this, after = near_leaf(tile_a, row)
        fill_tile(tile_c, row + LEAF, row + 2 * LEAF, LEAF)
        own = field[1, :, row + 2 * LEAF : row + 3 * LEAF].astype(bf16)
        after += lax.dot_general(own, tile_c[...], NT, preferred_element_type=f32)
        near[:, row : row + LEAF] += this
        near[:, row + LEAF : row + 2 * LEAF] += after
        for slot in (2, 3):
            local[slot - 1] = cousins(chain, slot)

    def set_edges():
        s1 = raise_skel(s0, every_second)
        s2 = raise_skel(s1, every_second)

        set_chain([(c0, s0), (c1, s1), (c2, s2)], chain)
        for at, (pairs, skels) in enumerate([(c0, s0), (c1, s1), (c2, s2)]):
            edge_send[0, at, 0] = pairs[-1]
            edge_send[0, at, 1] = skels[-1]
            edge_send[1, at, 0] = pairs[0]
            edge_send[1, at, 1] = skels[0]
    def set_leaf_paths():
        x2 = jnp.concatenate([path_map[...].T[:64], transfer[2].T], axis=0)
        x0 = lower(lower([x2], maps[1]), maps[0])
        leaf_high[...], leaf_low[...] = split(jnp.concatenate(x0, axis=1))

    @pl.when(early == 1)
    def _():
        set_field()
        lax.fori_loop(0, ahead, near_step, 0)

    pl.semaphore_wait(
        barrier,
        MEMBERS - 1
        + sum(has.astype(jnp.int32) for has in before + after)
        + 2 * open_rim.astype(jnp.int32)
        + 4 * (2 - to_later[0] - to_later[1])
        - alone.astype(jnp.int32)
        + 4 * (from_earlier[0] + from_earlier[1]),
    )

    def tell(target):
        pl.semaphore_signal(ready, inc=1, device_id=(target,), device_id_type=MESH)

    for turn in range(2):

        @pl.when(from_earlier[turn] == 1)
        def _(turn=turn):
            far_each(turn, lambda k: tell(far_from[k] * MEMBERS + far_member))

    def remote(src, dst, send_sem, recv_sem, target):
        return pltpu.make_async_remote_copy(
            src_ref=src,
            dst_ref=dst,
            send_sem=send_sem,
            recv_sem=recv_sem,
            device_id=(target,),
            device_id_type=MESH,
        )

    def send(*ends):
        copy = remote(*ends)
        copy.start()
        return copy

    def wait_all(ref, semaphore):
        pltpu.make_async_copy(ref, ref, semaphore).wait()

    first = (6, 2, 7, 3, 0, 4, 1, 5)
    place = sum(jnp.where(member == at, rank, 0) for rank, at in enumerate(first))
    for rank in range(MEMBERS - 1):
        mate = box * MEMBERS + jnp.where(place <= rank, first[rank + 1], first[rank])
        send(u_buf.at[member], u_buf.at[member], u_send_sem, u_recv_sem, mate)

    for mate in mates:
        send(g_buf.at[member], g_buf.at[member], g_send_sem, g_recv_sem, mate)

    rim_copies = [
        pltpu.make_async_remote_copy(
            src_ref=g_buf.at[member],
            dst_ref=rim_recv.at[core],
            send_sem=rim_send_sem.at[t],
            recv_sem=rim_recv_sem.at[core],
            device_id=(rim_devices[t],),
            device_id_type=MESH,
        )
        for t in range(2)
    ]

    @pl.when(open_rim)
    def _():
        for copy in rim_copies:
            copy.start()

    @pl.when(early == 0)
    def _():
        set_field()

    last = LEAF * LEAVES
    near_copies = [
        remote(
            field.at[:, :, last : last + LEAF],
            field.at[:, :, 0:LEAF],
            near_send_sem.at[0],
            near_recv_sem.at[0],
            right_device,
        ),
        remote(
            field.at[:, :, LEAF : 2 * LEAF],
            field.at[:, :, last + LEAF : last + 2 * LEAF],
            near_send_sem.at[1],
            near_recv_sem.at[1],
            left_device,
        ),
    ]

    def start(copies, at=0):
        for copy, has in zip(copies, (after[at], before[at])):
            pl.when(has)(copy.start)

    def receive(copies, at=0):
        for copy, has in zip(copies, (before[at], after[at])):
            pl.when(has)(copy.wait_recv)

    start(near_copies)

    edge_copies = [
        remote(
            edge_send.at[side],
            edge_recv.at[side],
            edge_send_sem.at[side],
            edge_recv_sem.at[side],
            (right_device, left_device)[side],
        )
        for side in range(2)
    ]

    set_edges()
    start(edge_copies)

    set_map(3)
    set_map(4)

    @pl.when(early == 1)
    def _():
        set_leaf_paths()

    wait_all(u_buf.at[pl.ds(0, MEMBERS - 1)], u_recv_sem)
    parts = [u_buf[at] for at in range(MEMBERS)]
    while len(parts) > 1:
        parts = [a + b for a, b in zip(parts[0::2], parts[1::2])]
    top_record = parts[0]
    swapped_record = pltpu.roll(top_record, 64, 1)
    far_send[...] = jnp.where(z_low == 0, top_record, swapped_record)

    @pl.when(alone)
    def _():
        far_buf[z_low] = far_send[...]

    def far_start(later):
        for to_x in (0, 3, 1, 2):
            slot = 2 * rem(to_x + across - x, across) + z_low
            for turn in range(2):
                own = jnp.logical_and(alone, jnp.logical_and(x == to_x, z_low == turn))

                @pl.when(jnp.logical_and(to_later[turn] == later, jnp.logical_not(own)))
                def _(to_x=to_x, turn=turn, slot=slot):
                    there = (to_x * depth + to_z[turn]) * 2 + far_half
                    remote(
                        far_send,
                        far_buf.at[slot],
                        far_send_sem,
                        far_recv_sem,
                        there * MEMBERS + far_member,
                    ).start()

    def far_wait(semaphore):
        @pl.when(alone)
        def _():
            wait_all(far_buf.at[pl.ds(1, strides - 1)], semaphore)

        @pl.when(jnp.logical_not(alone))
        def _():
            wait_all(far_buf, semaphore)

    far_start(0)

    wait_all(g_buf.at[pl.ds(0, MEMBERS - 1)], g_recv_sem)
    c3s, s3s = [], []
    for p in range(4):
        even, odd = g_buf[2 * p], g_buf[2 * p + 1]
        c3s.append(jnp.where(low, even, odd))
        s3s.append(pltpu.roll(jnp.where(low, odd, even), 64, 1))
    c4s, s4s = raise_coef(c3s, maps[3]), raise_skel(s3s, every_second)
    c5s, s5s = raise_coef(c4s, maps[4]), raise_skel(s4s, every_second)
    set_chain([(c3s, s3s), (c4s, s4s), (c5s, s5s)], g_chain)
    for at in range(2):
        bound_send[at, 0] = c5s[0]
        bound_send[at, 1] = s5s[0] + pltpu.roll(s4s[1 - at], 3, 0)
    bound_copies = [
        remote(
            bound_send.at[side],
            bound_recv.at[side],
            bound_send_sem.at[side],
            bound_recv_sem.at[side],
            (right_box, left_box)[side],
        )
        for side in range(2)
    ]
    quad_copy = remote(
        g_chain.at[7 + quad, 0],
        quad_recv,
        bound_send_sem.at[2],
        bound_recv_sem.at[2],
        quad_device,
    )
    start(bound_copies, 1)
    pl.when(inside)(quad_copy.start)

    def set_ends(ends, into):
        for level in range(3):
            into[(0, 6, 10)[level]] = ends[0, level]
            into[(5, 9, 12)[level]] = ends[1, level]

    def near_end(tile, row, col):
        fill_tile(tile, row, col, LEAF)
        near[:, row : row + LEAF] += lax.dot_general(
            field[1, :, col : col + LEAF].astype(bf16),
            tile[:, 0:LEAF],
            NT,
            preferred_element_type=f32,
        )

    def finish_ends():
        receive(near_copies)

        @pl.when(device == 0)
        def _():
            field[:, :, 0:LEAF] = jnp.zeros((2, 8, LEAF), f32)
            edge_recv[0] = jnp.zeros((3, 2, 8, 128), f32)

        @pl.when(device == total - 1)
        def _():
            field[:, :, last + LEAF : last + 2 * LEAF] = jnp.zeros((2, 8, LEAF), f32)
            edge_recv[1] = jnp.zeros((3, 2, 8, 128), f32)

        near_end(tile_c, 0, 0)
        near_end(tile_a, last - LEAF, last + LEAF)

        receive(edge_copies)
        set_ends(edge_recv, chain)
        for at, slot in [(0, 1), (3, 4), (4, 7), (5, 8), (6, 11)]:
            local[at] = cousins(chain, slot)

    @pl.when(early == 1)
    def _():
        lax.fori_loop(ahead, 3, near_step, 0)
        set_inner()
        finish_ends()

    later = to_later[0] + to_later[1]

    @pl.when(later > 0)
    def _():
        pl.semaphore_wait(ready, 4 * later)

    far_start(1)

    @pl.when(early == 0)
    def _():
        lax.fori_loop(0, 3, near_step, 0)
        set_inner()
        set_leaf_paths()
        finish_ends()

    top_column = swapped_record.T[:64]
    tx, ty, tz = top_column[:, 0:1], top_column[:, 1:2], top_column[:, 2:3]

    far_wait(far_recv_sem)

    top_coef, top_skel = [], []
    for k in range(0, strides, 2):
        halves = []
        for at in (k, k + 1):
            apart = far_from[at] - box
            counts = jnp.logical_or(apart >= 2, apart <= -2)
            halves.append((far_buf[at], counts))
        (one, one_counts), (two, two_counts) = halves
        coef = jnp.where(low, jnp.where(one_counts, one, 0.0), jnp.where(two_counts, two, 0.0))
        top_coef.append(pltpu.roll(coef, 64, 1))
        top_skel.append(jnp.where(low, two, one))
    top_tile = jnp.concatenate(
        [phi(tx, ty, tz, s[0:1], s[1:2], s[2:3], far_scale) for s in top_skel], axis=1
    )
    top = mm(jnp.concatenate(top_coef, axis=1), split(top_tile), NT)
    part_buf[member] = jnp.concatenate([top, jnp.zeros((8, 64), f32)], axis=1)
    for at in range(MEMBERS - 1):
        mate = box * MEMBERS + at + jnp.where(member <= at, 1, 0)
        send(part_buf.at[member], part_buf.at[member], part_send_sem, part_recv_sem, mate)

    wait_all(u_buf.at[pl.ds(0, MEMBERS - 1)], u_send_sem)
    wait_all(g_buf.at[pl.ds(0, MEMBERS - 1)], g_send_sem)
    far_wait(far_send_sem)
    for copies, at in ((near_copies, 0), (edge_copies, 0), (bound_copies, 1)):
        for copy, has in zip(copies, (after[at], before[at])):
            pl.when(has)(copy.wait_send)
    pl.when(inside)(quad_copy.wait_send)

    receive(bound_copies, 1)
    pl.when(inside)(quad_copy.wait_recv)
    start_skel = jnp.where(before[1], bound_recv[0, 1], 0.0)
    end_skel = jnp.where(after[1], bound_recv[1, 1], 0.0)
    g_chain[10, 0] = jnp.where(before[1], bound_recv[0, 0], 0.0)
    g_chain[10, 1] = start_skel
    g_chain[12, 0] = jnp.where(after[1], bound_recv[1, 0], 0.0)
    g_chain[12, 1] = end_skel
    quad_coef = jnp.where(inside, quad_recv[...], 0.0)
    g_chain[6, 0] = quad_coef
    g_chain[6, 1] = pltpu.roll(start_skel, 5, 0)
    g_chain[9, 0] = quad_coef
    g_chain[9, 1] = pltpu.roll(end_skel, 5, 0)

    @pl.when(jnp.logical_not(inside))
    def _():
        for slot in (0, 5):
            g_chain[slot] = jnp.zeros((2, 8, 128), f32)

    @pl.when(open_rim)
    def _():
        for copy in rim_copies:
            copy.wait_send()
        for t in range(2):
            pltpu.make_async_remote_copy(
                src_ref=g_buf.at[member],
                dst_ref=rim_recv.at[t],
                send_sem=rim_send_sem.at[t],
                recv_sem=rim_recv_sem.at[t],
                device_id=(rim_devices[t],),
                device_id_type=MESH,
            ).wait_recv()
        even, odd = rim_recv[0], rim_recv[1]
        rim_coef = jnp.where(low, even, odd)
        rim_skel = pltpu.roll(jnp.where(low, odd, even), 64, 1)
        for slot in (0, 5):
            g_chain[slot, 0] = rim_coef
            g_chain[slot, 1] = rim_skel

    local3 = cousins(g_chain, 1 + y)
    local4 = cousins(g_chain, 7 + quad)
    local5 = cousins(g_chain, 11)
    y2 = local[6]
    y1 = [x + local[4 + at] for at, x in enumerate(lower([y2], maps[1]))]
    y0 = [x + local[at] for at, x in enumerate(lower(y1, maps[0]))]
    y4 = local4 + mm(side(local5, quad), maps[4], NT)
    y3 = local3 + mm(side(y4, rem(y, 2)), maps[3], NT)
    y3 = jnp.where(core == 1, y3, pltpu.roll(y3, 64, 1))

    wait_all(part_buf.at[pl.ds(0, MEMBERS - 1)], part_recv_sem)
    parts = [part_buf[at] for at in range(MEMBERS)]
    while len(parts) > 1:
        parts = [a + b for a, b in zip(parts[0::2], parts[1::2])]
    d6 = parts[0]
    d63 = jnp.where(low, d6, y3)
    d0 = jnp.concatenate(y0, axis=1) + mm(d63, (leaf_high, leaf_low), NN)
    for p in range(4):
        pair = d0[:, 128 * p : 128 * p + 128]
        two = jnp.concatenate([jnp.where(low, pair, 0.0), jnp.where(low, 0.0, pair)], axis=0)
        rows = lax.dot_general(
            two.astype(bf16),
            basis[128 * p : 128 * p + 128, :],
            NN,
            preferred_element_type=f32,
        )
        for t in range(2):
            leaf = 2 * p + t
            at = leaf * LEAF
            out_ref[:, at : at + LEAF] = jnp.where(
                slots < occ[leaf], near[:, at : at + LEAF] + rows[8 * t : 8 * t + 8], 0.0
            )

    wait_all(part_buf.at[pl.ds(0, MEMBERS - 1)], part_send_sem)


def body(boxes, across, coords, loads, occupancy, basis, transfer):
    strides = boxes // MEMBERS
    hbm = pl.BlockSpec(memory_space=pl.ANY)
    dma = pltpu.SemaphoreType.DMA
    return pl.pallas_call(
        functools.partial(kernel, boxes, across),
        out_shape=jax.ShapeDtypeStruct((COLS, OWN), f32),
        in_specs=[hbm] * 5,
        out_specs=pl.BlockSpec(memory_space=pltpu.VMEM),
        scratch_shapes=[
            pltpu.VMEM((3, OWN), f32),
            pltpu.VMEM((COLS, OWN), bf16),
            pltpu.SMEM((LEAVES,), jnp.int32),
            pltpu.VMEM((LEAVES * 64, LEAF), bf16),
            pltpu.VMEM((6, 128, 64), f32),
            pltpu.VMEM((6, 128, 128), bf16),
            pltpu.VMEM((6, 128, 128), bf16),
            pltpu.VMEM((128, 128), f32),
            pltpu.VMEM((2, 8, OWN + 2 * LEAF), f32),
            pltpu.VMEM((OWN, 8), f32),
            pltpu.VMEM((128, 512), bf16),
            pltpu.VMEM((128, 512), bf16),
            pltpu.VMEM((COLS, OWN + LEAF), f32),
            pltpu.VMEM((LEAF, 2 * LEAF), bf16),
            pltpu.VMEM((LEAF, 2 * LEAF), bf16),
            pltpu.VMEM((LEAF, LEAF), bf16),
            pltpu.VMEM((13, 2, 8, 128), f32),
            pltpu.VMEM((13, 2, 8, 128), f32),
            pltpu.VMEM((7, 8, 128), f32),
            pltpu.VMEM((2, 3, 2, 8, 128), f32),
            pltpu.VMEM((2, 3, 2, 8, 128), f32),
            pltpu.VMEM((MEMBERS, 8, 128), f32),
            pltpu.VMEM((MEMBERS, 8, 128), f32),
            pltpu.VMEM((2, 2, 8, 128), f32),
            pltpu.VMEM((2, 2, 8, 128), f32),
            pltpu.VMEM((8, 128), f32),
            pltpu.VMEM((2, 8, 128), f32),
            pltpu.VMEM((8, 128), f32),
            pltpu.VMEM((strides, 8, 128), f32),
            pltpu.VMEM((MEMBERS, 8, 128), f32),
            dma((5,)),
            dma((2,)),
            dma((2,)),
            dma((2,)),
            dma((2,)),
            dma,
            dma,
            dma,
            dma,
            dma((3,)),
            dma((3,)),
            dma((2,)),
            dma((2,)),
            dma,
            dma,
            dma,
            dma,
            pltpu.SemaphoreType.REGULAR,
        ],
        compiler_params=pltpu.CompilerParams(
            collective_id=0, has_side_effects=True, vmem_limit_bytes=32 * 1024 * 1024
        ),
    )(
        *[
            pltpu.with_memory_space_constraint(x, pltpu.HBM)
            for x in (
                coords,
                loads,
                occupancy,
                basis.reshape(LEAVES * 64, LEAF),
                transfer.reshape(6, 128, 64),
            )
        ]
    )


def solution(mesh):
    boxes = mesh.shape["box"] // MEMBERS
    return jax.shard_map(
        functools.partial(body, boxes, 4),
        mesh=mesh,
        in_specs=(P(None, "box"), P(None, "box"), P("box"), P("box", None, None), P()),
        out_specs=P(None, "box"),
        check_vma=False,
    )
```

```python
import functools

import jax
import jax.numpy as jnp
from jax import lax
from jax.experimental import pallas as pl
from jax.experimental.pallas import tpu as pltpu
from jax.sharding import PartitionSpec as P

LEAF = 256
COLS = 8
LEAVES = 8
MEMBERS = 8
OWN = LEAF * LEAVES

f32 = jnp.float32
bf16 = jnp.bfloat16
soften = 0.0001
near_scale = 0.0625
far_scale = 0.125
NN = (((1,), (0,)), ((), ()))
NT = (((1,), (1,)), ((), ()))
MESH = pl.DeviceIdType.MESH


def div(a, b):
    return lax.div(a, jnp.int32(b))


def rem(a, b):
    return lax.rem(a, jnp.int32(b))


def phi(tx, ty, tz, sx, sy, sz, scale):
    dx = tx - sx
    dy = ty - sy
    dz = tz - sz
    r2 = dx * dx + dy * dy + dz * dz
    return (r2 * (0.5 * scale)) * jnp.log(r2 + soften)


def split(x):
    high = x.astype(bf16)
    return high, (x - high.astype(f32)).astype(bf16)


def mm(a, b, dims):
    rows = a.shape[0]
    high = a.astype(bf16).astype(f32)
    stacked = jnp.concatenate([high, a - high], axis=0).astype(bf16)
    both = lax.dot_general(stacked, b[0][...], dims, preferred_element_type=f32)
    low = lax.dot_general(stacked[:rows], b[1][...], dims, preferred_element_type=f32)
    return both[:rows] + (both[rows:] + low)


def low_half(shape):
    return lax.broadcasted_iota(jnp.int32, shape, len(shape) - 1) < 64


def merge(rows):
    count = rows.shape[0] // 16
    low = low_half((8, 128))
    return [
        jnp.where(low, rows[16 * i : 16 * i + 8], rows[16 * i + 8 : 16 * i + 16])
        for i in range(count)
    ]


def raise_coef(pairs, level_map):
    rows = mm(jnp.concatenate(pairs, axis=0), level_map, NN)
    return merge(rows) if len(pairs) > 1 else [rows]


def pick(x, entries):
    rows = x.shape[0]
    a = x.astype(bf16).astype(f32)
    b = (x - a).astype(bf16).astype(f32)
    c = (x - a) - b
    stacked = jnp.concatenate([a, b, c], axis=0).astype(bf16)
    picked = lax.dot_general(stacked, entries, NN, preferred_element_type=f32)
    return picked[:rows] + picked[rows : 2 * rows] + picked[2 * rows :]


def raise_skel(pairs, every_second):
    rows_up = pick(jnp.concatenate(pairs, axis=0), every_second)
    return merge(rows_up) if len(pairs) > 1 else [rows_up]


def cousins(chain, slot):
    low = low_half((8, 128))
    column = chain[slot, 1].T
    tx, ty, tz = column[:, 0:1], column[:, 1:2], column[:, 2:3]
    before, after = chain[slot - 1, 0], chain[slot + 1, 0]
    tiles = []
    for skel in (chain[slot - 1, 1], chain[slot + 1, 1]):
        tiles.append(phi(tx, ty, tz, skel[0:1], skel[1:2], skel[2:3], far_scale))
    tile = jnp.concatenate(tiles, axis=1)
    even = jnp.concatenate([jnp.where(low, before, 0.0), after], axis=1)
    odd = jnp.concatenate([before, jnp.where(low, 0.0, after)], axis=1)
    rows = mm(jnp.concatenate([even, odd], axis=0), split(tile), NT)
    return jnp.where(low, rows[:8], rows[8:])


def lower(pairs, level_map):
    height = pairs[0].shape[0]
    low = low_half((height, 128))
    stacked = []
    for pair in pairs:
        stacked += [jnp.where(low, pair, 0.0), jnp.where(low, 0.0, pair)]
    rows = mm(jnp.concatenate(stacked, axis=0), level_map, NT)
    return [rows[height * i : height * (i + 1)] for i in range(2 * len(pairs))]


def kernel(
    boxes,
    across,
    coords_hbm,
    loads_hbm,
    occ_hbm,
    basis_hbm,
    transfer_hbm,
    out_ref,
    coords,
    loads,
    occ,
    basis,
    transfer,
    map_high,
    map_low,
    path_map,
    field,
    column,
    leaf_high,
    leaf_low,
    near,
    tile_a,
    tile_b,
    tile_c,
    chain,
    g_chain,
    local,
    edge_send,
    edge_recv,
    u_buf,
    g_buf,
    bound_send,
    bound_recv,
    quad_recv,
    rim_recv,
    far_send,
    far_buf,
    part_buf,
    load_sem,
    near_send_sem,
    near_recv_sem,
    edge_send_sem,
    edge_recv_sem,
    u_send_sem,
    u_recv_sem,
    g_send_sem,
    g_recv_sem,
    bound_send_sem,
    bound_recv_sem,
    rim_send_sem,
    rim_recv_sem,
    far_send_sem,
    far_recv_sem,
    part_send_sem,
    part_recv_sem,
    ready,
):
    loading = [
        pltpu.make_async_copy(src, dst, load_sem.at[at])
        for at, (src, dst) in enumerate(
            [
                (coords_hbm, coords),
                (transfer_hbm, transfer),
                (loads_hbm, loads),
                (occ_hbm, occ),
                (basis_hbm, basis),
            ]
        )
    ]
    for copy in loading:
        copy.start()

    device = lax.axis_index("box")
    total = boxes * MEMBERS
    strides = boxes // MEMBERS
    depth = boxes // (2 * across)
    box, member = div(device, MEMBERS), rem(device, MEMBERS)
    x, z, y_half = div(box, 2 * depth), rem(div(box, 2), depth), rem(box, 2)
    y, core = div(member, 2), rem(member, 2)
    low = low_half((8, 128))
    half = jnp.where(low, 0, 1)

    top = jnp.where(y == 3, 1, 0)
    outer = jnp.where(y == 0, 1, top)
    side_to = jnp.where(outer == 1, top, 2 - y)
    side_from = jnp.where(outer == 1, 1 - top, 2 - y)
    far_half = jnp.where(outer == 1, 1 - y_half, y_half)
    z_core = rem(div(z, 2), 2)
    far_member = 2 * jnp.where(outer == 1, 3 - y, y) + z_core
    z_high, z_low = div(z, 4), rem(z, 2)
    far_x = [rem(x + dx, across) for dx in range(across)]
    far_steps = [(dx, turn) for dx in range(across) for turn in range(2)]

    def far_depths(side):
        first = 4 * rem(side + z_high, 2) + 2 * core
        return [first, first + 1]

    to_z, from_z = far_depths(side_to), far_depths(side_from)

    def far_box(depths, dx, turn):
        return (far_x[dx % across] * depth + depths[turn]) * 2 + far_half

    far_to = [far_box(to_z, dx, turn) * MEMBERS + far_member for dx, turn in far_steps]
    far_from = [far_box(from_z, -dx, turn) for dx, turn in far_steps]
    alone = jnp.logical_and(jnp.logical_and(outer == 0, side_to == 0), core == z_core)

    barrier = pltpu.get_barrier_semaphore()

    def greet(target):
        pl.semaphore_signal(barrier, inc=1, device_id=(target,), device_id_type=MESH)

    def order(at):
        return jnp.where(at == 0, 0, jnp.where(at >= 6, 2, 1))

    mine = order(z)
    to_later = [jnp.where(order(at) > mine, 1, 0) for at in to_z]
    from_earlier = [jnp.where(order(at) < mine, 1, 0) for at in from_z]
    far_order = [(2 * dx + turn) for turn in range(2) for dx in (2, 1, 3, 0)]

    def far_each(turn, act):
        for k in far_order[4 * turn : 4 * turn + 4]:
            if k == turn:
                pl.when(jnp.logical_not(jnp.logical_and(alone, z_low == turn)))(
                    functools.partial(act, k)
                )
            else:
                act(k)

    for turn in range(2):

        @pl.when(from_earlier[turn] == 0)
        def _(turn=turn):
            far_each(turn, lambda k: greet(far_from[k] * MEMBERS + far_member))

        @pl.when(to_later[turn] == 1)
        def _(turn=turn):
            far_each(turn, lambda k: greet(far_to[k]))

    left_device = rem(device + total - 1, total)
    right_device = rem(device + 1, total)
    mirror = 2 * (3 - y) + core
    left_box = rem(box + boxes - 1, boxes) * MEMBERS + mirror
    right_box = rem(box + 1, boxes) * MEMBERS + mirror
    mates = [box * MEMBERS + rem(member + r, MEMBERS) for r in (6, 2, 7, 3, 5, 4, 1)]
    at_rim = outer == 1
    rim_box = rem(box + boxes + 2 * top - 1, boxes)
    rim_devices = [rim_box * MEMBERS + 6 - 6 * top + t for t in range(2)]
    quad = div(member, 4)
    quad_device = rem(box + boxes + 2 * quad - 1, boxes) * MEMBERS + mirror
    early = jnp.where(z == 0, 1, 0)
    ahead = 2
    before = [device > 0, box > 0]
    after = [device < total - 1, box < boxes - 1]
    inside = jnp.where(quad == 0, box, boxes - 1 - box) > 0
    open_rim = jnp.logical_and(at_rim, inside)

    for target in mates:
        greet(target)
    for has, targets in ((before, (left_device, left_box)), (after, (right_device, right_box))):
        for at in range(2):
            pl.when(has[at])(functools.partial(greet, targets[at]))

    @pl.when(open_rim)
    def _():
        for target in rim_devices:
            greet(target)

    lanes = lax.broadcasted_iota(jnp.int32, (1, 128), 1)
    index = lax.broadcasted_iota(jnp.int32, (512, 128), 0)
    placed = (index == (lanes - 64 - 8 * member) * 64).astype(f32).astype(bf16)
    picks = (lax.broadcasted_iota(jnp.int32, (1, 128), 1) & 63) * 2
    every_second = (
        (lax.broadcasted_iota(jnp.int32, (128, 128), 0) == picks).astype(f32).astype(bf16)
    )
    for copy in loading:
        copy.wait()
    points = jnp.concatenate([coords[...], jnp.zeros((5, OWN), f32)], axis=0)
    s0 = [
        jnp.concatenate(
            [points[:, 512 * p : 512 * p + 64], points[:, 512 * p + 256 : 512 * p + 320]], axis=1
        )
        for p in range(4)
    ]
    s6 = pick(jnp.concatenate(s0, axis=1), placed)

    maps = [(map_high.at[level], map_low.at[level]) for level in range(6)]

    def set_map(level):
        once = transfer[level]
        map_high[level], map_low[level] = split(jnp.concatenate([once, once], axis=1))

    for level in range(2):
        set_map(level)
    slots = lax.broadcasted_iota(jnp.int32, (COLS, LEAF), 1)
    live = []
    for leaf in range(LEAVES):
        part = loads[:, leaf * LEAF : (leaf + 1) * LEAF].astype(f32)
        live.append(jnp.where(slots < occ[leaf], part, 0.0))
    c0 = []
    for p in range(4):
        two = jnp.concatenate([live[2 * p], live[2 * p + 1]], axis=0).astype(bf16)
        rows = lax.dot_general(
            two, basis[128 * p : 128 * p + 128, :], NT, preferred_element_type=f32
        )
        c0.append(jnp.where(low, rows[:8], rows[8:]))
    c1 = raise_coef(c0, maps[0])
    c2 = raise_coef(c1, maps[1])
    def factor(level, at):
        return transfer[level, pl.ds(pl.multiple_of(64 * at, 64), 64), :]

    map_34 = mm(transfer[2], split(factor(3, core)), NN)
    wide = jnp.concatenate([factor(5, quad), jnp.zeros((64, 64), f32)], axis=1)
    map_56 = mm(factor(4, rem(y, 2)), split(wide), NN)
    map_6 = mm(map_34, split(map_56), NN)
    u_buf[member] = mm(c2[0], split(map_6), NN) + s6
    path_map[...] = map_6

    def set_field():
        field[0, :, LEAF : LEAF + OWN] = points
        for leaf in range(LEAVES):
            field[1, :, (leaf + 1) * LEAF : (leaf + 2) * LEAF] = live[leaf]
        for at in range(0, OWN, 128):
            column[at : at + 128, :] = points[:, at : at + 128].T
        near[...] = jnp.zeros_like(near)

    def fill_tile(tile, row, col, width):
        sx = field[0, 0:1, pl.ds(col, width)]
        sy = field[0, 1:2, pl.ds(col, width)]
        sz = field[0, 2:3, pl.ds(col, width)]
        for at in range(0, LEAF, 16):
            rows = column[pl.ds(row + at, 16), :]
            tile[at : at + 16, 0:width] = phi(
                rows[:, 0:1], rows[:, 1:2], rows[:, 2:3], sx, sy, sz, near_scale
            ).astype(bf16)

    def near_leaf(tile, row):
        col = row + LEAF
        fill_tile(tile, row, col, 2 * LEAF)
        loads_two = field[1, :, pl.ds(col, 2 * LEAF)].astype(bf16)
        this = lax.dot_general(loads_two, tile[...], NT, preferred_element_type=f32)
        after = lax.dot_general(
            loads_two[:, :LEAF], tile[:, LEAF:], NN, preferred_element_type=f32
        )
        return this, after

    def near_two(row):
        first, second_part = near_leaf(tile_a, row)
        second, third = near_leaf(tile_b, row + LEAF)
        near[:, pl.ds(row, LEAF)] += first
        near[:, pl.ds(row + LEAF, LEAF)] += second_part + second
        near[:, pl.ds(row + 2 * LEAF, LEAF)] += third

    def near_step(pair, carry):
        near_two(pl.multiple_of(pair * (2 * LEAF), 2 * LEAF))
        return carry

    def side(block, at):
        lanes = jnp.where(low_half((1, 128)), 0, 1)
        return jnp.where(lanes == at, block, 0.0)

    def set_chain(levels, into):
        for at, (pairs, skels) in enumerate(levels):
            first = (1, 7, 11)[at]
            for p in range(len(pairs)):
                into[first + p, 0] = pairs[p]
                into[first + p, 1] = skels[p]

    def set_inner():
        row = (LEAVES - 2) * LEAF
        this, after = near_leaf(tile_a, row)
        fill_tile(tile_c, row + LEAF, row + 2 * LEAF, LEAF)
        own = field[1, :, row + 2 * LEAF : row + 3 * LEAF].astype(bf16)
        after += lax.dot_general(own, tile_c[...], NT, preferred_element_type=f32)
        near[:, row : row + LEAF] += this
        near[:, row + LEAF : row + 2 * LEAF] += after
        for slot in (2, 3):
            local[slot - 1] = cousins(chain, slot)

    def set_edges():
        s1 = raise_skel(s0, every_second)
        s2 = raise_skel(s1, every_second)

        set_chain([(c0, s0), (c1, s1), (c2, s2)], chain)
        for at, (pairs, skels) in enumerate([(c0, s0), (c1, s1), (c2, s2)]):
            edge_send[0, at, 0] = pairs[-1]
            edge_send[0, at, 1] = skels[-1]
            edge_send[1, at, 0] = pairs[0]
            edge_send[1, at, 1] = skels[0]
    def set_leaf_paths():
        x2 = jnp.concatenate([path_map[...].T[:64], transfer[2].T], axis=0)
        x0 = lower(lower([x2], maps[1]), maps[0])
        leaf_high[...], leaf_low[...] = split(jnp.concatenate(x0, axis=1))

    @pl.when(early == 1)
    def _():
        set_field()
        lax.fori_loop(0, ahead, near_step, 0)

    pl.semaphore_wait(
        barrier,
        MEMBERS - 1
        + sum(has.astype(jnp.int32) for has in before + after)
        + 2 * open_rim.astype(jnp.int32)
        + 4 * (2 - to_later[0] - to_later[1])
        - alone.astype(jnp.int32)
        + 4 * (from_earlier[0] + from_earlier[1]),
    )

    def tell(target):
        pl.semaphore_signal(ready, inc=1, device_id=(target,), device_id_type=MESH)

    for turn in range(2):

        @pl.when(from_earlier[turn] == 1)
        def _(turn=turn):
            far_each(turn, lambda k: tell(far_from[k] * MEMBERS + far_member))

    def remote(src, dst, send_sem, recv_sem, target):
        return pltpu.make_async_remote_copy(
            src_ref=src,
            dst_ref=dst,
            send_sem=send_sem,
            recv_sem=recv_sem,
            device_id=(target,),
            device_id_type=MESH,
        )

    def send(*ends):
        copy = remote(*ends)
        copy.start()
        return copy

    def wait_all(ref, semaphore):
        pltpu.make_async_copy(ref, ref, semaphore).wait()

    first = (6, 2, 7, 3, 0, 4, 1, 5)
    place = sum(jnp.where(member == at, rank, 0) for rank, at in enumerate(first))
    for rank in range(MEMBERS - 1):
        mate = box * MEMBERS + jnp.where(place <= rank, first[rank + 1], first[rank])
        send(u_buf.at[member], u_buf.at[member], u_send_sem, u_recv_sem, mate)

    set_map(2)
    every_eighth = (index == (lanes & 63) * 8).astype(f32).astype(bf16)
    s3 = pick(jnp.concatenate(s0, axis=1), every_eighth)
    c3 = raise_coef(c2, maps[2])[0]
    g_buf[member] = jnp.where(half == core, c3, s3)
    for mate in mates:
        send(g_buf.at[member], g_buf.at[member], g_send_sem, g_recv_sem, mate)

    rim_copies = [
        pltpu.make_async_remote_copy(
            src_ref=g_buf.at[member],
            dst_ref=rim_recv.at[core],
            send_sem=rim_send_sem.at[t],
            recv_sem=rim_recv_sem.at[core],
            device_id=(rim_devices[t],),
            device_id_type=MESH,
        )
        for t in range(2)
    ]

    @pl.when(open_rim)
    def _():
        for copy in rim_copies:
            copy.start()

    @pl.when(early == 0)
    def _():
        set_field()

    last = LEAF * LEAVES
    near_copies = [
        remote(
            field.at[:, :, last : last + LEAF],
            field.at[:, :, 0:LEAF],
            near_send_sem.at[0],
            near_recv_sem.at[0],
            right_device,
        ),
        remote(
            field.at[:, :, LEAF : 2 * LEAF],
            field.at[:, :, last + LEAF : last + 2 * LEAF],
            near_send_sem.at[1],
            near_recv_sem.at[1],
            left_device,
        ),
    ]

    def start(copies, at=0):
        for copy, has in zip(copies, (after[at], before[at])):
            pl.when(has)(copy.start)

    def receive(copies, at=0):
        for copy, has in zip(copies, (before[at], after[at])):
            pl.when(has)(copy.wait_recv)

    start(near_copies)

    edge_copies = [
        remote(
            edge_send.at[side],
            edge_recv.at[side],
            edge_send_sem.at[side],
            edge_recv_sem.at[side],
            (right_device, left_device)[side],
        )
        for side in range(2)
    ]

    set_edges()
    start(edge_copies)

    set_map(3)
    set_map(4)

    @pl.when(early == 1)
    def _():
        set_leaf_paths()

    wait_all(u_buf.at[pl.ds(0, MEMBERS - 1)], u_recv_sem)
    parts = [u_buf[at] for at in range(MEMBERS)]
    while len(parts) > 1:
        parts = [a + b for a, b in zip(parts[0::2], parts[1::2])]
    top_record = parts[0]
    swapped_record = pltpu.roll(top_record, 64, 1)
    far_send[...] = jnp.where(z_low == 0, top_record, swapped_record)

    @pl.when(alone)
    def _():
        far_buf[z_low] = far_send[...]

    def far_copy(k):
        slot = k - k % 2 + z_low
        return remote(far_send, far_buf.at[slot], far_send_sem, far_recv_sem, far_to[k])

    def far_wait(semaphore):
        @pl.when(alone)
        def _():
            wait_all(far_buf.at[pl.ds(1, strides - 1)], semaphore)

        @pl.when(jnp.logical_not(alone))
        def _():
            wait_all(far_buf, semaphore)

    for turn in range(2):

        @pl.when(to_later[turn] == 0)
        def _(turn=turn):
            far_each(turn, lambda k: far_copy(k).start())

    wait_all(g_buf.at[pl.ds(0, MEMBERS - 1)], g_recv_sem)
    c3s, s3s = [], []
    for p in range(4):
        even, odd = g_buf[2 * p], g_buf[2 * p + 1]
        c3s.append(jnp.where(low, even, odd))
        s3s.append(pltpu.roll(jnp.where(low, odd, even), 64, 1))
    c4s, s4s = raise_coef(c3s, maps[3]), raise_skel(s3s, every_second)
    c5s, s5s = raise_coef(c4s, maps[4]), raise_skel(s4s, every_second)
    set_chain([(c3s, s3s), (c4s, s4s), (c5s, s5s)], g_chain)
    for at in range(2):
        bound_send[at, 0] = c5s[0]
        bound_send[at, 1] = s5s[0] + pltpu.roll(s4s[1 - at], 3, 0)
    bound_copies = [
        remote(
            bound_send.at[side],
            bound_recv.at[side],
            bound_send_sem.at[side],
            bound_recv_sem.at[side],
            (right_box, left_box)[side],
        )
        for side in range(2)
    ]
    quad_copy = remote(
        g_chain.at[7 + quad, 0],
        quad_recv,
        bound_send_sem.at[2],
        bound_recv_sem.at[2],
        quad_device,
    )
    start(bound_copies, 1)
    pl.when(inside)(quad_copy.start)

    def set_ends(ends, into):
        for level in range(3):
            into[(0, 6, 10)[level]] = ends[0, level]
            into[(5, 9, 12)[level]] = ends[1, level]

    def near_end(tile, row, col):
        fill_tile(tile, row, col, LEAF)
        near[:, row : row + LEAF] += lax.dot_general(
            field[1, :, col : col + LEAF].astype(bf16),
            tile[:, 0:LEAF],
            NT,
            preferred_element_type=f32,
        )

    def finish_ends():
        receive(near_copies)

        @pl.when(device == 0)
        def _():
            field[:, :, 0:LEAF] = jnp.zeros((2, 8, LEAF), f32)
            edge_recv[0] = jnp.zeros((3, 2, 8, 128), f32)

        @pl.when(device == total - 1)
        def _():
            field[:, :, last + LEAF : last + 2 * LEAF] = jnp.zeros((2, 8, LEAF), f32)
            edge_recv[1] = jnp.zeros((3, 2, 8, 128), f32)

        near_end(tile_c, 0, 0)
        near_end(tile_a, last - LEAF, last + LEAF)

        receive(edge_copies)
        set_ends(edge_recv, chain)
        for at, slot in [(0, 1), (3, 4), (4, 7), (5, 8), (6, 11)]:
            local[at] = cousins(chain, slot)

    @pl.when(early == 1)
    def _():
        lax.fori_loop(ahead, 3, near_step, 0)
        set_inner()
        finish_ends()

    later = to_later[0] + to_later[1]

    @pl.when(later > 0)
    def _():
        pl.semaphore_wait(ready, 4 * later)

    for turn in range(2):

        @pl.when(to_later[turn] == 1)
        def _(turn=turn):
            far_each(turn, lambda k: far_copy(k).start())

    @pl.when(early == 0)
    def _():
        lax.fori_loop(0, 3, near_step, 0)
        set_inner()
        set_leaf_paths()
        finish_ends()

    top_column = swapped_record.T[:64]
    tx, ty, tz = top_column[:, 0:1], top_column[:, 1:2], top_column[:, 2:3]

    far_wait(far_recv_sem)

    top_coef, top_skel = [], []
    for k in range(0, strides, 2):
        halves = []
        for at in (k, k + 1):
            apart = far_from[at] - box
            counts = jnp.logical_or(apart >= 2, apart <= -2)
            halves.append((far_buf[at], counts))
        (one, one_counts), (two, two_counts) = halves
        coef = jnp.where(low, jnp.where(one_counts, one, 0.0), jnp.where(two_counts, two, 0.0))
        top_coef.append(pltpu.roll(coef, 64, 1))
        top_skel.append(jnp.where(low, two, one))
    top_tile = jnp.concatenate(
        [phi(tx, ty, tz, s[0:1], s[1:2], s[2:3], far_scale) for s in top_skel], axis=1
    )
    top = mm(jnp.concatenate(top_coef, axis=1), split(top_tile), NT)
    part_buf[member] = jnp.concatenate([top, jnp.zeros((8, 64), f32)], axis=1)
    for at in range(MEMBERS - 1):
        mate = box * MEMBERS + at + jnp.where(member <= at, 1, 0)
        send(part_buf.at[member], part_buf.at[member], part_send_sem, part_recv_sem, mate)

    wait_all(u_buf.at[pl.ds(0, MEMBERS - 1)], u_send_sem)
    wait_all(g_buf.at[pl.ds(0, MEMBERS - 1)], g_send_sem)
    far_wait(far_send_sem)
    for copies, at in ((near_copies, 0), (edge_copies, 0), (bound_copies, 1)):
        for copy, has in zip(copies, (after[at], before[at])):
            pl.when(has)(copy.wait_send)
    pl.when(inside)(quad_copy.wait_send)

    receive(bound_copies, 1)
    pl.when(inside)(quad_copy.wait_recv)
    start_skel = jnp.where(before[1], bound_recv[0, 1], 0.0)
    end_skel = jnp.where(after[1], bound_recv[1, 1], 0.0)
    g_chain[10, 0] = jnp.where(before[1], bound_recv[0, 0], 0.0)
    g_chain[10, 1] = start_skel
    g_chain[12, 0] = jnp.where(after[1], bound_recv[1, 0], 0.0)
    g_chain[12, 1] = end_skel
    quad_coef = jnp.where(inside, quad_recv[...], 0.0)
    g_chain[6, 0] = quad_coef
    g_chain[6, 1] = pltpu.roll(start_skel, 5, 0)
    g_chain[9, 0] = quad_coef
    g_chain[9, 1] = pltpu.roll(end_skel, 5, 0)

    @pl.when(jnp.logical_not(inside))
    def _():
        for slot in (0, 5):
            g_chain[slot] = jnp.zeros((2, 8, 128), f32)

    @pl.when(open_rim)
    def _():
        for copy in rim_copies:
            copy.wait_send()
        for t in range(2):
            pltpu.make_async_remote_copy(
                src_ref=g_buf.at[member],
                dst_ref=rim_recv.at[t],
                send_sem=rim_send_sem.at[t],
                recv_sem=rim_recv_sem.at[t],
                device_id=(rim_devices[t],),
                device_id_type=MESH,
            ).wait_recv()
        even, odd = rim_recv[0], rim_recv[1]
        rim_coef = jnp.where(low, even, odd)
        rim_skel = pltpu.roll(jnp.where(low, odd, even), 64, 1)
        for slot in (0, 5):
            g_chain[slot, 0] = rim_coef
            g_chain[slot, 1] = rim_skel

    local3 = cousins(g_chain, 1 + y)
    local4 = cousins(g_chain, 7 + quad)
    local5 = cousins(g_chain, 11)
    y2 = local[6]
    y1 = [x + local[4 + at] for at, x in enumerate(lower([y2], maps[1]))]
    y0 = [x + local[at] for at, x in enumerate(lower(y1, maps[0]))]
    y4 = local4 + mm(side(local5, quad), maps[4], NT)
    y3 = local3 + mm(side(y4, rem(y, 2)), maps[3], NT)
    y3 = jnp.where(core == 1, y3, pltpu.roll(y3, 64, 1))

    wait_all(part_buf.at[pl.ds(0, MEMBERS - 1)], part_recv_sem)
    parts = [part_buf[at] for at in range(MEMBERS)]
    while len(parts) > 1:
        parts = [a + b for a, b in zip(parts[0::2], parts[1::2])]
    d6 = parts[0]
    d63 = jnp.where(low, d6, y3)
    d0 = jnp.concatenate(y0, axis=1) + mm(d63, (leaf_high, leaf_low), NN)
    for p in range(4):
        pair = d0[:, 128 * p : 128 * p + 128]
        two = jnp.concatenate([jnp.where(low, pair, 0.0), jnp.where(low, 0.0, pair)], axis=0)
        rows = lax.dot_general(
            two.astype(bf16),
            basis[128 * p : 128 * p + 128, :],
            NN,
            preferred_element_type=f32,
        )
        for t in range(2):
            leaf = 2 * p + t
            at = leaf * LEAF
            out_ref[:, at : at + LEAF] = jnp.where(
                slots < occ[leaf], near[:, at : at + LEAF] + rows[8 * t : 8 * t + 8], 0.0
            )

    wait_all(part_buf.at[pl.ds(0, MEMBERS - 1)], part_send_sem)


def body(boxes, across, coords, loads, occupancy, basis, transfer):
    strides = boxes // MEMBERS
    hbm = pl.BlockSpec(memory_space=pl.ANY)
    dma = pltpu.SemaphoreType.DMA
    return pl.pallas_call(
        functools.partial(kernel, boxes, across),
        out_shape=jax.ShapeDtypeStruct((COLS, OWN), f32),
        in_specs=[hbm] * 5,
        out_specs=pl.BlockSpec(memory_space=pltpu.VMEM),
        scratch_shapes=[
            pltpu.VMEM((3, OWN), f32),
            pltpu.VMEM((COLS, OWN), bf16),
            pltpu.SMEM((LEAVES,), jnp.int32),
            pltpu.VMEM((LEAVES * 64, LEAF), bf16),
            pltpu.VMEM((6, 128, 64), f32),
            pltpu.VMEM((6, 128, 128), bf16),
            pltpu.VMEM((6, 128, 128), bf16),
            pltpu.VMEM((128, 128), f32),
            pltpu.VMEM((2, 8, OWN + 2 * LEAF), f32),
            pltpu.VMEM((OWN, 8), f32),
            pltpu.VMEM((128, 512), bf16),
            pltpu.VMEM((128, 512), bf16),
            pltpu.VMEM((COLS, OWN + LEAF), f32),
            pltpu.VMEM((LEAF, 2 * LEAF), bf16),
            pltpu.VMEM((LEAF, 2 * LEAF), bf16),
            pltpu.VMEM((LEAF, LEAF), bf16),
            pltpu.VMEM((13, 2, 8, 128), f32),
            pltpu.VMEM((13, 2, 8, 128), f32),
            pltpu.VMEM((7, 8, 128), f32),
            pltpu.VMEM((2, 3, 2, 8, 128), f32),
            pltpu.VMEM((2, 3, 2, 8, 128), f32),
            pltpu.VMEM((MEMBERS, 8, 128), f32),
            pltpu.VMEM((MEMBERS, 8, 128), f32),
            pltpu.VMEM((2, 2, 8, 128), f32),
            pltpu.VMEM((2, 2, 8, 128), f32),
            pltpu.VMEM((8, 128), f32),
            pltpu.VMEM((2, 8, 128), f32),
            pltpu.VMEM((8, 128), f32),
            pltpu.VMEM((strides, 8, 128), f32),
            pltpu.VMEM((MEMBERS, 8, 128), f32),
            dma((5,)),
            dma((2,)),
            dma((2,)),
            dma((2,)),
            dma((2,)),
            dma,
            dma,
            dma,
            dma,
            dma((3,)),
            dma((3,)),
            dma((2,)),
            dma((2,)),
            dma,
            dma,
            dma,
            dma,
            pltpu.SemaphoreType.REGULAR,
        ],
        compiler_params=pltpu.CompilerParams(
            collective_id=0, has_side_effects=True, vmem_limit_bytes=32 * 1024 * 1024
        ),
    )(
        *[
            pltpu.with_memory_space_constraint(x, pltpu.HBM)
            for x in (
                coords,
                loads,
                occupancy,
                basis.reshape(LEAVES * 64, LEAF),
                transfer.reshape(6, 128, 64),
            )
        ]
    )


def solution(mesh):
    boxes = mesh.shape["box"] // MEMBERS
    return jax.shard_map(
        functools.partial(body, boxes, 4),
        mesh=mesh,
        in_specs=(P(None, "box"), P(None, "box"), P("box"), P("box", None, None), P()),
        out_specs=P(None, "box"),
        check_vma=False,
    )
```

```python
import functools

import jax
import jax.numpy as jnp
from jax import lax
from jax.experimental import pallas as pl
from jax.experimental.pallas import tpu as pltpu
from jax.sharding import PartitionSpec as P

LEAF = 256
COLS = 8
LEAVES = 8
MEMBERS = 8
OWN = LEAF * LEAVES

f32 = jnp.float32
bf16 = jnp.bfloat16
soften = 0.0001
near_scale = 0.0625
far_scale = 0.125
NN = (((1,), (0,)), ((), ()))
NT = (((1,), (1,)), ((), ()))
MESH = pl.DeviceIdType.MESH


def div(a, b):
    return lax.div(a, jnp.int32(b))


def rem(a, b):
    return lax.rem(a, jnp.int32(b))


def phi(tx, ty, tz, sx, sy, sz, scale):
    dx = tx - sx
    dy = ty - sy
    dz = tz - sz
    r2 = dx * dx + dy * dy + dz * dz
    return (r2 * (0.5 * scale)) * jnp.log(r2 + soften)


def split(x):
    high = x.astype(bf16)
    return high, (x - high.astype(f32)).astype(bf16)


def mm(a, b, dims):
    rows = a.shape[0]
    high = a.astype(bf16).astype(f32)
    stacked = jnp.concatenate([high, a - high], axis=0).astype(bf16)
    both = lax.dot_general(stacked, b[0][...], dims, preferred_element_type=f32)
    low = lax.dot_general(stacked[:rows], b[1][...], dims, preferred_element_type=f32)
    return both[:rows] + (both[rows:] + low)


def low_half(shape):
    return lax.broadcasted_iota(jnp.int32, shape, len(shape) - 1) < 64


def merge(rows):
    count = rows.shape[0] // 16
    low = low_half((8, 128))
    return [
        jnp.where(low, rows[16 * i : 16 * i + 8], rows[16 * i + 8 : 16 * i + 16])
        for i in range(count)
    ]


def raise_coef(pairs, level_map):
    rows = mm(jnp.concatenate(pairs, axis=0), level_map, NN)
    return merge(rows) if len(pairs) > 1 else [rows]


def pick(x, entries):
    rows = x.shape[0]
    a = x.astype(bf16).astype(f32)
    b = (x - a).astype(bf16).astype(f32)
    c = (x - a) - b
    stacked = jnp.concatenate([a, b, c], axis=0).astype(bf16)
    picked = lax.dot_general(stacked, entries, NN, preferred_element_type=f32)
    return picked[:rows] + picked[rows : 2 * rows] + picked[2 * rows :]


def raise_skel(pairs, every_second):
    rows_up = pick(jnp.concatenate(pairs, axis=0), every_second)
    return merge(rows_up) if len(pairs) > 1 else [rows_up]


def cousins(chain, slot):
    low = low_half((8, 128))
    column = chain[slot, 1].T
    tx, ty, tz = column[:, 0:1], column[:, 1:2], column[:, 2:3]
    before, after = chain[slot - 1, 0], chain[slot + 1, 0]
    tiles = []
    for skel in (chain[slot - 1, 1], chain[slot + 1, 1]):
        tiles.append(phi(tx, ty, tz, skel[0:1], skel[1:2], skel[2:3], far_scale))
    tile = jnp.concatenate(tiles, axis=1)
    even = jnp.concatenate([jnp.where(low, before, 0.0), after], axis=1)
    odd = jnp.concatenate([before, jnp.where(low, 0.0, after)], axis=1)
    rows = mm(jnp.concatenate([even, odd], axis=0), split(tile), NT)
    return jnp.where(low, rows[:8], rows[8:])


def lower(pairs, level_map):
    height = pairs[0].shape[0]
    low = low_half((height, 128))
    stacked = []
    for pair in pairs:
        stacked += [jnp.where(low, pair, 0.0), jnp.where(low, 0.0, pair)]
    rows = mm(jnp.concatenate(stacked, axis=0), level_map, NT)
    return [rows[height * i : height * (i + 1)] for i in range(2 * len(pairs))]


def kernel(
    boxes,
    across,
    coords_hbm,
    loads_hbm,
    occ_hbm,
    basis_hbm,
    transfer_hbm,
    out_ref,
    coords,
    loads,
    occ,
    basis,
    transfer,
    map_high,
    map_low,
    path_map,
    field,
    column,
    leaf_high,
    leaf_low,
    near,
    tile_a,
    tile_b,
    tile_c,
    chain,
    g_chain,
    local,
    edge_send,
    edge_recv,
    u_buf,
    g_buf,
    bound_send,
    bound_recv,
    quad_recv,
    rim_recv,
    far_send,
    far_buf,
    part_buf,
    load_sem,
    near_send_sem,
    near_recv_sem,
    edge_send_sem,
    edge_recv_sem,
    u_send_sem,
    u_recv_sem,
    g_send_sem,
    g_recv_sem,
    bound_send_sem,
    bound_recv_sem,
    rim_send_sem,
    rim_recv_sem,
    far_send_sem,
    far_recv_sem,
    part_send_sem,
    part_recv_sem,
    ready,
):
    loading = [
        pltpu.make_async_copy(src, dst, load_sem.at[at])
        for at, (src, dst) in enumerate(
            [
                (coords_hbm, coords),
                (transfer_hbm, transfer),
                (loads_hbm, loads),
                (occ_hbm, occ),
                (basis_hbm, basis),
            ]
        )
    ]
    for copy in loading:
        copy.start()

    device = lax.axis_index("box")
    total = boxes * MEMBERS
    strides = boxes // MEMBERS
    depth = boxes // (2 * across)
    box, member = div(device, MEMBERS), rem(device, MEMBERS)
    x, z, y_half = div(box, 2 * depth), rem(div(box, 2), depth), rem(box, 2)
    y, core = div(member, 2), rem(member, 2)
    low = low_half((8, 128))
    half = jnp.where(low, 0, 1)

    top = jnp.where(y == 3, 1, 0)
    outer = jnp.where(y == 0, 1, top)
    side_to = jnp.where(outer == 1, top, 2 - y)
    side_from = jnp.where(outer == 1, 1 - top, 2 - y)
    far_half = jnp.where(outer == 1, 1 - y_half, y_half)
    z_core = rem(div(z, 2), 2)
    far_member = 2 * jnp.where(outer == 1, 3 - y, y) + z_core
    z_high, z_low = div(z, 4), rem(z, 2)
    far_x = [rem(x + dx, across) for dx in range(across)]
    far_steps = [(dx, turn) for dx in range(across) for turn in range(2)]

    def far_depths(side):
        first = 4 * rem(side + z_high, 2) + 2 * core
        return [first, first + 1]

    to_z, from_z = far_depths(side_to), far_depths(side_from)

    def far_box(depths, dx, turn):
        return (far_x[dx % across] * depth + depths[turn]) * 2 + far_half

    far_to = [far_box(to_z, dx, turn) * MEMBERS + far_member for dx, turn in far_steps]
    far_from = [far_box(from_z, -dx, turn) for dx, turn in far_steps]
    alone = jnp.logical_and(jnp.logical_and(outer == 0, side_to == 0), core == z_core)

    barrier = pltpu.get_barrier_semaphore()

    def greet(target):
        pl.semaphore_signal(barrier, inc=1, device_id=(target,), device_id_type=MESH)

    def order(at):
        return jnp.where(at == 0, 0, jnp.where(at >= 6, 2, 1))

    mine = order(z)
    to_later = [jnp.where(order(at) > mine, 1, 0) for at in to_z]
    from_earlier = [jnp.where(order(at) < mine, 1, 0) for at in from_z]
    far_order = [(2 * dx + turn) for turn in range(2) for dx in (2, 1, 3, 0)]

    def far_each(turn, act):
        for k in far_order[4 * turn : 4 * turn + 4]:
            if k == turn:
                pl.when(jnp.logical_not(jnp.logical_and(alone, z_low == turn)))(
                    functools.partial(act, k)
                )
            else:
                act(k)

    for turn in range(2):

        @pl.when(from_earlier[turn] == 0)
        def _(turn=turn):
            far_each(turn, lambda k: greet(far_from[k] * MEMBERS + far_member))

        @pl.when(to_later[turn] == 1)
        def _(turn=turn):
            far_each(turn, lambda k: greet(far_to[k]))

    left_device = rem(device + total - 1, total)
    right_device = rem(device + 1, total)
    mirror = 2 * (3 - y) + core
    left_box = rem(box + boxes - 1, boxes) * MEMBERS + mirror
    right_box = rem(box + 1, boxes) * MEMBERS + mirror
    mates = [box * MEMBERS + rem(member + r, MEMBERS) for r in (6, 2, 7, 3, 5, 4, 1)]
    at_rim = outer == 1
    rim_box = rem(box + boxes + 2 * top - 1, boxes)
    rim_devices = [rim_box * MEMBERS + 6 - 6 * top + t for t in range(2)]
    quad = div(member, 4)
    quad_device = rem(box + boxes + 2 * quad - 1, boxes) * MEMBERS + mirror
    early = jnp.where(z == 0, 1, 0)
    ahead = 2
    before = [device > 0, box > 0]
    after = [device < total - 1, box < boxes - 1]
    inside = jnp.where(quad == 0, box, boxes - 1 - box) > 0
    open_rim = jnp.logical_and(at_rim, inside)

    for target in mates:
        greet(target)
    for has, targets in ((before, (left_device, left_box)), (after, (right_device, right_box))):
        for at in range(2):
            pl.when(has[at])(functools.partial(greet, targets[at]))

    @pl.when(open_rim)
    def _():
        for target in rim_devices:
            greet(target)

    lanes = lax.broadcasted_iota(jnp.int32, (1, 128), 1)
    index = lax.broadcasted_iota(jnp.int32, (512, 128), 0)
    placed = (index == (lanes - 64 - 8 * member) * 64).astype(f32).astype(bf16)
    picks = (lax.broadcasted_iota(jnp.int32, (1, 128), 1) & 63) * 2
    every_second = (
        (lax.broadcasted_iota(jnp.int32, (128, 128), 0) == picks).astype(f32).astype(bf16)
    )
    for copy in loading:
        copy.wait()
    points = jnp.concatenate([coords[...], jnp.zeros((5, OWN), f32)], axis=0)
    s0 = [
        jnp.concatenate(
            [points[:, 512 * p : 512 * p + 64], points[:, 512 * p + 256 : 512 * p + 320]], axis=1
        )
        for p in range(4)
    ]
    s6 = pick(jnp.concatenate(s0, axis=1), placed)

    maps = [(map_high.at[level], map_low.at[level]) for level in range(6)]

    def set_map(level):
        once = transfer[level]
        map_high[level], map_low[level] = split(jnp.concatenate([once, once], axis=1))

    for level in range(2):
        set_map(level)
    slots = lax.broadcasted_iota(jnp.int32, (COLS, LEAF), 1)
    live = []
    for leaf in range(LEAVES):
        part = loads[:, leaf * LEAF : (leaf + 1) * LEAF].astype(f32)
        live.append(jnp.where(slots < occ[leaf], part, 0.0))
    c0 = []
    for p in range(4):
        two = jnp.concatenate([live[2 * p], live[2 * p + 1]], axis=0).astype(bf16)
        rows = lax.dot_general(
            two, basis[128 * p : 128 * p + 128, :], NT, preferred_element_type=f32
        )
        c0.append(jnp.where(low, rows[:8], rows[8:]))
    c1 = raise_coef(c0, maps[0])
    c2 = raise_coef(c1, maps[1])
    def factor(level, at):
        return transfer[level, pl.ds(pl.multiple_of(64 * at, 64), 64), :]

    map_34 = mm(transfer[2], split(factor(3, core)), NN)
    wide = jnp.concatenate([factor(5, quad), jnp.zeros((64, 64), f32)], axis=1)
    map_56 = mm(factor(4, rem(y, 2)), split(wide), NN)
    map_6 = mm(map_34, split(map_56), NN)
    u_buf[member] = mm(c2[0], split(map_6), NN) + s6
    path_map[...] = map_6

    def set_field():
        field[0, :, LEAF : LEAF + OWN] = points
        for leaf in range(LEAVES):
            field[1, :, (leaf + 1) * LEAF : (leaf + 2) * LEAF] = live[leaf]

    def set_column():
        for at in range(0, OWN, 128):
            column[at : at + 128, :] = points[:, at : at + 128].T
        near[...] = jnp.zeros_like(near)

    def fill_tile(tile, row, col, width):
        sx = field[0, 0:1, pl.ds(col, width)]
        sy = field[0, 1:2, pl.ds(col, width)]
        sz = field[0, 2:3, pl.ds(col, width)]
        for at in range(0, LEAF, 16):
            rows = column[pl.ds(row + at, 16), :]
            tile[at : at + 16, 0:width] = phi(
                rows[:, 0:1], rows[:, 1:2], rows[:, 2:3], sx, sy, sz, near_scale
            ).astype(bf16)

    def near_leaf(tile, row):
        col = row + LEAF
        fill_tile(tile, row, col, 2 * LEAF)
        loads_two = field[1, :, pl.ds(col, 2 * LEAF)].astype(bf16)
        this = lax.dot_general(loads_two, tile[...], NT, preferred_element_type=f32)
        after = lax.dot_general(
            loads_two[:, :LEAF], tile[:, LEAF:], NN, preferred_element_type=f32
        )
        return this, after

    def near_two(row):
        first, second_part = near_leaf(tile_a, row)
        second, third = near_leaf(tile_b, row + LEAF)
        near[:, pl.ds(row, LEAF)] += first
        near[:, pl.ds(row + LEAF, LEAF)] += second_part + second
        near[:, pl.ds(row + 2 * LEAF, LEAF)] += third

    def near_step(pair, carry):
        near_two(pl.multiple_of(pair * (2 * LEAF), 2 * LEAF))
        return carry

    def side(block, at):
        lanes = jnp.where(low_half((1, 128)), 0, 1)
        return jnp.where(lanes == at, block, 0.0)

    def set_chain(levels, into):
        for at, (pairs, skels) in enumerate(levels):
            first = (1, 7, 11)[at]
            for p in range(len(pairs)):
                into[first + p, 0] = pairs[p]
                into[first + p, 1] = skels[p]

    def set_inner():
        row = (LEAVES - 2) * LEAF
        this, after = near_leaf(tile_a, row)
        fill_tile(tile_c, row + LEAF, row + 2 * LEAF, LEAF)
        own = field[1, :, row + 2 * LEAF : row + 3 * LEAF].astype(bf16)
        after += lax.dot_general(own, tile_c[...], NT, preferred_element_type=f32)
        near[:, row : row + LEAF] += this
        near[:, row + LEAF : row + 2 * LEAF] += after
        for slot in (2, 3):
            local[slot - 1] = cousins(chain, slot)

    def set_edges():
        s1 = raise_skel(s0, every_second)
        s2 = raise_skel(s1, every_second)

        set_chain([(c0, s0), (c1, s1), (c2, s2)], chain)
        for at, (pairs, skels) in enumerate([(c0, s0), (c1, s1), (c2, s2)]):
            edge_send[0, at, 0] = pairs[-1]
            edge_send[0, at, 1] = skels[-1]
            edge_send[1, at, 0] = pairs[0]
            edge_send[1, at, 1] = skels[0]
    def set_leaf_paths():
        x2 = jnp.concatenate([path_map[...].T[:64], transfer[2].T], axis=0)
        x0 = lower(lower([x2], maps[1]), maps[0])
        leaf_high[...], leaf_low[...] = split(jnp.concatenate(x0, axis=1))

    @pl.when(early == 1)
    def _():
        set_field()
        set_column()
        lax.fori_loop(0, ahead, near_step, 0)

    pl.semaphore_wait(
        barrier,
        MEMBERS - 1
        + sum(has.astype(jnp.int32) for has in before + after)
        + 2 * open_rim.astype(jnp.int32)
        + 4 * (2 - to_later[0] - to_later[1])
        - alone.astype(jnp.int32)
        + 4 * (from_earlier[0] + from_earlier[1]),
    )

    def tell(target):
        pl.semaphore_signal(ready, inc=1, device_id=(target,), device_id_type=MESH)

    for turn in range(2):

        @pl.when(from_earlier[turn] == 1)
        def _(turn=turn):
            far_each(turn, lambda k: tell(far_from[k] * MEMBERS + far_member))

    def remote(src, dst, send_sem, recv_sem, target):
        return pltpu.make_async_remote_copy(
            src_ref=src,
            dst_ref=dst,
            send_sem=send_sem,
            recv_sem=recv_sem,
            device_id=(target,),
            device_id_type=MESH,
        )

    def send(*ends):
        copy = remote(*ends)
        copy.start()
        return copy

    def wait_all(ref, semaphore):
        pltpu.make_async_copy(ref, ref, semaphore).wait()

    first = (6, 2, 7, 3, 0, 4, 1, 5)
    place = sum(jnp.where(member == at, rank, 0) for rank, at in enumerate(first))
    for rank in range(MEMBERS - 1):
        mate = box * MEMBERS + jnp.where(place <= rank, first[rank + 1], first[rank])
        send(u_buf.at[member], u_buf.at[member], u_send_sem, u_recv_sem, mate)

    set_map(2)
    every_eighth = (index == (lanes & 63) * 8).astype(f32).astype(bf16)
    s3 = pick(jnp.concatenate(s0, axis=1), every_eighth)
    c3 = raise_coef(c2, maps[2])[0]
    g_buf[member] = jnp.where(half == core, c3, s3)
    for mate in mates:
        send(g_buf.at[member], g_buf.at[member], g_send_sem, g_recv_sem, mate)

    rim_copies = [
        pltpu.make_async_remote_copy(
            src_ref=g_buf.at[member],
            dst_ref=rim_recv.at[core],
            send_sem=rim_send_sem.at[t],
            recv_sem=rim_recv_sem.at[core],
            device_id=(rim_devices[t],),
            device_id_type=MESH,
        )
        for t in range(2)
    ]

    @pl.when(open_rim)
    def _():
        for copy in rim_copies:
            copy.start()

    @pl.when(early == 0)
    def _():
        set_field()

    last = LEAF * LEAVES
    near_copies = [
        remote(
            field.at[:, :, last : last + LEAF],
            field.at[:, :, 0:LEAF],
            near_send_sem.at[0],
            near_recv_sem.at[0],
            right_device,
        ),
        remote(
            field.at[:, :, LEAF : 2 * LEAF],
            field.at[:, :, last + LEAF : last + 2 * LEAF],
            near_send_sem.at[1],
            near_recv_sem.at[1],
            left_device,
        ),
    ]

    def start(copies, at=0):
        for copy, has in zip(copies, (after[at], before[at])):
            pl.when(has)(copy.start)

    def receive(copies, at=0):
        for copy, has in zip(copies, (before[at], after[at])):
            pl.when(has)(copy.wait_recv)

    start(near_copies)

    edge_copies = [
        remote(
            edge_send.at[side],
            edge_recv.at[side],
            edge_send_sem.at[side],
            edge_recv_sem.at[side],
            (right_device, left_device)[side],
        )
        for side in range(2)
    ]

    set_edges()
    start(edge_copies)

    @pl.when(early == 1)
    def _():
        set_leaf_paths()

    wait_all(u_buf.at[pl.ds(0, MEMBERS - 1)], u_recv_sem)
    parts = [u_buf[at] for at in range(MEMBERS)]
    while len(parts) > 1:
        parts = [a + b for a, b in zip(parts[0::2], parts[1::2])]
    top_record = parts[0]
    swapped_record = pltpu.roll(top_record, 64, 1)
    far_send[...] = jnp.where(z_low == 0, top_record, swapped_record)

    @pl.when(alone)
    def _():
        far_buf[z_low] = far_send[...]

    def far_copy(k):
        slot = k - k % 2 + z_low
        return remote(far_send, far_buf.at[slot], far_send_sem, far_recv_sem, far_to[k])

    def far_wait(semaphore):
        @pl.when(alone)
        def _():
            wait_all(far_buf.at[pl.ds(1, strides - 1)], semaphore)

        @pl.when(jnp.logical_not(alone))
        def _():
            wait_all(far_buf, semaphore)

    for turn in range(2):

        @pl.when(to_later[turn] == 0)
        def _(turn=turn):
            far_each(turn, lambda k: far_copy(k).start())

    set_map(3)
    set_map(4)
    wait_all(g_buf.at[pl.ds(0, MEMBERS - 1)], g_recv_sem)
    c3s, s3s = [], []
    for p in range(4):
        even, odd = g_buf[2 * p], g_buf[2 * p + 1]
        c3s.append(jnp.where(low, even, odd))
        s3s.append(pltpu.roll(jnp.where(low, odd, even), 64, 1))
    c4s, s4s = raise_coef(c3s, maps[3]), raise_skel(s3s, every_second)
    c5s, s5s = raise_coef(c4s, maps[4]), raise_skel(s4s, every_second)
    set_chain([(c3s, s3s), (c4s, s4s), (c5s, s5s)], g_chain)
    for at in range(2):
        bound_send[at, 0] = c5s[0]
        bound_send[at, 1] = s5s[0] + pltpu.roll(s4s[1 - at], 3, 0)
    bound_copies = [
        remote(
            bound_send.at[side],
            bound_recv.at[side],
            bound_send_sem.at[side],
            bound_recv_sem.at[side],
            (right_box, left_box)[side],
        )
        for side in range(2)
    ]
    quad_copy = remote(
        g_chain.at[7 + quad, 0],
        quad_recv,
        bound_send_sem.at[2],
        bound_recv_sem.at[2],
        quad_device,
    )
    start(bound_copies, 1)
    pl.when(inside)(quad_copy.start)

    def set_ends(ends, into):
        for level in range(3):
            into[(0, 6, 10)[level]] = ends[0, level]
            into[(5, 9, 12)[level]] = ends[1, level]

    def near_end(tile, row, col):
        fill_tile(tile, row, col, LEAF)
        near[:, row : row + LEAF] += lax.dot_general(
            field[1, :, col : col + LEAF].astype(bf16),
            tile[:, 0:LEAF],
            NT,
            preferred_element_type=f32,
        )

    def finish_ends():
        receive(near_copies)

        @pl.when(device == 0)
        def _():
            field[:, :, 0:LEAF] = jnp.zeros((2, 8, LEAF), f32)
            edge_recv[0] = jnp.zeros((3, 2, 8, 128), f32)

        @pl.when(device == total - 1)
        def _():
            field[:, :, last + LEAF : last + 2 * LEAF] = jnp.zeros((2, 8, LEAF), f32)
            edge_recv[1] = jnp.zeros((3, 2, 8, 128), f32)

        near_end(tile_c, 0, 0)
        near_end(tile_a, last - LEAF, last + LEAF)

        receive(edge_copies)
        set_ends(edge_recv, chain)
        for at, slot in [(0, 1), (3, 4), (4, 7), (5, 8), (6, 11)]:
            local[at] = cousins(chain, slot)

    @pl.when(early == 1)
    def _():
        lax.fori_loop(ahead, 3, near_step, 0)
        set_inner()
        finish_ends()

    later = to_later[0] + to_later[1]

    @pl.when(later > 0)
    def _():
        pl.semaphore_wait(ready, 4 * later)

    for turn in range(2):

        @pl.when(to_later[turn] == 1)
        def _(turn=turn):
            far_each(turn, lambda k: far_copy(k).start())

    @pl.when(early == 0)
    def _():
        set_column()
        lax.fori_loop(0, 3, near_step, 0)
        set_inner()
        set_leaf_paths()
        finish_ends()

    top_column = swapped_record.T[:64]
    tx, ty, tz = top_column[:, 0:1], top_column[:, 1:2], top_column[:, 2:3]

    far_wait(far_recv_sem)

    top_coef, top_skel = [], []
    for k in range(0, strides, 2):
        halves = []
        for at in (k, k + 1):
            apart = far_from[at] - box
            counts = jnp.logical_or(apart >= 2, apart <= -2)
            halves.append((far_buf[at], counts))
        (one, one_counts), (two, two_counts) = halves
        coef = jnp.where(low, jnp.where(one_counts, one, 0.0), jnp.where(two_counts, two, 0.0))
        top_coef.append(pltpu.roll(coef, 64, 1))
        top_skel.append(jnp.where(low, two, one))
    top_tile = jnp.concatenate(
        [phi(tx, ty, tz, s[0:1], s[1:2], s[2:3], far_scale) for s in top_skel], axis=1
    )
    top = mm(jnp.concatenate(top_coef, axis=1), split(top_tile), NT)
    part_buf[member] = jnp.concatenate([top, jnp.zeros((8, 64), f32)], axis=1)
    for at in range(MEMBERS - 1):
        mate = box * MEMBERS + at + jnp.where(member <= at, 1, 0)
        send(part_buf.at[member], part_buf.at[member], part_send_sem, part_recv_sem, mate)

    wait_all(u_buf.at[pl.ds(0, MEMBERS - 1)], u_send_sem)
    wait_all(g_buf.at[pl.ds(0, MEMBERS - 1)], g_send_sem)
    far_wait(far_send_sem)
    for copies, at in ((near_copies, 0), (edge_copies, 0), (bound_copies, 1)):
        for copy, has in zip(copies, (after[at], before[at])):
            pl.when(has)(copy.wait_send)
    pl.when(inside)(quad_copy.wait_send)

    receive(bound_copies, 1)
    pl.when(inside)(quad_copy.wait_recv)
    start_skel = jnp.where(before[1], bound_recv[0, 1], 0.0)
    end_skel = jnp.where(after[1], bound_recv[1, 1], 0.0)
    g_chain[10, 0] = jnp.where(before[1], bound_recv[0, 0], 0.0)
    g_chain[10, 1] = start_skel
    g_chain[12, 0] = jnp.where(after[1], bound_recv[1, 0], 0.0)
    g_chain[12, 1] = end_skel
    quad_coef = jnp.where(inside, quad_recv[...], 0.0)
    g_chain[6, 0] = quad_coef
    g_chain[6, 1] = pltpu.roll(start_skel, 5, 0)
    g_chain[9, 0] = quad_coef
    g_chain[9, 1] = pltpu.roll(end_skel, 5, 0)

    @pl.when(jnp.logical_not(inside))
    def _():
        for slot in (0, 5):
            g_chain[slot] = jnp.zeros((2, 8, 128), f32)

    @pl.when(open_rim)
    def _():
        for copy in rim_copies:
            copy.wait_send()
        for t in range(2):
            pltpu.make_async_remote_copy(
                src_ref=g_buf.at[member],
                dst_ref=rim_recv.at[t],
                send_sem=rim_send_sem.at[t],
                recv_sem=rim_recv_sem.at[t],
                device_id=(rim_devices[t],),
                device_id_type=MESH,
            ).wait_recv()
        even, odd = rim_recv[0], rim_recv[1]
        rim_coef = jnp.where(low, even, odd)
        rim_skel = pltpu.roll(jnp.where(low, odd, even), 64, 1)
        for slot in (0, 5):
            g_chain[slot, 0] = rim_coef
            g_chain[slot, 1] = rim_skel

    local3 = cousins(g_chain, 1 + y)
    local4 = cousins(g_chain, 7 + quad)
    local5 = cousins(g_chain, 11)
    y2 = local[6]
    y1 = [x + local[4 + at] for at, x in enumerate(lower([y2], maps[1]))]
    y0 = [x + local[at] for at, x in enumerate(lower(y1, maps[0]))]
    y4 = local4 + mm(side(local5, quad), maps[4], NT)
    y3 = local3 + mm(side(y4, rem(y, 2)), maps[3], NT)
    y3 = jnp.where(core == 1, y3, pltpu.roll(y3, 64, 1))

    wait_all(part_buf.at[pl.ds(0, MEMBERS - 1)], part_recv_sem)
    parts = [part_buf[at] for at in range(MEMBERS)]
    while len(parts) > 1:
        parts = [a + b for a, b in zip(parts[0::2], parts[1::2])]
    d6 = parts[0]
    d63 = jnp.where(low, d6, y3)
    d0 = jnp.concatenate(y0, axis=1) + mm(d63, (leaf_high, leaf_low), NN)
    for p in range(4):
        pair = d0[:, 128 * p : 128 * p + 128]
        two = jnp.concatenate([jnp.where(low, pair, 0.0), jnp.where(low, 0.0, pair)], axis=0)
        rows = lax.dot_general(
            two.astype(bf16),
            basis[128 * p : 128 * p + 128, :],
            NN,
            preferred_element_type=f32,
        )
        for t in range(2):
            leaf = 2 * p + t
            at = leaf * LEAF
            out_ref[:, at : at + LEAF] = jnp.where(
                slots < occ[leaf], near[:, at : at + LEAF] + rows[8 * t : 8 * t + 8], 0.0
            )

    wait_all(part_buf.at[pl.ds(0, MEMBERS - 1)], part_send_sem)


def body(boxes, across, coords, loads, occupancy, basis, transfer):
    strides = boxes // MEMBERS
    hbm = pl.BlockSpec(memory_space=pl.ANY)
    dma = pltpu.SemaphoreType.DMA
    return pl.pallas_call(
        functools.partial(kernel, boxes, across),
        out_shape=jax.ShapeDtypeStruct((COLS, OWN), f32),
        in_specs=[hbm] * 5,
        out_specs=pl.BlockSpec(memory_space=pltpu.VMEM),
        scratch_shapes=[
            pltpu.VMEM((3, OWN), f32),
            pltpu.VMEM((COLS, OWN), bf16),
            pltpu.SMEM((LEAVES,), jnp.int32),
            pltpu.VMEM((LEAVES * 64, LEAF), bf16),
            pltpu.VMEM((6, 128, 64), f32),
            pltpu.VMEM((6, 128, 128), bf16),
            pltpu.VMEM((6, 128, 128), bf16),
            pltpu.VMEM((128, 128), f32),
            pltpu.VMEM((2, 8, OWN + 2 * LEAF), f32),
            pltpu.VMEM((OWN, 8), f32),
            pltpu.VMEM((128, 512), bf16),
            pltpu.VMEM((128, 512), bf16),
            pltpu.VMEM((COLS, OWN + LEAF), f32),
            pltpu.VMEM((LEAF, 2 * LEAF), bf16),
            pltpu.VMEM((LEAF, 2 * LEAF), bf16),
            pltpu.VMEM((LEAF, LEAF), bf16),
            pltpu.VMEM((13, 2, 8, 128), f32),
            pltpu.VMEM((13, 2, 8, 128), f32),
            pltpu.VMEM((7, 8, 128), f32),
            pltpu.VMEM((2, 3, 2, 8, 128), f32),
            pltpu.VMEM((2, 3, 2, 8, 128), f32),
            pltpu.VMEM((MEMBERS, 8, 128), f32),
            pltpu.VMEM((MEMBERS, 8, 128), f32),
            pltpu.VMEM((2, 2, 8, 128), f32),
            pltpu.VMEM((2, 2, 8, 128), f32),
            pltpu.VMEM((8, 128), f32),
            pltpu.VMEM((2, 8, 128), f32),
            pltpu.VMEM((8, 128), f32),
            pltpu.VMEM((strides, 8, 128), f32),
            pltpu.VMEM((MEMBERS, 8, 128), f32),
            dma((5,)),
            dma((2,)),
            dma((2,)),
            dma((2,)),
            dma((2,)),
            dma,
            dma,
            dma,
            dma,
            dma((3,)),
            dma((3,)),
            dma((2,)),
            dma((2,)),
            dma,
            dma,
            dma,
            dma,
            pltpu.SemaphoreType.REGULAR,
        ],
        compiler_params=pltpu.CompilerParams(
            collective_id=0, has_side_effects=True, vmem_limit_bytes=32 * 1024 * 1024
        ),
    )(
        *[
            pltpu.with_memory_space_constraint(x, pltpu.HBM)
            for x in (
                coords,
                loads,
                occupancy,
                basis.reshape(LEAVES * 64, LEAF),
                transfer.reshape(6, 128, 64),
            )
        ]
    )


def solution(mesh):
    boxes = mesh.shape["box"] // MEMBERS
    return jax.shard_map(
        functools.partial(body, boxes, 4),
        mesh=mesh,
        in_specs=(P(None, "box"), P(None, "box"), P("box"), P("box", None, None), P()),
        out_specs=P(None, "box"),
        check_vma=False,
    )
```

```python
import functools

import jax
import jax.numpy as jnp
from jax import lax
from jax.experimental import pallas as pl
from jax.experimental.pallas import tpu as pltpu
from jax.sharding import PartitionSpec as P

LEAF = 256
COLS = 8
LEAVES = 8
MEMBERS = 8
OWN = LEAF * LEAVES

f32 = jnp.float32
bf16 = jnp.bfloat16
soften = 0.0001
near_scale = 0.0625
far_scale = 0.125
NN = (((1,), (0,)), ((), ()))
NT = (((1,), (1,)), ((), ()))
MESH = pl.DeviceIdType.MESH


def div(a, b):
    return lax.div(a, jnp.int32(b))


def rem(a, b):
    return lax.rem(a, jnp.int32(b))


def phi(tx, ty, tz, sx, sy, sz, scale):
    dx = tx - sx
    dy = ty - sy
    dz = tz - sz
    r2 = dx * dx + dy * dy + dz * dz
    return (r2 * (0.5 * scale)) * jnp.log(r2 + soften)


def split(x):
    high = x.astype(bf16)
    return high, (x - high.astype(f32)).astype(bf16)


def mm(a, b, dims):
    rows = a.shape[0]
    high = a.astype(bf16).astype(f32)
    stacked = jnp.concatenate([high, a - high], axis=0).astype(bf16)
    both = lax.dot_general(stacked, b[0][...], dims, preferred_element_type=f32)
    low = lax.dot_general(stacked[:rows], b[1][...], dims, preferred_element_type=f32)
    return both[:rows] + (both[rows:] + low)


def low_half(shape):
    return lax.broadcasted_iota(jnp.int32, shape, len(shape) - 1) < 64


def merge(rows):
    count = rows.shape[0] // 16
    low = low_half((8, 128))
    return [
        jnp.where(low, rows[16 * i : 16 * i + 8], rows[16 * i + 8 : 16 * i + 16])
        for i in range(count)
    ]


def raise_coef(pairs, level_map):
    rows = mm(jnp.concatenate(pairs, axis=0), level_map, NN)
    return merge(rows) if len(pairs) > 1 else [rows]


def pick(x, entries):
    rows = x.shape[0]
    a = x.astype(bf16).astype(f32)
    b = (x - a).astype(bf16).astype(f32)
    c = (x - a) - b
    stacked = jnp.concatenate([a, b, c], axis=0).astype(bf16)
    picked = lax.dot_general(stacked, entries, NN, preferred_element_type=f32)
    return picked[:rows] + picked[rows : 2 * rows] + picked[2 * rows :]


def raise_skel(pairs, every_second):
    rows_up = pick(jnp.concatenate(pairs, axis=0), every_second)
    return merge(rows_up) if len(pairs) > 1 else [rows_up]


def cousins(chain, slot):
    low = low_half((8, 128))
    column = chain[slot, 1].T
    tx, ty, tz = column[:, 0:1], column[:, 1:2], column[:, 2:3]
    before, after = chain[slot - 1, 0], chain[slot + 1, 0]
    tiles = []
    for skel in (chain[slot - 1, 1], chain[slot + 1, 1]):
        tiles.append(phi(tx, ty, tz, skel[0:1], skel[1:2], skel[2:3], far_scale))
    tile = jnp.concatenate(tiles, axis=1)
    even = jnp.concatenate([jnp.where(low, before, 0.0), after], axis=1)
    odd = jnp.concatenate([before, jnp.where(low, 0.0, after)], axis=1)
    rows = mm(jnp.concatenate([even, odd], axis=0), split(tile), NT)
    return jnp.where(low, rows[:8], rows[8:])


def lower(pairs, level_map):
    height = pairs[0].shape[0]
    low = low_half((height, 128))
    stacked = []
    for pair in pairs:
        stacked += [jnp.where(low, pair, 0.0), jnp.where(low, 0.0, pair)]
    rows = mm(jnp.concatenate(stacked, axis=0), level_map, NT)
    return [rows[height * i : height * (i + 1)] for i in range(2 * len(pairs))]


def kernel(
    boxes,
    across,
    coords_hbm,
    loads_hbm,
    occ_hbm,
    basis_hbm,
    transfer_hbm,
    out_ref,
    coords,
    loads,
    occ,
    basis,
    transfer,
    map_high,
    map_low,
    path_map,
    field,
    column,
    leaf_high,
    leaf_low,
    near,
    tile_a,
    tile_b,
    tile_c,
    chain,
    g_chain,
    local,
    edge_send,
    edge_recv,
    u_buf,
    g_buf,
    bound_send,
    bound_recv,
    quad_recv,
    rim_recv,
    far_send,
    far_buf,
    part_buf,
    load_sem,
    near_send_sem,
    near_recv_sem,
    edge_send_sem,
    edge_recv_sem,
    u_send_sem,
    u_recv_sem,
    g_send_sem,
    g_recv_sem,
    bound_send_sem,
    bound_recv_sem,
    rim_send_sem,
    rim_recv_sem,
    far_send_sem,
    far_recv_sem,
    part_send_sem,
    part_recv_sem,
    ready,
):
    loading = [
        pltpu.make_async_copy(src, dst, load_sem.at[at])
        for at, (src, dst) in enumerate(
            [
                (loads_hbm, loads),
                (occ_hbm, occ),
                (basis_hbm, basis),
                (coords_hbm, coords),
                (transfer_hbm, transfer),
            ]
        )
    ]
    for copy in loading:
        copy.start()

    device = lax.axis_index("box")
    total = boxes * MEMBERS
    strides = boxes // MEMBERS
    depth = boxes // (2 * across)
    box, member = div(device, MEMBERS), rem(device, MEMBERS)
    x, z, y_half = div(box, 2 * depth), rem(div(box, 2), depth), rem(box, 2)
    y, core = div(member, 2), rem(member, 2)
    low = low_half((8, 128))
    half = jnp.where(low, 0, 1)

    top = jnp.where(y == 3, 1, 0)
    outer = jnp.where(y == 0, 1, top)
    side_to = jnp.where(outer == 1, top, 2 - y)
    side_from = jnp.where(outer == 1, 1 - top, 2 - y)
    far_half = jnp.where(outer == 1, 1 - y_half, y_half)
    z_core = rem(div(z, 2), 2)
    far_member = 2 * jnp.where(outer == 1, 3 - y, y) + z_core
    z_high, z_low = div(z, 4), rem(z, 2)
    far_x = [rem(x + dx, across) for dx in range(across)]
    far_steps = [(dx, turn) for dx in range(across) for turn in range(2)]

    def far_depths(side):
        first = 4 * rem(side + z_high, 2) + 2 * core
        return [first, first + 1]

    to_z, from_z = far_depths(side_to), far_depths(side_from)

    def far_box(depths, dx, turn):
        return (far_x[dx % across] * depth + depths[turn]) * 2 + far_half

    far_to = [far_box(to_z, dx, turn) * MEMBERS + far_member for dx, turn in far_steps]
    far_from = [far_box(from_z, -dx, turn) for dx, turn in far_steps]
    alone = jnp.logical_and(jnp.logical_and(outer == 0, side_to == 0), core == z_core)

    barrier = pltpu.get_barrier_semaphore()

    def greet(target):
        pl.semaphore_signal(barrier, inc=1, device_id=(target,), device_id_type=MESH)

    def order(at):
        return jnp.where(at == 0, 0, jnp.where(at >= 6, 2, 1))

    mine = order(z)
    to_later = [jnp.where(order(at) > mine, 1, 0) for at in to_z]
    from_earlier = [jnp.where(order(at) < mine, 1, 0) for at in from_z]
    far_order = [(2 * dx + turn) for turn in range(2) for dx in (2, 1, 3, 0)]

    def far_each(turn, act):
        for k in far_order[4 * turn : 4 * turn + 4]:
            if k == turn:
                pl.when(jnp.logical_not(jnp.logical_and(alone, z_low == turn)))(
                    functools.partial(act, k)
                )
            else:
                act(k)

    for turn in range(2):

        @pl.when(from_earlier[turn] == 0)
        def _(turn=turn):
            far_each(turn, lambda k: greet(far_from[k] * MEMBERS + far_member))

        @pl.when(to_later[turn] == 1)
        def _(turn=turn):
            far_each(turn, lambda k: greet(far_to[k]))

    left_device = rem(device + total - 1, total)
    right_device = rem(device + 1, total)
    mirror = 2 * (3 - y) + core
    left_box = rem(box + boxes - 1, boxes) * MEMBERS + mirror
    right_box = rem(box + 1, boxes) * MEMBERS + mirror
    mates = [box * MEMBERS + rem(member + r, MEMBERS) for r in (6, 2, 7, 3, 5, 4, 1)]
    at_rim = outer == 1
    rim_box = rem(box + boxes + 2 * top - 1, boxes)
    rim_devices = [rim_box * MEMBERS + 6 - 6 * top + t for t in range(2)]
    quad = div(member, 4)
    quad_device = rem(box + boxes + 2 * quad - 1, boxes) * MEMBERS + mirror
    early = jnp.where(z == 0, 1, 0)
    ahead = 2
    before = [device > 0, box > 0]
    after = [device < total - 1, box < boxes - 1]
    inside = jnp.where(quad == 0, box, boxes - 1 - box) > 0
    open_rim = jnp.logical_and(at_rim, inside)

    for target in mates:
        greet(target)
    for has, targets in ((before, (left_device, left_box)), (after, (right_device, right_box))):
        for at in range(2):
            pl.when(has[at])(functools.partial(greet, targets[at]))

    @pl.when(open_rim)
    def _():
        for target in rim_devices:
            greet(target)

    lanes = lax.broadcasted_iota(jnp.int32, (1, 128), 1)
    index = lax.broadcasted_iota(jnp.int32, (512, 128), 0)
    placed = (index == (lanes - 64 - 8 * member) * 64).astype(f32).astype(bf16)
    picks = (lax.broadcasted_iota(jnp.int32, (1, 128), 1) & 63) * 2
    every_second = (
        (lax.broadcasted_iota(jnp.int32, (128, 128), 0) == picks).astype(f32).astype(bf16)
    )
    maps = [(map_high.at[level], map_low.at[level]) for level in range(6)]

    def set_map(level):
        once = transfer[level]
        map_high[level], map_low[level] = split(jnp.concatenate([once, once], axis=1))

    for copy in loading[:3]:
        copy.wait()
    slots = lax.broadcasted_iota(jnp.int32, (COLS, LEAF), 1)
    live = []
    for leaf in range(LEAVES):
        part = loads[:, leaf * LEAF : (leaf + 1) * LEAF].astype(f32)
        live.append(jnp.where(slots < occ[leaf], part, 0.0))
    c0 = []
    for p in range(4):
        two = jnp.concatenate([live[2 * p], live[2 * p + 1]], axis=0).astype(bf16)
        rows = lax.dot_general(
            two, basis[128 * p : 128 * p + 128, :], NT, preferred_element_type=f32
        )
        c0.append(jnp.where(low, rows[:8], rows[8:]))
    for copy in loading[3:]:
        copy.wait()
    points = jnp.concatenate([coords[...], jnp.zeros((5, OWN), f32)], axis=0)
    s0 = [
        jnp.concatenate(
            [points[:, 512 * p : 512 * p + 64], points[:, 512 * p + 256 : 512 * p + 320]], axis=1
        )
        for p in range(4)
    ]
    s6 = pick(jnp.concatenate(s0, axis=1), placed)

    for level in range(2):
        set_map(level)
    c1 = raise_coef(c0, maps[0])
    c2 = raise_coef(c1, maps[1])
    def factor(level, at):
        return transfer[level, pl.ds(pl.multiple_of(64 * at, 64), 64), :]

    map_34 = mm(transfer[2], split(factor(3, core)), NN)
    wide = jnp.concatenate([factor(5, quad), jnp.zeros((64, 64), f32)], axis=1)
    map_56 = mm(factor(4, rem(y, 2)), split(wide), NN)
    map_6 = mm(map_34, split(map_56), NN)
    u_buf[member] = mm(c2[0], split(map_6), NN) + s6
    path_map[...] = map_6

    def set_field():
        field[0, :, LEAF : LEAF + OWN] = points
        for leaf in range(LEAVES):
            field[1, :, (leaf + 1) * LEAF : (leaf + 2) * LEAF] = live[leaf]
        for at in range(0, OWN, 128):
            column[at : at + 128, :] = points[:, at : at + 128].T
        near[...] = jnp.zeros_like(near)

    def fill_tile(tile, row, col, width):
        sx = field[0, 0:1, pl.ds(col, width)]
        sy = field[0, 1:2, pl.ds(col, width)]
        sz = field[0, 2:3, pl.ds(col, width)]
        for at in range(0, LEAF, 16):
            rows = column[pl.ds(row + at, 16), :]
            tile[at : at + 16, 0:width] = phi(
                rows[:, 0:1], rows[:, 1:2], rows[:, 2:3], sx, sy, sz, near_scale
            ).astype(bf16)

    def near_leaf(tile, row):
        col = row + LEAF
        fill_tile(tile, row, col, 2 * LEAF)
        loads_two = field[1, :, pl.ds(col, 2 * LEAF)].astype(bf16)
        this = lax.dot_general(loads_two, tile[...], NT, preferred_element_type=f32)
        after = lax.dot_general(
            loads_two[:, :LEAF], tile[:, LEAF:], NN, preferred_element_type=f32
        )
        return this, after

    def near_two(row):
        first, second_part = near_leaf(tile_a, row)
        second, third = near_leaf(tile_b, row + LEAF)
        near[:, pl.ds(row, LEAF)] += first
        near[:, pl.ds(row + LEAF, LEAF)] += second_part + second
        near[:, pl.ds(row + 2 * LEAF, LEAF)] += third

    def near_step(pair, carry):
        near_two(pl.multiple_of(pair * (2 * LEAF), 2 * LEAF))
        return carry

    def side(block, at):
        lanes = jnp.where(low_half((1, 128)), 0, 1)
        return jnp.where(lanes == at, block, 0.0)

    def set_chain(levels, into):
        for at, (pairs, skels) in enumerate(levels):
            first = (1, 7, 11)[at]
            for p in range(len(pairs)):
                into[first + p, 0] = pairs[p]
                into[first + p, 1] = skels[p]

    def set_inner():
        row = (LEAVES - 2) * LEAF
        this, after = near_leaf(tile_a, row)
        fill_tile(tile_c, row + LEAF, row + 2 * LEAF, LEAF)
        own = field[1, :, row + 2 * LEAF : row + 3 * LEAF].astype(bf16)
        after += lax.dot_general(own, tile_c[...], NT, preferred_element_type=f32)
        near[:, row : row + LEAF] += this
        near[:, row + LEAF : row + 2 * LEAF] += after
        for slot in (2, 3):
            local[slot - 1] = cousins(chain, slot)

    def set_edges():
        s1 = raise_skel(s0, every_second)
        s2 = raise_skel(s1, every_second)

        set_chain([(c0, s0), (c1, s1), (c2, s2)], chain)
        for at, (pairs, skels) in enumerate([(c0, s0), (c1, s1), (c2, s2)]):
            edge_send[0, at, 0] = pairs[-1]
            edge_send[0, at, 1] = skels[-1]
            edge_send[1, at, 0] = pairs[0]
            edge_send[1, at, 1] = skels[0]
    def set_leaf_paths():
        x2 = jnp.concatenate([path_map[...].T[:64], transfer[2].T], axis=0)
        x0 = lower(lower([x2], maps[1]), maps[0])
        leaf_high[...], leaf_low[...] = split(jnp.concatenate(x0, axis=1))

    @pl.when(early == 1)
    def _():
        set_field()
        lax.fori_loop(0, ahead, near_step, 0)

    pl.semaphore_wait(
        barrier,
        MEMBERS - 1
        + sum(has.astype(jnp.int32) for has in before + after)
        + 2 * open_rim.astype(jnp.int32)
        + 4 * (2 - to_later[0] - to_later[1])
        - alone.astype(jnp.int32)
        + 4 * (from_earlier[0] + from_earlier[1]),
    )

    def tell(target):
        pl.semaphore_signal(ready, inc=1, device_id=(target,), device_id_type=MESH)

    for turn in range(2):

        @pl.when(from_earlier[turn] == 1)
        def _(turn=turn):
            far_each(turn, lambda k: tell(far_from[k] * MEMBERS + far_member))

    def remote(src, dst, send_sem, recv_sem, target):
        return pltpu.make_async_remote_copy(
            src_ref=src,
            dst_ref=dst,
            send_sem=send_sem,
            recv_sem=recv_sem,
            device_id=(target,),
            device_id_type=MESH,
        )

    def send(*ends):
        copy = remote(*ends)
        copy.start()
        return copy

    def wait_all(ref, semaphore):
        pltpu.make_async_copy(ref, ref, semaphore).wait()

    first = (6, 2, 7, 3, 0, 4, 1, 5)
    place = sum(jnp.where(member == at, rank, 0) for rank, at in enumerate(first))
    for rank in range(MEMBERS - 1):
        mate = box * MEMBERS + jnp.where(place <= rank, first[rank + 1], first[rank])
        send(u_buf.at[member], u_buf.at[member], u_send_sem, u_recv_sem, mate)

    set_map(2)
    every_eighth = (index == (lanes & 63) * 8).astype(f32).astype(bf16)
    s3 = pick(jnp.concatenate(s0, axis=1), every_eighth)
    c3 = raise_coef(c2, maps[2])[0]
    g_buf[member] = jnp.where(half == core, c3, s3)
    for mate in mates:
        send(g_buf.at[member], g_buf.at[member], g_send_sem, g_recv_sem, mate)

    rim_copies = [
        pltpu.make_async_remote_copy(
            src_ref=g_buf.at[member],
            dst_ref=rim_recv.at[core],
            send_sem=rim_send_sem.at[t],
            recv_sem=rim_recv_sem.at[core],
            device_id=(rim_devices[t],),
            device_id_type=MESH,
        )
        for t in range(2)
    ]

    @pl.when(open_rim)
    def _():
        for copy in rim_copies:
            copy.start()

    @pl.when(early == 0)
    def _():
        set_field()

    last = LEAF * LEAVES
    near_copies = [
        remote(
            field.at[:, :, last : last + LEAF],
            field.at[:, :, 0:LEAF],
            near_send_sem.at[0],
            near_recv_sem.at[0],
            right_device,
        ),
        remote(
            field.at[:, :, LEAF : 2 * LEAF],
            field.at[:, :, last + LEAF : last + 2 * LEAF],
            near_send_sem.at[1],
            near_recv_sem.at[1],
            left_device,
        ),
    ]

    def start(copies, at=0):
        for copy, has in zip(copies, (after[at], before[at])):
            pl.when(has)(copy.start)

    def receive(copies, at=0):
        for copy, has in zip(copies, (before[at], after[at])):
            pl.when(has)(copy.wait_recv)

    start(near_copies)

    edge_copies = [
        remote(
            edge_send.at[side],
            edge_recv.at[side],
            edge_send_sem.at[side],
            edge_recv_sem.at[side],
            (right_device, left_device)[side],
        )
        for side in range(2)
    ]

    set_edges()
    start(edge_copies)

    set_map(3)
    set_map(4)

    @pl.when(early == 1)
    def _():
        set_leaf_paths()

    wait_all(u_buf.at[pl.ds(0, MEMBERS - 1)], u_recv_sem)
    parts = [u_buf[at] for at in range(MEMBERS)]
    while len(parts) > 1:
        parts = [a + b for a, b in zip(parts[0::2], parts[1::2])]
    top_record = parts[0]
    swapped_record = pltpu.roll(top_record, 64, 1)
    far_send[...] = jnp.where(z_low == 0, top_record, swapped_record)

    @pl.when(alone)
    def _():
        far_buf[z_low] = far_send[...]

    def far_copy(k):
        slot = k - k % 2 + z_low
        return remote(far_send, far_buf.at[slot], far_send_sem, far_recv_sem, far_to[k])

    def far_wait(semaphore):
        @pl.when(alone)
        def _():
            wait_all(far_buf.at[pl.ds(1, strides - 1)], semaphore)

        @pl.when(jnp.logical_not(alone))
        def _():
            wait_all(far_buf, semaphore)

    for turn in range(2):

        @pl.when(to_later[turn] == 0)
        def _(turn=turn):
            far_each(turn, lambda k: far_copy(k).start())

    wait_all(g_buf.at[pl.ds(0, MEMBERS - 1)], g_recv_sem)
    c3s, s3s = [], []
    for p in range(4):
        even, odd = g_buf[2 * p], g_buf[2 * p + 1]
        c3s.append(jnp.where(low, even, odd))
        s3s.append(pltpu.roll(jnp.where(low, odd, even), 64, 1))
    c4s, s4s = raise_coef(c3s, maps[3]), raise_skel(s3s, every_second)
    c5s, s5s = raise_coef(c4s, maps[4]), raise_skel(s4s, every_second)
    set_chain([(c3s, s3s), (c4s, s4s), (c5s, s5s)], g_chain)
    for at in range(2):
        bound_send[at, 0] = c5s[0]
        bound_send[at, 1] = s5s[0] + pltpu.roll(s4s[1 - at], 3, 0)
    bound_copies = [
        remote(
            bound_send.at[side],
            bound_recv.at[side],
            bound_send_sem.at[side],
            bound_recv_sem.at[side],
            (right_box, left_box)[side],
        )
        for side in range(2)
    ]
    quad_copy = remote(
        g_chain.at[7 + quad, 0],
        quad_recv,
        bound_send_sem.at[2],
        bound_recv_sem.at[2],
        quad_device,
    )
    start(bound_copies, 1)
    pl.when(inside)(quad_copy.start)

    def set_ends(ends, into):
        for level in range(3):
            into[(0, 6, 10)[level]] = ends[0, level]
            into[(5, 9, 12)[level]] = ends[1, level]

    def near_end(tile, row, col):
        fill_tile(tile, row, col, LEAF)
        near[:, row : row + LEAF] += lax.dot_general(
            field[1, :, col : col + LEAF].astype(bf16),
            tile[:, 0:LEAF],
            NT,
            preferred_element_type=f32,
        )

    def finish_ends():
        receive(near_copies)

        @pl.when(device == 0)
        def _():
            field[:, :, 0:LEAF] = jnp.zeros((2, 8, LEAF), f32)
            edge_recv[0] = jnp.zeros((3, 2, 8, 128), f32)

        @pl.when(device == total - 1)
        def _():
            field[:, :, last + LEAF : last + 2 * LEAF] = jnp.zeros((2, 8, LEAF), f32)
            edge_recv[1] = jnp.zeros((3, 2, 8, 128), f32)

        near_end(tile_c, 0, 0)
        near_end(tile_a, last - LEAF, last + LEAF)

        receive(edge_copies)
        set_ends(edge_recv, chain)
        for at, slot in [(0, 1), (3, 4), (4, 7), (5, 8), (6, 11)]:
            local[at] = cousins(chain, slot)

    @pl.when(early == 1)
    def _():
        lax.fori_loop(ahead, 3, near_step, 0)
        set_inner()
        finish_ends()

    later = to_later[0] + to_later[1]

    @pl.when(later > 0)
    def _():
        pl.semaphore_wait(ready, 4 * later)

    for turn in range(2):

        @pl.when(to_later[turn] == 1)
        def _(turn=turn):
            far_each(turn, lambda k: far_copy(k).start())

    @pl.when(early == 0)
    def _():
        lax.fori_loop(0, 3, near_step, 0)
        set_inner()
        set_leaf_paths()
        finish_ends()

    top_column = swapped_record.T[:64]
    tx, ty, tz = top_column[:, 0:1], top_column[:, 1:2], top_column[:, 2:3]

    far_wait(far_recv_sem)

    top_coef, top_skel = [], []
    for k in range(0, strides, 2):
        halves = []
        for at in (k, k + 1):
            apart = far_from[at] - box
            counts = jnp.logical_or(apart >= 2, apart <= -2)
            halves.append((far_buf[at], counts))
        (one, one_counts), (two, two_counts) = halves
        coef = jnp.where(low, jnp.where(one_counts, one, 0.0), jnp.where(two_counts, two, 0.0))
        top_coef.append(pltpu.roll(coef, 64, 1))
        top_skel.append(jnp.where(low, two, one))
    top_tile = jnp.concatenate(
        [phi(tx, ty, tz, s[0:1], s[1:2], s[2:3], far_scale) for s in top_skel], axis=1
    )
    top = mm(jnp.concatenate(top_coef, axis=1), split(top_tile), NT)
    part_buf[member] = jnp.concatenate([top, jnp.zeros((8, 64), f32)], axis=1)
    for at in range(MEMBERS - 1):
        mate = box * MEMBERS + at + jnp.where(member <= at, 1, 0)
        send(part_buf.at[member], part_buf.at[member], part_send_sem, part_recv_sem, mate)

    wait_all(u_buf.at[pl.ds(0, MEMBERS - 1)], u_send_sem)
    wait_all(g_buf.at[pl.ds(0, MEMBERS - 1)], g_send_sem)
    far_wait(far_send_sem)
    for copies, at in ((near_copies, 0), (edge_copies, 0), (bound_copies, 1)):
        for copy, has in zip(copies, (after[at], before[at])):
            pl.when(has)(copy.wait_send)
    pl.when(inside)(quad_copy.wait_send)

    receive(bound_copies, 1)
    pl.when(inside)(quad_copy.wait_recv)
    start_skel = jnp.where(before[1], bound_recv[0, 1], 0.0)
    end_skel = jnp.where(after[1], bound_recv[1, 1], 0.0)
    g_chain[10, 0] = jnp.where(before[1], bound_recv[0, 0], 0.0)
    g_chain[10, 1] = start_skel
    g_chain[12, 0] = jnp.where(after[1], bound_recv[1, 0], 0.0)
    g_chain[12, 1] = end_skel
    quad_coef = jnp.where(inside, quad_recv[...], 0.0)
    g_chain[6, 0] = quad_coef
    g_chain[6, 1] = pltpu.roll(start_skel, 5, 0)
    g_chain[9, 0] = quad_coef
    g_chain[9, 1] = pltpu.roll(end_skel, 5, 0)

    @pl.when(jnp.logical_not(inside))
    def _():
        for slot in (0, 5):
            g_chain[slot] = jnp.zeros((2, 8, 128), f32)

    @pl.when(open_rim)
    def _():
        for copy in rim_copies:
            copy.wait_send()
        for t in range(2):
            pltpu.make_async_remote_copy(
                src_ref=g_buf.at[member],
                dst_ref=rim_recv.at[t],
                send_sem=rim_send_sem.at[t],
                recv_sem=rim_recv_sem.at[t],
                device_id=(rim_devices[t],),
                device_id_type=MESH,
            ).wait_recv()
        even, odd = rim_recv[0], rim_recv[1]
        rim_coef = jnp.where(low, even, odd)
        rim_skel = pltpu.roll(jnp.where(low, odd, even), 64, 1)
        for slot in (0, 5):
            g_chain[slot, 0] = rim_coef
            g_chain[slot, 1] = rim_skel

    local3 = cousins(g_chain, 1 + y)
    local4 = cousins(g_chain, 7 + quad)
    local5 = cousins(g_chain, 11)
    y2 = local[6]
    y1 = [x + local[4 + at] for at, x in enumerate(lower([y2], maps[1]))]
    y0 = [x + local[at] for at, x in enumerate(lower(y1, maps[0]))]
    y4 = local4 + mm(side(local5, quad), maps[4], NT)
    y3 = local3 + mm(side(y4, rem(y, 2)), maps[3], NT)
    y3 = jnp.where(core == 1, y3, pltpu.roll(y3, 64, 1))

    wait_all(part_buf.at[pl.ds(0, MEMBERS - 1)], part_recv_sem)
    parts = [part_buf[at] for at in range(MEMBERS)]
    while len(parts) > 1:
        parts = [a + b for a, b in zip(parts[0::2], parts[1::2])]
    d6 = parts[0]
    d63 = jnp.where(low, d6, y3)
    d0 = jnp.concatenate(y0, axis=1) + mm(d63, (leaf_high, leaf_low), NN)
    for p in range(4):
        pair = d0[:, 128 * p : 128 * p + 128]
        two = jnp.concatenate([jnp.where(low, pair, 0.0), jnp.where(low, 0.0, pair)], axis=0)
        rows = lax.dot_general(
            two.astype(bf16),
            basis[128 * p : 128 * p + 128, :],
            NN,
            preferred_element_type=f32,
        )
        for t in range(2):
            leaf = 2 * p + t
            at = leaf * LEAF
            out_ref[:, at : at + LEAF] = jnp.where(
                slots < occ[leaf], near[:, at : at + LEAF] + rows[8 * t : 8 * t + 8], 0.0
            )

    wait_all(part_buf.at[pl.ds(0, MEMBERS - 1)], part_send_sem)


def body(boxes, across, coords, loads, occupancy, basis, transfer):
    strides = boxes // MEMBERS
    hbm = pl.BlockSpec(memory_space=pl.ANY)
    dma = pltpu.SemaphoreType.DMA
    return pl.pallas_call(
        functools.partial(kernel, boxes, across),
        out_shape=jax.ShapeDtypeStruct((COLS, OWN), f32),
        in_specs=[hbm] * 5,
        out_specs=pl.BlockSpec(memory_space=pltpu.VMEM),
        scratch_shapes=[
            pltpu.VMEM((3, OWN), f32),
            pltpu.VMEM((COLS, OWN), bf16),
            pltpu.SMEM((LEAVES,), jnp.int32),
            pltpu.VMEM((LEAVES * 64, LEAF), bf16),
            pltpu.VMEM((6, 128, 64), f32),
            pltpu.VMEM((6, 128, 128), bf16),
            pltpu.VMEM((6, 128, 128), bf16),
            pltpu.VMEM((128, 128), f32),
            pltpu.VMEM((2, 8, OWN + 2 * LEAF), f32),
            pltpu.VMEM((OWN, 8), f32),
            pltpu.VMEM((128, 512), bf16),
            pltpu.VMEM((128, 512), bf16),
            pltpu.VMEM((COLS, OWN + LEAF), f32),
            pltpu.VMEM((LEAF, 2 * LEAF), bf16),
            pltpu.VMEM((LEAF, 2 * LEAF), bf16),
            pltpu.VMEM((LEAF, LEAF), bf16),
            pltpu.VMEM((13, 2, 8, 128), f32),
            pltpu.VMEM((13, 2, 8, 128), f32),
            pltpu.VMEM((7, 8, 128), f32),
            pltpu.VMEM((2, 3, 2, 8, 128), f32),
            pltpu.VMEM((2, 3, 2, 8, 128), f32),
            pltpu.VMEM((MEMBERS, 8, 128), f32),
            pltpu.VMEM((MEMBERS, 8, 128), f32),
            pltpu.VMEM((2, 2, 8, 128), f32),
            pltpu.VMEM((2, 2, 8, 128), f32),
            pltpu.VMEM((8, 128), f32),
            pltpu.VMEM((2, 8, 128), f32),
            pltpu.VMEM((8, 128), f32),
            pltpu.VMEM((strides, 8, 128), f32),
            pltpu.VMEM((MEMBERS, 8, 128), f32),
            dma((5,)),
            dma((2,)),
            dma((2,)),
            dma((2,)),
            dma((2,)),
            dma,
            dma,
            dma,
            dma,
            dma((3,)),
            dma((3,)),
            dma((2,)),
            dma((2,)),
            dma,
            dma,
            dma,
            dma,
            pltpu.SemaphoreType.REGULAR,
        ],
        compiler_params=pltpu.CompilerParams(
            collective_id=0, has_side_effects=True, vmem_limit_bytes=32 * 1024 * 1024
        ),
    )(
        *[
            pltpu.with_memory_space_constraint(x, pltpu.HBM)
            for x in (
                coords,
                loads,
                occupancy,
                basis.reshape(LEAVES * 64, LEAF),
                transfer.reshape(6, 128, 64),
            )
        ]
    )


def solution(mesh):
    boxes = mesh.shape["box"] // MEMBERS
    return jax.shard_map(
        functools.partial(body, boxes, 4),
        mesh=mesh,
        in_specs=(P(None, "box"), P(None, "box"), P("box"), P("box", None, None), P()),
        out_specs=P(None, "box"),
        check_vma=False,
    )
```
